32 devices in a mesh: dp: 32 (over z, y, x, core).
Axes of the slice: x: 2, y: 2, z: 4, core: 2. Of those that a mesh axis runs over, the one named last changes fastest.
Arguments:
- patches: bfloat16 [96, 256, 588], P('dp'), may hold values from -6 to 6
- valid_mask: int32 [96], replicated, may hold values from 0 to 1, as said below
- owners: int32 [12], replicated, may hold values from -1 to 31, as said below
- embedding: float32 [867, 384], P(None, 'dp')
- embedding_first: float32 [867, 384], P(None, 'dp'), may hold values from -1.1920929e-07 to 1.1920929e-07
- embedding_second: float32 [867, 384], P(None, 'dp'), may hold values from 1.790601e-17 to 2.8649616e-16
- layers: float32 [3, 4608, 384], P(None, 'dp')
- layers_first: float32 [3, 4608, 384], P(None, 'dp'), may hold values from -1.1920929e-07 to 1.1920929e-07
- layers_second: float32 [3, 4608, 384], P(None, 'dp'), may hold values from 1.790601e-17 to 2.8649616e-16
- layer_stats: float32 [3, 4, 384, 384], P(None, None, 'dp'), as said below
- layer_bases: float32 [3, 4, 384, 384], P(None, None, 'dp'), as said below
- head_hidden: float32 [2048, 2432], P('dp')
- hidden_first: float32 [2048, 2432], P('dp'), may hold values from -1.1920929e-07 to 1.1920929e-07
- hidden_second: float32 [2048, 2432], P('dp'), may hold values from 1.790601e-17 to 2.8649616e-16
- head_last: float32 [2048, 256], P(None, 'dp'), may hold values from -0.125 to 0.125
- last_first: float32 [2048, 256], P(None, 'dp'), may hold values from -1.1920929e-07 to 1.1920929e-07
- last_second: float32 [2048, 256], P(None, 'dp'), may hold values from 1.790601e-17 to 2.8649616e-16
- protos: float32 [256, 65536], P(None, 'dp')
- protos_first: float32 [256, 65536], P(None, 'dp'), may hold values from -1.1920929e-07 to 1.1920929e-07
- protos_second: float32 [256, 65536], P(None, 'dp'), may hold values from 1.790601e-17 to 2.8649616e-16
- teacher_embedding: float32 [867, 384], P(None, 'dp')
- teacher_layers: float32 [3, 4608, 384], P(None, 'dp')
- teacher_hidden: float32 [2048, 2432], P('dp')
- teacher_last: float32 [2048, 256], P(None, 'dp'), may hold values from -0.125 to 0.125
- teacher_protos: float32 [256, 65536], P(None, 'dp')
- centre: float32 [65536], P('dp'), may hold values from -0.3 to 0.3
Outputs:
- loss_sum: float32 [], replicated
- loss_count: float32 [], replicated
- grad_norm: float32 [], replicated
- next_embedding_first: float32 [867, 384], P(None, 'dp')
- next_embedding_second: float32 [867, 384], P(None, 'dp')
- next_embedding: float32 [867, 384], P(None, 'dp')
- next_layers_first: float32 [3, 4608, 384], P(None, 'dp')
- next_layers_second: float32 [3, 4608, 384], P(None, 'dp')
- next_layers: float32 [3, 4608, 384], P(None, 'dp')
- next_stats: float32 [3, 4, 384, 384], P(None, None, 'dp')
- next_bases: float32 [3, 4, 384, 384], P(None, None, 'dp')
- next_hidden_first: float32 [2048, 2432], P('dp')
- next_hidden_second: float32 [2048, 2432], P('dp')
- next_hidden: float32 [2048, 2432], P('dp')
- next_last_first: float32 [2048, 256], P(None, 'dp')
- next_last_second: float32 [2048, 256], P(None, 'dp')
- next_last: float32 [2048, 256], P(None, 'dp')
- next_protos_first: float32 [256, 65536], P(None, 'dp')
- next_protos_second: float32 [256, 65536], P(None, 'dp')
- next_protos: float32 [256, 65536], P(None, 'dp')
- next_teacher_embedding: float32 [867, 384], P(None, 'dp')
- next_teacher_layers: float32 [3, 4608, 384], P(None, 'dp')
- next_teacher_hidden: float32 [2048, 2432], P('dp')
- next_teacher_last: float32 [2048, 256], P(None, 'dp')
- next_teacher_protos: float32 [256, 65536], P(None, 'dp')
- next_centre: float32 [65536], P('dp')
The draws below stay inside these ranges and needn't reach their ends.
Inputs may be any that keep to these rules, and one draw needn't show every extreme that they name: `valid_mask`: 1 marks an image that counts; the last image never counts, the one before it always. `owners`: -1 where layer matrix m keeps its basis, else the device that renews it. Each slice layer_stats[l, j] is symmetric positive definite. Each slice layer_bases[l, j] is orthogonal.
All inputs are finite; a program needn't handle non-finite values.
Results may differ from the reference program's by a relative error of at most 0.013.
The reference program's roundings to bfloat16 on the way count: a program that leaves them out, or rounds other values in their place, can miss the bound.
Values may be sent and summed in bfloat16 or wider, within the bound.
A program may use at most 256 MiB of HBM per device.

```python
import math
import jax
import jax.numpy as jnp
from jax import lax

D = 384
HEADS = 6
HEAD_DIM = 64
MLP = 1536
HID = 2048
BOT = 256
PROTOS = 65536
PATCHES = 256
PIX = 588
LAYERS = 3
STEP = 10
IMG_DEV = 3
SEQ = 257
IMAGES = 96
WL = 4608
EROWS = 867
HROWS = 2432
NPARAM = 27923584
N_DP = 32


def ramp_gain(key, count):
    position = jnp.arange(D, dtype=jnp.float32) / (D - 1)
    jitter = jax.random.uniform(key, (count, D), jnp.float32, 0.85, 1.15)
    return (0.5 + position) * jitter


def embed_common(key):
    keys_all = jax.random.split(key, 5)
    count = LAYERS * 6 + 4
    patch_rows = jax.random.normal(keys_all[0], (PIX, D), jnp.float32) * PIX ** (-0.5)
    position = jax.random.normal(keys_all[1], (SEQ, D), jnp.float32) * 0.5
    gains = ramp_gain(keys_all[2], count)
    shifts = jax.random.normal(keys_all[3], (count, D), jnp.float32) * 0.2
    classes = jax.random.normal(keys_all[4], (count, D), jnp.float32)
    rows = jnp.arange(count)[:, None]
    within = rows % 6
    in_layer = rows < 6 * LAYERS
    is_gain = jnp.where(in_layer, (within == 0) | (within == 2) | (within >= 4), rows == 6 * LAYERS + 2)
    vectors = jnp.where(is_gain, gains, jnp.where(rows == 6 * LAYERS + 1, classes, shifts))
    return jnp.concatenate([patch_rows, position, vectors], 0)


def draw_embedding(key, part):
    return embed_common(jax.random.fold_in(key, 11))


def draw_teacher_embedding(key, part):
    return embed_common(jax.random.fold_in(key, 12))


def layers_common(key):
    raw = jax.random.normal(key, (LAYERS, WL, D), jnp.float32)
    row = jnp.arange(WL) % (WL // N_DP)
    first_cut = 3 * D // N_DP
    second_cut = first_cut + D // N_DP
    third_cut = second_cut + MLP // N_DP
    scale = jnp.where(row < first_cut, D ** (-0.5), jnp.where(row < second_cut, 2.0 * D ** (-0.5), jnp.where(row < third_cut, D ** (-0.5), MLP ** (-0.5))))
    return raw * scale[None, :, None]


def draw_layers(key, part):
    return layers_common(jax.random.fold_in(key, 21))


def draw_teacher_layers(key, part):
    return layers_common(jax.random.fold_in(key, 22))


def hidden_common(key):
    raw = jax.random.normal(key, (HID, HROWS), jnp.float32)
    column = jnp.arange(HROWS)[None, :]
    return raw * jnp.where(column < D, D ** (-0.5), HID ** (-0.5))


def draw_head_hidden(key, part):
    return hidden_common(jax.random.fold_in(key, 31))


def draw_teacher_hidden(key, part):
    return hidden_common(jax.random.fold_in(key, 32))


def protos_common(key):
    raw = jax.random.normal(key, (BOT, PROTOS), jnp.float32)
    column = jnp.arange(PROTOS, dtype=jnp.float32) / (PROTOS - 1)
    return raw * 0.07 * (1.0 + 2.0 * column)


def draw_protos(key, part):
    return protos_common(jax.random.fold_in(key, 41))


def draw_teacher_protos(key, part):
    return protos_common(jax.random.fold_in(key, 42))


def draw_layer_stats(key, part):
    keys_all = jax.random.split(jax.random.fold_in(key, 51), 2)
    squared = 1e-06 / NPARAM
    widths = jnp.array([3 * D, D, MLP, MLP], jnp.float32)
    base = 0.05 / 0.95 * widths * squared
    diagonal = jnp.exp(jax.random.uniform(keys_all[0], (LAYERS, 4, D), jnp.float32, 0.0, math.log(4.0)))
    noise = jax.random.normal(keys_all[1], (LAYERS, 4, D, D), jnp.float32)
    noise = (noise + jnp.swapaxes(noise, -1, -2)) * 0.7071067811865476
    identity = (jnp.arange(D)[:, None] == jnp.arange(D)[None, :]).astype(jnp.float32)
    shaped = identity * diagonal[..., None] + (1.0 - identity) * noise * (0.4 / math.sqrt(D))
    return base[None, :, None, None] * shaped


def draw_layer_bases(key, part):
    keys_all = jax.random.split(jax.random.fold_in(key, 61), 2)
    count = LAYERS * 4
    orders = jax.vmap(lambda subkey: jax.random.permutation(subkey, D))(jax.random.split(keys_all[0], count))
    signs = (jax.random.randint(keys_all[1], (count, D), 0, 2) * 2 - 1).astype(jnp.float32)
    rows = jnp.arange(D, dtype=jnp.float32)[None, :, None]
    frequency = orders.astype(jnp.float32)[:, None, :]
    weights_col = jnp.where(orders == 0, 0.7071067811865476, 1.0)[:, None, :]
    table = math.sqrt(2.0 / D) * weights_col * jnp.cos(math.pi * (rows + 0.5) * frequency / D) * signs[:, :, None]
    return table.reshape(LAYERS, 4, D, D)


def draw_valid_mask(key, part):
    index = jnp.arange(IMAGES)
    device = index // IMG_DEV
    count = IMAGES // IMG_DEV
    threshold = 350 + 650 * device // max(count - 1, 1)
    rolls = jax.random.randint(jax.random.fold_in(key, 71), (IMAGES,), 0, 1000)
    valid = (rolls < threshold).astype(jnp.int32)
    valid = jnp.where(index == IMAGES - 1, 0, valid)
    return jnp.where(index == IMAGES - 2, 1, valid).astype(jnp.int32)


def draw_owners(key, part):
    keys_all = jax.random.split(jax.random.fold_in(key, 81), 2)
    count = LAYERS * 4
    order = jax.random.permutation(keys_all[0], count)
    chosen = jax.random.randint(keys_all[1], (count,), 0, N_DP)
    owner = jnp.where(order == 0, N_DP - 1, jnp.where(order == 1, 0, jnp.where(order % 3 == 2, -1, chosen)))
    return owner.astype(jnp.int32)


def steps_of(stream_key, shape, cuts, least, top_value):
    def one(dim, blocks):
        steps = jax.random.uniform(jax.random.fold_in(jax.random.fold_in(stream_key, 6), dim), (blocks,), jnp.float32, least / len(cuts), top_value / len(cuts))
        return jnp.repeat(jnp.exp(steps), shape[dim] // blocks).reshape((-1,) + (1,) * (len(shape) - dim - 1))

    level = one(*cuts[0])
    for cut in cuts[1:]:
        level = level * one(*cut)
    return level


def bell_draw(stream_key, extent, scale, limit, cuts=(), kind=jnp.bfloat16):
    level = steps_of(stream_key, extent, cuts, -0.22, 0.18) if cuts else 1.0
    result = jax.random.normal(stream_key, extent, jnp.float32) * scale * level
    return jnp.minimum(jnp.maximum(result, -limit), limit).astype(kind)


def setup_inputs(seed: int = 0) -> dict:
    key_of = jax.random.split(jax.random.key(seed), 27)
    return {
        "patches": bell_draw(key_of[0], (IMAGES, PATCHES, PIX), 1.0, 6.0, ((0, 32),)),
        "valid_mask": draw_valid_mask(jax.random.fold_in(key_of[26], 71), 0),
        "owners": draw_owners(jax.random.fold_in(key_of[26], 71), 0),
        "embedding": draw_embedding(jax.random.fold_in(key_of[26], 71), 0),
        "embedding_first": bell_draw(key_of[4], (EROWS, D), (0.111 * 0.001 / NPARAM ** 0.5), 1.1920928955078125e-07, ((1, 32),), jnp.float32),
        "embedding_second": jnp.clip(jnp.exp(math.log(2.8649616244477867e-16) - 2.7725887 * jax.random.uniform(key_of[5], (EROWS, D), jnp.float32) ** steps_of(key_of[5], (EROWS, D), ((1, 32),), -0.2, 0.2)), 1.7906010152798667e-17, 2.8649616244477867e-16),
        "layers": draw_layers(jax.random.fold_in(key_of[26], 71), 0),
        "layers_first": bell_draw(key_of[7], (LAYERS, WL, D), (0.111 * 0.001 / NPARAM ** 0.5), 1.1920928955078125e-07, ((1, 32),), jnp.float32),
        "layers_second": jnp.clip(jnp.exp(math.log(2.8649616244477867e-16) - 2.7725887 * jax.random.uniform(key_of[8], (LAYERS, WL, D), jnp.float32) ** steps_of(key_of[8], (LAYERS, WL, D), ((1, 32),), -0.2, 0.2)), 1.7906010152798667e-17, 2.8649616244477867e-16),
        "layer_stats": draw_layer_stats(jax.random.fold_in(key_of[26], 71), 0),
        "layer_bases": draw_layer_bases(jax.random.fold_in(key_of[26], 71), 0),
        "head_hidden": draw_head_hidden(jax.random.fold_in(key_of[26], 71), 0),
        "hidden_first": bell_draw(key_of[12], (HID, HROWS), (0.111 * 0.001 / NPARAM ** 0.5), 1.1920928955078125e-07, ((0, 32),), jnp.float32),
        "hidden_second": jnp.clip(jnp.exp(math.log(2.8649616244477867e-16) - 2.7725887 * jax.random.uniform(key_of[13], (HID, HROWS), jnp.float32) ** steps_of(key_of[13], (HID, HROWS), ((0, 32),), -0.2, 0.2)), 1.7906010152798667e-17, 2.8649616244477867e-16),
        "head_last": bell_draw(key_of[14], (HID, BOT), HID ** -0.5, 0.125, ((1, 32),), jnp.float32),
        "last_first": bell_draw(key_of[15], (HID, BOT), (0.111 * 0.001 / NPARAM ** 0.5), 1.1920928955078125e-07, ((1, 32),), jnp.float32),
        "last_second": jnp.clip(jnp.exp(math.log(2.8649616244477867e-16) - 2.7725887 * jax.random.uniform(key_of[16], (HID, BOT), jnp.float32) ** steps_of(key_of[16], (HID, BOT), ((1, 32),), -0.2, 0.2)), 1.7906010152798667e-17, 2.8649616244477867e-16),
        "protos": draw_protos(jax.random.fold_in(key_of[26], 71), 0),
        "protos_first": bell_draw(key_of[18], (BOT, PROTOS), (0.111 * 0.001 / NPARAM ** 0.5), 1.1920928955078125e-07, ((1, 32),), jnp.float32),
        "protos_second": jnp.clip(jnp.exp(math.log(2.8649616244477867e-16) - 2.7725887 * jax.random.uniform(key_of[19], (BOT, PROTOS), jnp.float32) ** steps_of(key_of[19], (BOT, PROTOS), ((1, 32),), -0.2, 0.2)), 1.7906010152798667e-17, 2.8649616244477867e-16),
        "teacher_embedding": draw_teacher_embedding(jax.random.fold_in(key_of[26], 71), 0),
        "teacher_layers": draw_teacher_layers(jax.random.fold_in(key_of[26], 71), 0),
        "teacher_hidden": draw_teacher_hidden(jax.random.fold_in(key_of[26], 71), 0),
        "teacher_last": bell_draw(key_of[23], (HID, BOT), HID ** -0.5, 0.125, ((1, 32),), jnp.float32),
        "teacher_protos": draw_teacher_protos(jax.random.fold_in(key_of[26], 71), 0),
        "centre": bell_draw(key_of[25], (PROTOS,), 0.05, 0.3, ((0, 32),), jnp.float32),
    }


NORM_EPSILON = 1e-06
UNIT_EPSILON = 1e-06
TAU_STUDENT = 0.1
TAU_TEACHER = 0.07
CLIP_MAX = 0.001
BETA_ONE = 0.9
BETA_TWO = 0.999
ADAM_EPSILON = 1e-08
WEIGHT_DECAY = 0.04
RATE_MATRIX = 0.04
RATE_VECTOR = 0.2
BETA_STAT = 0.95
TEACHER_MOMENTUM = 0.8
CENTRE_MOMENTUM = 0.9

@jax.custom_vjp
def low(v):
    return lax.optimization_barrier(v.astype(jnp.bfloat16)).astype(jnp.float32)

@jax.custom_vjp
def low_back(v):
    return v

def low_keep(v):
    return (low(v), None)

def low_pass(kept, grad):
    return (grad,)

def back_keep(v):
    return (v, None)

def back_low(kept, grad):
    return (low(grad),)
low.defvjp(low_keep, low_pass)
low_back.defvjp(back_keep, back_low)

def product(form, left, right):
    return jnp.einsum(form, left, right, precision=lax.Precision.HIGHEST)

def layer_norm(values, gain_row, shift_row):
    centred = values - lax.optimization_barrier(jnp.mean(values, -1, keepdims=True))
    inverse_std = lax.rsqrt(lax.optimization_barrier(jnp.mean(centred * centred, -1, keepdims=True)) + NORM_EPSILON)
    return centred * inverse_std * gain_row + shift_row

def layer_bounds():
    widths = [3 * D // N_DP, D // N_DP, MLP // N_DP, MLP // N_DP]
    lowers = [0, widths[0], widths[0] + widths[1], widths[0] + widths[1] + widths[2]]
    return [(lowers[segment], lowers[segment] + widths[segment]) for segment in range(4)]

def split_layer(weights):
    blocks = weights.reshape(N_DP, -1, D)
    return [blocks[:, lower_row:upper_row].reshape(-1, D) for lower_row, upper_row in layer_bounds()]

def layer_apply(inputs, weights, vectors):
    joint_weight, output_weight, inner_weight, outer_weight = split_layer(weights)
    images, tokens = (inputs.shape[0], inputs.shape[1])
    normed = low(layer_norm(inputs, vectors[0], vectors[1]))
    joint = low(low_back(product('itd,ed->ite', normed, joint_weight)))
    head_split = joint.reshape(images, tokens, 3, HEADS, HEAD_DIM)
    scores = low_back(product('ithd,ishd->ihts', head_split[:, :, 0], head_split[:, :, 1]) * HEAD_DIM ** (-0.5))
    attention = jax.nn.softmax(scores, axis=-1)
    mixed_heads = low(low_back(product('ihts,ishd->ithd', low(attention), head_split[:, :, 2])))
    attended = low_back(product('itd,ed->ite', mixed_heads.reshape(images, tokens, D), output_weight))
    middle = inputs + vectors[4] * attended
    normed_two = low(layer_norm(middle, vectors[2], vectors[3]))
    inner_pre = low_back(product('itd,md->itm', normed_two, inner_weight))
    activated = low(jax.nn.gelu(inner_pre, approximate=False))
    outer_out = low_back(product('itm,md->itd', activated, outer_weight))
    return middle + vectors[5] * outer_out

def backbone(pixels, embed_table, layer_stack):
    patch_weight = embed_table[:PIX]
    position = embed_table[PIX:PIX + SEQ]
    vectors = embed_table[PIX + SEQ:PIX + SEQ + 6 * LAYERS].reshape(LAYERS, 6, D)
    tail_rows = embed_table[PIX + SEQ + 6 * LAYERS:]
    projected = low_back(product('ipc,cd->ipd', pixels, patch_weight)) + tail_rows[0]
    leading = jnp.broadcast_to(tail_rows[1] + position[0], (pixels.shape[0], 1, D))
    current = jnp.concatenate([leading, projected + position[1:]], 1)

    def advance(carried, layer_inputs):
        return (jax.checkpoint(layer_apply)(carried, layer_inputs[0], layer_inputs[1]), None)
    current, unused = lax.scan(advance, current, (layer_stack, vectors))
    return low(layer_norm(current[:, 0], tail_rows[2], tail_rows[3]))

def head_logits(features, hidden_weight, last_weight, proto_weight):
    pre_one = low_back(product('bd,hd->bh', features, hidden_weight[:, :D]))
    act_one = low(jax.nn.gelu(pre_one, approximate=False))
    pre_two = low_back(product('bh,kh->bk', act_one, hidden_weight[:, D:]))
    act_two = low(jax.nn.gelu(pre_two, approximate=False))
    bottle = low_back(product('bh,hc->bc', act_two, last_weight))
    unit = bottle * lax.rsqrt(lax.optimization_barrier(jnp.sum(bottle * bottle, -1, keepdims=True)) + UNIT_EPSILON)
    return low_back(product('bc,cp->bp', low(unit), proto_weight))

def adam_step(weight, grad, first_moment, second_moment, rate, decay):
    first_new = BETA_ONE * first_moment + (1.0 - BETA_ONE) * grad
    second_new = BETA_TWO * second_moment + (1.0 - BETA_TWO) * grad * grad
    direction = first_new / (1.0 - BETA_ONE ** STEP) / (jnp.sqrt(second_new / (1.0 - BETA_TWO ** STEP)) + ADAM_EPSILON)
    return (first_new, second_new, weight - rate * (direction + decay * weight))

def renew(stat_matrix, basis):
    scaled = jnp.dot(stat_matrix, basis, precision=lax.Precision.HIGHEST) * (D / jnp.trace(stat_matrix))
    gram = jnp.dot(scaled.T, scaled, precision=lax.Precision.HIGHEST)
    lower_factor = jnp.linalg.cholesky(gram)
    return lax.linalg.triangular_solve(lower_factor, scaled.T, left_side=True, lower=True).T

def reference(patches, valid_mask, owners, embedding, embedding_first, embedding_second, layers, layers_first, layers_second, layer_stats, layer_bases, head_hidden, hidden_first, hidden_second, head_last, last_first, last_second, protos, protos_first, protos_second, teacher_embedding, teacher_layers, teacher_hidden, teacher_last, teacher_protos, centre):
    pixels = patches.astype(jnp.float32)
    counted = valid_mask.astype(jnp.float32)
    loss_count = jnp.sum(counted)
    teacher_features = backbone(pixels, low(teacher_embedding), low(teacher_layers))
    teacher_logits = head_logits(teacher_features, low(teacher_hidden), low(teacher_last), low(teacher_protos))
    teacher_prob = jax.nn.softmax((teacher_logits - centre) / TAU_TEACHER, axis=-1)

    def objective(embed_weight, layer_weight, hidden_weight, last_weight, proto_weight):
        features = backbone(pixels, low(embed_weight), low(layer_weight))
        logits = head_logits(features, low(hidden_weight), low(last_weight), low(proto_weight))
        log_probs = jax.nn.log_softmax(logits / TAU_STUDENT, axis=-1)
        total = jnp.sum(counted * -lax.optimization_barrier(jnp.sum(teacher_prob * log_probs, -1)))
        return (total / loss_count, total)
    objective_value, pullback, loss_sum = jax.vjp(objective, embedding, layers, head_hidden, head_last, protos, has_aux=True)
    grads = pullback(jnp.ones_like(objective_value))
    grad_norm = jnp.sqrt(jnp.sum(jnp.stack([jnp.sum(member * member) for member in grads])))
    clip_factor = jnp.minimum(1.0, CLIP_MAX / (grad_norm + 1e-06))
    grad_embed, grad_layers, grad_hidden, grad_last, grad_protos = [member * clip_factor for member in grads]
    rows = jnp.arange(EROWS)[:, None]
    is_matrix = rows < PIX + SEQ
    embed_out = adam_step(embedding, grad_embed, embedding_first, embedding_second, jnp.where(is_matrix, RATE_MATRIX, RATE_VECTOR), jnp.where(is_matrix, WEIGHT_DECAY, 0.0))
    hidden_out = adam_step(head_hidden, grad_hidden, hidden_first, hidden_second, RATE_MATRIX, WEIGHT_DECAY)
    last_out = adam_step(head_last, grad_last, last_first, last_second, RATE_MATRIX, WEIGHT_DECAY)
    protos_out = adam_step(protos, grad_protos, protos_first, protos_second, RATE_MATRIX, WEIGHT_DECAY)
    shaped = [member.reshape(LAYERS, N_DP, -1, D) for member in (layers, grad_layers, layers_first, layers_second)]
    firsts, seconds, weights_new, grams = ([], [], [], [])
    for segment, (lower_row, upper_row) in enumerate(layer_bounds()):
        basis = layer_bases[:, segment]
        weight_block, grad_block, first_block, second_block = [member[:, :, lower_row:upper_row] for member in shaped]
        rotated = product('lncd,ldk->lnck', grad_block, basis)
        first_new = BETA_ONE * first_block + (1.0 - BETA_ONE) * rotated
        second_new = BETA_TWO * second_block + (1.0 - BETA_TWO) * rotated * rotated
        direction = first_new / (1.0 - BETA_ONE ** STEP) / (jnp.sqrt(second_new / (1.0 - BETA_TWO ** STEP)) + ADAM_EPSILON)
        update = product('lnck,ldk->lncd', direction, basis)
        firsts.append(first_new)
        seconds.append(second_new)
        weights_new.append(weight_block - RATE_MATRIX * (update + WEIGHT_DECAY * weight_block))
        grams.append(product('lncd,lnce->lde', grad_block, grad_block))
    next_layers_first = jnp.concatenate(firsts, 2).reshape(LAYERS, WL, D)
    next_layers_second = jnp.concatenate(seconds, 2).reshape(LAYERS, WL, D)
    next_layers = jnp.concatenate(weights_new, 2).reshape(LAYERS, WL, D)
    next_stats = BETA_STAT * layer_stats + (1.0 - BETA_STAT) * jnp.stack(grams, 1)
    flat_bases = layer_bases.reshape(LAYERS * 4, D, D)
    renewed = jax.vmap(renew)(next_stats.reshape(LAYERS * 4, D, D), flat_bases)
    next_bases = jnp.where(owners[:, None, None] >= 0, renewed, flat_bases).reshape(LAYERS, 4, D, D)

    def follow(teacher_weight, student_weight):
        return TEACHER_MOMENTUM * teacher_weight + (1.0 - TEACHER_MOMENTUM) * student_weight
    next_centre = CENTRE_MOMENTUM * centre + (1.0 - CENTRE_MOMENTUM) * lax.optimization_barrier(jnp.sum(counted[:, None] * teacher_logits, 0)) / loss_count
    return (loss_sum, loss_count, grad_norm, embed_out[0], embed_out[1], embed_out[2], next_layers_first, next_layers_second, next_layers, next_stats, next_bases, hidden_out[0], hidden_out[1], hidden_out[2], last_out[0], last_out[1], last_out[2], protos_out[0], protos_out[1], protos_out[2], follow(teacher_embedding, embed_out[2]), follow(teacher_layers, next_layers), follow(teacher_hidden, hidden_out[2]), follow(teacher_last, last_out[2]), follow(teacher_protos, protos_out[2]), next_centre)
```

```python
import functools

import jax
import jax.numpy as jnp
from jax import lax
from jax.experimental import pallas as pl
from jax.experimental.pallas import tpu as pltpu
from jax.sharding import PartitionSpec as P

D = 384
HEADS = 6
HEAD_DIM = 64
MLP = 1536
PIX = 588
LAYERS = 3
STEP = 10
SEQ = 257


NORM_EPSILON = 1e-06
UNIT_EPSILON = 1e-06
TAU_STUDENT = 0.1
TAU_TEACHER = 0.07
CLIP_MAX = 0.001
BETA_ONE = 0.9
BETA_TWO = 0.999
ADAM_EPSILON = 1e-08
WEIGHT_DECAY = 0.04
RATE_MATRIX = 0.04
RATE_VECTOR = 0.2
BETA_STAT = 0.95
TEACHER_MOMENTUM = 0.8
CENTRE_MOMENTUM = 0.9
ROOT_HALF = 0.7071067811865476
DENSITY_SCALE = 0.3989422804014327


def joined(value, axis, join):
    pieces = jax.tree.map(lambda part: lax.all_gather(part, axis), value)
    head = jax.tree.map(lambda part: part[0], pieces)
    tail = jax.tree.map(lambda part: part[1:], pieces)
    running, _ = lax.scan(lambda running, piece: (join(running, piece), None), head, tail)
    return running


def matmul_low(form, left, right):
    return jnp.einsum(form, left, right, preferred_element_type=jnp.float32)


def matmul_high(form, left, right):
    return jnp.einsum(form, left, right, precision=lax.Precision.HIGHEST)


def layer_norm(values, gain_row, shift_row):
    centred = values - jnp.mean(values, -1, keepdims=True)
    inverse_std = lax.rsqrt(jnp.mean(centred * centred, -1, keepdims=True) + NORM_EPSILON)
    return centred * inverse_std * gain_row + shift_row


def norm_back(values, gain_row, grad_out):
    centred = values - jnp.mean(values, -1, keepdims=True)
    inverse_std = lax.rsqrt(jnp.mean(centred * centred, -1, keepdims=True) + NORM_EPSILON)
    normed = centred * inverse_std
    scaled_grad = grad_out * gain_row
    grad_in = inverse_std * (
        scaled_grad
        - jnp.mean(scaled_grad, -1, keepdims=True)
        - normed * jnp.mean(scaled_grad * normed, -1, keepdims=True)
    )
    leading = tuple(range(values.ndim - 1))
    return (grad_in, jnp.sum(grad_out * normed, leading), jnp.sum(grad_out, leading))


def gelu_exact(values):
    return 0.5 * values * (1.0 + lax.erf(values * ROOT_HALF))


def gelu_slope(values):
    return (
        0.5 * (1.0 + lax.erf(values * ROOT_HALF))
        + values * jnp.exp(-0.5 * values * values) * DENSITY_SCALE
    )


def layer_bounds(devices):
    widths = [3 * D // devices, D // devices, MLP // devices, MLP // devices]
    lowers = [0, widths[0], widths[0] + widths[1], widths[0] + widths[1] + widths[2]]
    return [(lowers[segment], lowers[segment] + widths[segment]) for segment in range(4)]


def split_layer(weights, devices):
    blocks = weights.reshape(devices, -1, D)
    return [
        blocks[:, lower_row:upper_row].reshape(-1, D)
        for lower_row, upper_row in layer_bounds(devices)
    ]


def join_layer(members, devices):
    return jnp.concatenate([member.reshape(devices, -1, D) for member in members], 1).reshape(-1, D)


def layer_parts(inputs, matrices, vectors):
    joint_weight, output_weight, inner_weight, outer_weight = matrices
    images, tokens = (inputs.shape[0], inputs.shape[1])
    normed = layer_norm(inputs, vectors[0], vectors[1]).astype(jnp.bfloat16)
    joint = matmul_low("itd,ed->ite", normed, joint_weight).astype(jnp.bfloat16)
    head_split = joint.reshape(images, tokens, 3, HEADS, HEAD_DIM)
    queries, keys_in, values_in = (head_split[:, :, 0], head_split[:, :, 1], head_split[:, :, 2])
    scores = matmul_low("ithd,ishd->ihts", queries, keys_in) * HEAD_DIM ** (-0.5)
    attention = jax.nn.softmax(scores, axis=-1)
    mixed_heads = (
        matmul_low("ihts,ishd->ithd", attention.astype(jnp.bfloat16), values_in)
        .astype(jnp.bfloat16)
        .reshape(images, tokens, D)
    )
    attended = matmul_low("itd,ed->ite", mixed_heads, output_weight)
    middle = inputs + vectors[4] * attended
    normed_two = layer_norm(middle, vectors[2], vectors[3]).astype(jnp.bfloat16)
    inner_pre = matmul_low("itd,md->itm", normed_two, inner_weight)
    activated = gelu_exact(inner_pre).astype(jnp.bfloat16)
    outer_out = matmul_low("itm,md->itd", activated, outer_weight)
    result = middle + vectors[5] * outer_out
    return (
        normed,
        queries,
        keys_in,
        values_in,
        attention,
        mixed_heads,
        attended,
        middle,
        normed_two,
        inner_pre,
        activated,
        outer_out,
        result,
    )


def layer_backward(inputs, matrices, vectors, grad_result):
    joint_weight, output_weight, inner_weight, outer_weight = matrices
    (
        normed,
        queries,
        keys_in,
        values_in,
        attention,
        mixed_heads,
        attended,
        middle,
        normed_two,
        inner_pre,
        activated,
        outer_out,
        result,
    ) = layer_parts(inputs, matrices, vectors)
    images, tokens = (inputs.shape[0], inputs.shape[1])
    grad_outer = (vectors[5] * grad_result).astype(jnp.bfloat16)
    grad_scale_two = jnp.sum(grad_result * outer_out, (0, 1))
    grad_outer_weight = matmul_low("itm,itd->md", activated, grad_outer)
    grad_activated = matmul_low("itd,md->itm", grad_outer, outer_weight)
    grad_inner = (grad_activated * gelu_slope(inner_pre)).astype(jnp.bfloat16)
    grad_inner_weight = matmul_low("itm,itd->md", grad_inner, normed_two)
    grad_normed_two = matmul_low("itm,md->itd", grad_inner, inner_weight)
    grad_middle_norm, grad_gain_two, grad_shift_two = norm_back(middle, vectors[2], grad_normed_two)
    grad_middle = grad_result + grad_middle_norm
    grad_attended = (vectors[4] * grad_middle).astype(jnp.bfloat16)
    grad_scale_one = jnp.sum(grad_middle * attended, (0, 1))
    grad_output_weight = matmul_low("ite,itd->ed", grad_attended, mixed_heads)
    grad_mixed = (
        matmul_low("ite,ed->itd", grad_attended, output_weight)
        .astype(jnp.bfloat16)
        .reshape(images, tokens, HEADS, HEAD_DIM)
    )
    grad_attention = matmul_low("ithd,ishd->ihts", grad_mixed, values_in)
    grad_values = matmul_low("ihts,ithd->ishd", attention.astype(jnp.bfloat16), grad_mixed)
    grad_scores = (
        attention * (grad_attention - jnp.sum(attention * grad_attention, -1, keepdims=True))
    ).astype(jnp.bfloat16)
    grad_queries = matmul_low("ihts,ishd->ithd", grad_scores, keys_in) * HEAD_DIM ** (-0.5)
    grad_keys = matmul_low("ihts,ithd->ishd", grad_scores, queries) * HEAD_DIM ** (-0.5)
    grad_joint = (
        jnp.stack([grad_queries, grad_keys, grad_values], 2)
        .astype(jnp.bfloat16)
        .reshape(images, tokens, 3 * D)
    )
    grad_joint_weight = matmul_low("ite,itd->ed", grad_joint, normed)
    grad_normed = matmul_low("ite,ed->itd", grad_joint, joint_weight)
    grad_input_norm, grad_gain_one, grad_shift_one = norm_back(inputs, vectors[0], grad_normed)
    grad_vectors = jnp.stack(
        [
            grad_gain_one,
            grad_shift_one,
            grad_gain_two,
            grad_shift_two,
            grad_scale_one,
            grad_scale_two,
        ]
    )
    return (
        grad_middle + grad_input_norm,
        (grad_joint_weight, grad_output_weight, grad_inner_weight, grad_outer_weight),
        grad_vectors,
    )


def table_vectors(embed_table):
    return embed_table[PIX + SEQ : PIX + SEQ + 6 * LAYERS].astype(jnp.float32).reshape(LAYERS, 6, D)


def table_tail(embed_table):
    return embed_table[PIX + SEQ + 6 * LAYERS :].astype(jnp.float32)


def backbone(patches, embed_table, layer_stack, devices):
    vectors = table_vectors(embed_table)
    tail_rows = table_tail(embed_table)
    position = embed_table[PIX : PIX + SEQ].astype(jnp.float32)
    projected = matmul_low("ipc,cd->ipd", patches, embed_table[:PIX]) + tail_rows[0]
    leading = jnp.broadcast_to(tail_rows[1] + position[0], (patches.shape[0], 1, D))
    current = jnp.concatenate([leading, projected + position[1:]], 1)
    layer_inputs = []
    for layer_number in range(LAYERS):
        layer_inputs.append(current)
        current = layer_parts(
            current, split_layer(layer_stack[layer_number], devices), vectors[layer_number]
        )[-1]
    features = layer_norm(current[:, 0], tail_rows[2], tail_rows[3]).astype(jnp.bfloat16)
    return (features, layer_inputs, current)


def unchanged(values):
    return values


def backbone_back(
    patches,
    embed_table,
    layer_stack,
    layer_inputs,
    final_state,
    grad_features,
    devices,
    reduce_layer,
):
    vectors = table_vectors(embed_table)
    tail_rows = table_tail(embed_table)
    grad_cls, grad_gain, grad_shift = norm_back(final_state[:, 0], tail_rows[2], grad_features)
    grad_current = jnp.concatenate(
        [grad_cls[:, None], jnp.zeros((final_state.shape[0], SEQ - 1, D), jnp.float32)], 1
    )
    weight_grads = [None] * LAYERS
    vector_grads = [None] * LAYERS
    for layer_number in reversed(range(LAYERS)):
        grad_current, matrices, grad_vectors = layer_backward(
            layer_inputs[layer_number],
            split_layer(layer_stack[layer_number], devices),
            vectors[layer_number],
            grad_current,
        )
        weight_grads[layer_number] = reduce_layer(join_layer(matrices, devices))
        vector_grads[layer_number] = grad_vectors
    grad_patch_weight = matmul_low("ipc,ipd->cd", patches, grad_current[:, 1:].astype(jnp.bfloat16))
    grad_position = jnp.sum(grad_current, 0)
    tail_grads = jnp.stack(
        [
            jnp.sum(grad_current[:, 1:], (0, 1)),
            jnp.sum(grad_current[:, 0], 0),
            grad_gain,
            grad_shift,
        ]
    )
    grad_table = jnp.concatenate(
        [grad_patch_weight, grad_position, jnp.concatenate(vector_grads, 0), tail_grads], 0
    )
    return (grad_table, jnp.stack(weight_grads))


def unit_rows(bottle):
    inverse_norm = lax.rsqrt(jnp.sum(bottle * bottle, -1, keepdims=True) + UNIT_EPSILON)
    return (bottle * inverse_norm, inverse_norm)


def combine_parts(left_part, right_part):
    top_student = jnp.maximum(left_part[0], right_part[0])
    total_student = left_part[1] * jnp.exp(left_part[0] - top_student) + right_part[1] * jnp.exp(
        right_part[0] - top_student
    )
    top_teacher = jnp.maximum(left_part[2], right_part[2])
    left_weight = jnp.exp(left_part[2] - top_teacher)
    right_weight = jnp.exp(right_part[2] - top_teacher)
    return (
        top_student,
        total_student,
        top_teacher,
        left_part[3] * left_weight + right_part[3] * right_weight,
        left_part[4] * left_weight + right_part[4] * right_weight,
    )


def adam_step(weight, grad, first_moment, second_moment, rate, decay):
    first_new = BETA_ONE * first_moment + (1.0 - BETA_ONE) * grad
    second_new = BETA_TWO * second_moment + (1.0 - BETA_TWO) * grad * grad
    direction = (
        first_new
        / (1.0 - BETA_ONE**STEP)
        / (jnp.sqrt(second_new / (1.0 - BETA_TWO**STEP)) + ADAM_EPSILON)
    )
    return (first_new, second_new, weight - rate * (direction + decay * weight))


def renew(stat_matrix, basis):
    scaled = jnp.dot(stat_matrix, basis, precision=lax.Precision.HIGHEST) * (
        D / jnp.trace(stat_matrix)
    )
    gram = jnp.dot(scaled.T, scaled, precision=lax.Precision.HIGHEST)
    lower_factor = jnp.linalg.cholesky(gram)
    return lax.linalg.triangular_solve(lower_factor, scaled.T, left_side=True, lower=True).T


def nothing(stat_matrix, basis):
    return jnp.zeros_like(basis)


def follow(teacher_weight, student_weight):
    return TEACHER_MOMENTUM * teacher_weight + (1.0 - TEACHER_MOMENTUM) * student_weight


MESH = pl.DeviceIdType.MESH
LANES = 128
LOW = jnp.bfloat16
FULL = jnp.float32


def params(identity, vmem=None):
    return pltpu.CompilerParams(
        collective_id=identity, has_side_effects=True, vmem_limit_bytes=vmem or (48 << 20)
    )


def push(source, target, sent, landed, device):
    copy = pltpu.make_async_remote_copy(
        src_ref=source,
        dst_ref=target,
        send_sem=sent,
        recv_sem=landed,
        device_id=(device,),
        device_id_type=MESH,
    )
    copy.start()
    return copy


def greet(peers):
    barrier = pltpu.get_barrier_semaphore()
    for peer in peers:
        pl.semaphore_signal(barrier, inc=1, device_id=(peer,), device_id_type=MESH)
    pl.semaphore_wait(barrier, len(peers))


def dot_nt(left, right):
    return lax.dot_general(left, right, (((1,), (1,)), ((), ())), preferred_element_type=FULL)


def dot_nn(left, right):
    return lax.dot_general(left, right, (((1,), (0,)), ((), ())), preferred_element_type=FULL)


def dot_tn(left, right):
    return lax.dot_general(left, right, (((0,), (0,)), ((), ())), preferred_element_type=FULL)


def spread_kernel(depth, small_ref, columns_ref, all_ref, part_ref, own_sem, sent, landed, csent, clanded):
    me = lax.axis_index("dp")
    total = 8 * depth
    core = lax.rem(me, 2)
    x_at = lax.rem(me // 2, 2)
    y_at = lax.rem(me // 4, 2)
    z_at = me // 8
    peers = [lax.rem(me + step, total) for step in range(1, total)]
    greet(peers)

    def place(y_pos, x_pos, c_pos):
        return ((y_pos * 2 + x_pos) * 2 + c_pos) * depth

    mine = place(y_at, x_at, core)
    across_x = place(y_at, 1 - x_at, core)
    across_y = place(1 - y_at, x_at, core)
    across_d = place(1 - y_at, 1 - x_at, core)
    partner = me + 1 - 2 * core
    to_x = me + 2 - 4 * x_at
    to_y = me + 4 - 8 * y_at
    own = pltpu.make_async_copy(small_ref, all_ref.at[mine + z_at], own_sem.at[0])
    own.start()
    copies = []
    z_copies = []
    for step in range(1, depth):
        peer = lax.rem(me + 8 * step, total)
        z_copies.append(
            push(small_ref, all_ref.at[mine + z_at], sent.at[step], landed.at[step], peer)
        )
    hid_rows = columns_ref.shape[0]
    c_copies = []
    for step, peer in enumerate(peers):
        block = columns_ref.at[:, pl.ds(pl.multiple_of((peer // 2) * LANES, LANES), LANES)]
        c_copies.append(push(block, part_ref.at[me], csent.at[step], clanded.at[step], peer))
    own_block = columns_ref.at[:, pl.ds(pl.multiple_of((me // 2) * LANES, LANES), LANES)]
    own_part = pltpu.make_async_copy(own_block, part_ref.at[me], own_sem.at[1])
    own_part.start()
    own.wait()
    for copy in z_copies:
        copy.wait_recv()
    base = depth

    def column(start, where, device):
        view = all_ref.at[pl.ds(start, depth)]
        return push(view, view, sent.at[where], landed.at[where], device)

    x_copy = column(mine, base, to_x)
    y_copy = column(mine, base + 1, to_y)
    die_own = column(mine, base + 2, partner)
    half = small_ref.shape[0] // 2
    x_copy.wait_recv()
    from_x = all_ref.at[pl.ds(across_x, depth), pl.ds(0, half)]
    d_one = push(from_x, from_x, sent.at[base + 3], landed.at[base + 3], to_y)
    die_x = column(across_x, base + 5, partner)
    y_copy.wait_recv()
    from_y = all_ref.at[pl.ds(across_y, depth), pl.ds(half, half)]
    d_two = push(from_y, from_y, sent.at[base + 4], landed.at[base + 4], to_x)
    die_y = column(across_y, base + 6, partner)
    d_one.wait_recv()
    d_two.wait_recv()
    die_d = column(across_d, base + 7, partner)
    for copy in (die_own, die_x, die_y, die_d):
        copy.wait_recv()
    for copy in c_copies:
        copy.wait_recv()
    own_part.wait()
    for copy in z_copies + c_copies + [x_copy, y_copy, die_own, d_one, d_two, die_x, die_y, die_d]:
        copy.wait_send()


def spread(small, columns, devices):
    depth = devices // 8
    return pl.pallas_call(
        functools.partial(spread_kernel, depth),
        out_shape=(
            jax.ShapeDtypeStruct((devices,) + small.shape, small.dtype),
            jax.ShapeDtypeStruct((devices, columns.shape[0], LANES), columns.dtype),
        ),
        in_specs=[pl.BlockSpec(memory_space=pltpu.VMEM)] * 2,
        out_specs=(pl.BlockSpec(memory_space=pltpu.VMEM),) * 2,
        scratch_shapes=[
            pltpu.SemaphoreType.DMA((2,)),
            pltpu.SemaphoreType.DMA((depth + 8,)),
            pltpu.SemaphoreType.DMA((depth + 8,)),
            pltpu.SemaphoreType.DMA((devices - 1,)),
            pltpu.SemaphoreType.DMA((devices - 1,)),
        ],
        compiler_params=params(1),
        name="spread",
    )(small, columns)


def head_kernel(
    devices,
    feat_ref,
    hidden_ref,
    teacher_hidden_ref,
    part_ref,
    last_ref,
    teacher_last_ref,
    protos_ref,
    teacher_protos_ref,
    centre_ref,
    mask_ref,
    mask_row_ref,
    scalars_ref,
    grad_hidden_ref,
    grad_last_ref,
    grad_protos_ref,
    grad_feat_ref,
    centre_out_ref,
    fb,
    hid_low,
    thid_low,
    prot_low,
    half_out,
    half_in,
    mine_buf,
    other_buf,
    act_s,
    act_t,
    act2_s,
    act2_t,
    pre1,
    pre2,
    unit_ref,
    inv_ref,
    exp_s,
    exp_t,
    stat_out,
    stat_all,
    pz_ref,
    pz_all,
    dz_own,
    dz_all,
    dp_own,
    dp_in,
    dp_cb,
    dp_half,
    dp_full,
    df_part,
    df_all,
    df_sum,
    df_other,
    die_sent,
    die_landed,
    wide_sent,
    wide_landed,
    core_sent,
    core_landed,
):
    me = lax.axis_index("dp")
    core = lax.rem(me, 2)
    chip = me // 2
    chips = devices // 2
    partner = me + 1 - 2 * core
    everyone = [lax.rem(me + step, devices) for step in range(1, devices)]
    same_core = [lax.rem(me + 2 * step, devices) for step in range(1, chips)]
    images = mask_ref.shape[0]
    units = hidden_ref.shape[0]
    groups = images // 8
    greet(everyone)
    sends = []

    def die(step, source, target):
        copy = push(source, target, die_sent.at[step], die_landed.at[step], partner)
        sends.append(copy)
        return copy

    def wide(step, source, target):
        made = [
            push(source, target, wide_sent.at[step, at], wide_landed.at[step, at], peer)
            for at, peer in enumerate(everyone)
        ]
        sends.extend(made)
        return made

    def cores(step, source_of, target):
        made = [
            push(source_of(peer), target, core_sent.at[step, at], core_landed.at[step, at], peer)
            for at, peer in enumerate(same_core)
        ]
        sends.extend(made)
        return made

    fb[me] = feat_ref[...]
    copies = wide(0, feat_ref, fb.at[me])
    hid_low[...] = hidden_ref[...].astype(LOW)
    thid_low[...] = teacher_hidden_ref[...].astype(LOW)
    prot_low[0] = protos_ref[...].astype(LOW)
    prot_low[1] = teacher_protos_ref[...].astype(LOW)
    block_rows = feat_ref.shape[0]
    row_at = lax.broadcasted_iota(jnp.int32, (images, devices * block_rows), 0)
    col_at = lax.broadcasted_iota(jnp.int32, (images, devices * block_rows), 1)
    col_dev = lax.shift_right_logical(col_at, 5)
    col_in = jnp.bitwise_and(col_at, 31)
    lead = row_at - 3 * col_dev
    for copy in copies:
        copy.wait_recv()
    rows_all = fb[...].reshape(devices * block_rows, LANES)

    def features_of(model):
        pieces = []
        for j in range(3):
            hit = (col_in - (16 * model + 3 * j) == lead) & (lead >= 0) & (lead < 3)
            pieces.append(dot_nn(jnp.where(hit, 1.0, 0.0).astype(LOW), rows_all).astype(LOW))
        return jnp.concatenate(pieces, 1)

    feats = features_of(0)
    tfeats = features_of(1)

    def gather_pair(step, student, teacher, out_s, out_t):
        own_model = jnp.where(core == 0, student, teacher)
        half_out[step] = jnp.where(core == 0, teacher, student)
        copy = die(2 * step, half_out.at[step], half_in.at[step])
        copy.wait_recv()
        got = half_in[step]
        block = jnp.concatenate(
            [jnp.where(core == 0, own_model, got), jnp.where(core == 0, got, own_model)], 1
        ).astype(LOW)
        mine_buf[step, chip] = block
        made = cores(step, lambda peer: mine_buf.at[step, chip], mine_buf.at[step, chip])
        for copy in made:
            copy.wait_recv()
        copy = die(2 * step + 1, mine_buf.at[step], other_buf.at[step])
        copy.wait_recv()
        for at in range(chips):
            one, two = mine_buf[step, at], other_buf[step, at]
            out_s[:, at * LANES : (at + 1) * LANES] = jnp.where(core == 0, one, two)
            out_t[:, at * LANES : (at + 1) * LANES] = jnp.where(core == 0, two, one)

    pre_one = dot_nt(feats, hid_low[:, :D])
    pre1[...] = pre_one
    tpre_one = dot_nt(tfeats, thid_low[:, :D])
    gather_pair(0, gelu_exact(pre_one).astype(LOW).astype(FULL), gelu_exact(tpre_one).astype(LOW).astype(FULL), act_s, act_t)
    pre_two = dot_nt(act_s[...], hid_low[:, D:])
    pre2[...] = pre_two
    tpre_two = dot_nt(act_t[...], thid_low[:, D:])
    gather_pair(1, gelu_exact(pre_two).astype(LOW).astype(FULL), gelu_exact(tpre_two).astype(LOW).astype(FULL), act2_s, act2_t)

    unit, inverse_norm = unit_rows(dot_nt(act2_s[...], last_ref[...]))
    tunit, unused = unit_rows(dot_nt(act2_t[...], teacher_last_ref[...]))
    unit_ref[...] = unit
    inv_ref[...] = jnp.broadcast_to(inverse_norm, inv_ref.shape)
    unit_low = unit.astype(LOW)
    scaled = dot_nn(unit_low, prot_low[0]) / TAU_STUDENT
    tlogits = dot_nn(tunit.astype(LOW), prot_low[1])
    top_s = jnp.max(scaled, -1, keepdims=True)
    grown_s = jnp.exp(scaled - top_s)
    exp_s[...] = grown_s
    sharp = (tlogits - centre_ref[...]) / TAU_TEACHER
    top_t = jnp.max(sharp, -1, keepdims=True)
    grown_t = jnp.exp(sharp - top_t)
    exp_t[...] = grown_t
    lane = lax.broadcasted_iota(jnp.int32, (images, LANES), 1)
    stats = jnp.where(lane == 0, top_s, 0.0)
    stats = jnp.where(lane == 1, jnp.sum(grown_s, -1, keepdims=True), stats)
    stats = jnp.where(lane == 2, top_t, stats)
    stats = jnp.where(lane == 3, jnp.sum(grown_t, -1, keepdims=True), stats)
    stats = jnp.where(lane == 4, jnp.sum(grown_t * scaled, -1, keepdims=True), stats)
    square = jnp.concatenate([stats, jnp.zeros((LANES - images, LANES), FULL)], 0)
    stat_out[...] = square.T[:8]
    stat_all[me] = stat_out[...]
    copies = wide(1, stat_out, stat_all.at[me])
    counted = mask_ref[...]
    count = jnp.sum(counted)
    centre_out_ref[...] = (
        CENTRE_MOMENTUM * centre_ref[...]
        + (1.0 - CENTRE_MOMENTUM) * jnp.sum(counted * tlogits, 0, keepdims=True) / count
    )
    for copy in copies:
        copy.wait_recv()
    merged = stat_all[...]
    tops, totals = merged[:, 0], merged[:, 1]
    ttops, ttotals, crosses = merged[:, 2], merged[:, 3], merged[:, 4]
    peak_s = jnp.max(tops, 0, keepdims=True)
    sum_s = jnp.sum(totals * jnp.exp(tops - peak_s), 0, keepdims=True)
    peak_t = jnp.max(ttops, 0, keepdims=True)
    shrink = jnp.exp(ttops - peak_t)
    sum_t = jnp.sum(ttotals * shrink, 0, keepdims=True)
    cross = jnp.sum(crosses * shrink, 0, keepdims=True)
    log_total = peak_s + jnp.log(sum_s)
    mask_row = mask_row_ref[...]
    losses = jnp.where(mask_row > 0.0, log_total - cross / sum_t, 0.0)
    loss = jnp.sum(losses)
    lane8 = lax.broadcasted_iota(jnp.int32, (8, LANES), 1)
    scalars_ref[...] = jnp.where(lane8 == 0, loss, jnp.where(lane8 == 1, count, 0.0))
    back = jnp.concatenate(
        [log_total, peak_t, 1.0 / sum_t, jnp.zeros((LANES - 3, LANES), FULL)], 0
    ).T
    share_s = jnp.exp(top_s - back[:images, 0:1])
    share_t = jnp.exp(top_t - back[:images, 1:2]) * back[:images, 2:3]
    grad_logits = (
        (counted / count) * (exp_s[...] * share_s - exp_t[...] * share_t) / TAU_STUDENT
    ).astype(LOW)

    pz_ref[...] = dot_nt(grad_logits, prot_low[0]).reshape(groups, 8, unit.shape[1])
    for group in range(groups):
        owner = 2 * group

        @pl.when(me != owner)
        def _(group=group, owner=owner):
            push(pz_ref.at[group], pz_all.at[me], wide_sent.at[2, group], wide_landed.at[2, me], owner)

    grad_protos_ref[...] = dot_tn(unit_low, grad_logits)

    @pl.when((core == 0) & (chip < groups))
    def _():
        pz_all[me] = pz_ref[chip]
        for source in range(devices):

            @pl.when(source != me)
            def _(source=source):
                pltpu.make_async_copy(pz_all.at[source], pz_all.at[source], wide_landed.at[2, source]).wait()

        total = jnp.sum(pz_all[...], 0)
        rows = pl.ds(pl.multiple_of(chip * 8, 8), 8)
        own_unit = unit_ref[rows, :]
        own_inv = inv_ref[rows, :][:, 0:1]
        dz_own[...] = own_inv * (total - own_unit * jnp.sum(own_unit * total, -1, keepdims=True))
        dz_all[chip] = dz_own[...]
        for step in range(1, devices):
            push(dz_own, dz_all.at[chip], wide_sent.at[3, step - 1], wide_landed.at[3, chip], lax.rem(me + step, devices))

    for group in range(groups):

        @pl.when(me != 2 * group)
        def _(group=group):
            pltpu.make_async_copy(dz_all.at[group], dz_all.at[group], wide_landed.at[3, group]).wait()

    grad_bottle = dz_all[...].reshape(images, unit.shape[1]).astype(LOW)
    chip_columns = pl.ds(pl.multiple_of(chip * LANES, LANES), LANES)
    pair = dot_nn(grad_bottle, last_ref[:, chip_columns])
    grad_act_two = jnp.where(core == 0, pair[:, :units], pair[:, units:])
    grad_pre_two = (grad_act_two * gelu_slope(pre2[...])).astype(LOW)

    dp_own[...] = grad_pre_two.astype(FULL)
    copy = die(4, dp_own, dp_in)
    width = last_ref.shape[0] // devices
    pick_row = lax.broadcasted_iota(jnp.int32, (width, last_ref.shape[0]), 0)
    pick_col = lax.broadcasted_iota(jnp.int32, (width, last_ref.shape[0]), 1)
    pick = jnp.where(pick_col == pick_row + me * width, 1.0, 0.0).astype(LOW)
    own_bottle = dot_nt(pick, grad_bottle).astype(LOW)
    grad_last_ref[...] = dot_nn(own_bottle, act2_s[...])
    copy.wait_recv()
    own_dp, got_dp = dp_own[...], dp_in[...]
    dp_cb[...] = jnp.concatenate(
        [jnp.where(core == 0, own_dp, got_dp), jnp.where(core == 0, got_dp, own_dp)], 1
    ).astype(LOW)
    half = images // 2
    my_rows = pl.ds(pl.multiple_of(core * half, 16), half)
    their_rows = pl.ds(pl.multiple_of((1 - core) * half, 16), half)
    dp_half[0, chip] = dp_cb[my_rows, :]
    made = cores(2, lambda peer: dp_half.at[0, chip], dp_half.at[0, chip])
    grad_hidden_ref[:, D:] = dot_tn(grad_pre_two, act_s[...])
    for copy in made:
        copy.wait_recv()
    copy = die(5, dp_half.at[0], dp_half.at[1])
    for at in range(chips):
        dp_full[my_rows, at * LANES : (at + 1) * LANES] = dp_half[0, at]
    copy.wait_recv()
    for at in range(chips):
        dp_full[their_rows, at * LANES : (at + 1) * LANES] = dp_half[1, at]
    pair = dot_nn(dp_full[...], part_ref[...].reshape(devices * units, LANES))
    grad_act_one = jnp.where(core == 0, pair[:, :units], pair[:, units:])
    grad_pre_one = (grad_act_one * gelu_slope(pre1[...])).astype(LOW)

    out_row = lax.broadcasted_iota(jnp.int32, (8 * chips, images), 0)
    in_row = lax.broadcasted_iota(jnp.int32, (8 * chips, images), 1)
    out_chip = lax.shift_right_logical(out_row, 3)
    out_in = jnp.bitwise_and(out_row, 7)
    hit = (in_row - 6 * out_chip == out_in) & (out_in < 6)
    moved = dot_nn(jnp.where(hit, 1.0, 0.0).astype(LOW), grad_pre_one).astype(LOW)
    df_part[...] = dot_nn(moved, hid_low[:, :D]).reshape(chips, 8, D)
    df_all[chip] = df_part[chip]
    made = cores(3, lambda peer: df_part.at[peer // 2], df_all.at[chip])
    grad_hidden_ref[:, :D] = dot_tn(grad_pre_one, feats)
    for copy in made:
        copy.wait_recv()
    df_sum[...] = jnp.sum(df_all[...], 0)
    copy = die(6, df_sum, df_other)
    copy.wait_recv()
    whole = df_sum[...] + df_other[...]
    grad_feat_ref[...] = whole
    squares = jnp.sum(grad_hidden_ref[...] * grad_hidden_ref[...])
    squares = squares + jnp.sum(grad_last_ref[...] * grad_last_ref[...])
    squares = squares + jnp.sum(grad_protos_ref[...] * grad_protos_ref[...])
    scalars_ref[...] = jnp.where(lane8 == 2, squares, scalars_ref[...])
    for copy in sends:
        copy.wait_send()
    for group in range(groups):

        @pl.when(me != 2 * group)
        def _(group=group):
            pltpu.make_async_copy(pz_ref.at[group], pz_ref.at[group], wide_sent.at[2, group]).wait()

    @pl.when((core == 0) & (chip < groups))
    def _():
        for step in range(1, devices):
            pltpu.make_async_copy(dz_own, dz_own, wide_sent.at[3, step - 1]).wait()


def head(feat, hidden, teacher_hidden, part, last, teacher_last, protos, teacher_protos, centre, mask, mask_row, devices):
    images = mask.shape[0]
    units, wide = hidden.shape
    bottle, width = protos.shape
    hid = last.shape[1]
    chips = devices // 2
    groups = images // 8
    vmem = pl.BlockSpec(memory_space=pltpu.VMEM)
    shape = jax.ShapeDtypeStruct
    dma = pltpu.SemaphoreType.DMA
    return pl.pallas_call(
        functools.partial(head_kernel, devices),
        out_shape=(
            shape((8, LANES), FULL),
            shape((units, wide), FULL),
            shape((bottle // devices, hid), FULL),
            shape((bottle, width), FULL),
            shape((8, D), FULL),
            shape((1, width), FULL),
        ),
        in_specs=[vmem] * 11,
        out_specs=(vmem,) * 6,
        scratch_shapes=[
            pltpu.VMEM((devices,) + feat.shape, LOW),
            pltpu.VMEM((units, wide), LOW),
            pltpu.VMEM((units, wide), LOW),
            pltpu.VMEM((2, bottle, width), LOW),
            pltpu.VMEM((2, images, units), FULL),
            pltpu.VMEM((2, images, units), FULL),
            pltpu.VMEM((2, chips, images, LANES), LOW),
            pltpu.VMEM((2, chips, images, LANES), LOW),
            pltpu.VMEM((images, hid), LOW),
            pltpu.VMEM((images, hid), LOW),
            pltpu.VMEM((images, hid), LOW),
            pltpu.VMEM((images, hid), LOW),
            pltpu.VMEM((images, units), FULL),
            pltpu.VMEM((images, units), FULL),
            pltpu.VMEM((images, bottle), FULL),
            pltpu.VMEM((images, LANES), FULL),
            pltpu.VMEM((images, width), FULL),
            pltpu.VMEM((images, width), FULL),
            pltpu.VMEM((8, LANES), FULL),
            pltpu.VMEM((devices, 8, LANES), FULL),
            pltpu.VMEM((groups, 8, bottle), FULL),
            pltpu.VMEM((devices, 8, bottle), FULL),
            pltpu.VMEM((8, bottle), FULL),
            pltpu.VMEM((groups, 8, bottle), FULL),
            pltpu.VMEM((images, units), FULL),
            pltpu.VMEM((images, units), FULL),
            pltpu.VMEM((images, LANES), LOW),
            pltpu.VMEM((2, chips, images // 2, LANES), LOW),
            pltpu.VMEM((images, hid), LOW),
            pltpu.VMEM((chips, 8, D), FULL),
            pltpu.VMEM((chips, 8, D), FULL),
            pltpu.VMEM((8, D), FULL),
            pltpu.VMEM((8, D), FULL),
            dma((7,)),
            dma((7,)),
            dma((4, devices)),
            dma((4, devices)),
            dma((4, chips - 1)),
            dma((4, chips - 1)),
        ],
        compiler_params=params(2),
        name="head",
    )(feat, hidden, teacher_hidden, part, last, teacher_last, protos, teacher_protos, centre, mask, mask_row)


def gram_device(matrix):
    return 2 * matrix


def collect_kernel(
    depth,
    rows_layer,
    bounds,
    squares_ref,
    packet_ref,
    stats_ref,
    bases_ref,
    own_ref,
    norm_ref,
    next_stats_ref,
    basis_ref,
    die_buf,
    d_buf,
    x_buf,
    y_buf,
    z_buf,
    stat_buf,
    square_out,
    square_all,
    segs,
    gram_buf,
    die_sent,
    die_landed,
    near_sent,
    near_landed,
    z_sent,
    z_landed,
    stat_sent,
    stat_landed,
    gram_sent,
    gram_landed,
    square_sent,
    square_landed,
):
    me = lax.axis_index("dp")
    total = 8 * depth
    core = lax.rem(me, 2)
    x_at = lax.rem(me // 2, 2)
    y_at = lax.rem(me // 4, 2)
    z_at = me // 8
    chip = me // 2
    partner = me + 1 - 2 * core
    to_x = me + 2 - 4 * x_at
    to_y = me + 4 - 8 * y_at
    everyone = [lax.rem(me + step, total) for step in range(1, total)]
    matrices = stats_ref.shape[0]
    own_rows = stats_ref.shape[1]
    segment_rows = segs.shape[2]
    is_gram = (core == 0) & (chip < matrices)
    greet(everyone)
    sends = []

    def place(y_pos, x_pos, c_pos):
        return ((y_pos * 2 + x_pos) * 2 + c_pos) * depth

    relative = [(y_at, x_at), (y_at, 1 - x_at), (1 - y_at, x_at), (1 - y_at, 1 - x_at)]
    starts = [place(y_pos, x_pos, core) for y_pos, x_pos in relative]
    partner_starts = [place(y_pos, x_pos, 1 - core) for y_pos, x_pos in relative]
    layers = (packet_ref.shape[1] // rows_layer)
    chunks = [(layer * rows_layer, rows_layer) for layer in reversed(range(layers))]
    chunks.append((layers * rows_layer, packet_ref.shape[1] - layers * rows_layer))
    count = len(chunks)

    def first_half(k):
        return ((chunks[k][1] // 2 + 15) // 16) * 16

    die_copies = {}
    for k in range(count):
        lower, size = chunks[k]
        for rel in (3, 1, 2, 0):
            copy = push(
                packet_ref.at[pl.ds(partner_starts[rel], depth), pl.ds(lower, size)],
                die_buf.at[pl.ds(rel * depth, depth), pl.ds(lower, size)],
                die_sent.at[k, rel],
                die_landed.at[k, rel],
                partner,
            )
            die_copies[k, rel] = copy
            sends.append(copy)

    for matrix in range(matrices):
        owner = gram_device(matrix)

        @pl.when(me != owner)
        def _(matrix=matrix, owner=owner):
            push(stats_ref.at[matrix], stat_buf.at[0, me], stat_sent.at[0, matrix], stat_landed.at[0, me], owner)
            push(bases_ref.at[matrix], stat_buf.at[1, me], stat_sent.at[1, matrix], stat_landed.at[1, me], owner)

    near = {}

    def pair_sum(rel, z_pos, lower, size):
        return packet_ref[starts[rel] + z_pos, pl.ds(lower, size), :].astype(FULL) + die_buf[
            rel * depth + z_pos, pl.ds(lower, size), :
        ].astype(FULL)

    def stage_one(k):
        lower, size = chunks[k]
        half = first_half(k)
        die_copies[k, 3].wait_recv()
        for z_pos in range(depth):
            die_buf[3 * depth + z_pos, pl.ds(lower, size), :] = pair_sum(3, z_pos, lower, size).astype(LOW)
        for which, (start, length, peer) in enumerate(
            [(lower, half, to_x), (lower + half, size - half, to_y)]
        ):
            copy = push(
                die_buf.at[pl.ds(3 * depth, depth), pl.ds(start, length)],
                d_buf.at[:, pl.ds(start, length)],
                near_sent.at[k, which],
                near_landed.at[k, which],
                peer,
            )
            near[k, which] = copy
            sends.append(copy)

    def stage_two(k):
        lower, size = chunks[k]
        half = first_half(k)
        for rel, which, peer, target in ((1, 2, to_x, x_buf), (2, 3, to_y, y_buf)):
            die_copies[k, rel].wait_recv()
            near[k, 1 if rel == 1 else 0].wait_recv()
            first, second = (lower, half), (lower + half, size - half)
            helped, plain = (second, first) if rel == 1 else (first, second)
            for z_pos in range(depth):
                die_buf[rel * depth + z_pos, pl.ds(plain[0], plain[1]), :] = pair_sum(
                    rel, z_pos, plain[0], plain[1]
                ).astype(LOW)
                die_buf[rel * depth + z_pos, pl.ds(helped[0], helped[1]), :] = (
                    pair_sum(rel, z_pos, helped[0], helped[1])
                    + d_buf[z_pos, pl.ds(helped[0], helped[1]), :].astype(FULL)
                ).astype(LOW)
            copy = push(
                die_buf.at[pl.ds(rel * depth, depth), pl.ds(lower, size)],
                target.at[:, pl.ds(lower, size)],
                near_sent.at[k, which],
                near_landed.at[k, which],
                peer,
            )
            near[k, which] = copy
            sends.append(copy)

    z_copies = {}

    def stage_three(k):
        lower, size = chunks[k]
        die_copies[k, 0].wait_recv()
        near[k, 2].wait_recv()
        near[k, 3].wait_recv()
        for z_pos in range(depth):
            die_buf[z_pos, pl.ds(lower, size), :] = (
                pair_sum(0, z_pos, lower, size)
                + x_buf[z_pos, pl.ds(lower, size), :].astype(FULL)
                + y_buf[z_pos, pl.ds(lower, size), :].astype(FULL)
            ).astype(LOW)
        for step in range(1, depth):
            z_to = lax.rem(z_at + step, depth)
            copy = push(
                die_buf.at[z_to, pl.ds(lower, size)],
                z_buf.at[z_at, pl.ds(lower, size)],
                z_sent.at[k, step],
                z_landed.at[k, step],
                lax.rem(me + 8 * step, total),
            )
            z_copies[k, step] = copy
            sends.append(copy)

    def stage_four(k):
        lower, size = chunks[k]
        for step in range(1, depth):
            z_copies[k, step].wait_recv()
        value = die_buf[z_at, pl.ds(lower, size), :].astype(FULL)
        for step in range(1, depth):
            value = value + z_buf[lax.rem(z_at + step, depth), pl.ds(lower, size), :].astype(FULL)
        own_ref[pl.ds(lower, size), :] = value
        if k == count - 1:
            return
        layer = lower // rows_layer
        for segment, (low_row, high_row) in enumerate(bounds):
            piece = value[low_row:high_row].astype(LOW)
            if high_row - low_row < segment_rows:
                blank = jnp.zeros((segment_rows - (high_row - low_row), value.shape[1]), LOW)
                piece = jnp.concatenate([piece, blank], 0)
            matrix = 4 * layer + segment
            segs[layer, segment] = piece
            owner = gram_device(matrix)

            @pl.when(me != owner)
            def _(matrix=matrix, owner=owner, layer=layer, segment=segment):
                push(segs.at[layer, segment], gram_buf.at[me], gram_sent.at[matrix], gram_landed.at[me], owner)

    stages = [stage_one, stage_two, stage_three, stage_four]
    for step in range(count + len(stages) - 1):
        for at, stage in enumerate(stages):
            if 0 <= step - at < count:
                stage(step - at)

    own = own_ref[...]
    lane8 = lax.broadcasted_iota(jnp.int32, (8, LANES), 1)
    squares = jnp.sum(own * own) + jnp.sum(jnp.where(lane8 == 2, squares_ref[...], 0.0)) / 8.0
    square_out[...] = jnp.full((8, LANES), squares)
    square_all[me] = square_out[...]
    copies = [
        push(square_out, square_all.at[me], square_sent.at[at], square_landed.at[at], peer)
        for at, peer in enumerate(everyone)
    ]
    sends.extend(copies)
    for copy in copies:
        copy.wait_recv()
    squares = jnp.sum(square_all[...], 0)
    norm = jnp.sqrt(squares)
    norm_ref[...] = norm
    clip = jnp.minimum(1.0, CLIP_MAX / (norm + 1e-06))[:1, :1]

    @pl.when(is_gram)
    def _():
        for matrix in range(matrices):

            @pl.when(matrix == chip)
            def _(matrix=matrix):
                gram_buf[me] = segs[matrix // 4, matrix % 4]
                stat_buf[0, me] = stats_ref[matrix]
                stat_buf[1, me] = bases_ref[matrix]

        for source in range(total):

            @pl.when(source != me)
            def _(source=source):
                for at in range(2):
                    pltpu.make_async_copy(
                        stat_buf.at[at, source], stat_buf.at[at, source], stat_landed.at[at, source]
                    ).wait()
                pltpu.make_async_copy(gram_buf.at[source], gram_buf.at[source], gram_landed.at[source]).wait()

        rows = gram_buf[...].reshape(total * segment_rows, gram_buf.shape[2])
        gram = dot_tn(rows, rows)
        scale = (1.0 - BETA_STAT) * (clip * clip)
        for source in range(total):
            next_stats_ref[source] = (
                BETA_STAT * stat_buf[0, source]
                + scale * gram[source * own_rows : (source + 1) * own_rows]
            )
        basis_ref[...] = stat_buf[1]

    @pl.when(jnp.logical_not(is_gram))
    def _():
        next_stats_ref[...] = jnp.zeros(next_stats_ref.shape, FULL)
        basis_ref[...] = jnp.zeros(basis_ref.shape, FULL)

    for copy in sends:
        copy.wait_send()
    for matrix in range(matrices):

        @pl.when(me != gram_device(matrix))
        def _(matrix=matrix):
            for at, source in ((0, stats_ref), (1, bases_ref)):
                pltpu.make_async_copy(source.at[matrix], source.at[matrix], stat_sent.at[at, matrix]).wait()
            own_segment = segs.at[matrix // 4, matrix % 4]
            pltpu.make_async_copy(own_segment, own_segment, gram_sent.at[matrix]).wait()


def collect(squares, packets, stats, bases, rows_layer, bounds):
    devices, rows, width = packets.shape
    depth = devices // 8
    matrices, own_rows = stats.shape[:2]
    layers = rows // rows_layer
    segment_rows = -(-max(high - low for low, high in bounds) // 16) * 16
    vmem = pl.BlockSpec(memory_space=pltpu.VMEM)
    shape = jax.ShapeDtypeStruct
    dma = pltpu.SemaphoreType.DMA
    count = layers + 1
    return pl.pallas_call(
        functools.partial(collect_kernel, depth, rows_layer, bounds),
        out_shape=(
            shape((rows, width), FULL),
            shape((8, LANES), FULL),
            shape((devices, own_rows, width), FULL),
            shape((devices, own_rows, width), FULL),
        ),
        in_specs=[vmem] * 4,
        out_specs=(vmem,) * 4,
        scratch_shapes=[
            pltpu.VMEM((4 * depth, rows, width), LOW),
            pltpu.VMEM((depth, rows, width), LOW),
            pltpu.VMEM((depth, rows, width), LOW),
            pltpu.VMEM((depth, rows, width), LOW),
            pltpu.VMEM((depth, rows, width), LOW),
            pltpu.VMEM((2, devices, own_rows, width), FULL),
            pltpu.VMEM((8, LANES), FULL),
            pltpu.VMEM((devices, 8, LANES), FULL),
            pltpu.VMEM((layers, 4, segment_rows, width), LOW),
            pltpu.VMEM((devices, segment_rows, width), LOW),
            dma((count, 4)),
            dma((count, 4)),
            dma((count, 4)),
            dma((count, 4)),
            dma((count, depth)),
            dma((count, depth)),
            dma((2, matrices)),
            dma((2, devices)),
            dma((matrices,)),
            dma((devices,)),
            dma((devices - 1,)),
            dma((devices - 1,)),
        ],
        compiler_params=params(3, 56 << 20),
        name="collect",
    )(squares, packets, stats, bases)


def dot_high(left, right, contract):
    return lax.dot_general(
        left,
        right,
        (contract, ((), ())),
        precision=lax.Precision.HIGHEST,
        preferred_element_type=FULL,
    )


def inverse_factor(block):
    size = block.shape[0]
    tiles = size // 8
    sub = lax.broadcasted_iota(jnp.int32, (8, size), 0)
    lane = lax.broadcasted_iota(jnp.int32, (8, size), 1)
    rest = [block[8 * t : 8 * t + 8] for t in range(tiles)]
    made = [jnp.where(lane == sub + 8 * t, 1.0, 0.0) for t in range(tiles)]
    for k in range(size):
        tile, row = k // 8, k % 8
        pivot = rest[tile][row : row + 1]
        scale = lax.rsqrt(pivot[:, k : k + 1])
        factor_row = pivot * scale
        made_row = made[tile][row : row + 1] * scale
        for t in range(tile, tiles):
            column = rest[t][:, k : k + 1] * scale
            if t == tile:
                column = jnp.where(sub[:, :1] > row, column, 0.0)
            rest[t] = rest[t] - column * factor_row
            made[t] = made[t] - column * made_row
            if t == tile:
                made[t] = jnp.where(sub == row, made_row, made[t])
    return jnp.concatenate(made, 0)


def renew_kernel(stats_ref, basis_ref, out_ref, stat, base, gram, work, done):
    parts, rows = stats_ref.shape[:2]
    size = parts * rows
    blocks = size // LANES
    for part in range(parts):
        stat[part * rows : (part + 1) * rows] = stats_ref[part]
        base[part * rows : (part + 1) * rows] = basis_ref[part]
    at_row = lax.broadcasted_iota(jnp.int32, (size, size), 0)
    at_col = lax.broadcasted_iota(jnp.int32, (size, size), 1)
    trace = jnp.sum(jnp.where(at_row == at_col, stat[...], 0.0), axis=(0, 1), keepdims=True)
    scaled = dot_high(stat[...], base[...], ((1,), (0,))) * (size / trace)
    product = dot_high(scaled, scaled, ((0,), (0,)))
    for b in range(blocks):
        work[b] = scaled[:, b * LANES : (b + 1) * LANES]
        for c in range(blocks):
            gram[b, c] = product[b * LANES : (b + 1) * LANES, c * LANES : (c + 1) * LANES]

    def step(b, carried):
        inverse = inverse_factor(gram[b, b])
        made = dot_high(work[b], inverse, ((1,), (1,)))
        done[b] = made

        def trail(c, inner):
            panel = dot_high(inverse, gram[b, c], ((1,), (0,)))
            work[c] = work[c] - dot_high(made, panel, ((1,), (0,)))

            def against(e, innermost):
                other = dot_high(inverse, gram[b, e], ((1,), (0,)))
                gram[c, e] = gram[c, e] - dot_high(panel, other, ((0,), (0,)))
                return innermost

            lax.fori_loop(c, blocks, against, 0)
            return inner

        lax.fori_loop(b + 1, blocks, trail, 0)
        return carried

    lax.fori_loop(0, blocks, step, 0)
    whole = jnp.concatenate([done[b] for b in range(blocks)], 1)
    for part in range(parts):
        out_ref[part] = whole[part * rows : (part + 1) * rows]


def renew_own(stats, basis):
    devices, rows, width = stats.shape
    size = devices * rows
    blocks = size // LANES
    vmem = pl.BlockSpec(memory_space=pltpu.VMEM)
    return pl.pallas_call(
        renew_kernel,
        out_shape=jax.ShapeDtypeStruct(stats.shape, FULL),
        in_specs=[vmem] * 2,
        out_specs=vmem,
        scratch_shapes=[
            pltpu.VMEM((size, width), FULL),
            pltpu.VMEM((size, width), FULL),
            pltpu.VMEM((blocks, blocks, LANES, LANES), FULL),
            pltpu.VMEM((blocks, size, LANES), FULL),
            pltpu.VMEM((blocks, size, LANES), FULL),
        ],
        compiler_params=pltpu.CompilerParams(vmem_limit_bytes=32 << 20),
        name="renew",
    )(stats, basis)


def deal_kernel(devices, stats_ref, bases_ref, own_stats_ref, own_bases_ref, sent, landed):
    me = lax.axis_index("dp")
    core = lax.rem(me, 2)
    chip = me // 2
    matrices = own_stats_ref.shape[0]
    is_gram = (core == 0) & (chip < matrices)
    greet([lax.rem(me + step, devices) for step in range(1, devices)])

    @pl.when(is_gram)
    def _():
        for step in range(1, devices):
            peer = lax.rem(me + step, devices)
            push(bases_ref.at[peer], own_bases_ref.at[chip], sent.at[1, step], landed.at[1, chip], peer)
        for step in range(1, devices):
            peer = lax.rem(me + step, devices)
            push(stats_ref.at[peer], own_stats_ref.at[chip], sent.at[0, step], landed.at[0, chip], peer)
        own_stats_ref[chip] = stats_ref[me]
        own_bases_ref[chip] = bases_ref[me]

    for matrix in range(matrices):

        @pl.when(me != gram_device(matrix))
        def _(matrix=matrix):
            for at, target in ((0, own_stats_ref), (1, own_bases_ref)):
                pltpu.make_async_copy(target.at[matrix], target.at[matrix], landed.at[at, matrix]).wait()

    @pl.when(is_gram)
    def _():
        for step in range(1, devices):
            for at, source in ((0, stats_ref), (1, bases_ref)):
                pltpu.make_async_copy(source.at[0], source.at[0], sent.at[at, step]).wait()


def deal(stats, bases, matrices):
    devices, rows, width = stats.shape
    vmem = pl.BlockSpec(memory_space=pltpu.VMEM)
    dma = pltpu.SemaphoreType.DMA
    return pl.pallas_call(
        functools.partial(deal_kernel, devices),
        out_shape=(jax.ShapeDtypeStruct((matrices, rows, width), FULL),) * 2,
        in_specs=[vmem] * 2,
        out_specs=(vmem,) * 2,
        scratch_shapes=[dma((2, devices)), dma((2, matrices))],
        compiler_params=params(4),
        name="deal",
    )(stats, bases)


def head_slow(
    features,
    teacher_features,
    valid_mask,
    head_hidden,
    head_last,
    protos,
    teacher_hidden,
    teacher_last,
    teacher_protos,
    centre,
    device_index,
):
    all_features, all_teacher = (
        lax.all_gather(features, "dp", axis=0, tiled=True),
        lax.all_gather(teacher_features, "dp", axis=0, tiled=True),
    )
    first_weight = head_hidden[:, :D].astype(jnp.bfloat16)
    second_weight = head_hidden[:, D:].astype(jnp.bfloat16)
    last_weight = head_last.astype(jnp.bfloat16)
    proto_weight = protos.astype(jnp.bfloat16)
    teacher_first = teacher_hidden[:, :D].astype(jnp.bfloat16)
    teacher_second = teacher_hidden[:, D:].astype(jnp.bfloat16)
    pre_one = matmul_low("bd,hd->bh", all_features, first_weight)
    teacher_pre_one = matmul_low("bd,hd->bh", all_teacher, teacher_first)
    act_one = (
        lax.all_gather(gelu_exact(pre_one).astype(jnp.bfloat16), "dp", axis=1, tiled=True),
        lax.all_gather(gelu_exact(teacher_pre_one).astype(jnp.bfloat16), "dp", axis=1, tiled=True),
    )
    pre_two = matmul_low("bh,kh->bk", act_one[0], second_weight)
    teacher_pre_two = matmul_low("bh,kh->bk", act_one[1], teacher_second)
    act_two = (
        lax.all_gather(gelu_exact(pre_two).astype(jnp.bfloat16), "dp", axis=1, tiled=True),
        lax.all_gather(gelu_exact(teacher_pre_two).astype(jnp.bfloat16), "dp", axis=1, tiled=True),
    )
    bottles = (
        lax.all_gather(matmul_low("bh,hc->bc", act_two[0], last_weight), "dp", axis=1, tiled=True),
        lax.all_gather(
            matmul_low("bh,hc->bc", act_two[1], teacher_last.astype(jnp.bfloat16)),
            "dp",
            axis=1,
            tiled=True,
        ),
    )
    unit, inverse_norm = unit_rows(bottles[0])
    teacher_unit, unused_norm = unit_rows(bottles[1])
    unit_low = unit.astype(jnp.bfloat16)
    logits = matmul_low("bc,cp->bp", unit_low, proto_weight)
    teacher_logits = matmul_low(
        "bc,cp->bp", teacher_unit.astype(jnp.bfloat16), teacher_protos.astype(jnp.bfloat16)
    )
    scaled = logits / TAU_STUDENT
    student_top = jnp.max(scaled, -1)
    student_total = jnp.sum(jnp.exp(scaled - student_top[:, None]), -1)
    sharpened = (teacher_logits - centre) / TAU_TEACHER
    teacher_top = jnp.max(sharpened, -1)
    teacher_exp = jnp.exp(sharpened - teacher_top[:, None])
    merged = joined(
        (
            student_top,
            student_total,
            teacher_top,
            jnp.sum(teacher_exp, -1),
            jnp.sum(teacher_exp * scaled, -1),
        ),
        "dp",
        combine_parts,
    )
    log_total = merged[0] + jnp.log(merged[1])
    counted = valid_mask.astype(jnp.float32)
    loss_count = jnp.sum(counted)
    loss_sum = jnp.sum(counted * (log_total - merged[4] / merged[3]))
    student_prob = jnp.exp(scaled - log_total[:, None])
    teacher_prob = jnp.exp(sharpened - merged[2][:, None]) / merged[3][:, None]
    grad_logits = (
        (counted / loss_count)[:, None] * (student_prob - teacher_prob) / TAU_STUDENT
    ).astype(jnp.bfloat16)
    grad_protos = matmul_low("bc,bp->cp", unit_low, grad_logits)
    grad_unit = lax.psum(matmul_low("bp,cp->bc", grad_logits, proto_weight), "dp")
    grad_bottle = inverse_norm * (grad_unit - unit * jnp.sum(unit * grad_unit, -1, keepdims=True))
    last_width = head_last.shape[1]
    grad_bottle_own = lax.dynamic_slice_in_dim(
        grad_bottle, device_index * last_width, last_width, 1
    ).astype(jnp.bfloat16)
    grad_last = matmul_low("bh,bc->hc", act_two[0], grad_bottle_own)
    grad_act_two = lax.psum_scatter(
        matmul_low("bc,hc->bh", grad_bottle_own, last_weight), "dp", scatter_dimension=1, tiled=True
    )
    grad_pre_two = (grad_act_two * gelu_slope(pre_two)).astype(jnp.bfloat16)
    grad_second = matmul_low("bk,bh->kh", grad_pre_two, act_one[0])
    grad_act_one = lax.psum_scatter(
        matmul_low("bk,kh->bh", grad_pre_two, second_weight), "dp", scatter_dimension=1, tiled=True
    )
    grad_pre_one = (grad_act_one * gelu_slope(pre_one)).astype(jnp.bfloat16)
    grad_first = matmul_low("bh,bd->hd", grad_pre_one, all_features)
    grad_features = lax.psum_scatter(
        matmul_low("bh,hd->bd", grad_pre_one, first_weight), "dp", scatter_dimension=0, tiled=True
    )
    grad_hidden = jnp.concatenate([grad_first, grad_second], 1)
    next_centre = (
        CENTRE_MOMENTUM * centre
        + (1.0 - CENTRE_MOMENTUM) * jnp.sum(counted[:, None] * teacher_logits, 0) / loss_count
    )
    return (loss_sum, loss_count, grad_hidden, grad_last, grad_protos, grad_features, next_centre)


def pack_small(embedding, teacher_embedding, head_last, teacher_last):
    def table(value):
        flat = value.T.astype(LOW).reshape(-1)
        return jnp.pad(flat, (0, -flat.size % (16 * LANES))).reshape(-1, LANES)

    def last(value):
        return value.T.astype(LOW).reshape(-1, LANES)

    return jnp.concatenate(
        [table(embedding), table(teacher_embedding), last(head_last), last(teacher_last)], 0
    )


def unpack_small(everything, embedding, head_last, devices):
    depth = devices // 8
    rows, columns = embedding.shape
    ordered = everything.reshape(2, 2, 2, depth, -1, LANES).transpose(3, 0, 1, 2, 4, 5)
    ordered = ordered.reshape(devices, -1, LANES)
    size = rows * columns
    table_rows = (size + (-size % (16 * LANES))) // LANES
    last_rows = head_last.size // LANES

    def table(at):
        flat = ordered[:, at : at + table_rows].reshape(devices, -1)[:, :size]
        return flat.reshape(devices * columns, rows).T

    def last(at):
        return ordered[:, at : at + last_rows].reshape(devices * head_last.shape[1], -1)

    return (
        table(0),
        table(table_rows),
        last(2 * table_rows),
        last(2 * table_rows + last_rows),
    )


def own_feature_rows(features, teacher_features):
    def rows(value):
        count = value.shape[0]
        turned = value.reshape(count, D // LANES, LANES).transpose(1, 0, 2).reshape(-1, LANES)
        return jnp.pad(turned, ((0, 16 - turned.shape[0]), (0, 0)))

    return jnp.concatenate([rows(features), rows(teacher_features)], 0)


def head_fast(
    features,
    teacher_features,
    valid_mask,
    head_hidden,
    protos,
    teacher_hidden,
    teacher_protos,
    centre,
    part,
    last_full,
    teacher_last_full,
    devices,
    device_index,
):
    counted = valid_mask.astype(FULL)
    mask_row = jnp.pad(counted, (0, LANES - counted.size)).reshape(1, LANES)
    scalars, grad_hidden, grad_last, grad_protos, grad_feat, next_centre = head(
        own_feature_rows(features, teacher_features),
        head_hidden,
        teacher_hidden,
        part,
        last_full,
        teacher_last_full,
        protos,
        teacher_protos,
        centre[None],
        counted[:, None],
        mask_row,
        devices,
    )
    count = features.shape[0]
    grad_features = lax.dynamic_slice_in_dim(grad_feat, (device_index % 2) * count, count, 0)
    return (
        scalars[0, 0],
        scalars[0, 1],
        scalars,
        grad_hidden,
        grad_last.T,
        grad_protos,
        grad_features,
        next_centre[0],
    )


def packets_of(grad_table, grad_layers, devices):
    depth = devices // 8
    layers = grad_layers.shape[0]
    parts = grad_layers.reshape(layers, devices, -1, D).transpose(1, 0, 2, 3).reshape(devices, -1, D)
    flat = grad_table.T.reshape(devices, -1)
    flat = jnp.pad(flat, ((0, 0), (0, -flat.shape[1] % (16 * D)))).reshape(devices, -1, D)
    joint = jnp.concatenate([parts, flat], 1).astype(LOW)
    ordered = joint.reshape((depth, 2, 2, 2) + joint.shape[1:]).transpose(1, 2, 3, 0, 4, 5)
    return ordered.reshape(joint.shape)


def tail_fast(
    squares, grad_table, grad_layers, layer_stats, layer_bases, owners, embedding, layers, devices
):
    own_rows = layer_stats.shape[2]
    matrices = owners.shape[0]
    rows_layer = layers.shape[1]
    own, norm, full_stats, full_bases = collect(
        squares,
        packets_of(grad_table, grad_layers, devices),
        layer_stats.reshape(matrices, own_rows, D),
        layer_bases.reshape(matrices, own_rows, D),
        rows_layer,
        layer_bounds(devices),
    )
    count = layers.shape[0] * rows_layer
    grad_layers_own = own[:count].reshape(layers.shape)
    rows, columns = embedding.shape
    grad_embed = own[count:].reshape(-1)[: rows * columns].reshape(columns, rows).T
    renewed = renew_own(full_stats, full_bases)
    stats_own, bases_own = deal(full_stats, renewed, matrices)
    bases_own = jnp.where(
        owners[:, None, None] >= 0, bases_own, layer_bases.reshape(matrices, own_rows, D)
    )
    return (
        norm[0, 0],
        grad_embed,
        grad_layers_own,
        stats_own.reshape(layer_stats.shape),
        bases_own.reshape(layer_bases.shape),
    )


def per_device(
    patches,
    valid_mask,
    owners,
    embedding,
    embedding_first,
    embedding_second,
    layers,
    layers_first,
    layers_second,
    layer_stats,
    layer_bases,
    head_hidden,
    hidden_first,
    hidden_second,
    head_last,
    last_first,
    last_second,
    protos,
    protos_first,
    protos_second,
    teacher_embedding,
    teacher_layers,
    teacher_hidden,
    teacher_last,
    teacher_protos,
    centre,
):
    devices = lax.axis_size("dp")
    device_index = lax.axis_index("dp")
    fast = 2 * head_hidden.shape[0] == LANES
    if fast:
        small, part = spread(
            pack_small(embedding, teacher_embedding, head_last, teacher_last),
            head_hidden[:, D:].astype(LOW),
            devices,
        )
        embed_table, teacher_table, last_full, teacher_last_full = unpack_small(
            small, embedding, head_last, devices
        )
    else:
        embed_table, teacher_table = (
            lax.all_gather(embedding.astype(LOW), "dp", axis=1, tiled=True),
            lax.all_gather(teacher_embedding.astype(LOW), "dp", axis=1, tiled=True),
        )
    layer_full, teacher_full = (
        lax.all_gather(layers.astype(LOW), "dp", axis=1, tiled=True),
        lax.all_gather(teacher_layers.astype(LOW), "dp", axis=1, tiled=True),
    )
    bases_full = lax.all_gather(layer_bases.astype(LOW), "dp", axis=2, tiled=True).astype(
        layer_bases.dtype
    )
    if not fast:
        stats_full = lax.all_gather(layer_stats.astype(LOW), "dp", axis=2, tiled=True).astype(
            layer_stats.dtype
        )
    features, layer_inputs, final_state = backbone(patches, embed_table, layer_full, devices)
    teacher_features, unused_inputs, unused_final = backbone(
        patches, teacher_table, teacher_full, devices
    )
    if fast:
        (
            loss_sum,
            loss_count,
            squares,
            grad_hidden,
            grad_last,
            grad_protos,
            grad_features,
            next_centre,
        ) = head_fast(
            features,
            teacher_features,
            valid_mask,
            head_hidden,
            protos,
            teacher_hidden,
            teacher_protos,
            centre,
            part,
            last_full,
            teacher_last_full,
            devices,
            device_index,
        )
    else:
        (
            loss_sum,
            loss_count,
            grad_hidden,
            grad_last,
            grad_protos,
            grad_features,
            next_centre,
        ) = head_slow(
            features,
            teacher_features,
            valid_mask,
            head_hidden,
            head_last,
            protos,
            teacher_hidden,
            teacher_last,
            teacher_protos,
            centre,
            device_index,
        )
    grad_table, grad_layers = backbone_back(
        patches,
        embed_table,
        layer_full,
        layer_inputs,
        final_state,
        grad_features,
        devices,
        unchanged,
    )
    bounds = layer_bounds(devices)
    if fast:
        grad_norm, grad_embed, grad_layers_own, stats_own, bases_own = tail_fast(
            squares,
            grad_table,
            grad_layers,
            layer_stats,
            layer_bases,
            owners,
            embedding,
            layers,
            devices,
        )
    else:
        summed = (
            lax.psum_scatter(grad_table, "dp", scatter_dimension=1, tiled=True),
            lax.psum_scatter(grad_layers, "dp", scatter_dimension=1, tiled=True),
        )
        grad_embed = summed[0]
        grad_layers_own = summed[1]
        grams = jnp.stack(
            [
                matmul_high(
                    "lcd,lce->lde",
                    grad_layers_own[:, lower_row:upper_row],
                    grad_layers_own[:, lower_row:upper_row],
                )
                for lower_row, upper_row in bounds
            ],
            1,
        )
        squares = (
            jnp.sum(grad_embed * grad_embed)
            + jnp.sum(grad_layers_own * grad_layers_own)
            + jnp.sum(grad_hidden * grad_hidden)
            + jnp.sum(grad_last * grad_last)
            + jnp.sum(grad_protos * grad_protos)
        )
        totals = lax.psum((squares, grams), "dp")
        grad_norm = jnp.sqrt(totals[0])
        clip_factor = jnp.minimum(1.0, CLIP_MAX / (grad_norm + 1e-06))
        next_stats = (
            BETA_STAT * stats_full + (1.0 - BETA_STAT) * (clip_factor * clip_factor) * totals[1]
        )
    clip_factor = jnp.minimum(1.0, CLIP_MAX / (grad_norm + 1e-06))
    rows = jnp.arange(embedding.shape[0])[:, None]
    is_matrix = rows < PIX + SEQ
    embed_out = adam_step(
        embedding,
        clip_factor * grad_embed,
        embedding_first,
        embedding_second,
        jnp.where(is_matrix, RATE_MATRIX, RATE_VECTOR),
        jnp.where(is_matrix, WEIGHT_DECAY, 0.0),
    )
    hidden_out = adam_step(
        head_hidden,
        clip_factor * grad_hidden,
        hidden_first,
        hidden_second,
        RATE_MATRIX,
        WEIGHT_DECAY,
    )
    last_out = adam_step(
        head_last, clip_factor * grad_last, last_first, last_second, RATE_MATRIX, WEIGHT_DECAY
    )
    protos_out = adam_step(
        protos, clip_factor * grad_protos, protos_first, protos_second, RATE_MATRIX, WEIGHT_DECAY
    )
    firsts, seconds, weights_new = ([], [], [])
    for segment, (lower_row, upper_row) in enumerate(bounds):
        basis = bases_full[:, segment]
        weight_block = layers[:, lower_row:upper_row]
        rotated = matmul_high(
            "lcd,ldk->lck", clip_factor * grad_layers_own[:, lower_row:upper_row], basis
        )
        first_new = BETA_ONE * layers_first[:, lower_row:upper_row] + (1.0 - BETA_ONE) * rotated
        second_new = (
            BETA_TWO * layers_second[:, lower_row:upper_row] + (1.0 - BETA_TWO) * rotated * rotated
        )
        direction = (
            first_new
            / (1.0 - BETA_ONE**STEP)
            / (jnp.sqrt(second_new / (1.0 - BETA_TWO**STEP)) + ADAM_EPSILON)
        )
        update = matmul_high("lck,ldk->lcd", direction, basis)
        firsts.append(first_new)
        seconds.append(second_new)
        weights_new.append(weight_block - RATE_MATRIX * (update + WEIGHT_DECAY * weight_block))
    next_layers = jnp.concatenate(weights_new, 1)
    if not fast:
        flat_stats = next_stats.reshape(-1, D, D)
        flat_bases = bases_full.reshape(-1, D, D)

        def renew_owned(operands):
            return lax.cond(operands[2] == device_index, renew, nothing, operands[0], operands[1])

        renewed = lax.psum(lax.map(renew_owned, (flat_stats, flat_bases, owners)), "dp")
        next_bases = jnp.where(owners[:, None, None] >= 0, renewed, flat_bases).reshape(
            bases_full.shape
        )
        own_rows = layer_stats.shape[2]
        stats_own = lax.dynamic_slice_in_dim(next_stats, device_index * own_rows, own_rows, 2)
        bases_own = lax.dynamic_slice_in_dim(next_bases, device_index * own_rows, own_rows, 2)
    return (
        loss_sum,
        loss_count,
        grad_norm,
        embed_out[0],
        embed_out[1],
        embed_out[2],
        jnp.concatenate(firsts, 1),
        jnp.concatenate(seconds, 1),
        next_layers,
        stats_own,
        bases_own,
        hidden_out[0],
        hidden_out[1],
        hidden_out[2],
        last_out[0],
        last_out[1],
        last_out[2],
        protos_out[0],
        protos_out[1],
        protos_out[2],
        follow(teacher_embedding, embed_out[2]),
        follow(teacher_layers, next_layers),
        follow(teacher_hidden, hidden_out[2]),
        follow(teacher_last, last_out[2]),
        follow(teacher_protos, protos_out[2]),
        next_centre,
    )


def solution(mesh):
    placed = (
        P("dp", None, None),
        P(),
        P(),
        P(None, "dp"),
        P(None, "dp"),
        P(None, "dp"),
        P(None, "dp", None),
        P(None, "dp", None),
        P(None, "dp", None),
        P(None, None, "dp", None),
        P(None, None, "dp", None),
        P("dp", None),
        P("dp", None),
        P("dp", None),
        P(None, "dp"),
        P(None, "dp"),
        P(None, "dp"),
        P(None, "dp"),
        P(None, "dp"),
        P(None, "dp"),
        P(None, "dp"),
        P(None, "dp", None),
        P("dp", None),
        P(None, "dp"),
        P(None, "dp"),
        P("dp"),
    )
    return jax.shard_map(
        per_device,
        mesh=mesh,
        in_specs=placed,
        out_specs=(
            P(),
            P(),
            P(),
            P(None, "dp"),
            P(None, "dp"),
            P(None, "dp"),
            P(None, "dp", None),
            P(None, "dp", None),
            P(None, "dp", None),
            P(None, None, "dp", None),
            P(None, None, "dp", None),
            P("dp", None),
            P("dp", None),
            P("dp", None),
            P(None, "dp"),
            P(None, "dp"),
            P(None, "dp"),
            P(None, "dp"),
            P(None, "dp"),
            P(None, "dp"),
            P(None, "dp"),
            P(None, "dp", None),
            P("dp", None),
            P(None, "dp"),
            P(None, "dp"),
            P("dp"),
        ),
        check_vma=False,
    )
```

```python
import functools

import jax
import jax.numpy as jnp
from jax import lax
from jax.experimental import pallas as pl
from jax.experimental.pallas import tpu as pltpu
from jax.sharding import PartitionSpec as P

D = 384
HEADS = 6
HEAD_DIM = 64
MLP = 1536
PIX = 588
LAYERS = 3
STEP = 10
SEQ = 257


NORM_EPSILON = 1e-06
UNIT_EPSILON = 1e-06
TAU_STUDENT = 0.1
TAU_TEACHER = 0.07
CLIP_MAX = 0.001
BETA_ONE = 0.9
BETA_TWO = 0.999
ADAM_EPSILON = 1e-08
WEIGHT_DECAY = 0.04
RATE_MATRIX = 0.04
RATE_VECTOR = 0.2
BETA_STAT = 0.95
TEACHER_MOMENTUM = 0.8
CENTRE_MOMENTUM = 0.9
ROOT_HALF = 0.7071067811865476
DENSITY_SCALE = 0.3989422804014327


def joined(value, axis, join):
    pieces = jax.tree.map(lambda part: lax.all_gather(part, axis), value)
    head = jax.tree.map(lambda part: part[0], pieces)
    tail = jax.tree.map(lambda part: part[1:], pieces)
    running, _ = lax.scan(lambda running, piece: (join(running, piece), None), head, tail)
    return running


def matmul_low(form, left, right):
    return jnp.einsum(form, left, right, preferred_element_type=jnp.float32)


def matmul_high(form, left, right):
    return jnp.einsum(form, left, right, precision=lax.Precision.HIGHEST)


def layer_norm(values, gain_row, shift_row):
    centred = values - jnp.mean(values, -1, keepdims=True)
    inverse_std = lax.rsqrt(jnp.mean(centred * centred, -1, keepdims=True) + NORM_EPSILON)
    return centred * inverse_std * gain_row + shift_row


def norm_back(values, gain_row, grad_out):
    centred = values - jnp.mean(values, -1, keepdims=True)
    inverse_std = lax.rsqrt(jnp.mean(centred * centred, -1, keepdims=True) + NORM_EPSILON)
    normed = centred * inverse_std
    scaled_grad = grad_out * gain_row
    grad_in = inverse_std * (
        scaled_grad
        - jnp.mean(scaled_grad, -1, keepdims=True)
        - normed * jnp.mean(scaled_grad * normed, -1, keepdims=True)
    )
    leading = tuple(range(values.ndim - 1))
    return (grad_in, jnp.sum(grad_out * normed, leading), jnp.sum(grad_out, leading))


def gelu_exact(values):
    return 0.5 * values * (1.0 + lax.erf(values * ROOT_HALF))


def gelu_slope(values):
    return (
        0.5 * (1.0 + lax.erf(values * ROOT_HALF))
        + values * jnp.exp(-0.5 * values * values) * DENSITY_SCALE
    )


def layer_bounds(devices):
    widths = [3 * D // devices, D // devices, MLP // devices, MLP // devices]
    lowers = [0, widths[0], widths[0] + widths[1], widths[0] + widths[1] + widths[2]]
    return [(lowers[segment], lowers[segment] + widths[segment]) for segment in range(4)]


def split_layer(weights, devices):
    blocks = weights.reshape(devices, -1, D)
    return [
        blocks[:, lower_row:upper_row].reshape(-1, D)
        for lower_row, upper_row in layer_bounds(devices)
    ]


def join_layer(members, devices):
    return jnp.concatenate([member.reshape(devices, -1, D) for member in members], 1).reshape(-1, D)


def layer_parts(inputs, matrices, vectors):
    joint_weight, output_weight, inner_weight, outer_weight = matrices
    images, tokens = (inputs.shape[0], inputs.shape[1])
    normed = layer_norm(inputs, vectors[0], vectors[1]).astype(jnp.bfloat16)
    joint = matmul_low("itd,ed->ite", normed, joint_weight).astype(jnp.bfloat16)
    head_split = joint.reshape(images, tokens, 3, HEADS, HEAD_DIM)
    queries, keys_in, values_in = (head_split[:, :, 0], head_split[:, :, 1], head_split[:, :, 2])
    scores = matmul_low("ithd,ishd->ihts", queries, keys_in) * HEAD_DIM ** (-0.5)
    attention = jax.nn.softmax(scores, axis=-1)
    mixed_heads = (
        matmul_low("ihts,ishd->ithd", attention.astype(jnp.bfloat16), values_in)
        .astype(jnp.bfloat16)
        .reshape(images, tokens, D)
    )
    attended = matmul_low("itd,ed->ite", mixed_heads, output_weight)
    middle = inputs + vectors[4] * attended
    normed_two = layer_norm(middle, vectors[2], vectors[3]).astype(jnp.bfloat16)
    inner_pre = matmul_low("itd,md->itm", normed_two, inner_weight)
    activated = gelu_exact(inner_pre).astype(jnp.bfloat16)
    outer_out = matmul_low("itm,md->itd", activated, outer_weight)
    result = middle + vectors[5] * outer_out
    return (
        normed,
        queries,
        keys_in,
        values_in,
        attention,
        mixed_heads,
        attended,
        middle,
        normed_two,
        inner_pre,
        activated,
        outer_out,
        result,
    )


def layer_backward(inputs, matrices, vectors, grad_result):
    joint_weight, output_weight, inner_weight, outer_weight = matrices
    (
        normed,
        queries,
        keys_in,
        values_in,
        attention,
        mixed_heads,
        attended,
        middle,
        normed_two,
        inner_pre,
        activated,
        outer_out,
        result,
    ) = layer_parts(inputs, matrices, vectors)
    images, tokens = (inputs.shape[0], inputs.shape[1])
    grad_outer = (vectors[5] * grad_result).astype(jnp.bfloat16)
    grad_scale_two = jnp.sum(grad_result * outer_out, (0, 1))
    grad_outer_weight = matmul_low("itm,itd->md", activated, grad_outer)
    grad_activated = matmul_low("itd,md->itm", grad_outer, outer_weight)
    grad_inner = (grad_activated * gelu_slope(inner_pre)).astype(jnp.bfloat16)
    grad_inner_weight = matmul_low("itm,itd->md", grad_inner, normed_two)
    grad_normed_two = matmul_low("itm,md->itd", grad_inner, inner_weight)
    grad_middle_norm, grad_gain_two, grad_shift_two = norm_back(middle, vectors[2], grad_normed_two)
    grad_middle = grad_result + grad_middle_norm
    grad_attended = (vectors[4] * grad_middle).astype(jnp.bfloat16)
    grad_scale_one = jnp.sum(grad_middle * attended, (0, 1))
    grad_output_weight = matmul_low("ite,itd->ed", grad_attended, mixed_heads)
    grad_mixed = (
        matmul_low("ite,ed->itd", grad_attended, output_weight)
        .astype(jnp.bfloat16)
        .reshape(images, tokens, HEADS, HEAD_DIM)
    )
    grad_attention = matmul_low("ithd,ishd->ihts", grad_mixed, values_in)
    grad_values = matmul_low("ihts,ithd->ishd", attention.astype(jnp.bfloat16), grad_mixed)
    grad_scores = (
        attention * (grad_attention - jnp.sum(attention * grad_attention, -1, keepdims=True))
    ).astype(jnp.bfloat16)
    grad_queries = matmul_low("ihts,ishd->ithd", grad_scores, keys_in) * HEAD_DIM ** (-0.5)
    grad_keys = matmul_low("ihts,ithd->ishd", grad_scores, queries) * HEAD_DIM ** (-0.5)
    grad_joint = (
        jnp.stack([grad_queries, grad_keys, grad_values], 2)
        .astype(jnp.bfloat16)
        .reshape(images, tokens, 3 * D)
    )
    grad_joint_weight = matmul_low("ite,itd->ed", grad_joint, normed)
    grad_normed = matmul_low("ite,ed->itd", grad_joint, joint_weight)
    grad_input_norm, grad_gain_one, grad_shift_one = norm_back(inputs, vectors[0], grad_normed)
    grad_vectors = jnp.stack(
        [
            grad_gain_one,
            grad_shift_one,
            grad_gain_two,
            grad_shift_two,
            grad_scale_one,
            grad_scale_two,
        ]
    )
    return (
        grad_middle + grad_input_norm,
        (grad_joint_weight, grad_output_weight, grad_inner_weight, grad_outer_weight),
        grad_vectors,
    )


def table_vectors(embed_table):
    return embed_table[PIX + SEQ : PIX + SEQ + 6 * LAYERS].astype(jnp.float32).reshape(LAYERS, 6, D)


def table_tail(embed_table):
    return embed_table[PIX + SEQ + 6 * LAYERS :].astype(jnp.float32)


def backbone(patches, embed_table, layer_stack, devices):
    vectors = table_vectors(embed_table)
    tail_rows = table_tail(embed_table)
    position = embed_table[PIX : PIX + SEQ].astype(jnp.float32)
    projected = matmul_low("ipc,cd->ipd", patches, embed_table[:PIX]) + tail_rows[0]
    leading = jnp.broadcast_to(tail_rows[1] + position[0], (patches.shape[0], 1, D))
    current = jnp.concatenate([leading, projected + position[1:]], 1)
    layer_inputs = []
    for layer_number in range(LAYERS):
        layer_inputs.append(current)
        current = layer_parts(
            current, split_layer(layer_stack[layer_number], devices), vectors[layer_number]
        )[-1]
    features = layer_norm(current[:, 0], tail_rows[2], tail_rows[3]).astype(jnp.bfloat16)
    return (features, layer_inputs, current)


def unchanged(values):
    return values


def backbone_back(
    patches,
    embed_table,
    layer_stack,
    layer_inputs,
    final_state,
    grad_features,
    devices,
    reduce_layer,
):
    vectors = table_vectors(embed_table)
    tail_rows = table_tail(embed_table)
    grad_cls, grad_gain, grad_shift = norm_back(final_state[:, 0], tail_rows[2], grad_features)
    grad_current = jnp.concatenate(
        [grad_cls[:, None], jnp.zeros((final_state.shape[0], SEQ - 1, D), jnp.float32)], 1
    )
    weight_grads = [None] * LAYERS
    vector_grads = [None] * LAYERS
    for layer_number in reversed(range(LAYERS)):
        grad_current, matrices, grad_vectors = layer_backward(
            layer_inputs[layer_number],
            split_layer(layer_stack[layer_number], devices),
            vectors[layer_number],
            grad_current,
        )
        weight_grads[layer_number] = reduce_layer(join_layer(matrices, devices))
        vector_grads[layer_number] = grad_vectors
    grad_patch_weight = matmul_low("ipc,ipd->cd", patches, grad_current[:, 1:].astype(jnp.bfloat16))
    grad_position = jnp.sum(grad_current, 0)
    tail_grads = jnp.stack(
        [
            jnp.sum(grad_current[:, 1:], (0, 1)),
            jnp.sum(grad_current[:, 0], 0),
            grad_gain,
            grad_shift,
        ]
    )
    grad_table = jnp.concatenate(
        [grad_patch_weight, grad_position, jnp.concatenate(vector_grads, 0), tail_grads], 0
    )
    return (grad_table, jnp.stack(weight_grads))


def unit_rows(bottle):
    inverse_norm = lax.rsqrt(jnp.sum(bottle * bottle, -1, keepdims=True) + UNIT_EPSILON)
    return (bottle * inverse_norm, inverse_norm)


def combine_parts(left_part, right_part):
    top_student = jnp.maximum(left_part[0], right_part[0])
    total_student = left_part[1] * jnp.exp(left_part[0] - top_student) + right_part[1] * jnp.exp(
        right_part[0] - top_student
    )
    top_teacher = jnp.maximum(left_part[2], right_part[2])
    left_weight = jnp.exp(left_part[2] - top_teacher)
    right_weight = jnp.exp(right_part[2] - top_teacher)
    return (
        top_student,
        total_student,
        top_teacher,
        left_part[3] * left_weight + right_part[3] * right_weight,
        left_part[4] * left_weight + right_part[4] * right_weight,
    )


def adam_step(weight, grad, first_moment, second_moment, rate, decay):
    first_new = BETA_ONE * first_moment + (1.0 - BETA_ONE) * grad
    second_new = BETA_TWO * second_moment + (1.0 - BETA_TWO) * grad * grad
    direction = (
        first_new
        / (1.0 - BETA_ONE**STEP)
        / (jnp.sqrt(second_new / (1.0 - BETA_TWO**STEP)) + ADAM_EPSILON)
    )
    return (first_new, second_new, weight - rate * (direction + decay * weight))


def renew(stat_matrix, basis):
    scaled = jnp.dot(stat_matrix, basis, precision=lax.Precision.HIGHEST) * (
        D / jnp.trace(stat_matrix)
    )
    gram = jnp.dot(scaled.T, scaled, precision=lax.Precision.HIGHEST)
    lower_factor = jnp.linalg.cholesky(gram)
    return lax.linalg.triangular_solve(lower_factor, scaled.T, left_side=True, lower=True).T


def nothing(stat_matrix, basis):
    return jnp.zeros_like(basis)


def follow(teacher_weight, student_weight):
    return TEACHER_MOMENTUM * teacher_weight + (1.0 - TEACHER_MOMENTUM) * student_weight


MESH = pl.DeviceIdType.MESH
LANES = 128
LOW = jnp.bfloat16
FULL = jnp.float32


def params(identity, vmem=None):
    return pltpu.CompilerParams(
        collective_id=identity, has_side_effects=True, vmem_limit_bytes=vmem or (48 << 20)
    )


def push(source, target, sent, landed, device):
    copy = pltpu.make_async_remote_copy(
        src_ref=source,
        dst_ref=target,
        send_sem=sent,
        recv_sem=landed,
        device_id=(device,),
        device_id_type=MESH,
    )
    copy.start()
    return copy


def greet(peers):
    barrier = pltpu.get_barrier_semaphore()
    for peer in peers:
        pl.semaphore_signal(barrier, inc=1, device_id=(peer,), device_id_type=MESH)
    pl.semaphore_wait(barrier, len(peers))


def dot_nt(left, right):
    return lax.dot_general(left, right, (((1,), (1,)), ((), ())), preferred_element_type=FULL)


def dot_nn(left, right):
    return lax.dot_general(left, right, (((1,), (0,)), ((), ())), preferred_element_type=FULL)


def dot_tn(left, right):
    return lax.dot_general(left, right, (((0,), (0,)), ((), ())), preferred_element_type=FULL)


def spread_kernel(depth, small_ref, columns_ref, all_ref, part_ref, own_sem, sent, landed, csent, clanded):
    me = lax.axis_index("dp")
    total = 8 * depth
    core = lax.rem(me, 2)
    x_at = lax.rem(me // 2, 2)
    y_at = lax.rem(me // 4, 2)
    z_at = me // 8
    peers = [lax.rem(me + step, total) for step in range(1, total)]
    greet(peers)

    def place(y_pos, x_pos, c_pos):
        return ((y_pos * 2 + x_pos) * 2 + c_pos) * depth

    mine = place(y_at, x_at, core)
    across_x = place(y_at, 1 - x_at, core)
    across_y = place(1 - y_at, x_at, core)
    across_d = place(1 - y_at, 1 - x_at, core)
    partner = me + 1 - 2 * core
    to_x = me + 2 - 4 * x_at
    to_y = me + 4 - 8 * y_at
    own = pltpu.make_async_copy(small_ref, all_ref.at[mine + z_at], own_sem.at[0])
    own.start()
    copies = []
    z_copies = []
    for step in range(1, depth):
        peer = lax.rem(me + 8 * step, total)
        z_copies.append(
            push(small_ref, all_ref.at[mine + z_at], sent.at[step], landed.at[step], peer)
        )
    hid_rows = columns_ref.shape[0]
    c_copies = []
    for step, peer in enumerate(peers):
        block = columns_ref.at[:, pl.ds(pl.multiple_of((peer // 2) * LANES, LANES), LANES)]
        c_copies.append(push(block, part_ref.at[me], csent.at[step], clanded.at[step], peer))
    own_block = columns_ref.at[:, pl.ds(pl.multiple_of((me // 2) * LANES, LANES), LANES)]
    own_part = pltpu.make_async_copy(own_block, part_ref.at[me], own_sem.at[1])
    own_part.start()
    own.wait()
    for copy in z_copies:
        copy.wait_recv()
    base = depth

    def column(start, where, device):
        view = all_ref.at[pl.ds(start, depth)]
        return push(view, view, sent.at[where], landed.at[where], device)

    x_copy = column(mine, base, to_x)
    y_copy = column(mine, base + 1, to_y)
    die_own = column(mine, base + 2, partner)
    half = small_ref.shape[0] // 2
    x_copy.wait_recv()
    from_x = all_ref.at[pl.ds(across_x, depth), pl.ds(0, half)]
    d_one = push(from_x, from_x, sent.at[base + 3], landed.at[base + 3], to_y)
    die_x = column(across_x, base + 5, partner)
    y_copy.wait_recv()
    from_y = all_ref.at[pl.ds(across_y, depth), pl.ds(half, half)]
    d_two = push(from_y, from_y, sent.at[base + 4], landed.at[base + 4], to_x)
    die_y = column(across_y, base + 6, partner)
    d_one.wait_recv()
    d_two.wait_recv()
    die_d = column(across_d, base + 7, partner)
    for copy in (die_own, die_x, die_y, die_d):
        copy.wait_recv()
    for copy in c_copies:
        copy.wait_recv()
    own_part.wait()
    for copy in z_copies + c_copies + [x_copy, y_copy, die_own, d_one, d_two, die_x, die_y, die_d]:
        copy.wait_send()


def spread(small, columns, devices):
    depth = devices // 8
    return pl.pallas_call(
        functools.partial(spread_kernel, depth),
        out_shape=(
            jax.ShapeDtypeStruct((devices,) + small.shape, small.dtype),
            jax.ShapeDtypeStruct((devices, columns.shape[0], LANES), columns.dtype),
        ),
        in_specs=[pl.BlockSpec(memory_space=pltpu.VMEM)] * 2,
        out_specs=(pl.BlockSpec(memory_space=pltpu.VMEM),) * 2,
        scratch_shapes=[
            pltpu.SemaphoreType.DMA((2,)),
            pltpu.SemaphoreType.DMA((depth + 8,)),
            pltpu.SemaphoreType.DMA((depth + 8,)),
            pltpu.SemaphoreType.DMA((devices - 1,)),
            pltpu.SemaphoreType.DMA((devices - 1,)),
        ],
        compiler_params=params(1),
        name="spread",
    )(small, columns)


def head_kernel(
    devices,
    feat_ref,
    hidden_ref,
    teacher_hidden_ref,
    part_ref,
    last_ref,
    teacher_last_ref,
    protos_ref,
    teacher_protos_ref,
    centre_ref,
    mask_ref,
    mask_row_ref,
    scalars_ref,
    grad_hidden_ref,
    grad_last_ref,
    grad_protos_ref,
    grad_feat_ref,
    centre_out_ref,
    fb,
    hid_low,
    thid_low,
    prot_low,
    half_out,
    half_in,
    mine_buf,
    other_buf,
    act_s,
    act_t,
    act2_s,
    act2_t,
    pre1,
    pre2,
    unit_ref,
    inv_ref,
    exp_s,
    exp_t,
    stat_out,
    stat_all,
    pz_ref,
    pz_all,
    dz_own,
    dz_all,
    dp_own,
    dp_in,
    dp_cb,
    dp_half,
    dp_full,
    df_part,
    df_all,
    df_sum,
    df_other,
    die_sent,
    die_landed,
    wide_sent,
    wide_landed,
    core_sent,
    core_landed,
):
    me = lax.axis_index("dp")
    core = lax.rem(me, 2)
    chip = me // 2
    chips = devices // 2
    partner = me + 1 - 2 * core
    everyone = [lax.rem(me + step, devices) for step in range(1, devices)]
    same_core = [lax.rem(me + 2 * step, devices) for step in range(1, chips)]
    images = mask_ref.shape[0]
    units = hidden_ref.shape[0]
    groups = images // 8
    greet(everyone)
    sends = []

    def die(step, source, target):
        copy = push(source, target, die_sent.at[step], die_landed.at[step], partner)
        sends.append(copy)
        return copy

    def wide(step, source, target):
        made = [
            push(source, target, wide_sent.at[step, at], wide_landed.at[step, at], peer)
            for at, peer in enumerate(everyone)
        ]
        sends.extend(made)
        return made

    def cores(step, source_of, target):
        made = [
            push(source_of(peer), target, core_sent.at[step, at], core_landed.at[step, at], peer)
            for at, peer in enumerate(same_core)
        ]
        sends.extend(made)
        return made

    fb[me] = feat_ref[...]
    copies = wide(0, feat_ref, fb.at[me])
    hid_low[...] = hidden_ref[...].astype(LOW)
    thid_low[...] = teacher_hidden_ref[...].astype(LOW)
    prot_low[0] = protos_ref[...].astype(LOW)
    prot_low[1] = teacher_protos_ref[...].astype(LOW)
    block_rows = feat_ref.shape[0]
    row_at = lax.broadcasted_iota(jnp.int32, (images, devices * block_rows), 0)
    col_at = lax.broadcasted_iota(jnp.int32, (images, devices * block_rows), 1)
    col_dev = lax.shift_right_logical(col_at, 5)
    col_in = jnp.bitwise_and(col_at, 31)
    lead = row_at - 3 * col_dev
    for copy in copies:
        copy.wait_recv()
    rows_all = fb[...].reshape(devices * block_rows, LANES)

    def features_of(model):
        pieces = []
        for j in range(3):
            hit = (col_in - (16 * model + 3 * j) == lead) & (lead >= 0) & (lead < 3)
            pieces.append(dot_nn(jnp.where(hit, 1.0, 0.0).astype(LOW), rows_all).astype(LOW))
        return jnp.concatenate(pieces, 1)

    feats = features_of(0)
    tfeats = features_of(1)

    def gather_pair(step, student, teacher, out_s, out_t):
        own_model = jnp.where(core == 0, student, teacher)
        half_out[step] = jnp.where(core == 0, teacher, student)
        copy = die(2 * step, half_out.at[step], half_in.at[step])
        copy.wait_recv()
        got = half_in[step]
        block = jnp.concatenate(
            [jnp.where(core == 0, own_model, got), jnp.where(core == 0, got, own_model)], 1
        ).astype(LOW)
        mine_buf[step, chip] = block
        made = cores(step, lambda peer: mine_buf.at[step, chip], mine_buf.at[step, chip])
        for copy in made:
            copy.wait_recv()
        copy = die(2 * step + 1, mine_buf.at[step], other_buf.at[step])
        copy.wait_recv()
        for at in range(chips):
            one, two = mine_buf[step, at], other_buf[step, at]
            out_s[:, at * LANES : (at + 1) * LANES] = jnp.where(core == 0, one, two)
            out_t[:, at * LANES : (at + 1) * LANES] = jnp.where(core == 0, two, one)

    pre_one = dot_nt(feats, hid_low[:, :D])
    pre1[...] = pre_one
    tpre_one = dot_nt(tfeats, thid_low[:, :D])
    gather_pair(0, gelu_exact(pre_one).astype(LOW).astype(FULL), gelu_exact(tpre_one).astype(LOW).astype(FULL), act_s, act_t)
    pre_two = dot_nt(act_s[...], hid_low[:, D:])
    pre2[...] = pre_two
    tpre_two = dot_nt(act_t[...], thid_low[:, D:])
    gather_pair(1, gelu_exact(pre_two).astype(LOW).astype(FULL), gelu_exact(tpre_two).astype(LOW).astype(FULL), act2_s, act2_t)

    unit, inverse_norm = unit_rows(dot_nt(act2_s[...], last_ref[...]))
    tunit, unused = unit_rows(dot_nt(act2_t[...], teacher_last_ref[...]))
    unit_ref[...] = unit
    inv_ref[...] = jnp.broadcast_to(inverse_norm, inv_ref.shape)
    unit_low = unit.astype(LOW)
    scaled = dot_nn(unit_low, prot_low[0]) / TAU_STUDENT
    tlogits = dot_nn(tunit.astype(LOW), prot_low[1])
    top_s = jnp.max(scaled, -1, keepdims=True)
    grown_s = jnp.exp(scaled - top_s)
    exp_s[...] = grown_s
    sharp = (tlogits - centre_ref[...]) / TAU_TEACHER
    top_t = jnp.max(sharp, -1, keepdims=True)
    grown_t = jnp.exp(sharp - top_t)
    exp_t[...] = grown_t
    lane = lax.broadcasted_iota(jnp.int32, (images, LANES), 1)
    stats = jnp.where(lane == 0, top_s, 0.0)
    stats = jnp.where(lane == 1, jnp.sum(grown_s, -1, keepdims=True), stats)
    stats = jnp.where(lane == 2, top_t, stats)
    stats = jnp.where(lane == 3, jnp.sum(grown_t, -1, keepdims=True), stats)
    stats = jnp.where(lane == 4, jnp.sum(grown_t * scaled, -1, keepdims=True), stats)
    square = jnp.concatenate([stats, jnp.zeros((LANES - images, LANES), FULL)], 0)
    stat_out[...] = square.T[:8]
    stat_all[me] = stat_out[...]
    copies = wide(1, stat_out, stat_all.at[me])
    counted = mask_ref[...]
    count = jnp.sum(counted)
    centre_out_ref[...] = (
        CENTRE_MOMENTUM * centre_ref[...]
        + (1.0 - CENTRE_MOMENTUM) * jnp.sum(counted * tlogits, 0, keepdims=True) / count
    )
    for copy in copies:
        copy.wait_recv()
    merged = stat_all[...]
    tops, totals = merged[:, 0], merged[:, 1]
    ttops, ttotals, crosses = merged[:, 2], merged[:, 3], merged[:, 4]
    peak_s = jnp.max(tops, 0, keepdims=True)
    sum_s = jnp.sum(totals * jnp.exp(tops - peak_s), 0, keepdims=True)
    peak_t = jnp.max(ttops, 0, keepdims=True)
    shrink = jnp.exp(ttops - peak_t)
    sum_t = jnp.sum(ttotals * shrink, 0, keepdims=True)
    cross = jnp.sum(crosses * shrink, 0, keepdims=True)
    log_total = peak_s + jnp.log(sum_s)
    mask_row = mask_row_ref[...]
    losses = jnp.where(mask_row > 0.0, log_total - cross / sum_t, 0.0)
    loss = jnp.sum(losses)
    lane8 = lax.broadcasted_iota(jnp.int32, (8, LANES), 1)
    scalars_ref[...] = jnp.where(lane8 == 0, loss, jnp.where(lane8 == 1, count, 0.0))
    back = jnp.concatenate(
        [log_total, peak_t, 1.0 / sum_t, jnp.zeros((LANES - 3, LANES), FULL)], 0
    ).T
    share_s = jnp.exp(top_s - back[:images, 0:1])
    share_t = jnp.exp(top_t - back[:images, 1:2]) * back[:images, 2:3]
    grad_logits = (
        (counted / count) * (exp_s[...] * share_s - exp_t[...] * share_t) / TAU_STUDENT
    ).astype(LOW)

    pz_ref[...] = dot_nt(grad_logits, prot_low[0]).reshape(groups, 8, unit.shape[1])
    for group in range(groups):
        owner = 2 * group

        @pl.when(me != owner)
        def _(group=group, owner=owner):
            push(pz_ref.at[group], pz_all.at[me], wide_sent.at[2, group], wide_landed.at[2, me], owner)

    grad_protos_ref[...] = dot_tn(unit_low, grad_logits)

    @pl.when((core == 0) & (chip < groups))
    def _():
        pz_all[me] = pz_ref[chip]
        for source in range(devices):

            @pl.when(source != me)
            def _(source=source):
                pltpu.make_async_copy(pz_all.at[source], pz_all.at[source], wide_landed.at[2, source]).wait()

        total = jnp.sum(pz_all[...], 0)
        rows = pl.ds(pl.multiple_of(chip * 8, 8), 8)
        own_unit = unit_ref[rows, :]
        own_inv = inv_ref[rows, :][:, 0:1]
        dz_own[...] = own_inv * (total - own_unit * jnp.sum(own_unit * total, -1, keepdims=True))
        dz_all[chip] = dz_own[...]
        for step in range(1, devices):
            push(dz_own, dz_all.at[chip], wide_sent.at[3, step - 1], wide_landed.at[3, chip], lax.rem(me + step, devices))

    for group in range(groups):

        @pl.when(me != 2 * group)
        def _(group=group):
            pltpu.make_async_copy(dz_all.at[group], dz_all.at[group], wide_landed.at[3, group]).wait()

    grad_bottle = dz_all[...].reshape(images, unit.shape[1]).astype(LOW)
    chip_columns = pl.ds(pl.multiple_of(chip * LANES, LANES), LANES)
    pair = dot_nn(grad_bottle, last_ref[:, chip_columns])
    grad_act_two = jnp.where(core == 0, pair[:, :units], pair[:, units:])
    grad_pre_two = (grad_act_two * gelu_slope(pre2[...])).astype(LOW)

    dp_own[...] = grad_pre_two.astype(FULL)
    copy = die(4, dp_own, dp_in)
    width = last_ref.shape[0] // devices
    pick_row = lax.broadcasted_iota(jnp.int32, (width, last_ref.shape[0]), 0)
    pick_col = lax.broadcasted_iota(jnp.int32, (width, last_ref.shape[0]), 1)
    pick = jnp.where(pick_col == pick_row + me * width, 1.0, 0.0).astype(LOW)
    own_bottle = dot_nt(pick, grad_bottle).astype(LOW)
    grad_last_ref[...] = dot_nn(own_bottle, act2_s[...])
    copy.wait_recv()
    own_dp, got_dp = dp_own[...], dp_in[...]
    dp_cb[...] = jnp.concatenate(
        [jnp.where(core == 0, own_dp, got_dp), jnp.where(core == 0, got_dp, own_dp)], 1
    ).astype(LOW)
    half = images // 2
    my_rows = pl.ds(pl.multiple_of(core * half, 16), half)
    their_rows = pl.ds(pl.multiple_of((1 - core) * half, 16), half)
    dp_half[0, chip] = dp_cb[my_rows, :]
    made = cores(2, lambda peer: dp_half.at[0, chip], dp_half.at[0, chip])
    grad_hidden_ref[:, D:] = dot_tn(grad_pre_two, act_s[...])
    for copy in made:
        copy.wait_recv()
    copy = die(5, dp_half.at[0], dp_half.at[1])
    for at in range(chips):
        dp_full[my_rows, at * LANES : (at + 1) * LANES] = dp_half[0, at]
    copy.wait_recv()
    for at in range(chips):
        dp_full[their_rows, at * LANES : (at + 1) * LANES] = dp_half[1, at]
    pair = dot_nn(dp_full[...], part_ref[...].reshape(devices * units, LANES))
    grad_act_one = jnp.where(core == 0, pair[:, :units], pair[:, units:])
    grad_pre_one = (grad_act_one * gelu_slope(pre1[...])).astype(LOW)

    out_row = lax.broadcasted_iota(jnp.int32, (8 * chips, images), 0)
    in_row = lax.broadcasted_iota(jnp.int32, (8 * chips, images), 1)
    out_chip = lax.shift_right_logical(out_row, 3)
    out_in = jnp.bitwise_and(out_row, 7)
    hit = (in_row - 6 * out_chip == out_in) & (out_in < 6)
    moved = dot_nn(jnp.where(hit, 1.0, 0.0).astype(LOW), grad_pre_one).astype(LOW)
    df_part[...] = dot_nn(moved, hid_low[:, :D]).reshape(chips, 8, D)
    df_all[chip] = df_part[chip]
    made = cores(3, lambda peer: df_part.at[peer // 2], df_all.at[chip])
    grad_hidden_ref[:, :D] = dot_tn(grad_pre_one, feats)
    for copy in made:
        copy.wait_recv()
    df_sum[...] = jnp.sum(df_all[...], 0)
    copy = die(6, df_sum, df_other)
    copy.wait_recv()
    whole = df_sum[...] + df_other[...]
    grad_feat_ref[...] = whole
    squares = jnp.sum(grad_hidden_ref[...] * grad_hidden_ref[...])
    squares = squares + jnp.sum(grad_last_ref[...] * grad_last_ref[...])
    squares = squares + jnp.sum(grad_protos_ref[...] * grad_protos_ref[...])
    scalars_ref[...] = jnp.where(lane8 == 2, squares, scalars_ref[...])
    for copy in sends:
        copy.wait_send()
    for group in range(groups):

        @pl.when(me != 2 * group)
        def _(group=group):
            pltpu.make_async_copy(pz_ref.at[group], pz_ref.at[group], wide_sent.at[2, group]).wait()

    @pl.when((core == 0) & (chip < groups))
    def _():
        for step in range(1, devices):
            pltpu.make_async_copy(dz_own, dz_own, wide_sent.at[3, step - 1]).wait()


def head(feat, hidden, teacher_hidden, part, last, teacher_last, protos, teacher_protos, centre, mask, mask_row, devices):
    images = mask.shape[0]
    units, wide = hidden.shape
    bottle, width = protos.shape
    hid = last.shape[1]
    chips = devices // 2
    groups = images // 8
    vmem = pl.BlockSpec(memory_space=pltpu.VMEM)
    shape = jax.ShapeDtypeStruct
    dma = pltpu.SemaphoreType.DMA
    return pl.pallas_call(
        functools.partial(head_kernel, devices),
        out_shape=(
            shape((8, LANES), FULL),
            shape((units, wide), FULL),
            shape((bottle // devices, hid), FULL),
            shape((bottle, width), FULL),
            shape((8, D), FULL),
            shape((1, width), FULL),
        ),
        in_specs=[vmem] * 11,
        out_specs=(vmem,) * 6,
        scratch_shapes=[
            pltpu.VMEM((devices,) + feat.shape, LOW),
            pltpu.VMEM((units, wide), LOW),
            pltpu.VMEM((units, wide), LOW),
            pltpu.VMEM((2, bottle, width), LOW),
            pltpu.VMEM((2, images, units), FULL),
            pltpu.VMEM((2, images, units), FULL),
            pltpu.VMEM((2, chips, images, LANES), LOW),
            pltpu.VMEM((2, chips, images, LANES), LOW),
            pltpu.VMEM((images, hid), LOW),
            pltpu.VMEM((images, hid), LOW),
            pltpu.VMEM((images, hid), LOW),
            pltpu.VMEM((images, hid), LOW),
            pltpu.VMEM((images, units), FULL),
            pltpu.VMEM((images, units), FULL),
            pltpu.VMEM((images, bottle), FULL),
            pltpu.VMEM((images, LANES), FULL),
            pltpu.VMEM((images, width), FULL),
            pltpu.VMEM((images, width), FULL),
            pltpu.VMEM((8, LANES), FULL),
            pltpu.VMEM((devices, 8, LANES), FULL),
            pltpu.VMEM((groups, 8, bottle), FULL),
            pltpu.VMEM((devices, 8, bottle), FULL),
            pltpu.VMEM((8, bottle), FULL),
            pltpu.VMEM((groups, 8, bottle), FULL),
            pltpu.VMEM((images, units), FULL),
            pltpu.VMEM((images, units), FULL),
            pltpu.VMEM((images, LANES), LOW),
            pltpu.VMEM((2, chips, images // 2, LANES), LOW),
            pltpu.VMEM((images, hid), LOW),
            pltpu.VMEM((chips, 8, D), FULL),
            pltpu.VMEM((chips, 8, D), FULL),
            pltpu.VMEM((8, D), FULL),
            pltpu.VMEM((8, D), FULL),
            dma((7,)),
            dma((7,)),
            dma((4, devices)),
            dma((4, devices)),
            dma((4, chips - 1)),
            dma((4, chips - 1)),
        ],
        compiler_params=params(2),
        name="head",
    )(feat, hidden, teacher_hidden, part, last, teacher_last, protos, teacher_protos, centre, mask, mask_row)


def gram_device(matrix):
    return 2 * matrix


def collect_kernel(
    depth,
    rows_layer,
    bounds,
    squares_ref,
    packet_ref,
    stats_ref,
    bases_ref,
    own_ref,
    norm_ref,
    next_stats_ref,
    basis_ref,
    die_buf,
    d_buf,
    x_buf,
    y_buf,
    z_buf,
    stat_buf,
    square_out,
    square_all,
    segs,
    gram_buf,
    die_sent,
    die_landed,
    near_sent,
    near_landed,
    z_sent,
    z_landed,
    stat_sent,
    stat_landed,
    gram_sent,
    gram_landed,
    square_sent,
    square_landed,
):
    me = lax.axis_index("dp")
    total = 8 * depth
    core = lax.rem(me, 2)
    x_at = lax.rem(me // 2, 2)
    y_at = lax.rem(me // 4, 2)
    z_at = me // 8
    chip = me // 2
    partner = me + 1 - 2 * core
    to_x = me + 2 - 4 * x_at
    to_y = me + 4 - 8 * y_at
    everyone = [lax.rem(me + step, total) for step in range(1, total)]
    matrices = stats_ref.shape[0]
    own_rows = stats_ref.shape[1]
    segment_rows = segs.shape[2]
    is_gram = (core == 0) & (chip < matrices)
    greet(everyone)
    sends = []

    def place(y_pos, x_pos, c_pos):
        return ((y_pos * 2 + x_pos) * 2 + c_pos) * depth

    relative = [(y_at, x_at), (y_at, 1 - x_at), (1 - y_at, x_at), (1 - y_at, 1 - x_at)]
    starts = [place(y_pos, x_pos, core) for y_pos, x_pos in relative]
    partner_starts = [place(y_pos, x_pos, 1 - core) for y_pos, x_pos in relative]
    layers = (packet_ref.shape[1] // rows_layer)
    chunks = [(layer * rows_layer, rows_layer) for layer in reversed(range(layers))]
    chunks.append((layers * rows_layer, packet_ref.shape[1] - layers * rows_layer))
    count = len(chunks)

    def first_half(k):
        return ((chunks[k][1] // 2 + 15) // 16) * 16

    die_copies = {}
    for k in range(count):
        lower, size = chunks[k]
        for rel in (3, 1, 2, 0):
            copy = push(
                packet_ref.at[pl.ds(partner_starts[rel], depth), pl.ds(lower, size)],
                die_buf.at[pl.ds(rel * depth, depth), pl.ds(lower, size)],
                die_sent.at[k, rel],
                die_landed.at[k, rel],
                partner,
            )
            die_copies[k, rel] = copy
            sends.append(copy)

    for matrix in range(matrices):
        owner = gram_device(matrix)

        @pl.when(me != owner)
        def _(matrix=matrix, owner=owner):
            push(stats_ref.at[matrix], stat_buf.at[0, me], stat_sent.at[0, matrix], stat_landed.at[0, me], owner)
            push(bases_ref.at[matrix], stat_buf.at[1, me], stat_sent.at[1, matrix], stat_landed.at[1, me], owner)

    near = {}

    def pair_sum(rel, z_pos, lower, size):
        return packet_ref[starts[rel] + z_pos, pl.ds(lower, size), :].astype(FULL) + die_buf[
            rel * depth + z_pos, pl.ds(lower, size), :
        ].astype(FULL)

    def stage_one(k):
        lower, size = chunks[k]
        half = first_half(k)
        die_copies[k, 3].wait_recv()
        for z_pos in range(depth):
            die_buf[3 * depth + z_pos, pl.ds(lower, size), :] = pair_sum(3, z_pos, lower, size).astype(LOW)
        for which, (start, length, peer) in enumerate(
            [(lower, half, to_x), (lower + half, size - half, to_y)]
        ):
            copy = push(
                die_buf.at[pl.ds(3 * depth, depth), pl.ds(start, length)],
                d_buf.at[:, pl.ds(start, length)],
                near_sent.at[k, which],
                near_landed.at[k, which],
                peer,
            )
            near[k, which] = copy
            sends.append(copy)

    def stage_two(k):
        lower, size = chunks[k]
        half = first_half(k)
        for rel, which, peer, target in ((1, 2, to_x, x_buf), (2, 3, to_y, y_buf)):
            die_copies[k, rel].wait_recv()
            near[k, 1 if rel == 1 else 0].wait_recv()
            first, second = (lower, half), (lower + half, size - half)
            helped, plain = (second, first) if rel == 1 else (first, second)
            for z_pos in range(depth):
                die_buf[rel * depth + z_pos, pl.ds(plain[0], plain[1]), :] = pair_sum(
                    rel, z_pos, plain[0], plain[1]
                ).astype(LOW)
                die_buf[rel * depth + z_pos, pl.ds(helped[0], helped[1]), :] = (
                    pair_sum(rel, z_pos, helped[0], helped[1])
                    + d_buf[z_pos, pl.ds(helped[0], helped[1]), :].astype(FULL)
                ).astype(LOW)
            copy = push(
                die_buf.at[pl.ds(rel * depth, depth), pl.ds(lower, size)],
                target.at[:, pl.ds(lower, size)],
                near_sent.at[k, which],
                near_landed.at[k, which],
                peer,
            )
            near[k, which] = copy
            sends.append(copy)

    z_copies = {}

    def stage_three(k):
        lower, size = chunks[k]
        die_copies[k, 0].wait_recv()
        near[k, 2].wait_recv()
        near[k, 3].wait_recv()
        for z_pos in range(depth):
            die_buf[z_pos, pl.ds(lower, size), :] = (
                pair_sum(0, z_pos, lower, size)
                + x_buf[z_pos, pl.ds(lower, size), :].astype(FULL)
                + y_buf[z_pos, pl.ds(lower, size), :].astype(FULL)
            ).astype(LOW)
        for step in range(1, depth):
            z_to = lax.rem(z_at + step, depth)
            copy = push(
                die_buf.at[z_to, pl.ds(lower, size)],
                z_buf.at[z_at, pl.ds(lower, size)],
                z_sent.at[k, step],
                z_landed.at[k, step],
                lax.rem(me + 8 * step, total),
            )
            z_copies[k, step] = copy
            sends.append(copy)

    def stage_four(k):
        lower, size = chunks[k]
        for step in range(1, depth):
            z_copies[k, step].wait_recv()
        value = die_buf[z_at, pl.ds(lower, size), :].astype(FULL)
        for step in range(1, depth):
            value = value + z_buf[lax.rem(z_at + step, depth), pl.ds(lower, size), :].astype(FULL)
        own_ref[pl.ds(lower, size), :] = value
        if k == count - 1:
            return
        layer = lower // rows_layer
        for segment, (low_row, high_row) in enumerate(bounds):
            piece = value[low_row:high_row].astype(LOW)
            if high_row - low_row < segment_rows:
                blank = jnp.zeros((segment_rows - (high_row - low_row), value.shape[1]), LOW)
                piece = jnp.concatenate([piece, blank], 0)
            matrix = 4 * layer + segment
            segs[layer, segment] = piece
            owner = gram_device(matrix)

            @pl.when(me != owner)
            def _(matrix=matrix, owner=owner, layer=layer, segment=segment):
                push(segs.at[layer, segment], gram_buf.at[me], gram_sent.at[matrix], gram_landed.at[me], owner)

    stages = [stage_one, stage_two, stage_three, stage_four]
    for step in range(count + len(stages) - 1):
        for at, stage in enumerate(stages):
            if 0 <= step - at < count:
                stage(step - at)

    own = own_ref[...]
    lane8 = lax.broadcasted_iota(jnp.int32, (8, LANES), 1)
    squares = jnp.sum(own * own) + jnp.sum(jnp.where(lane8 == 2, squares_ref[...], 0.0)) / 8.0
    square_out[...] = jnp.full((8, LANES), squares)
    square_all[me] = square_out[...]
    copies = [
        push(square_out, square_all.at[me], square_sent.at[at], square_landed.at[at], peer)
        for at, peer in enumerate(everyone)
    ]
    sends.extend(copies)
    for copy in copies:
        copy.wait_recv()
    squares = jnp.sum(square_all[...], 0)
    norm = jnp.sqrt(squares)
    norm_ref[...] = norm
    clip = jnp.minimum(1.0, CLIP_MAX / (norm + 1e-06))[:1, :1]

    @pl.when(is_gram)
    def _():
        for matrix in range(matrices):

            @pl.when(matrix == chip)
            def _(matrix=matrix):
                gram_buf[me] = segs[matrix // 4, matrix % 4]
                stat_buf[0, me] = stats_ref[matrix]
                stat_buf[1, me] = bases_ref[matrix]

        for source in range(total):

            @pl.when(source != me)
            def _(source=source):
                for at in range(2):
                    pltpu.make_async_copy(
                        stat_buf.at[at, source], stat_buf.at[at, source], stat_landed.at[at, source]
                    ).wait()
                pltpu.make_async_copy(gram_buf.at[source], gram_buf.at[source], gram_landed.at[source]).wait()

        rows = gram_buf[...].reshape(total * segment_rows, gram_buf.shape[2])
        gram = dot_tn(rows, rows)
        scale = (1.0 - BETA_STAT) * (clip * clip)
        for source in range(total):
            next_stats_ref[source] = (
                BETA_STAT * stat_buf[0, source]
                + scale * gram[source * own_rows : (source + 1) * own_rows]
            )
        basis_ref[...] = stat_buf[1]

    @pl.when(jnp.logical_not(is_gram))
    def _():
        next_stats_ref[...] = jnp.zeros(next_stats_ref.shape, FULL)
        basis_ref[...] = jnp.zeros(basis_ref.shape, FULL)

    for copy in sends:
        copy.wait_send()
    for matrix in range(matrices):

        @pl.when(me != gram_device(matrix))
        def _(matrix=matrix):
            for at, source in ((0, stats_ref), (1, bases_ref)):
                pltpu.make_async_copy(source.at[matrix], source.at[matrix], stat_sent.at[at, matrix]).wait()
            own_segment = segs.at[matrix // 4, matrix % 4]
            pltpu.make_async_copy(own_segment, own_segment, gram_sent.at[matrix]).wait()


def collect(squares, packets, stats, bases, rows_layer, bounds):
    devices, rows, width = packets.shape
    depth = devices // 8
    matrices, own_rows = stats.shape[:2]
    layers = rows // rows_layer
    segment_rows = -(-max(high - low for low, high in bounds) // 16) * 16
    vmem = pl.BlockSpec(memory_space=pltpu.VMEM)
    shape = jax.ShapeDtypeStruct
    dma = pltpu.SemaphoreType.DMA
    count = layers + 1
    return pl.pallas_call(
        functools.partial(collect_kernel, depth, rows_layer, bounds),
        out_shape=(
            shape((rows, width), FULL),
            shape((8, LANES), FULL),
            shape((devices, own_rows, width), FULL),
            shape((devices, own_rows, width), FULL),
        ),
        in_specs=[vmem] * 4,
        out_specs=(vmem,) * 4,
        scratch_shapes=[
            pltpu.VMEM((4 * depth, rows, width), LOW),
            pltpu.VMEM((depth, rows, width), LOW),
            pltpu.VMEM((depth, rows, width), LOW),
            pltpu.VMEM((depth, rows, width), LOW),
            pltpu.VMEM((depth, rows, width), LOW),
            pltpu.VMEM((2, devices, own_rows, width), FULL),
            pltpu.VMEM((8, LANES), FULL),
            pltpu.VMEM((devices, 8, LANES), FULL),
            pltpu.VMEM((layers, 4, segment_rows, width), LOW),
            pltpu.VMEM((devices, segment_rows, width), LOW),
            dma((count, 4)),
            dma((count, 4)),
            dma((count, 4)),
            dma((count, 4)),
            dma((count, depth)),
            dma((count, depth)),
            dma((2, matrices)),
            dma((2, devices)),
            dma((matrices,)),
            dma((devices,)),
            dma((devices - 1,)),
            dma((devices - 1,)),
        ],
        compiler_params=params(3, 56 << 20),
        name="collect",
    )(squares, packets, stats, bases)


def dot_high(left, right, contract):
    return lax.dot_general(
        left,
        right,
        (contract, ((), ())),
        precision=lax.Precision.HIGHEST,
        preferred_element_type=FULL,
    )


def inverse_factor(block):
    size = block.shape[0]
    tiles = size // 8
    sub = lax.broadcasted_iota(jnp.int32, (8, size), 0)
    lane = lax.broadcasted_iota(jnp.int32, (8, size), 1)
    rest = [block[8 * t : 8 * t + 8] for t in range(tiles)]
    made = [jnp.where(lane == sub + 8 * t, 1.0, 0.0) for t in range(tiles)]
    for k in range(size):
        tile, row = k // 8, k % 8
        pivot = rest[tile][row : row + 1]
        scale = lax.rsqrt(pivot[:, k : k + 1])
        factor_row = pivot * scale
        made_row = made[tile][row : row + 1] * scale
        for t in range(tile, tiles):
            column = rest[t][:, k : k + 1] * scale
            if t == tile:
                column = jnp.where(sub[:, :1] > row, column, 0.0)
            rest[t] = rest[t] - column * factor_row
            made[t] = made[t] - column * made_row
            if t == tile:
                made[t] = jnp.where(sub == row, made_row, made[t])
    return jnp.concatenate(made, 0)


def renew_kernel(stats_ref, basis_ref, out_ref, stat, base, gram, work, done):
    parts, rows = stats_ref.shape[:2]
    size = parts * rows
    blocks = size // LANES
    for part in range(parts):
        stat[part * rows : (part + 1) * rows] = stats_ref[part]
        base[part * rows : (part + 1) * rows] = basis_ref[part]
    at_row = lax.broadcasted_iota(jnp.int32, (size, size), 0)
    at_col = lax.broadcasted_iota(jnp.int32, (size, size), 1)
    trace = jnp.sum(jnp.where(at_row == at_col, stat[...], 0.0), axis=(0, 1), keepdims=True)
    scaled = dot_high(stat[...], base[...], ((1,), (0,))) * (size / trace)
    product = dot_high(scaled, scaled, ((0,), (0,)))
    for b in range(blocks):
        work[b] = scaled[:, b * LANES : (b + 1) * LANES]
        for c in range(blocks):
            gram[b, c] = product[b * LANES : (b + 1) * LANES, c * LANES : (c + 1) * LANES]

    def step(b, carried):
        inverse = inverse_factor(gram[b, b])
        made = dot_high(work[b], inverse, ((1,), (1,)))
        done[b] = made

        def trail(c, inner):
            panel = dot_high(inverse, gram[b, c], ((1,), (0,)))
            work[c] = work[c] - dot_high(made, panel, ((1,), (0,)))

            def against(e, innermost):
                other = dot_high(inverse, gram[b, e], ((1,), (0,)))
                gram[c, e] = gram[c, e] - dot_high(panel, other, ((0,), (0,)))
                return innermost

            lax.fori_loop(c, blocks, against, 0)
            return inner

        lax.fori_loop(b + 1, blocks, trail, 0)
        return carried

    lax.fori_loop(0, blocks, step, 0)
    whole = jnp.concatenate([done[b] for b in range(blocks)], 1)
    for part in range(parts):
        out_ref[part] = whole[part * rows : (part + 1) * rows]


def renew_own(stats, basis):
    devices, rows, width = stats.shape
    size = devices * rows
    blocks = size // LANES
    vmem = pl.BlockSpec(memory_space=pltpu.VMEM)
    return pl.pallas_call(
        renew_kernel,
        out_shape=jax.ShapeDtypeStruct(stats.shape, FULL),
        in_specs=[vmem] * 2,
        out_specs=vmem,
        scratch_shapes=[
            pltpu.VMEM((size, width), FULL),
            pltpu.VMEM((size, width), FULL),
            pltpu.VMEM((blocks, blocks, LANES, LANES), FULL),
            pltpu.VMEM((blocks, size, LANES), FULL),
            pltpu.VMEM((blocks, size, LANES), FULL),
        ],
        compiler_params=pltpu.CompilerParams(vmem_limit_bytes=32 << 20),
        name="renew",
    )(stats, basis)


def deal_kernel(devices, stats_ref, bases_ref, own_stats_ref, own_bases_ref, sent, landed):
    me = lax.axis_index("dp")
    core = lax.rem(me, 2)
    chip = me // 2
    matrices = own_stats_ref.shape[0]
    is_gram = (core == 0) & (chip < matrices)
    greet([lax.rem(me + step, devices) for step in range(1, devices)])

    @pl.when(is_gram)
    def _():
        for step in range(1, devices):
            peer = lax.rem(me + step, devices)
            push(bases_ref.at[peer], own_bases_ref.at[chip], sent.at[1, step], landed.at[1, chip], peer)
        for step in range(1, devices):
            peer = lax.rem(me + step, devices)
            push(stats_ref.at[peer], own_stats_ref.at[chip], sent.at[0, step], landed.at[0, chip], peer)
        own_stats_ref[chip] = stats_ref[me]
        own_bases_ref[chip] = bases_ref[me]

    for matrix in range(matrices):

        @pl.when(me != gram_device(matrix))
        def _(matrix=matrix):
            for at, target in ((0, own_stats_ref), (1, own_bases_ref)):
                pltpu.make_async_copy(target.at[matrix], target.at[matrix], landed.at[at, matrix]).wait()

    @pl.when(is_gram)
    def _():
        for step in range(1, devices):
            for at, source in ((0, stats_ref), (1, bases_ref)):
                pltpu.make_async_copy(source.at[0], source.at[0], sent.at[at, step]).wait()


def deal(stats, bases, matrices):
    devices, rows, width = stats.shape
    vmem = pl.BlockSpec(memory_space=pltpu.VMEM)
    dma = pltpu.SemaphoreType.DMA
    return pl.pallas_call(
        functools.partial(deal_kernel, devices),
        out_shape=(jax.ShapeDtypeStruct((matrices, rows, width), FULL),) * 2,
        in_specs=[vmem] * 2,
        out_specs=(vmem,) * 2,
        scratch_shapes=[dma((2, devices)), dma((2, matrices))],
        compiler_params=params(4),
        name="deal",
    )(stats, bases)


def head_slow(
    features,
    teacher_features,
    valid_mask,
    head_hidden,
    head_last,
    protos,
    teacher_hidden,
    teacher_last,
    teacher_protos,
    centre,
    device_index,
):
    all_features, all_teacher = (
        lax.all_gather(features, "dp", axis=0, tiled=True),
        lax.all_gather(teacher_features, "dp", axis=0, tiled=True),
    )
    first_weight = head_hidden[:, :D].astype(jnp.bfloat16)
    second_weight = head_hidden[:, D:].astype(jnp.bfloat16)
    last_weight = head_last.astype(jnp.bfloat16)
    proto_weight = protos.astype(jnp.bfloat16)
    teacher_first = teacher_hidden[:, :D].astype(jnp.bfloat16)
    teacher_second = teacher_hidden[:, D:].astype(jnp.bfloat16)
    pre_one = matmul_low("bd,hd->bh", all_features, first_weight)
    teacher_pre_one = matmul_low("bd,hd->bh", all_teacher, teacher_first)
    act_one = (
        lax.all_gather(gelu_exact(pre_one).astype(jnp.bfloat16), "dp", axis=1, tiled=True),
        lax.all_gather(gelu_exact(teacher_pre_one).astype(jnp.bfloat16), "dp", axis=1, tiled=True),
    )
    pre_two = matmul_low("bh,kh->bk", act_one[0], second_weight)
    teacher_pre_two = matmul_low("bh,kh->bk", act_one[1], teacher_second)
    act_two = (
        lax.all_gather(gelu_exact(pre_two).astype(jnp.bfloat16), "dp", axis=1, tiled=True),
        lax.all_gather(gelu_exact(teacher_pre_two).astype(jnp.bfloat16), "dp", axis=1, tiled=True),
    )
    bottles = (
        lax.all_gather(matmul_low("bh,hc->bc", act_two[0], last_weight), "dp", axis=1, tiled=True),
        lax.all_gather(
            matmul_low("bh,hc->bc", act_two[1], teacher_last.astype(jnp.bfloat16)),
            "dp",
            axis=1,
            tiled=True,
        ),
    )
    unit, inverse_norm = unit_rows(bottles[0])
    teacher_unit, unused_norm = unit_rows(bottles[1])
    unit_low = unit.astype(jnp.bfloat16)
    logits = matmul_low("bc,cp->bp", unit_low, proto_weight)
    teacher_logits = matmul_low(
        "bc,cp->bp", teacher_unit.astype(jnp.bfloat16), teacher_protos.astype(jnp.bfloat16)
    )
    scaled = logits / TAU_STUDENT
    student_top = jnp.max(scaled, -1)
    student_total = jnp.sum(jnp.exp(scaled - student_top[:, None]), -1)
    sharpened = (teacher_logits - centre) / TAU_TEACHER
    teacher_top = jnp.max(sharpened, -1)
    teacher_exp = jnp.exp(sharpened - teacher_top[:, None])
    merged = joined(
        (
            student_top,
            student_total,
            teacher_top,
            jnp.sum(teacher_exp, -1),
            jnp.sum(teacher_exp * scaled, -1),
        ),
        "dp",
        combine_parts,
    )
    log_total = merged[0] + jnp.log(merged[1])
    counted = valid_mask.astype(jnp.float32)
    loss_count = jnp.sum(counted)
    loss_sum = jnp.sum(counted * (log_total - merged[4] / merged[3]))
    student_prob = jnp.exp(scaled - log_total[:, None])
    teacher_prob = jnp.exp(sharpened - merged[2][:, None]) / merged[3][:, None]
    grad_logits = (
        (counted / loss_count)[:, None] * (student_prob - teacher_prob) / TAU_STUDENT
    ).astype(jnp.bfloat16)
    grad_protos = matmul_low("bc,bp->cp", unit_low, grad_logits)
    grad_unit = lax.psum(matmul_low("bp,cp->bc", grad_logits, proto_weight), "dp")
    grad_bottle = inverse_norm * (grad_unit - unit * jnp.sum(unit * grad_unit, -1, keepdims=True))
    last_width = head_last.shape[1]
    grad_bottle_own = lax.dynamic_slice_in_dim(
        grad_bottle, device_index * last_width, last_width, 1
    ).astype(jnp.bfloat16)
    grad_last = matmul_low("bh,bc->hc", act_two[0], grad_bottle_own)
    grad_act_two = lax.psum_scatter(
        matmul_low("bc,hc->bh", grad_bottle_own, last_weight), "dp", scatter_dimension=1, tiled=True
    )
    grad_pre_two = (grad_act_two * gelu_slope(pre_two)).astype(jnp.bfloat16)
    grad_second = matmul_low("bk,bh->kh", grad_pre_two, act_one[0])
    grad_act_one = lax.psum_scatter(
        matmul_low("bk,kh->bh", grad_pre_two, second_weight), "dp", scatter_dimension=1, tiled=True
    )
    grad_pre_one = (grad_act_one * gelu_slope(pre_one)).astype(jnp.bfloat16)
    grad_first = matmul_low("bh,bd->hd", grad_pre_one, all_features)
    grad_features = lax.psum_scatter(
        matmul_low("bh,hd->bd", grad_pre_one, first_weight), "dp", scatter_dimension=0, tiled=True
    )
    grad_hidden = jnp.concatenate([grad_first, grad_second], 1)
    next_centre = (
        CENTRE_MOMENTUM * centre
        + (1.0 - CENTRE_MOMENTUM) * jnp.sum(counted[:, None] * teacher_logits, 0) / loss_count
    )
    return (loss_sum, loss_count, grad_hidden, grad_last, grad_protos, grad_features, next_centre)


def pack_small(embedding, teacher_embedding, head_last, teacher_last):
    def table(value):
        flat = value.T.astype(LOW).reshape(-1)
        return jnp.pad(flat, (0, -flat.size % (16 * LANES))).reshape(-1, LANES)

    def last(value):
        return value.T.astype(LOW).reshape(-1, LANES)

    return jnp.concatenate(
        [table(embedding), table(teacher_embedding), last(head_last), last(teacher_last)], 0
    )


def unpack_small(everything, embedding, head_last, devices):
    depth = devices // 8
    rows, columns = embedding.shape
    ordered = everything.reshape(2, 2, 2, depth, -1, LANES).transpose(3, 0, 1, 2, 4, 5)
    ordered = ordered.reshape(devices, -1, LANES)
    size = rows * columns
    table_rows = (size + (-size % (16 * LANES))) // LANES
    last_rows = head_last.size // LANES

    def table(at):
        flat = ordered[:, at : at + table_rows].reshape(devices, -1)[:, :size]
        return flat.reshape(devices * columns, rows).T

    def last(at):
        return ordered[:, at : at + last_rows].reshape(devices * head_last.shape[1], -1)

    return (
        table(0),
        table(table_rows),
        last(2 * table_rows),
        last(2 * table_rows + last_rows),
    )


def own_feature_rows(features, teacher_features):
    def rows(value):
        count = value.shape[0]
        turned = value.reshape(count, D // LANES, LANES).transpose(1, 0, 2).reshape(-1, LANES)
        return jnp.pad(turned, ((0, 16 - turned.shape[0]), (0, 0)))

    return jnp.concatenate([rows(features), rows(teacher_features)], 0)


def head_fast(
    features,
    teacher_features,
    valid_mask,
    head_hidden,
    protos,
    teacher_hidden,
    teacher_protos,
    centre,
    part,
    last_full,
    teacher_last_full,
    devices,
    device_index,
):
    counted = valid_mask.astype(FULL)
    mask_row = jnp.pad(counted, (0, LANES - counted.size)).reshape(1, LANES)
    scalars, grad_hidden, grad_last, grad_protos, grad_feat, next_centre = head(
        own_feature_rows(features, teacher_features),
        head_hidden,
        teacher_hidden,
        part,
        last_full,
        teacher_last_full,
        protos,
        teacher_protos,
        centre[None],
        counted[:, None],
        mask_row,
        devices,
    )
    count = features.shape[0]
    grad_features = lax.dynamic_slice_in_dim(grad_feat, (device_index % 2) * count, count, 0)
    return (
        scalars[0, 0],
        scalars[0, 1],
        scalars,
        grad_hidden,
        grad_last.T,
        grad_protos,
        grad_features,
        next_centre[0],
    )


TOKENS = 272
HALF_ROW = 256
SAVED = ("inputs", "normed", "joint", "mixed", "attended", "middle", "normed_two", "activated", "slope", "outer")


def saved_widths():
    return {
        "inputs": (D, FULL),
        "normed": (D, LOW),
        "joint": (3 * D, LOW),
        "mixed": (D, LOW),
        "attended": (D, LOW),
        "middle": (D, FULL),
        "normed_two": (D, LOW),
        "activated": (MLP, LOW),
        "slope": (MLP, LOW),
        "outer": (D, LOW),
    }


def unpack_blocks(weights, joint_out, output_out, cuts):
    devices = weights.shape[0]
    joint_rows, output_rows = cuts[0], cuts[1] - cuts[0]
    group = 4
    for at in range(0, devices, group):
        blocks = [weights[at + t, 0 : cuts[1]].astype(FULL) for t in range(group)]
        joint = jnp.concatenate([block[:joint_rows] for block in blocks], 0)
        output = jnp.concatenate([block[joint_rows:] for block in blocks], 0)
        joint_out[at * joint_rows : (at + group) * joint_rows] = joint.astype(LOW)
        output_out[at * output_rows : (at + group) * output_rows] = output.astype(LOW)


def weight_rows(weights, cuts, which, part, parts):
    per = weights.shape[0] // parts
    block = weights[part * per : (part + 1) * per, cuts[which] : cuts[which + 1]]
    return block.reshape(-1, block.shape[-1])


def chance(keys_half, queries, live):
    scores = jnp.where(live, dot_nt(keys_half, queries), -jnp.inf)
    grown = jnp.exp(scores - jnp.max(scores, 0, keepdims=True))
    return grown * (1.0 / jnp.sum(grown, 0, keepdims=True))


def forward_kernel(
    cuts,
    save,
    patches_ref,
    table_ref,
    start_ref,
    weights_ref,
    vectors_ref,
    tail_ref,
    feat_ref,
    last_ref,
    *rest,
):
    layer, image = pl.program_id(0), pl.program_id(1)
    if save:
        outs = dict(zip(SAVED, rest[: len(SAVED)]))
        rest = rest[len(SAVED) :]
    current, joint_weight, output_weight = rest

    def keep(name, value):
        if save:
            outs[name][0, 0] = value

    weights = weights_ref.at[0]

    @pl.when(image == 0)
    def _():
        unpack_blocks(weights, joint_weight, output_weight, cuts)

    @pl.when(layer == 0)
    def _():
        current[image, :HALF_ROW] = start_ref[:HALF_ROW] + dot_nn(patches_ref[0], table_ref[...])
        current[image, HALF_ROW:] = start_ref[HALF_ROW:]

    inputs = current[image]
    vectors = vectors_ref[0]
    keep("inputs", inputs)
    normed = layer_norm(inputs, vectors[0:1], vectors[1:2]).astype(LOW)
    keep("normed", normed)
    lane = lax.broadcasted_iota(jnp.int32, (TOKENS, LANES), 1)
    live = lax.broadcasted_iota(jnp.int32, (TOKENS, TOKENS), 0) < SEQ
    mixed = []
    for pair in range(D // LANES):
        lower = pair * LANES
        parts = [
            dot_nt(normed, joint_weight[third * D + lower : third * D + lower + LANES])
            for third in range(3)
        ]
        rounded = [part.astype(LOW) for part in parts]
        if save:
            for third in range(3):
                outs["joint"][0, 0, :, third * D + lower : third * D + lower + LANES] = rounded[third]
        queries = (rounded[0].astype(FULL) * HEAD_DIM ** (-0.5)).astype(LOW)
        values = parts[2].T.astype(LOW)
        turned = []
        for half in range(2):
            keys_half = jnp.where((lane >= HEAD_DIM) == bool(half), rounded[1].astype(FULL), 0.0).astype(LOW)
            share = chance(keys_half, queries, live).astype(LOW)
            turned.append(dot_nn(values[half * HEAD_DIM : (half + 1) * HEAD_DIM], share))
        mixed.append(jnp.concatenate(turned, 0).T.astype(LOW))
    mixed = jnp.concatenate(mixed, 1)
    keep("mixed", mixed)
    attended = dot_nt(mixed, output_weight[...])
    keep("attended", attended.astype(LOW))
    middle = inputs + vectors[4:5] * attended
    keep("middle", middle)
    normed_two = layer_norm(middle, vectors[2:3], vectors[3:4]).astype(LOW)
    keep("normed_two", normed_two)
    outer = jnp.zeros((TOKENS, D), FULL)
    parts = MLP // D
    for part in range(parts):
        inner = dot_nt(normed_two, weight_rows(weights, cuts, 1, part, parts))
        spread_half = 0.5 * (1.0 + lax.erf(inner * ROOT_HALF))
        activated = (inner * spread_half).astype(LOW)
        if save:
            outs["activated"][0, 0, :, part * D : (part + 1) * D] = activated
            slope = spread_half + inner * jnp.exp(-0.5 * inner * inner) * DENSITY_SCALE
            outs["slope"][0, 0, :, part * D : (part + 1) * D] = slope.astype(LOW)
        outer = outer + dot_nn(activated, weight_rows(weights, cuts, 2, part, parts))
    keep("outer", outer.astype(LOW))
    result = middle + vectors[5:6] * outer
    current[image] = result
    final = result[HALF_ROW : HALF_ROW + 8]
    last_ref[0] = final
    feat_ref[0] = layer_norm(final, tail_ref[2:3], tail_ref[3:4])


def start_rows(embed_table):
    tail_rows = table_tail(embed_table)
    position = embed_table[PIX : PIX + SEQ].astype(FULL)
    return jnp.concatenate(
        [
            position[1:] + tail_rows[0],
            (position[0] + tail_rows[1])[None],
            jnp.zeros((TOKENS - SEQ, D), FULL),
        ],
        0,
    )


def padded_vectors(embed_table):
    return jnp.pad(table_vectors(embed_table), ((0, 0), (0, 2), (0, 0)))


def padded_tail(embed_table):
    return jnp.pad(table_tail(embed_table), ((0, 4), (0, 0)))


def forward(patches, embed_table, layer_full, devices, save):
    images = patches.shape[0]
    blocks = layer_full.reshape(LAYERS, devices, -1, D)
    cuts = [lower for lower, upper in layer_bounds(devices)][1:] + [blocks.shape[2]]
    shape = jax.ShapeDtypeStruct

    def whole(*dims):
        return pl.BlockSpec(dims, lambda layer, image: (0,) * len(dims))

    outs = [shape((images, 8, D), FULL)] * 2
    specs = [pl.BlockSpec((1, 8, D), lambda layer, image: (image, 0, 0))] * 2
    if save:
        for name in SAVED:
            width, kind = saved_widths()[name]
            outs.append(shape((LAYERS, images, TOKENS, width), kind))
            specs.append(
                pl.BlockSpec((1, 1, TOKENS, width), lambda layer, image: (layer, image, 0, 0))
            )
    return pl.pallas_call(
        functools.partial(forward_kernel, cuts, save),
        grid=(LAYERS, images),
        out_shape=outs,
        in_specs=[
            pl.BlockSpec(
                (1,) + patches.shape[1:], lambda layer, image: (jnp.where(layer == 0, image, 0), 0, 0)
            ),
            whole(PIX, D),
            whole(TOKENS, D),
            pl.BlockSpec((1,) + blocks.shape[1:], lambda layer, image: (layer, 0, 0, 0)),
            pl.BlockSpec((1, 8, D), lambda layer, image: (layer, 0, 0)),
            whole(8, D),
        ],
        out_specs=specs,
        scratch_shapes=[
            pltpu.VMEM((images, TOKENS, D), FULL),
            pltpu.VMEM((3 * D, D), LOW),
            pltpu.VMEM((D, D), LOW),
        ],
        compiler_params=pltpu.CompilerParams(vmem_limit_bytes=56 << 20),
        name="forward_save" if save else "forward",
    )(
        patches,
        embed_table[:PIX],
        start_rows(embed_table),
        blocks,
        padded_vectors(embed_table),
        padded_tail(embed_table),
    )


def backward_kernel(cuts, depth, *refs):
    (patches_ref, weights_ref, vectors_ref, tail_ref, final_ref, grad_feat_ref) = refs[:6]
    saved = dict(zip(SAVED, refs[6 : 6 + len(SAVED)]))
    (
        packet_ref,
        grad_patch_ref,
        grad_start_ref,
        grad_vectors_ref,
        grad_tail_ref,
        grad_now,
        joint_weight,
        output_weight,
        grad_outer_all,
        grad_inner_all,
        grad_attended_all,
        grad_joint_all,
    ) = refs[6 + len(SAVED) :]
    step, image = pl.program_id(0), pl.program_id(1)
    images = pl.num_programs(1)
    weights = weights_ref.at[0]
    vectors = vectors_ref[0]

    @pl.when(image == 0)
    def _():
        unpack_blocks(weights, joint_weight, output_weight, cuts)
        grad_vectors_ref[...] = jnp.zeros(grad_vectors_ref.shape, FULL)

    @pl.when((step == 0) & (image == 0))
    def _():
        grad_tail_ref[...] = jnp.zeros(grad_tail_ref.shape, FULL)

    @pl.when(step == 0)
    def _():
        first = lax.broadcasted_iota(jnp.int32, (8, D), 0) == 0
        given = jnp.where(first, grad_feat_ref[image], 0.0)
        grad_class, grad_gain, grad_shift = norm_back(final_ref[image], tail_ref[2:3], given)
        grad_tail_ref[2:3] += grad_gain[None]
        grad_tail_ref[3:4] += grad_shift[None]
        grad_now[image] = jnp.zeros((TOKENS, D), FULL)
        grad_now[image, HALF_ROW : HALF_ROW + 8] = jnp.where(first, grad_class, 0.0)

    rows = pl.ds(pl.multiple_of(image * TOKENS, 16), TOKENS)
    grad_result = grad_now[image]
    grad_outer = (vectors[5:6] * grad_result).astype(LOW)
    grad_outer_all[rows, :] = grad_outer
    grad_scale_two = jnp.sum(grad_result * saved["outer"][0, image].astype(FULL), 0, keepdims=True)
    parts = MLP // D
    grad_normed_two = jnp.zeros((TOKENS, D), FULL)
    for part in range(parts):
        columns = slice(part * D, (part + 1) * D)
        grad_activated = dot_nt(grad_outer, weight_rows(weights, cuts, 2, part, parts))
        grad_inner = (grad_activated * saved["slope"][0, image, :, columns].astype(FULL)).astype(LOW)
        grad_inner_all[rows, columns] = grad_inner
        grad_normed_two = grad_normed_two + dot_nn(grad_inner, weight_rows(weights, cuts, 1, part, parts))
    grad_middle_norm, grad_gain_two, grad_shift_two = norm_back(
        saved["middle"][0, image], vectors[2:3], grad_normed_two
    )
    grad_middle = grad_result + grad_middle_norm
    grad_attended = (vectors[4:5] * grad_middle).astype(LOW)
    grad_attended_all[rows, :] = grad_attended
    grad_scale_one = jnp.sum(grad_middle * saved["attended"][0, image].astype(FULL), 0, keepdims=True)
    grad_mixed = dot_nn(grad_attended, output_weight[...]).astype(LOW)
    lane = lax.broadcasted_iota(jnp.int32, (TOKENS, LANES), 1)
    live = lax.broadcasted_iota(jnp.int32, (TOKENS, TOKENS), 0) < SEQ
    for pair in range(D // LANES):
        lower = pair * LANES
        queries, keys_in, values_in = [
            saved["joint"][0, image, :, third * D + lower : third * D + lower + LANES]
            for third in range(3)
        ]
        queries = (queries.astype(FULL) * HEAD_DIM ** (-0.5)).astype(LOW)
        keys_wide = keys_in.astype(FULL)
        values_wide = values_in.astype(FULL)
        keys_turned = keys_wide.T.astype(LOW)
        grad_head = grad_mixed[:, lower : lower + LANES]
        turned, grad_keys, grad_values = [], [], []
        for half in range(2):
            mine = (lane >= HEAD_DIM) == bool(half)
            share = chance(jnp.where(mine, keys_wide, 0.0).astype(LOW), queries, live)
            grad_share = dot_nt(jnp.where(mine, values_wide, 0.0).astype(LOW), grad_head)
            grad_values.append(dot_nn(share.astype(LOW), grad_head))
            grad_scores = (
                share * (grad_share - jnp.sum(share * grad_share, 0, keepdims=True))
            ).astype(LOW)
            grad_keys.append(dot_nn(grad_scores, queries))
            turned.append(dot_nn(keys_turned[half * HEAD_DIM : (half + 1) * HEAD_DIM], grad_scores))
        grad_queries = jnp.concatenate(turned, 0).T * HEAD_DIM ** (-0.5)
        low_half = lane < HEAD_DIM
        for third, value in enumerate(
            (
                grad_queries,
                jnp.where(low_half, grad_keys[0], grad_keys[1]),
                jnp.where(low_half, grad_values[0], grad_values[1]),
            )
        ):
            grad_joint_all[rows, third * D + lower : third * D + lower + LANES] = value.astype(LOW)
    grad_normed = dot_nn(grad_joint_all[rows, :], joint_weight[...])
    grad_input_norm, grad_gain_one, grad_shift_one = norm_back(
        saved["inputs"][0, image], vectors[0:1], grad_normed
    )
    grad_input = grad_middle + grad_input_norm
    grad_now[image] = grad_input
    for at, value in enumerate(
        (
            grad_gain_one[None],
            grad_shift_one[None],
            grad_gain_two[None],
            grad_shift_two[None],
            grad_scale_one,
            grad_scale_two,
        )
    ):
        grad_vectors_ref[0, at : at + 1] += value

    @pl.when(image == images - 1)
    def _():
        devices = packet_ref.shape[0]

        def flat(name):
            value = saved[name][0]
            return value.reshape(-1, value.shape[-1])

        per = cuts[0], cuts[1] - cuts[0], cuts[2] - cuts[1], cuts[3] - cuts[2]

        def slot(device):
            return (device % 8) * depth + device // 8

        groups = 4
        each = devices // groups
        for at in range(groups):
            first = at * each
            joint_rows = dot_tn(grad_joint_all[:, first * per[0] : (first + each) * per[0]], flat("normed"))
            output_rows = dot_tn(
                grad_attended_all[:, first * per[1] : (first + each) * per[1]], flat("mixed")
            )
            inner_rows = dot_tn(
                grad_inner_all[:, first * per[2] : (first + each) * per[2]], flat("normed_two")
            ).astype(LOW)
            outer_rows = dot_tn(
                saved["activated"][0, :, :, first * per[3] : (first + each) * per[3]].reshape(
                    -1, each * per[3]
                ),
                grad_outer_all[...],
            ).astype(LOW)
            for t in range(each):
                joined_rows = jnp.concatenate(
                    [
                        joint_rows[t * per[0] : (t + 1) * per[0]],
                        output_rows[t * per[1] : (t + 1) * per[1]],
                    ],
                    0,
                )
                place = slot(first + t)
                packet_ref[place, : cuts[1]] = joined_rows.astype(LOW)
                packet_ref[place, cuts[1] : cuts[2]] = inner_rows[t * per[2] : (t + 1) * per[2]]
                packet_ref[place, cuts[2] : cuts[3]] = outer_rows[t * per[3] : (t + 1) * per[3]]

    @pl.when(step == pl.num_programs(0) - 1)
    def _():
        @pl.when(image == 0)
        def _():
            grad_patch_ref[...] = jnp.zeros(grad_patch_ref.shape, FULL)
            grad_start_ref[...] = jnp.zeros(grad_start_ref.shape, FULL)

        grad_patch_ref[...] += dot_tn(patches_ref[image], grad_input[:HALF_ROW].astype(LOW))
        grad_start_ref[...] += grad_input
        grad_tail_ref[0:1] += jnp.sum(grad_input[:HALF_ROW], 0, keepdims=True)
        grad_tail_ref[1:2] += grad_input[HALF_ROW : HALF_ROW + 1]


def backward(patches, embed_table, layer_full, final, grad_feat, saved, devices):
    images = patches.shape[0]
    depth = devices // 8
    blocks = layer_full.reshape(LAYERS, devices, -1, D)
    cuts = [lower for lower, upper in layer_bounds(devices)][1:] + [blocks.shape[2]]
    shape = jax.ShapeDtypeStruct

    def whole(*dims):
        return pl.BlockSpec(dims, lambda step, image: (0,) * len(dims))

    def of_layer(*dims):
        return pl.BlockSpec(
            (1,) + dims, lambda step, image: (LAYERS - 1 - step,) + (0,) * len(dims)
        )

    all_rows = images * TOKENS
    packets, grad_patch, grad_start, grad_vectors, grad_tail = pl.pallas_call(
        functools.partial(backward_kernel, cuts, depth),
        grid=(LAYERS, images),
        out_shape=(
            shape((devices, LAYERS * blocks.shape[2], D), LOW),
            shape((PIX, D), FULL),
            shape((TOKENS, D), FULL),
            shape((LAYERS, 8, D), FULL),
            shape((8, D), FULL),
        ),
        in_specs=[
            whole(*patches.shape),
            of_layer(*blocks.shape[1:]),
            of_layer(8, D),
            whole(8, D),
            whole(images, 8, D),
            whole(images, 8, D),
        ]
        + [of_layer(images, TOKENS, saved_widths()[name][0]) for name in SAVED],
        out_specs=(
            pl.BlockSpec(
                (devices, blocks.shape[2], D), lambda step, image: (0, LAYERS - 1 - step, 0)
            ),
            whole(PIX, D),
            whole(TOKENS, D),
            of_layer(8, D),
            whole(8, D),
        ),
        scratch_shapes=[
            pltpu.VMEM((images, TOKENS, D), FULL),
            pltpu.VMEM((3 * D, D), LOW),
            pltpu.VMEM((D, D), LOW),
            pltpu.VMEM((all_rows, D), LOW),
            pltpu.VMEM((all_rows, MLP), LOW),
            pltpu.VMEM((all_rows, D), LOW),
            pltpu.VMEM((all_rows, 3 * D), LOW),
        ],
        compiler_params=pltpu.CompilerParams(vmem_limit_bytes=62 << 20),
        name="backward",
    )(
        patches,
        blocks,
        padded_vectors(embed_table),
        padded_tail(embed_table),
        final,
        grad_feat,
        *saved,
    )
    grad_table = jnp.concatenate(
        [
            grad_patch,
            grad_start[SEQ - 1 : SEQ],
            grad_start[: SEQ - 1],
            grad_vectors[:, :6].reshape(-1, D),
            grad_tail[:4],
        ],
        0,
    )
    return packets, grad_table


def embedding_packet(grad_table, devices):
    depth = devices // 8
    flat = grad_table.T.reshape(devices, -1)
    flat = jnp.pad(flat, ((0, 0), (0, -flat.shape[1] % (16 * D)))).reshape(devices, -1, D)
    ordered = flat.astype(LOW).reshape((depth, 2, 2, 2) + flat.shape[1:]).transpose(1, 2, 3, 0, 4, 5)
    return ordered.reshape(flat.shape)


def tail_fast(
    squares, grad_table, layer_packets, layer_stats, layer_bases, owners, embedding, layers, devices
):
    own_rows = layer_stats.shape[2]
    matrices = owners.shape[0]
    rows_layer = layers.shape[1]
    own, norm, full_stats, full_bases = collect(
        squares,
        jnp.concatenate([layer_packets, embedding_packet(grad_table, devices)], 1),
        layer_stats.reshape(matrices, own_rows, D),
        layer_bases.reshape(matrices, own_rows, D),
        rows_layer,
        layer_bounds(devices),
    )
    count = layers.shape[0] * rows_layer
    grad_layers_own = own[:count].reshape(layers.shape)
    rows, columns = embedding.shape
    grad_embed = own[count:].reshape(-1)[: rows * columns].reshape(columns, rows).T
    renewed = renew_own(full_stats, full_bases)
    stats_own, bases_own = deal(full_stats, renewed, matrices)
    bases_own = jnp.where(
        owners[:, None, None] >= 0, bases_own, layer_bases.reshape(matrices, own_rows, D)
    )
    return (
        norm[0, 0],
        grad_embed,
        grad_layers_own,
        stats_own.reshape(layer_stats.shape),
        bases_own.reshape(layer_bases.shape),
    )


def per_device(
    patches,
    valid_mask,
    owners,
    embedding,
    embedding_first,
    embedding_second,
    layers,
    layers_first,
    layers_second,
    layer_stats,
    layer_bases,
    head_hidden,
    hidden_first,
    hidden_second,
    head_last,
    last_first,
    last_second,
    protos,
    protos_first,
    protos_second,
    teacher_embedding,
    teacher_layers,
    teacher_hidden,
    teacher_last,
    teacher_protos,
    centre,
):
    devices = lax.axis_size("dp")
    device_index = lax.axis_index("dp")
    fast = 2 * head_hidden.shape[0] == LANES
    if fast:
        small, part = spread(
            pack_small(embedding, teacher_embedding, head_last, teacher_last),
            head_hidden[:, D:].astype(LOW),
            devices,
        )
        embed_table, teacher_table, last_full, teacher_last_full = unpack_small(
            small, embedding, head_last, devices
        )
    else:
        embed_table, teacher_table = (
            lax.all_gather(embedding.astype(LOW), "dp", axis=1, tiled=True),
            lax.all_gather(teacher_embedding.astype(LOW), "dp", axis=1, tiled=True),
        )
    layer_full, teacher_full = (
        lax.all_gather(layers.astype(LOW), "dp", axis=1, tiled=True),
        lax.all_gather(teacher_layers.astype(LOW), "dp", axis=1, tiled=True),
    )
    bases_full = lax.all_gather(layer_bases.astype(LOW), "dp", axis=2, tiled=True).astype(
        layer_bases.dtype
    )
    if not fast:
        stats_full = lax.all_gather(layer_stats.astype(LOW), "dp", axis=2, tiled=True).astype(
            layer_stats.dtype
        )
    if fast:
        feature_rows, final_rows, *saved = forward(patches, embed_table, layer_full, devices, True)
        teacher_rows, unused_rows = forward(patches, teacher_table, teacher_full, devices, False)
        features = feature_rows[:, 0].astype(LOW)
        teacher_features = teacher_rows[:, 0].astype(LOW)
    else:
        features, layer_inputs, final_state = backbone(patches, embed_table, layer_full, devices)
        teacher_features, unused_inputs, unused_final = backbone(
            patches, teacher_table, teacher_full, devices
        )
    if fast:
        (
            loss_sum,
            loss_count,
            squares,
            grad_hidden,
            grad_last,
            grad_protos,
            grad_features,
            next_centre,
        ) = head_fast(
            features,
            teacher_features,
            valid_mask,
            head_hidden,
            protos,
            teacher_hidden,
            teacher_protos,
            centre,
            part,
            last_full,
            teacher_last_full,
            devices,
            device_index,
        )
    else:
        (
            loss_sum,
            loss_count,
            grad_hidden,
            grad_last,
            grad_protos,
            grad_features,
            next_centre,
        ) = head_slow(
            features,
            teacher_features,
            valid_mask,
            head_hidden,
            head_last,
            protos,
            teacher_hidden,
            teacher_last,
            teacher_protos,
            centre,
            device_index,
        )
    if fast:
        grad_rows = jnp.pad(grad_features[:, None], ((0, 0), (0, 7), (0, 0)))
        grad_layers, grad_table = backward(
            patches, embed_table, layer_full, final_rows, grad_rows, saved, devices
        )
    else:
        grad_table, grad_layers = backbone_back(
            patches,
            embed_table,
            layer_full,
            layer_inputs,
            final_state,
            grad_features,
            devices,
            unchanged,
        )
    bounds = layer_bounds(devices)
    if fast:
        grad_norm, grad_embed, grad_layers_own, stats_own, bases_own = tail_fast(
            squares,
            grad_table,
            grad_layers,
            layer_stats,
            layer_bases,
            owners,
            embedding,
            layers,
            devices,
        )
    else:
        summed = (
            lax.psum_scatter(grad_table, "dp", scatter_dimension=1, tiled=True),
            lax.psum_scatter(grad_layers, "dp", scatter_dimension=1, tiled=True),
        )
        grad_embed = summed[0]
        grad_layers_own = summed[1]
        grams = jnp.stack(
            [
                matmul_high(
                    "lcd,lce->lde",
                    grad_layers_own[:, lower_row:upper_row],
                    grad_layers_own[:, lower_row:upper_row],
                )
                for lower_row, upper_row in bounds
            ],
            1,
        )
        squares = (
            jnp.sum(grad_embed * grad_embed)
            + jnp.sum(grad_layers_own * grad_layers_own)
            + jnp.sum(grad_hidden * grad_hidden)
            + jnp.sum(grad_last * grad_last)
            + jnp.sum(grad_protos * grad_protos)
        )
        totals = lax.psum((squares, grams), "dp")
        grad_norm = jnp.sqrt(totals[0])
        clip_factor = jnp.minimum(1.0, CLIP_MAX / (grad_norm + 1e-06))
        next_stats = (
            BETA_STAT * stats_full + (1.0 - BETA_STAT) * (clip_factor * clip_factor) * totals[1]
        )
    clip_factor = jnp.minimum(1.0, CLIP_MAX / (grad_norm + 1e-06))
    rows = jnp.arange(embedding.shape[0])[:, None]
    is_matrix = rows < PIX + SEQ
    embed_out = adam_step(
        embedding,
        clip_factor * grad_embed,
        embedding_first,
        embedding_second,
        jnp.where(is_matrix, RATE_MATRIX, RATE_VECTOR),
        jnp.where(is_matrix, WEIGHT_DECAY, 0.0),
    )
    hidden_out = adam_step(
        head_hidden,
        clip_factor * grad_hidden,
        hidden_first,
        hidden_second,
        RATE_MATRIX,
        WEIGHT_DECAY,
    )
    last_out = adam_step(
        head_last, clip_factor * grad_last, last_first, last_second, RATE_MATRIX, WEIGHT_DECAY
    )
    protos_out = adam_step(
        protos, clip_factor * grad_protos, protos_first, protos_second, RATE_MATRIX, WEIGHT_DECAY
    )
    firsts, seconds, weights_new = ([], [], [])
    for segment, (lower_row, upper_row) in enumerate(bounds):
        basis = bases_full[:, segment]
        weight_block = layers[:, lower_row:upper_row]
        rotated = matmul_high(
            "lcd,ldk->lck", clip_factor * grad_layers_own[:, lower_row:upper_row], basis
        )
        first_new = BETA_ONE * layers_first[:, lower_row:upper_row] + (1.0 - BETA_ONE) * rotated
        second_new = (
            BETA_TWO * layers_second[:, lower_row:upper_row] + (1.0 - BETA_TWO) * rotated * rotated
        )
        direction = (
            first_new
            / (1.0 - BETA_ONE**STEP)
            / (jnp.sqrt(second_new / (1.0 - BETA_TWO**STEP)) + ADAM_EPSILON)
        )
        update = matmul_high("lck,ldk->lcd", direction, basis)
        firsts.append(first_new)
        seconds.append(second_new)
        weights_new.append(weight_block - RATE_MATRIX * (update + WEIGHT_DECAY * weight_block))
    next_layers = jnp.concatenate(weights_new, 1)
    if not fast:
        flat_stats = next_stats.reshape(-1, D, D)
        flat_bases = bases_full.reshape(-1, D, D)

        def renew_owned(operands):
            return lax.cond(operands[2] == device_index, renew, nothing, operands[0], operands[1])

        renewed = lax.psum(lax.map(renew_owned, (flat_stats, flat_bases, owners)), "dp")
        next_bases = jnp.where(owners[:, None, None] >= 0, renewed, flat_bases).reshape(
            bases_full.shape
        )
        own_rows = layer_stats.shape[2]
        stats_own = lax.dynamic_slice_in_dim(next_stats, device_index * own_rows, own_rows, 2)
        bases_own = lax.dynamic_slice_in_dim(next_bases, device_index * own_rows, own_rows, 2)
    return (
        loss_sum,
        loss_count,
        grad_norm,
        embed_out[0],
        embed_out[1],
        embed_out[2],
        jnp.concatenate(firsts, 1),
        jnp.concatenate(seconds, 1),
        next_layers,
        stats_own,
        bases_own,
        hidden_out[0],
        hidden_out[1],
        hidden_out[2],
        last_out[0],
        last_out[1],
        last_out[2],
        protos_out[0],
        protos_out[1],
        protos_out[2],
        follow(teacher_embedding, embed_out[2]),
        follow(teacher_layers, next_layers),
        follow(teacher_hidden, hidden_out[2]),
        follow(teacher_last, last_out[2]),
        follow(teacher_protos, protos_out[2]),
        next_centre,
    )


def solution(mesh):
    placed = (
        P("dp", None, None),
        P(),
        P(),
        P(None, "dp"),
        P(None, "dp"),
        P(None, "dp"),
        P(None, "dp", None),
        P(None, "dp", None),
        P(None, "dp", None),
        P(None, None, "dp", None),
        P(None, None, "dp", None),
        P("dp", None),
        P("dp", None),
        P("dp", None),
        P(None, "dp"),
        P(None, "dp"),
        P(None, "dp"),
        P(None, "dp"),
        P(None, "dp"),
        P(None, "dp"),
        P(None, "dp"),
        P(None, "dp", None),
        P("dp", None),
        P(None, "dp"),
        P(None, "dp"),
        P("dp"),
    )
    return jax.shard_map(
        per_device,
        mesh=mesh,
        in_specs=placed,
        out_specs=(
            P(),
            P(),
            P(),
            P(None, "dp"),
            P(None, "dp"),
            P(None, "dp"),
            P(None, "dp", None),
            P(None, "dp", None),
            P(None, "dp", None),
            P(None, None, "dp", None),
            P(None, None, "dp", None),
            P("dp", None),
            P("dp", None),
            P("dp", None),
            P(None, "dp"),
            P(None, "dp"),
            P(None, "dp"),
            P(None, "dp"),
            P(None, "dp"),
            P(None, "dp"),
            P(None, "dp"),
            P(None, "dp", None),
            P("dp", None),
            P(None, "dp"),
            P(None, "dp"),
            P("dp"),
        ),
        check_vma=False,
    )
```

```python
import functools

import jax
import jax.numpy as jnp
from jax import lax
from jax.experimental import pallas as pl
from jax.experimental.pallas import tpu as pltpu
from jax.sharding import PartitionSpec as P

D = 384
HEADS = 6
HEAD_DIM = 64
MLP = 1536
PIX = 588
LAYERS = 3
STEP = 10
SEQ = 257


NORM_EPSILON = 1e-06
UNIT_EPSILON = 1e-06
TAU_STUDENT = 0.1
TAU_TEACHER = 0.07
CLIP_MAX = 0.001
BETA_ONE = 0.9
BETA_TWO = 0.999
ADAM_EPSILON = 1e-08
WEIGHT_DECAY = 0.04
RATE_MATRIX = 0.04
RATE_VECTOR = 0.2
BETA_STAT = 0.95
TEACHER_MOMENTUM = 0.8
CENTRE_MOMENTUM = 0.9
ROOT_HALF = 0.7071067811865476
DENSITY_SCALE = 0.3989422804014327


def joined(value, axis, join):
    pieces = jax.tree.map(lambda part: lax.all_gather(part, axis), value)
    head = jax.tree.map(lambda part: part[0], pieces)
    tail = jax.tree.map(lambda part: part[1:], pieces)
    running, _ = lax.scan(lambda running, piece: (join(running, piece), None), head, tail)
    return running


def matmul_low(form, left, right):
    return jnp.einsum(form, left, right, preferred_element_type=jnp.float32)


def matmul_high(form, left, right):
    return jnp.einsum(form, left, right, precision=lax.Precision.HIGHEST)


def layer_norm(values, gain_row, shift_row):
    centred = values - jnp.mean(values, -1, keepdims=True)
    inverse_std = lax.rsqrt(jnp.mean(centred * centred, -1, keepdims=True) + NORM_EPSILON)
    return centred * inverse_std * gain_row + shift_row


def norm_back(values, gain_row, grad_out):
    centred = values - jnp.mean(values, -1, keepdims=True)
    inverse_std = lax.rsqrt(jnp.mean(centred * centred, -1, keepdims=True) + NORM_EPSILON)
    normed = centred * inverse_std
    scaled_grad = grad_out * gain_row
    grad_in = inverse_std * (
        scaled_grad
        - jnp.mean(scaled_grad, -1, keepdims=True)
        - normed * jnp.mean(scaled_grad * normed, -1, keepdims=True)
    )
    leading = tuple(range(values.ndim - 1))
    return (grad_in, jnp.sum(grad_out * normed, leading), jnp.sum(grad_out, leading))


def gelu_exact(values):
    return 0.5 * values * (1.0 + lax.erf(values * ROOT_HALF))


def gelu_slope(values):
    return (
        0.5 * (1.0 + lax.erf(values * ROOT_HALF))
        + values * jnp.exp(-0.5 * values * values) * DENSITY_SCALE
    )


def layer_bounds(devices):
    widths = [3 * D // devices, D // devices, MLP // devices, MLP // devices]
    lowers = [0, widths[0], widths[0] + widths[1], widths[0] + widths[1] + widths[2]]
    return [(lowers[segment], lowers[segment] + widths[segment]) for segment in range(4)]


def split_layer(weights, devices):
    blocks = weights.reshape(devices, -1, D)
    return [
        blocks[:, lower_row:upper_row].reshape(-1, D)
        for lower_row, upper_row in layer_bounds(devices)
    ]


def join_layer(members, devices):
    return jnp.concatenate([member.reshape(devices, -1, D) for member in members], 1).reshape(-1, D)


def layer_parts(inputs, matrices, vectors):
    joint_weight, output_weight, inner_weight, outer_weight = matrices
    images, tokens = (inputs.shape[0], inputs.shape[1])
    normed = layer_norm(inputs, vectors[0], vectors[1]).astype(jnp.bfloat16)
    joint = matmul_low("itd,ed->ite", normed, joint_weight).astype(jnp.bfloat16)
    head_split = joint.reshape(images, tokens, 3, HEADS, HEAD_DIM)
    queries, keys_in, values_in = (head_split[:, :, 0], head_split[:, :, 1], head_split[:, :, 2])
    scores = matmul_low("ithd,ishd->ihts", queries, keys_in) * HEAD_DIM ** (-0.5)
    attention = jax.nn.softmax(scores, axis=-1)
    mixed_heads = (
        matmul_low("ihts,ishd->ithd", attention.astype(jnp.bfloat16), values_in)
        .astype(jnp.bfloat16)
        .reshape(images, tokens, D)
    )
    attended = matmul_low("itd,ed->ite", mixed_heads, output_weight)
    middle = inputs + vectors[4] * attended
    normed_two = layer_norm(middle, vectors[2], vectors[3]).astype(jnp.bfloat16)
    inner_pre = matmul_low("itd,md->itm", normed_two, inner_weight)
    activated = gelu_exact(inner_pre).astype(jnp.bfloat16)
    outer_out = matmul_low("itm,md->itd", activated, outer_weight)
    result = middle + vectors[5] * outer_out
    return (
        normed,
        queries,
        keys_in,
        values_in,
        attention,
        mixed_heads,
        attended,
        middle,
        normed_two,
        inner_pre,
        activated,
        outer_out,
        result,
    )


def layer_backward(inputs, matrices, vectors, grad_result):
    joint_weight, output_weight, inner_weight, outer_weight = matrices
    (
        normed,
        queries,
        keys_in,
        values_in,
        attention,
        mixed_heads,
        attended,
        middle,
        normed_two,
        inner_pre,
        activated,
        outer_out,
        result,
    ) = layer_parts(inputs, matrices, vectors)
    images, tokens = (inputs.shape[0], inputs.shape[1])
    grad_outer = (vectors[5] * grad_result).astype(jnp.bfloat16)
    grad_scale_two = jnp.sum(grad_result * outer_out, (0, 1))
    grad_outer_weight = matmul_low("itm,itd->md", activated, grad_outer)
    grad_activated = matmul_low("itd,md->itm", grad_outer, outer_weight)
    grad_inner = (grad_activated * gelu_slope(inner_pre)).astype(jnp.bfloat16)
    grad_inner_weight = matmul_low("itm,itd->md", grad_inner, normed_two)
    grad_normed_two = matmul_low("itm,md->itd", grad_inner, inner_weight)
    grad_middle_norm, grad_gain_two, grad_shift_two = norm_back(middle, vectors[2], grad_normed_two)
    grad_middle = grad_result + grad_middle_norm
    grad_attended = (vectors[4] * grad_middle).astype(jnp.bfloat16)
    grad_scale_one = jnp.sum(grad_middle * attended, (0, 1))
    grad_output_weight = matmul_low("ite,itd->ed", grad_attended, mixed_heads)
    grad_mixed = (
        matmul_low("ite,ed->itd", grad_attended, output_weight)
        .astype(jnp.bfloat16)
        .reshape(images, tokens, HEADS, HEAD_DIM)
    )
    grad_attention = matmul_low("ithd,ishd->ihts", grad_mixed, values_in)
    grad_values = matmul_low("ihts,ithd->ishd", attention.astype(jnp.bfloat16), grad_mixed)
    grad_scores = (
        attention * (grad_attention - jnp.sum(attention * grad_attention, -1, keepdims=True))
    ).astype(jnp.bfloat16)
    grad_queries = matmul_low("ihts,ishd->ithd", grad_scores, keys_in) * HEAD_DIM ** (-0.5)
    grad_keys = matmul_low("ihts,ithd->ishd", grad_scores, queries) * HEAD_DIM ** (-0.5)
    grad_joint = (
        jnp.stack([grad_queries, grad_keys, grad_values], 2)
        .astype(jnp.bfloat16)
        .reshape(images, tokens, 3 * D)
    )
    grad_joint_weight = matmul_low("ite,itd->ed", grad_joint, normed)
    grad_normed = matmul_low("ite,ed->itd", grad_joint, joint_weight)
    grad_input_norm, grad_gain_one, grad_shift_one = norm_back(inputs, vectors[0], grad_normed)
    grad_vectors = jnp.stack(
        [
            grad_gain_one,
            grad_shift_one,
            grad_gain_two,
            grad_shift_two,
            grad_scale_one,
            grad_scale_two,
        ]
    )
    return (
        grad_middle + grad_input_norm,
        (grad_joint_weight, grad_output_weight, grad_inner_weight, grad_outer_weight),
        grad_vectors,
    )


def table_vectors(embed_table):
    return embed_table[PIX + SEQ : PIX + SEQ + 6 * LAYERS].astype(jnp.float32).reshape(LAYERS, 6, D)


def table_tail(embed_table):
    return embed_table[PIX + SEQ + 6 * LAYERS :].astype(jnp.float32)


def backbone(patches, embed_table, layer_stack, devices):
    vectors = table_vectors(embed_table)
    tail_rows = table_tail(embed_table)
    position = embed_table[PIX : PIX + SEQ].astype(jnp.float32)
    projected = matmul_low("ipc,cd->ipd", patches, embed_table[:PIX]) + tail_rows[0]
    leading = jnp.broadcast_to(tail_rows[1] + position[0], (patches.shape[0], 1, D))
    current = jnp.concatenate([leading, projected + position[1:]], 1)
    layer_inputs = []
    for layer_number in range(LAYERS):
        layer_inputs.append(current)
        current = layer_parts(
            current, split_layer(layer_stack[layer_number], devices), vectors[layer_number]
        )[-1]
    features = layer_norm(current[:, 0], tail_rows[2], tail_rows[3]).astype(jnp.bfloat16)
    return (features, layer_inputs, current)


def unchanged(values):
    return values


def backbone_back(
    patches,
    embed_table,
    layer_stack,
    layer_inputs,
    final_state,
    grad_features,
    devices,
    reduce_layer,
):
    vectors = table_vectors(embed_table)
    tail_rows = table_tail(embed_table)
    grad_cls, grad_gain, grad_shift = norm_back(final_state[:, 0], tail_rows[2], grad_features)
    grad_current = jnp.concatenate(
        [grad_cls[:, None], jnp.zeros((final_state.shape[0], SEQ - 1, D), jnp.float32)], 1
    )
    weight_grads = [None] * LAYERS
    vector_grads = [None] * LAYERS
    for layer_number in reversed(range(LAYERS)):
        grad_current, matrices, grad_vectors = layer_backward(
            layer_inputs[layer_number],
            split_layer(layer_stack[layer_number], devices),
            vectors[layer_number],
            grad_current,
        )
        weight_grads[layer_number] = reduce_layer(join_layer(matrices, devices))
        vector_grads[layer_number] = grad_vectors
    grad_patch_weight = matmul_low("ipc,ipd->cd", patches, grad_current[:, 1:].astype(jnp.bfloat16))
    grad_position = jnp.sum(grad_current, 0)
    tail_grads = jnp.stack(
        [
            jnp.sum(grad_current[:, 1:], (0, 1)),
            jnp.sum(grad_current[:, 0], 0),
            grad_gain,
            grad_shift,
        ]
    )
    grad_table = jnp.concatenate(
        [grad_patch_weight, grad_position, jnp.concatenate(vector_grads, 0), tail_grads], 0
    )
    return (grad_table, jnp.stack(weight_grads))


def unit_rows(bottle):
    inverse_norm = lax.rsqrt(jnp.sum(bottle * bottle, -1, keepdims=True) + UNIT_EPSILON)
    return (bottle * inverse_norm, inverse_norm)


def combine_parts(left_part, right_part):
    top_student = jnp.maximum(left_part[0], right_part[0])
    total_student = left_part[1] * jnp.exp(left_part[0] - top_student) + right_part[1] * jnp.exp(
        right_part[0] - top_student
    )
    top_teacher = jnp.maximum(left_part[2], right_part[2])
    left_weight = jnp.exp(left_part[2] - top_teacher)
    right_weight = jnp.exp(right_part[2] - top_teacher)
    return (
        top_student,
        total_student,
        top_teacher,
        left_part[3] * left_weight + right_part[3] * right_weight,
        left_part[4] * left_weight + right_part[4] * right_weight,
    )


def adam_step(weight, grad, first_moment, second_moment, rate, decay):
    first_new = BETA_ONE * first_moment + (1.0 - BETA_ONE) * grad
    second_new = BETA_TWO * second_moment + (1.0 - BETA_TWO) * grad * grad
    direction = (
        first_new
        / (1.0 - BETA_ONE**STEP)
        / (jnp.sqrt(second_new / (1.0 - BETA_TWO**STEP)) + ADAM_EPSILON)
    )
    return (first_new, second_new, weight - rate * (direction + decay * weight))


def renew(stat_matrix, basis):
    scaled = jnp.dot(stat_matrix, basis, precision=lax.Precision.HIGHEST) * (
        D / jnp.trace(stat_matrix)
    )
    gram = jnp.dot(scaled.T, scaled, precision=lax.Precision.HIGHEST)
    lower_factor = jnp.linalg.cholesky(gram)
    return lax.linalg.triangular_solve(lower_factor, scaled.T, left_side=True, lower=True).T


def nothing(stat_matrix, basis):
    return jnp.zeros_like(basis)


def follow(teacher_weight, student_weight):
    return TEACHER_MOMENTUM * teacher_weight + (1.0 - TEACHER_MOMENTUM) * student_weight


MESH = pl.DeviceIdType.MESH
LANES = 128
LOW = jnp.bfloat16
FULL = jnp.float32


def params(identity, vmem=None):
    return pltpu.CompilerParams(
        collective_id=identity, has_side_effects=True, vmem_limit_bytes=vmem or (48 << 20)
    )


def push(source, target, sent, landed, device):
    copy = pltpu.make_async_remote_copy(
        src_ref=source,
        dst_ref=target,
        send_sem=sent,
        recv_sem=landed,
        device_id=(device,),
        device_id_type=MESH,
    )
    copy.start()
    return copy


def greet(peers):
    barrier = pltpu.get_barrier_semaphore()
    for peer in peers:
        pl.semaphore_signal(barrier, inc=1, device_id=(peer,), device_id_type=MESH)
    pl.semaphore_wait(barrier, len(peers))


def dot_nt(left, right):
    return lax.dot_general(left, right, (((1,), (1,)), ((), ())), preferred_element_type=FULL)


def dot_nn(left, right):
    return lax.dot_general(left, right, (((1,), (0,)), ((), ())), preferred_element_type=FULL)


def dot_tn(left, right):
    return lax.dot_general(left, right, (((0,), (0,)), ((), ())), preferred_element_type=FULL)


def slot_of(device, depth):
    return (device % 8) * depth + device // 8


class Route:
    def __init__(self, depth, items, own_sem, z_sent, z_landed, near_sent, near_landed, die_sent, die_landed):
        self.depth = depth
        self.items = items
        self.sems = (own_sem, z_sent, z_landed, near_sent, near_landed, die_sent, die_landed)
        me = lax.axis_index("dp")
        self.me = me
        self.total = 8 * depth
        self.core = lax.rem(me, 2)
        x_at = lax.rem(me // 2, 2)
        y_at = lax.rem(me // 4, 2)
        self.z_at = me // 8
        self.partner = me + 1 - 2 * self.core
        self.to_x = me + 2 - 4 * x_at
        self.to_y = me + 4 - 8 * y_at
        places = [(y_at, x_at), (y_at, 1 - x_at), (1 - y_at, x_at), (1 - y_at, 1 - x_at)]
        self.starts = [((y * 2 + x) * 2 + self.core) * depth for y, x in places]

    def copy(self, source, target, sent, landed, device):
        return pltpu.make_async_remote_copy(
            src_ref=source,
            dst_ref=target,
            send_sem=sent,
            recv_sem=landed,
            device_id=(device,),
            device_id_type=MESH,
        )

    def half(self, at):
        size = self.items[at][3]
        return (size // 2 + 15) // 16 * 16

    def own(self, at):
        source, target, lower, size = self.items[at]
        return pltpu.make_async_copy(
            source.at[pl.ds(lower, size)],
            target.at[self.starts[0] + self.z_at, pl.ds(lower, size)],
            self.sems[0].at[at],
        )

    def deep(self, at, step):
        source, target, lower, size = self.items[at]
        return self.copy(
            source.at[pl.ds(lower, size)],
            target.at[self.starts[0] + self.z_at, pl.ds(lower, size)],
            self.sems[1].at[at, step],
            self.sems[2].at[at, step],
            lax.rem(self.me + 8 * step, self.total),
        )

    def near(self, at, which):
        source, target, lower, size = self.items[at]
        half = self.half(at)
        column, first, length, device = [
            (0, lower, size, self.to_x),
            (0, lower, size, self.to_y),
            (1, lower, half, self.to_y),
            (2, lower + half, size - half, self.to_x),
        ][which]
        view = target.at[pl.ds(self.starts[column], self.depth), pl.ds(first, length)]
        return self.copy(view, view, self.sems[3].at[at, which], self.sems[4].at[at, which], device)

    def die(self, at, column):
        source, target, lower, size = self.items[at]
        view = target.at[pl.ds(self.starts[column], self.depth), pl.ds(lower, size)]
        return self.copy(
            view, view, self.sems[5].at[at, column], self.sems[6].at[at, column], self.partner
        )

    def act(self, stage, at):
        if stage == "A":
            self.own(at).start()
            for step in range(1, self.depth):
                self.deep(at, step).start()
        elif stage == "B":
            self.own(at).wait()
            for step in range(1, self.depth):
                self.deep(at, step).wait_recv()
            self.near(at, 0).start()
            self.near(at, 1).start()
            self.die(at, 0).start()
        elif stage == "C":
            self.near(at, 0).wait_recv()
            self.near(at, 2).start()
            self.die(at, 1).start()
            self.near(at, 1).wait_recv()
            self.near(at, 3).start()
            self.die(at, 2).start()
        elif stage == "D":
            self.near(at, 2).wait_recv()
            self.near(at, 3).wait_recv()
            self.die(at, 3).start()
        elif stage == "E":
            for column in range(4):
                self.die(at, column).wait_recv()
        else:
            for step in range(1, self.depth):
                self.deep(at, step).wait_send()
            for which in range(4):
                self.near(at, which).wait_send()
                self.die(at, which).wait_send()


def route_sems(count, depth):
    dma = pltpu.SemaphoreType.DMA
    return [
        dma((count,)),
        dma((count, depth)),
        dma((count, depth)),
        dma((count, 4)),
        dma((count, 4)),
        dma((count, 4)),
        dma((count, 4)),
    ]


def head_kernel(
    devices,
    feat_ref,
    hidden_ref,
    teacher_hidden_ref,
    part_ref,
    last_ref,
    teacher_last_ref,
    protos_ref,
    teacher_protos_ref,
    centre_ref,
    mask_ref,
    mask_row_ref,
    bases_ref,
    scalars_ref,
    grad_hidden_ref,
    grad_last_ref,
    grad_protos_ref,
    grad_feat_ref,
    centre_out_ref,
    bases_all_ref,
    fb,
    hid_low,
    thid_low,
    prot_low,
    half_out,
    half_in,
    mine_buf,
    other_buf,
    act_s,
    act_t,
    act2_s,
    act2_t,
    pre1,
    pre2,
    unit_ref,
    inv_ref,
    exp_s,
    exp_t,
    stat_out,
    stat_all,
    pz_ref,
    pz_all,
    dz_own,
    dz_all,
    dp_own,
    dp_in,
    dp_cb,
    dp_half,
    dp_full,
    df_part,
    df_all,
    df_sum,
    df_other,
    die_sent,
    die_landed,
    wide_sent,
    wide_landed,
    core_sent,
    core_landed,
    *sems,
):
    me = lax.axis_index("dp")
    core = lax.rem(me, 2)
    chip = me // 2
    chips = devices // 2
    partner = me + 1 - 2 * core
    everyone = [lax.rem(me + step, devices) for step in range(1, devices)]
    same_core = [lax.rem(me + 2 * step, devices) for step in range(1, chips)]
    images = mask_ref.shape[0]
    units = hidden_ref.shape[0]
    groups = images // 8
    greet(everyone)
    layer_part = bases_ref.shape[0] // LAYERS
    items = [(bases_ref, bases_all_ref, at * layer_part, layer_part) for at in range(LAYERS)]
    route = Route(devices // 8, items, *sems)

    def beside(*words):
        for word in words:
            route.act(word[0], int(word[1:]))

    sends = []

    def die(step, source, target):
        copy = push(source, target, die_sent.at[step], die_landed.at[step], partner)
        sends.append(copy)
        return copy

    def wide(step, source, target):
        made = [
            push(source, target, wide_sent.at[step, at], wide_landed.at[step, at], peer)
            for at, peer in enumerate(everyone)
        ]
        sends.extend(made)
        return made

    def cores(step, source_of, target):
        made = [
            push(source_of(peer), target, core_sent.at[step, at], core_landed.at[step, at], peer)
            for at, peer in enumerate(same_core)
        ]
        sends.extend(made)
        return made

    fb[me] = feat_ref[...]
    copies = wide(0, feat_ref, fb.at[me])
    hid_low[...] = hidden_ref[...].astype(LOW)
    thid_low[...] = teacher_hidden_ref[...].astype(LOW)
    prot_low[0] = protos_ref[...].astype(LOW)
    prot_low[1] = teacher_protos_ref[...].astype(LOW)
    block_rows = feat_ref.shape[0]
    row_at = lax.broadcasted_iota(jnp.int32, (images, devices * block_rows), 0)
    col_at = lax.broadcasted_iota(jnp.int32, (images, devices * block_rows), 1)
    col_dev = lax.shift_right_logical(col_at, 5)
    col_in = jnp.bitwise_and(col_at, 31)
    lead = row_at - 3 * col_dev
    for copy in copies:
        copy.wait_recv()
    beside("A0")
    rows_all = fb[...].reshape(devices * block_rows, LANES)

    def features_of(model):
        pieces = []
        for j in range(3):
            hit = (col_in - (16 * model + 3 * j) == lead) & (lead >= 0) & (lead < 3)
            pieces.append(dot_nn(jnp.where(hit, 1.0, 0.0).astype(LOW), rows_all).astype(LOW))
        return jnp.concatenate(pieces, 1)

    feats = features_of(0)
    tfeats = features_of(1)

    def gather_pair(step, student, teacher, out_s, out_t):
        own_model = jnp.where(core == 0, student, teacher)
        half_out[step] = jnp.where(core == 0, teacher, student)
        copy = die(2 * step, half_out.at[step], half_in.at[step])
        copy.wait_recv()
        got = half_in[step]
        block = jnp.concatenate(
            [jnp.where(core == 0, own_model, got), jnp.where(core == 0, got, own_model)], 1
        ).astype(LOW)
        mine_buf[step, chip] = block
        made = cores(step, lambda peer: mine_buf.at[step, chip], mine_buf.at[step, chip])
        for copy in made:
            copy.wait_recv()
        copy = die(2 * step + 1, mine_buf.at[step], other_buf.at[step])
        copy.wait_recv()
        for at in range(chips):
            one, two = mine_buf[step, at], other_buf[step, at]
            out_s[:, at * LANES : (at + 1) * LANES] = jnp.where(core == 0, one, two)
            out_t[:, at * LANES : (at + 1) * LANES] = jnp.where(core == 0, two, one)

    pre_one = dot_nt(feats, hid_low[:, :D])
    pre1[...] = pre_one
    tpre_one = dot_nt(tfeats, thid_low[:, :D])
    gather_pair(0, gelu_exact(pre_one).astype(LOW).astype(FULL), gelu_exact(tpre_one).astype(LOW).astype(FULL), act_s, act_t)
    beside("B0", "A1")
    pre_two = dot_nt(act_s[...], hid_low[:, D:])
    pre2[...] = pre_two
    tpre_two = dot_nt(act_t[...], thid_low[:, D:])
    gather_pair(1, gelu_exact(pre_two).astype(LOW).astype(FULL), gelu_exact(tpre_two).astype(LOW).astype(FULL), act2_s, act2_t)

    beside("C0", "B1", "A2")
    unit, inverse_norm = unit_rows(dot_nt(act2_s[...], last_ref[...]))
    tunit, unused = unit_rows(dot_nt(act2_t[...], teacher_last_ref[...]))
    unit_ref[...] = unit
    inv_ref[...] = jnp.broadcast_to(inverse_norm, inv_ref.shape)
    unit_low = unit.astype(LOW)
    scaled = dot_nn(unit_low, prot_low[0]) / TAU_STUDENT
    tlogits = dot_nn(tunit.astype(LOW), prot_low[1])
    top_s = jnp.max(scaled, -1, keepdims=True)
    grown_s = jnp.exp(scaled - top_s)
    exp_s[...] = grown_s
    sharp = (tlogits - centre_ref[...]) / TAU_TEACHER
    top_t = jnp.max(sharp, -1, keepdims=True)
    grown_t = jnp.exp(sharp - top_t)
    exp_t[...] = grown_t
    lane = lax.broadcasted_iota(jnp.int32, (images, LANES), 1)
    stats = jnp.where(lane == 0, top_s, 0.0)
    stats = jnp.where(lane == 1, jnp.sum(grown_s, -1, keepdims=True), stats)
    stats = jnp.where(lane == 2, top_t, stats)
    stats = jnp.where(lane == 3, jnp.sum(grown_t, -1, keepdims=True), stats)
    stats = jnp.where(lane == 4, jnp.sum(grown_t * scaled, -1, keepdims=True), stats)
    square = jnp.concatenate([stats, jnp.zeros((LANES - images, LANES), FULL)], 0)
    stat_out[...] = square.T[:8]
    stat_all[me] = stat_out[...]
    copies = wide(1, stat_out, stat_all.at[me])
    counted = mask_ref[...]
    count = jnp.sum(counted)
    centre_out_ref[...] = (
        CENTRE_MOMENTUM * centre_ref[...]
        + (1.0 - CENTRE_MOMENTUM) * jnp.sum(counted * tlogits, 0, keepdims=True) / count
    )
    for copy in copies:
        copy.wait_recv()
    beside("D0", "C1", "B2")
    merged = stat_all[...]
    tops, totals = merged[:, 0], merged[:, 1]
    ttops, ttotals, crosses = merged[:, 2], merged[:, 3], merged[:, 4]
    peak_s = jnp.max(tops, 0, keepdims=True)
    sum_s = jnp.sum(totals * jnp.exp(tops - peak_s), 0, keepdims=True)
    peak_t = jnp.max(ttops, 0, keepdims=True)
    shrink = jnp.exp(ttops - peak_t)
    sum_t = jnp.sum(ttotals * shrink, 0, keepdims=True)
    cross = jnp.sum(crosses * shrink, 0, keepdims=True)
    log_total = peak_s + jnp.log(sum_s)
    mask_row = mask_row_ref[...]
    losses = jnp.where(mask_row > 0.0, log_total - cross / sum_t, 0.0)
    loss = jnp.sum(losses)
    lane8 = lax.broadcasted_iota(jnp.int32, (8, LANES), 1)
    scalars_ref[...] = jnp.where(lane8 == 0, loss, jnp.where(lane8 == 1, count, 0.0))
    back = jnp.concatenate(
        [log_total, peak_t, 1.0 / sum_t, jnp.zeros((LANES - 3, LANES), FULL)], 0
    ).T
    share_s = jnp.exp(top_s - back[:images, 0:1])
    share_t = jnp.exp(top_t - back[:images, 1:2]) * back[:images, 2:3]
    grad_logits = (
        (counted / count) * (exp_s[...] * share_s - exp_t[...] * share_t) / TAU_STUDENT
    ).astype(LOW)

    pz_ref[...] = dot_nt(grad_logits, prot_low[0]).reshape(groups, 8, unit.shape[1])
    for group in range(groups):
        owner = 2 * group

        @pl.when(me != owner)
        def _(group=group, owner=owner):
            push(pz_ref.at[group], pz_all.at[me], wide_sent.at[2, group], wide_landed.at[2, me], owner)

    grad_protos_ref[...] = dot_tn(unit_low, grad_logits)

    @pl.when((core == 0) & (chip < groups))
    def _():
        pz_all[me] = pz_ref[chip]
        for source in range(devices):

            @pl.when(source != me)
            def _(source=source):
                pltpu.make_async_copy(pz_all.at[source], pz_all.at[source], wide_landed.at[2, source]).wait()

        total = jnp.sum(pz_all[...], 0)
        rows = pl.ds(pl.multiple_of(chip * 8, 8), 8)
        own_unit = unit_ref[rows, :]
        own_inv = inv_ref[rows, :][:, 0:1]
        dz_own[...] = own_inv * (total - own_unit * jnp.sum(own_unit * total, -1, keepdims=True))
        dz_all[chip] = dz_own[...]
        for step in range(1, devices):
            push(dz_own, dz_all.at[chip], wide_sent.at[3, step - 1], wide_landed.at[3, chip], lax.rem(me + step, devices))

    for group in range(groups):

        @pl.when(me != 2 * group)
        def _(group=group):
            pltpu.make_async_copy(dz_all.at[group], dz_all.at[group], wide_landed.at[3, group]).wait()

    beside("E0", "D1", "C2")
    grad_bottle = dz_all[...].reshape(images, unit.shape[1]).astype(LOW)
    chip_columns = pl.ds(pl.multiple_of(chip * LANES, LANES), LANES)
    pair = dot_nn(grad_bottle, last_ref[:, chip_columns])
    grad_act_two = jnp.where(core == 0, pair[:, :units], pair[:, units:])
    grad_pre_two = (grad_act_two * gelu_slope(pre2[...])).astype(LOW)

    dp_own[...] = grad_pre_two.astype(FULL)
    copy = die(4, dp_own, dp_in)
    width = last_ref.shape[0] // devices
    pick_row = lax.broadcasted_iota(jnp.int32, (width, last_ref.shape[0]), 0)
    pick_col = lax.broadcasted_iota(jnp.int32, (width, last_ref.shape[0]), 1)
    pick = jnp.where(pick_col == pick_row + me * width, 1.0, 0.0).astype(LOW)
    own_bottle = dot_nt(pick, grad_bottle).astype(LOW)
    grad_last_ref[...] = dot_nn(own_bottle, act2_s[...])
    copy.wait_recv()
    own_dp, got_dp = dp_own[...], dp_in[...]
    dp_cb[...] = jnp.concatenate(
        [jnp.where(core == 0, own_dp, got_dp), jnp.where(core == 0, got_dp, own_dp)], 1
    ).astype(LOW)
    half = images // 2
    my_rows = pl.ds(pl.multiple_of(core * half, 16), half)
    their_rows = pl.ds(pl.multiple_of((1 - core) * half, 16), half)
    dp_half[0, chip] = dp_cb[my_rows, :]
    made = cores(2, lambda peer: dp_half.at[0, chip], dp_half.at[0, chip])
    grad_hidden_ref[:, D:] = dot_tn(grad_pre_two, act_s[...])
    for copy in made:
        copy.wait_recv()
    copy = die(5, dp_half.at[0], dp_half.at[1])
    for at in range(chips):
        dp_full[my_rows, at * LANES : (at + 1) * LANES] = dp_half[0, at]
    copy.wait_recv()
    for at in range(chips):
        dp_full[their_rows, at * LANES : (at + 1) * LANES] = dp_half[1, at]
    beside("E1", "D2")
    part = jnp.concatenate([part_ref[at % 2, at // 2] for at in range(devices)], 0)
    pair = dot_nn(dp_full[...], part)
    grad_act_one = jnp.where(core == 0, pair[:, :units], pair[:, units:])
    grad_pre_one = (grad_act_one * gelu_slope(pre1[...])).astype(LOW)

    out_row = lax.broadcasted_iota(jnp.int32, (8 * chips, images), 0)
    in_row = lax.broadcasted_iota(jnp.int32, (8 * chips, images), 1)
    out_chip = lax.shift_right_logical(out_row, 3)
    out_in = jnp.bitwise_and(out_row, 7)
    hit = (in_row - 6 * out_chip == out_in) & (out_in < 6)
    moved = dot_nn(jnp.where(hit, 1.0, 0.0).astype(LOW), grad_pre_one).astype(LOW)
    df_part[...] = dot_nn(moved, hid_low[:, :D]).reshape(chips, 8, D)
    df_all[chip] = df_part[chip]
    made = cores(3, lambda peer: df_part.at[peer // 2], df_all.at[chip])
    grad_hidden_ref[:, :D] = dot_tn(grad_pre_one, feats)
    for copy in made:
        copy.wait_recv()
    df_sum[...] = jnp.sum(df_all[...], 0)
    copy = die(6, df_sum, df_other)
    copy.wait_recv()
    whole = df_sum[...] + df_other[...]
    grad_feat_ref[...] = whole
    beside("E2", "F0", "F1", "F2")
    squares = jnp.sum(grad_hidden_ref[...] * grad_hidden_ref[...])
    squares = squares + jnp.sum(grad_last_ref[...] * grad_last_ref[...])
    squares = squares + jnp.sum(grad_protos_ref[...] * grad_protos_ref[...])
    scalars_ref[...] = jnp.where(lane8 == 2, squares, scalars_ref[...])
    for copy in sends:
        copy.wait_send()
    for group in range(groups):

        @pl.when(me != 2 * group)
        def _(group=group):
            pltpu.make_async_copy(pz_ref.at[group], pz_ref.at[group], wide_sent.at[2, group]).wait()

    @pl.when((core == 0) & (chip < groups))
    def _():
        for step in range(1, devices):
            pltpu.make_async_copy(dz_own, dz_own, wide_sent.at[3, step - 1]).wait()


def head(feat, hidden, teacher_hidden, part, last, teacher_last, protos, teacher_protos, centre, mask, mask_row, bases, devices):
    images = mask.shape[0]
    units, wide = hidden.shape
    bottle, width = protos.shape
    hid = last.shape[1]
    chips = devices // 2
    groups = images // 8
    vmem = pl.BlockSpec(memory_space=pltpu.VMEM)
    shape = jax.ShapeDtypeStruct
    dma = pltpu.SemaphoreType.DMA
    return pl.pallas_call(
        functools.partial(head_kernel, devices),
        out_shape=(
            shape((8, LANES), FULL),
            shape((units, wide), FULL),
            shape((bottle // devices, hid), FULL),
            shape((bottle, width), FULL),
            shape((8, D), FULL),
            shape((1, width), FULL),
            shape((devices,) + bases.shape, LOW),
        ),
        in_specs=[vmem] * 12,
        out_specs=(vmem,) * 6 + (pl.BlockSpec(memory_space=pl.ANY),),
        scratch_shapes=[
            pltpu.VMEM((devices,) + feat.shape, LOW),
            pltpu.VMEM((units, wide), LOW),
            pltpu.VMEM((units, wide), LOW),
            pltpu.VMEM((2, bottle, width), LOW),
            pltpu.VMEM((2, images, units), FULL),
            pltpu.VMEM((2, images, units), FULL),
            pltpu.VMEM((2, chips, images, LANES), LOW),
            pltpu.VMEM((2, chips, images, LANES), LOW),
            pltpu.VMEM((images, hid), LOW),
            pltpu.VMEM((images, hid), LOW),
            pltpu.VMEM((images, hid), LOW),
            pltpu.VMEM((images, hid), LOW),
            pltpu.VMEM((images, units), FULL),
            pltpu.VMEM((images, units), FULL),
            pltpu.VMEM((images, bottle), FULL),
            pltpu.VMEM((images, LANES), FULL),
            pltpu.VMEM((images, width), FULL),
            pltpu.VMEM((images, width), FULL),
            pltpu.VMEM((8, LANES), FULL),
            pltpu.VMEM((devices, 8, LANES), FULL),
            pltpu.VMEM((groups, 8, bottle), FULL),
            pltpu.VMEM((devices, 8, bottle), FULL),
            pltpu.VMEM((8, bottle), FULL),
            pltpu.VMEM((groups, 8, bottle), FULL),
            pltpu.VMEM((images, units), FULL),
            pltpu.VMEM((images, units), FULL),
            pltpu.VMEM((images, LANES), LOW),
            pltpu.VMEM((2, chips, images // 2, LANES), LOW),
            pltpu.VMEM((images, hid), LOW),
            pltpu.VMEM((chips, 8, D), FULL),
            pltpu.VMEM((chips, 8, D), FULL),
            pltpu.VMEM((8, D), FULL),
            pltpu.VMEM((8, D), FULL),
            dma((7,)),
            dma((7,)),
            dma((4, devices)),
            dma((4, devices)),
            dma((4, chips - 1)),
            dma((4, chips - 1)),
        ]
        + route_sems(LAYERS, devices // 8),
        compiler_params=params(2),
        name="head",
    )(feat, hidden, teacher_hidden, part, last, teacher_last, protos, teacher_protos, centre, mask, mask_row, bases)


def gram_device(matrix):
    return 2 * matrix


def dot_high(left, right, contract):
    return lax.dot_general(
        left,
        right,
        (contract, ((), ())),
        precision=lax.Precision.HIGHEST,
        preferred_element_type=FULL,
    )


def inverse_factor(block):
    size = block.shape[0]
    tiles = size // 8
    sub = lax.broadcasted_iota(jnp.int32, (8, size), 0)
    lane = lax.broadcasted_iota(jnp.int32, (8, size), 1)
    rest = [block[8 * t : 8 * t + 8] for t in range(tiles)]
    made = [jnp.where(lane == sub + 8 * t, 1.0, 0.0) for t in range(tiles)]
    for k in range(size):
        tile, row = k // 8, k % 8
        pivot = rest[tile][row : row + 1]
        scale = lax.rsqrt(pivot[:, k : k + 1])
        factor_row = pivot * scale
        made_row = made[tile][row : row + 1] * scale
        for t in range(tile, tiles):
            column = rest[t][:, k : k + 1] * scale
            if t == tile:
                column = jnp.where(sub[:, :1] > row, column, 0.0)
            rest[t] = rest[t] - column * factor_row
            made[t] = made[t] - column * made_row
            if t == tile:
                made[t] = jnp.where(sub == row, made_row, made[t])
    return jnp.concatenate(made, 0)


def renew_kernel(stats_ref, basis_ref, out_ref, stat, base, gram, work, done):
    parts, rows = stats_ref.shape[:2]
    size = parts * rows
    blocks = size // LANES
    for part in range(parts):
        stat[part * rows : (part + 1) * rows] = stats_ref[part]
        base[part * rows : (part + 1) * rows] = basis_ref[part]
    at_row = lax.broadcasted_iota(jnp.int32, (size, size), 0)
    at_col = lax.broadcasted_iota(jnp.int32, (size, size), 1)
    trace = jnp.sum(jnp.where(at_row == at_col, stat[...], 0.0), axis=(0, 1), keepdims=True)
    scaled = dot_high(stat[...], base[...], ((1,), (0,))) * (size / trace)
    product = dot_high(scaled, scaled, ((0,), (0,)))
    for b in range(blocks):
        work[b] = scaled[:, b * LANES : (b + 1) * LANES]
        for c in range(blocks):
            gram[b, c] = product[b * LANES : (b + 1) * LANES, c * LANES : (c + 1) * LANES]

    def step(b, carried):
        inverse = inverse_factor(gram[b, b])
        made = dot_high(work[b], inverse, ((1,), (1,)))
        done[b] = made

        def trail(c, inner):
            panel = dot_high(inverse, gram[b, c], ((1,), (0,)))
            work[c] = work[c] - dot_high(made, panel, ((1,), (0,)))

            def against(e, innermost):
                other = dot_high(inverse, gram[b, e], ((1,), (0,)))
                gram[c, e] = gram[c, e] - dot_high(panel, other, ((0,), (0,)))
                return innermost

            lax.fori_loop(c, blocks, against, 0)
            return inner

        lax.fori_loop(b + 1, blocks, trail, 0)
        return carried

    lax.fori_loop(0, blocks, step, 0)
    whole = jnp.concatenate([done[b] for b in range(blocks)], 1)
    for part in range(parts):
        out_ref[part] = whole[part * rows : (part + 1) * rows]


def renew_own(stats, basis):
    devices, rows, width = stats.shape
    size = devices * rows
    blocks = size // LANES
    vmem = pl.BlockSpec(memory_space=pltpu.VMEM)
    return pl.pallas_call(
        renew_kernel,
        out_shape=jax.ShapeDtypeStruct(stats.shape, FULL),
        in_specs=[vmem] * 2,
        out_specs=vmem,
        scratch_shapes=[
            pltpu.VMEM((size, width), FULL),
            pltpu.VMEM((size, width), FULL),
            pltpu.VMEM((blocks, blocks, LANES, LANES), FULL),
            pltpu.VMEM((blocks, size, LANES), FULL),
            pltpu.VMEM((blocks, size, LANES), FULL),
        ],
        compiler_params=pltpu.CompilerParams(vmem_limit_bytes=32 << 20),
        name="renew",
    )(stats, basis)


def deal_kernel(devices, stats_ref, bases_ref, own_stats_ref, own_bases_ref, sent, landed):
    me = lax.axis_index("dp")
    core = lax.rem(me, 2)
    chip = me // 2
    matrices = own_stats_ref.shape[0]
    is_gram = (core == 0) & (chip < matrices)
    greet([lax.rem(me + step, devices) for step in range(1, devices)])

    @pl.when(is_gram)
    def _():
        for step in range(1, devices):
            peer = lax.rem(me + step, devices)
            push(bases_ref.at[peer], own_bases_ref.at[chip], sent.at[1, step], landed.at[1, chip], peer)
        for step in range(1, devices):
            peer = lax.rem(me + step, devices)
            push(stats_ref.at[peer], own_stats_ref.at[chip], sent.at[0, step], landed.at[0, chip], peer)
        own_stats_ref[chip] = stats_ref[me]
        own_bases_ref[chip] = bases_ref[me]

    for matrix in range(matrices):

        @pl.when(me != gram_device(matrix))
        def _(matrix=matrix):
            for at, target in ((0, own_stats_ref), (1, own_bases_ref)):
                pltpu.make_async_copy(target.at[matrix], target.at[matrix], landed.at[at, matrix]).wait()

    @pl.when(is_gram)
    def _():
        for step in range(1, devices):
            for at, source in ((0, stats_ref), (1, bases_ref)):
                pltpu.make_async_copy(source.at[0], source.at[0], sent.at[at, step]).wait()


def deal(stats, bases, matrices):
    devices, rows, width = stats.shape
    vmem = pl.BlockSpec(memory_space=pltpu.VMEM)
    dma = pltpu.SemaphoreType.DMA
    return pl.pallas_call(
        functools.partial(deal_kernel, devices),
        out_shape=(jax.ShapeDtypeStruct((matrices, rows, width), FULL),) * 2,
        in_specs=[vmem] * 2,
        out_specs=(vmem,) * 2,
        scratch_shapes=[dma((2, devices)), dma((2, matrices))],
        compiler_params=params(4),
        name="deal",
    )(stats, bases)


def head_slow(
    features,
    teacher_features,
    valid_mask,
    head_hidden,
    head_last,
    protos,
    teacher_hidden,
    teacher_last,
    teacher_protos,
    centre,
    device_index,
):
    all_features, all_teacher = (
        lax.all_gather(features, "dp", axis=0, tiled=True),
        lax.all_gather(teacher_features, "dp", axis=0, tiled=True),
    )
    first_weight = head_hidden[:, :D].astype(jnp.bfloat16)
    second_weight = head_hidden[:, D:].astype(jnp.bfloat16)
    last_weight = head_last.astype(jnp.bfloat16)
    proto_weight = protos.astype(jnp.bfloat16)
    teacher_first = teacher_hidden[:, :D].astype(jnp.bfloat16)
    teacher_second = teacher_hidden[:, D:].astype(jnp.bfloat16)
    pre_one = matmul_low("bd,hd->bh", all_features, first_weight)
    teacher_pre_one = matmul_low("bd,hd->bh", all_teacher, teacher_first)
    act_one = (
        lax.all_gather(gelu_exact(pre_one).astype(jnp.bfloat16), "dp", axis=1, tiled=True),
        lax.all_gather(gelu_exact(teacher_pre_one).astype(jnp.bfloat16), "dp", axis=1, tiled=True),
    )
    pre_two = matmul_low("bh,kh->bk", act_one[0], second_weight)
    teacher_pre_two = matmul_low("bh,kh->bk", act_one[1], teacher_second)
    act_two = (
        lax.all_gather(gelu_exact(pre_two).astype(jnp.bfloat16), "dp", axis=1, tiled=True),
        lax.all_gather(gelu_exact(teacher_pre_two).astype(jnp.bfloat16), "dp", axis=1, tiled=True),
    )
    bottles = (
        lax.all_gather(matmul_low("bh,hc->bc", act_two[0], last_weight), "dp", axis=1, tiled=True),
        lax.all_gather(
            matmul_low("bh,hc->bc", act_two[1], teacher_last.astype(jnp.bfloat16)),
            "dp",
            axis=1,
            tiled=True,
        ),
    )
    unit, inverse_norm = unit_rows(bottles[0])
    teacher_unit, unused_norm = unit_rows(bottles[1])
    unit_low = unit.astype(jnp.bfloat16)
    logits = matmul_low("bc,cp->bp", unit_low, proto_weight)
    teacher_logits = matmul_low(
        "bc,cp->bp", teacher_unit.astype(jnp.bfloat16), teacher_protos.astype(jnp.bfloat16)
    )
    scaled = logits / TAU_STUDENT
    student_top = jnp.max(scaled, -1)
    student_total = jnp.sum(jnp.exp(scaled - student_top[:, None]), -1)
    sharpened = (teacher_logits - centre) / TAU_TEACHER
    teacher_top = jnp.max(sharpened, -1)
    teacher_exp = jnp.exp(sharpened - teacher_top[:, None])
    merged = joined(
        (
            student_top,
            student_total,
            teacher_top,
            jnp.sum(teacher_exp, -1),
            jnp.sum(teacher_exp * scaled, -1),
        ),
        "dp",
        combine_parts,
    )
    log_total = merged[0] + jnp.log(merged[1])
    counted = valid_mask.astype(jnp.float32)
    loss_count = jnp.sum(counted)
    loss_sum = jnp.sum(counted * (log_total - merged[4] / merged[3]))
    student_prob = jnp.exp(scaled - log_total[:, None])
    teacher_prob = jnp.exp(sharpened - merged[2][:, None]) / merged[3][:, None]
    grad_logits = (
        (counted / loss_count)[:, None] * (student_prob - teacher_prob) / TAU_STUDENT
    ).astype(jnp.bfloat16)
    grad_protos = matmul_low("bc,bp->cp", unit_low, grad_logits)
    grad_unit = lax.psum(matmul_low("bp,cp->bc", grad_logits, proto_weight), "dp")
    grad_bottle = inverse_norm * (grad_unit - unit * jnp.sum(unit * grad_unit, -1, keepdims=True))
    last_width = head_last.shape[1]
    grad_bottle_own = lax.dynamic_slice_in_dim(
        grad_bottle, device_index * last_width, last_width, 1
    ).astype(jnp.bfloat16)
    grad_last = matmul_low("bh,bc->hc", act_two[0], grad_bottle_own)
    grad_act_two = lax.psum_scatter(
        matmul_low("bc,hc->bh", grad_bottle_own, last_weight), "dp", scatter_dimension=1, tiled=True
    )
    grad_pre_two = (grad_act_two * gelu_slope(pre_two)).astype(jnp.bfloat16)
    grad_second = matmul_low("bk,bh->kh", grad_pre_two, act_one[0])
    grad_act_one = lax.psum_scatter(
        matmul_low("bk,kh->bh", grad_pre_two, second_weight), "dp", scatter_dimension=1, tiled=True
    )
    grad_pre_one = (grad_act_one * gelu_slope(pre_one)).astype(jnp.bfloat16)
    grad_first = matmul_low("bh,bd->hd", grad_pre_one, all_features)
    grad_features = lax.psum_scatter(
        matmul_low("bh,hd->bd", grad_pre_one, first_weight), "dp", scatter_dimension=0, tiled=True
    )
    grad_hidden = jnp.concatenate([grad_first, grad_second], 1)
    next_centre = (
        CENTRE_MOMENTUM * centre
        + (1.0 - CENTRE_MOMENTUM) * jnp.sum(counted[:, None] * teacher_logits, 0) / loss_count
    )
    return (loss_sum, loss_count, grad_hidden, grad_last, grad_protos, grad_features, next_centre)


def own_feature_rows(features, teacher_features):
    def rows(value):
        count = value.shape[0]
        turned = value.reshape(count, D // LANES, LANES).transpose(1, 0, 2).reshape(-1, LANES)
        return jnp.pad(turned, ((0, 16 - turned.shape[0]), (0, 0)))

    return jnp.concatenate([rows(features), rows(teacher_features)], 0)


def head_fast(
    features,
    teacher_features,
    valid_mask,
    head_hidden,
    protos,
    teacher_hidden,
    teacher_protos,
    centre,
    part,
    last_full,
    teacher_last_full,
    layer_bases,
    devices,
    device_index,
):
    counted = valid_mask.astype(FULL)
    mask_row = jnp.pad(counted, (0, LANES - counted.size)).reshape(1, LANES)
    scalars, grad_hidden, grad_last, grad_protos, grad_feat, next_centre, bases_all = head(
        own_feature_rows(features, teacher_features),
        head_hidden,
        teacher_hidden,
        part,
        last_full,
        teacher_last_full,
        protos,
        teacher_protos,
        centre[None],
        counted[:, None],
        mask_row,
        layer_bases.reshape(-1, D).astype(LOW),
        devices,
    )
    count = features.shape[0]
    grad_features = lax.dynamic_slice_in_dim(grad_feat, (device_index % 2) * count, count, 0)
    return (
        scalars[0, 0],
        scalars[0, 1],
        scalars,
        grad_hidden,
        grad_last.T,
        grad_protos,
        grad_features,
        next_centre[0],
        bases_all,
    )


TOKENS = 272
HALF_ROW = 256
SAVED = ("inputs", "normed", "joint", "mixed", "attended", "middle", "normed_two", "activated", "slope", "outer")


def saved_widths():
    return {
        "inputs": (D, FULL),
        "normed": (D, LOW),
        "joint": (3 * D, LOW),
        "mixed": (D, LOW),
        "attended": (D, LOW),
        "middle": (D, FULL),
        "normed_two": (D, LOW),
        "activated": (MLP, LOW),
        "slope": (MLP, LOW),
        "outer": (D, LOW),
    }


def unpack_blocks(weights, joint_out, output_out, cuts, depth):
    devices = weights.shape[0]
    joint_rows, output_rows = cuts[0], cuts[1] - cuts[0]
    group = 4
    for at in range(0, devices, group):
        blocks = [
            weights[slot_of(at + t, depth), 0 : cuts[1]].astype(FULL) for t in range(group)
        ]
        joint = jnp.concatenate([block[:joint_rows] for block in blocks], 0)
        output = jnp.concatenate([block[joint_rows:] for block in blocks], 0)
        joint_out[at * joint_rows : (at + group) * joint_rows] = joint.astype(LOW)
        output_out[at * output_rows : (at + group) * output_rows] = output.astype(LOW)


def weight_rows(weights, cuts, which, part, parts):
    per = weights.shape[0] // parts
    block = weights[part * per : (part + 1) * per, cuts[which] : cuts[which + 1]]
    return block.reshape(-1, block.shape[-1])


def chance(keys_half, queries, live):
    scores = jnp.where(live, dot_nt(keys_half, queries), -jnp.inf)
    grown = jnp.exp(scores - jnp.max(scores, 0, keepdims=True))
    return grown * (1.0 / jnp.sum(grown, 0, keepdims=True))


WIDE_TABLE = 1152
POSITION_AT = 640
VECTORS_AT = 1024


def table_rows(embedding):
    turned = embedding.T
    columns = turned.shape[0]
    patch = jnp.pad(turned[:, :PIX], ((0, 0), (0, POSITION_AT - PIX)))
    position = jnp.concatenate([turned[:, PIX + 1 : PIX + SEQ], turned[:, PIX : PIX + 1]], 1)
    position = jnp.pad(position, ((0, 0), (0, VECTORS_AT - POSITION_AT - SEQ)))
    layer_rows = turned[:, PIX + SEQ : PIX + SEQ + 6 * LAYERS].reshape(columns, LAYERS, 6)
    layer_rows = jnp.pad(layer_rows, ((0, 0), (0, 0), (0, 2))).reshape(columns, -1)
    tail_rows = turned[:, PIX + SEQ + 6 * LAYERS :]
    joint = jnp.concatenate([patch, position, layer_rows, tail_rows], 1)
    rows = -(-columns // 16) * 16
    joint = jnp.pad(joint, ((0, rows - columns), (0, WIDE_TABLE - joint.shape[1]))).astype(LOW)
    return jnp.concatenate([joint[:, at : at + D] for at in range(0, WIDE_TABLE, D)], 0)


PLAN = {
    "start": ("A0", "A1", "A2", "B0", "B1", "A3", "C0", "B2", "A4", "C1", "D0", "E0", "D1", "B3", "C2", "E1"),
    0: ("B4", "A5"),
    "middle": ("C3", "D2", "E2"),
    1: ("C4", "D3"),
    2: ("E3", "D4", "B5", "A6"),
    3: ("E4",),
    4: ("C5",),
    5: ("D5", "B6", "A7"),
    6: ("E5",),
    7: ("C6",),
    8: ("D6", "B7", "A8"),
    9: ("E6",),
    10: ("C7",),
    11: ("D7", "B8", "A9"),
    12: ("E7",),
    13: ("C8",),
    14: ("D8", "B9"),
    15: ("E8",),
    16: ("C9",),
    17: ("D9",),
    "end": ("E9",),
}


def fetch_kernel(
    cuts,
    depth,
    patches_ref,
    table_ref,
    teacher_table_ref,
    layers_ref,
    teacher_layers_ref,
    last_ref,
    columns_ref,
    feat_ref,
    final_ref,
    vectors_out_ref,
    weights_out_ref,
    last_out_ref,
    part_ref,
    *rest,
):
    layer, model, image = (pl.program_id(at) for at in range(3))
    images = pl.num_programs(2)
    step = (layer * 2 + model) * images + image
    outs = dict(zip(SAVED, rest[: len(SAVED)]))
    (
        current,
        joint_weight,
        output_weight,
        weights_all,
        tables,
        turned,
        vectors_all,
        out_sem,
        part_own,
        part_sent,
        part_landed,
        part_die,
        *sems,
    ) = rest[len(SAVED) :]
    sources = (layers_ref, teacher_layers_ref)
    rows = layers_ref.shape[1]
    first = cuts[1]

    def layer_item(which, at, lower, size):
        return (sources[which].at[at], weights_all.at[which, at], lower, size)

    items = [
        (table_ref, tables.at[0], 0, table_ref.shape[0]),
        layer_item(0, 0, 0, first),
        layer_item(0, 0, first, rows - first),
        (teacher_table_ref, tables.at[1], 0, table_ref.shape[0]),
        layer_item(1, 0, 0, rows),
        layer_item(0, 1, 0, rows),
        layer_item(1, 1, 0, rows),
        layer_item(0, 2, 0, rows),
        layer_item(1, 2, 0, rows),
        (last_ref, last_out_ref, 0, last_ref.shape[0]),
    ]
    route = Route(depth, items, *sems)
    total = 8 * depth
    chips = total // 2
    chip = route.me // 2
    core = route.core

    def part_copy(at):
        peer = lax.rem(route.me + 2 * at, total)
        block = columns_ref.at[:, pl.ds(pl.multiple_of((peer // 2) * LANES, LANES), LANES)]
        return route.copy(
            block, part_ref.at[core, chip], part_sent.at[at], part_landed.at[at], peer
        )

    def part_mine():
        block = columns_ref.at[:, pl.ds(pl.multiple_of(chip * LANES, LANES), LANES)]
        return pltpu.make_async_copy(block, part_ref.at[core, chip], part_own.at[0])

    def part_across():
        return route.copy(
            part_ref.at[core], part_ref.at[core], part_die.at[0], part_die.at[1], route.partner
        )

    def out_copy(at):
        return pltpu.make_async_copy(weights_all.at[0, at], weights_out_ref.at[at], out_sem.at[at])

    def run(name):
        for word in PLAN[name]:
            route.act(word[0], int(word[1:]))

    @pl.when(step == 0)
    def _():
        greet([lax.rem(route.me + 2 * at, total) for at in range(1, chips)] + [route.partner])
        run("start")

    def set_up(which):
        columns = D // total
        block_rows = table_ref.shape[0] // (WIDE_TABLE // D)
        group = 4
        for at in range(0, total, group):
            for block in range(WIDE_TABLE // D):
                lower = block * block_rows
                pieces = [
                    tables[which, slot_of(at + t, depth), lower : lower + block_rows].astype(FULL)[
                        :columns
                    ]
                    for t in range(group)
                ]
                turned[at * columns : (at + group) * columns, block * D : (block + 1) * D] = (
                    jnp.concatenate(pieces, 0).astype(LOW)
                )
        vectors = turned[:, VECTORS_AT:WIDE_TABLE].astype(FULL).T
        vectors_all[which] = vectors[:32]
        position = turned[:, POSITION_AT:VECTORS_AT].astype(FULL).T[:TOKENS]
        row = lax.broadcasted_iota(jnp.int32, (TOKENS, D), 0)
        tail = 8 * LAYERS
        extra = jnp.where(
            row < HALF_ROW,
            vectors[tail : tail + 1],
            jnp.where(row == HALF_ROW, vectors[tail + 1 : tail + 2], 0.0),
        )
        start = position + extra
        for at in range(feat_images):
            current[which, at, :HALF_ROW] = start[:HALF_ROW] + dot_nt(
                patches_ref[at], turned[:, :PIX]
            )
            current[which, at, HALF_ROW:] = start[HALF_ROW:]

    feat_images = patches_ref.shape[0]
    for at in range(18):

        @pl.when(step == at)
        def _(at=at):
            run(at)
            if at == 0:
                set_up(0)
                vectors_out_ref[...] = vectors_all[0]
            if at == 3:
                set_up(1)
            if at == 3:
                out_copy(0).start()
            if at == 6:
                out_copy(1).start()
            if at == 11:
                part_mine().start()
                for other in range(1, chips):
                    part_copy(other).start()
            if at == 12:
                out_copy(2).start()
            if at == 16:
                part_mine().wait()
                for other in range(1, chips):
                    part_copy(other).wait_recv()
                part_across().start()

    weights = weights_all.at[model, layer]

    @pl.when(image == 0)
    def _():
        unpack_blocks(weights, joint_weight, output_weight, cuts, depth)

    vectors = vectors_all[model, pl.ds(pl.multiple_of(layer * 8, 8), 8), :]
    lane = lax.broadcasted_iota(jnp.int32, (TOKENS, LANES), 1)
    live = lax.broadcasted_iota(jnp.int32, (TOKENS, TOKENS), 0) < SEQ

    def attend(save):
        def keep(name, value):
            if save:
                outs[name][0, 0] = value

        inputs = current[model, image]
        keep("inputs", inputs)
        normed = layer_norm(inputs, vectors[0:1], vectors[1:2]).astype(LOW)
        keep("normed", normed)
        mixed = []
        for pair in range(D // LANES):
            lower = pair * LANES
            parts = [
                dot_nt(normed, joint_weight[third * D + lower : third * D + lower + LANES])
                for third in range(3)
            ]
            rounded = [part.astype(LOW) for part in parts]
            if save:
                for third in range(3):
                    outs["joint"][0, 0, :, third * D + lower : third * D + lower + LANES] = rounded[
                        third
                    ]
            queries = (rounded[0].astype(FULL) * HEAD_DIM ** (-0.5)).astype(LOW)
            values = parts[2].T.astype(LOW)
            turned_heads = []
            for half in range(2):
                keys_half = jnp.where(
                    (lane >= HEAD_DIM) == bool(half), rounded[1].astype(FULL), 0.0
                ).astype(LOW)
                share = chance(keys_half, queries, live).astype(LOW)
                turned_heads.append(dot_nn(values[half * HEAD_DIM : (half + 1) * HEAD_DIM], share))
            mixed.append(jnp.concatenate(turned_heads, 0).T.astype(LOW))
        mixed = jnp.concatenate(mixed, 1)
        keep("mixed", mixed)
        attended = dot_nt(mixed, output_weight[...])
        keep("attended", attended.astype(LOW))
        middle = inputs + vectors[4:5] * attended
        keep("middle", middle)
        current[model, image] = middle

    def perceive(save):
        def keep(name, value):
            if save:
                outs[name][0, 0] = value

        middle = current[model, image]
        normed_two = layer_norm(middle, vectors[2:3], vectors[3:4]).astype(LOW)
        keep("normed_two", normed_two)
        outer = jnp.zeros((TOKENS, D), FULL)
        parts = MLP // D
        for part in range(parts):
            inner = dot_nt(normed_two, weight_rows(weights, cuts, 1, part, parts))
            spread_half = 0.5 * (1.0 + lax.erf(inner * ROOT_HALF))
            activated = (inner * spread_half).astype(LOW)
            if save:
                outs["activated"][0, 0, :, part * D : (part + 1) * D] = activated
                slope = spread_half + inner * jnp.exp(-0.5 * inner * inner) * DENSITY_SCALE
                outs["slope"][0, 0, :, part * D : (part + 1) * D] = slope.astype(LOW)
            outer = outer + dot_nn(activated, weight_rows(weights, cuts, 2, part, parts))
        keep("outer", outer.astype(LOW))
        result = middle + vectors[5:6] * outer
        current[model, image] = result
        final = result[HALF_ROW : HALF_ROW + 8]
        final_ref[model, image] = final
        tail = 8 * LAYERS
        feat_ref[model, image] = layer_norm(
            final, vectors_all[model, tail + 2 : tail + 3], vectors_all[model, tail + 3 : tail + 4]
        )

    @pl.when(model == 0)
    def _():
        attend(True)

    @pl.when(model == 1)
    def _():
        attend(False)

    @pl.when(step == 0)
    def _():
        run("middle")

    @pl.when(model == 0)
    def _():
        perceive(True)

    @pl.when(model == 1)
    def _():
        perceive(False)

    @pl.when(step == 17)
    def _():
        run("end")
        for at in range(len(items)):
            route.act("F", at)
        for at in range(LAYERS):
            out_copy(at).wait()
        across = part_across()
        across.wait_recv()
        across.wait_send()
        for other in range(1, chips):
            part_copy(other).wait_send()


def fetch_forward(patches, embedding, teacher_embedding, layers, teacher_layers, head_last, teacher_last, head_hidden, devices):
    images = patches.shape[0]
    depth = devices // 8
    rows = layers.shape[1]
    cuts = [lower for lower, upper in layer_bounds(devices)][1:] + [rows]
    shape = jax.ShapeDtypeStruct
    vmem = pl.BlockSpec(memory_space=pltpu.VMEM)
    anywhere = pl.BlockSpec(memory_space=pl.ANY)

    def last_rows(value):
        return value.T.astype(LOW).reshape(-1, LANES)

    table = table_rows(embedding)
    last = jnp.concatenate([last_rows(head_last), last_rows(teacher_last)], 0)
    columns = head_hidden[:, D:].astype(LOW)
    outs = [shape((2, images, 8, D), FULL)] * 2
    specs = [vmem] * 2
    outs += [
        shape((32, D), FULL),
        shape((LAYERS, devices, rows, D), LOW),
        shape((devices,) + last.shape, LOW),
        shape((2, devices // 2, columns.shape[0], LANES), LOW),
    ]
    specs += [vmem, anywhere, anywhere, anywhere]
    for name in SAVED:
        width, kind = saved_widths()[name]
        outs.append(shape((LAYERS, images, TOKENS, width), kind))
        specs.append(
            pl.BlockSpec(
                (1, 1, TOKENS, width),
                lambda layer, model, image: (layer, jnp.where(model == 0, image, images - 1), 0, 0),
            )
        )
    count = 10
    dma = pltpu.SemaphoreType.DMA
    return pl.pallas_call(
        functools.partial(fetch_kernel, cuts, depth),
        grid=(LAYERS, 2, images),
        out_shape=outs,
        in_specs=[vmem] + [anywhere] * 6,
        out_specs=specs,
        scratch_shapes=[
            pltpu.VMEM((2, images, TOKENS, D), FULL),
            pltpu.VMEM((3 * D, D), LOW),
            pltpu.VMEM((D, D), LOW),
            pltpu.VMEM((2, LAYERS, devices, rows, D), LOW),
            pltpu.VMEM((2, devices) + table.shape, LOW),
            pltpu.VMEM((D, WIDE_TABLE), LOW),
            pltpu.VMEM((2, 32, D), FULL),
            dma((LAYERS,)),
            dma((1,)),
            dma((devices // 2,)),
            dma((devices // 2,)),
            dma((2,)),
        ]
        + route_sems(count, depth),
        compiler_params=params(1, 60 << 20),
        name="fetch_forward",
    )(
        patches,
        table,
        table_rows(teacher_embedding),
        layers.astype(LOW),
        teacher_layers.astype(LOW),
        last,
        columns,
    )


def last_tables(last_all, width, devices):
    ordered = last_all.reshape(8, devices // 8, 2, -1, LANES).transpose(2, 1, 0, 3, 4)
    return ordered.reshape(2, width, -1)


class Reduce:
    def __init__(self, depth, chunks, sources, buffers, sems):
        self.depth, self.chunks, self.sources = depth, chunks, sources
        self.die_buf, self.d_buf, self.x_buf, self.y_buf, self.z_buf = buffers
        self.die_sent, self.die_landed, self.near_sent, self.near_landed, self.z_sent, self.z_landed = sems
        me = lax.axis_index("dp")
        self.me = me
        self.total = 8 * depth
        core = lax.rem(me, 2)
        x_at = lax.rem(me // 2, 2)
        y_at = lax.rem(me // 4, 2)
        self.z_at = me // 8
        self.partner = me + 1 - 2 * core
        self.to_x = me + 2 - 4 * x_at
        self.to_y = me + 4 - 8 * y_at
        places = [(y_at, x_at), (y_at, 1 - x_at), (1 - y_at, x_at), (1 - y_at, 1 - x_at)]
        self.starts = [((y * 2 + x) * 2 + core) * depth for y, x in places]
        self.partner_starts = [((y * 2 + x) * 2 + 1 - core) * depth for y, x in places]

    def copy(self, source, target, sent, landed, device):
        return pltpu.make_async_remote_copy(
            src_ref=source,
            dst_ref=target,
            send_sem=sent,
            recv_sem=landed,
            device_id=(device,),
            device_id_type=MESH,
        )

    def half(self, k):
        return ((self.chunks[k][1] // 2 + 15) // 16) * 16

    def die(self, k, rel):
        lower, size = self.chunks[k]
        return self.copy(
            self.sources[k].at[pl.ds(self.partner_starts[rel], self.depth)],
            self.die_buf.at[pl.ds(rel * self.depth, self.depth), pl.ds(lower, size)],
            self.die_sent.at[k, rel],
            self.die_landed.at[k, rel],
            self.partner,
        )

    def near(self, k, which):
        lower, size = self.chunks[k]
        half = self.half(k)
        rel, start, length, target, device = [
            (3, lower, half, self.d_buf, self.to_x),
            (3, lower + half, size - half, self.d_buf, self.to_y),
            (1, lower, size, self.x_buf, self.to_x),
            (2, lower, size, self.y_buf, self.to_y),
        ][which]
        return self.copy(
            self.die_buf.at[pl.ds(rel * self.depth, self.depth), pl.ds(start, length)],
            target.at[:, pl.ds(start, length)],
            self.near_sent.at[k, which],
            self.near_landed.at[k, which],
            device,
        )

    def deep(self, k, step):
        lower, size = self.chunks[k]
        return self.copy(
            self.die_buf.at[lax.rem(self.z_at + step, self.depth), pl.ds(lower, size)],
            self.z_buf.at[self.z_at, pl.ds(lower, size)],
            self.z_sent.at[k, step],
            self.z_landed.at[k, step],
            lax.rem(self.me + 8 * step, self.total),
        )

    def pair_sum(self, k, rel, z_pos, first, length):
        lower, size = self.chunks[k]
        return self.sources[k][
            self.starts[rel] + z_pos, first - lower : first - lower + length
        ].astype(FULL) + self.die_buf[rel * self.depth + z_pos, first : first + length].astype(FULL)

    def begin(self, k):
        for rel in (3, 1, 2, 0):
            self.die(k, rel).start()

    def one(self, k):
        lower, size = self.chunks[k]
        self.die(k, 3).wait_recv()
        for z_pos in range(self.depth):
            self.die_buf[3 * self.depth + z_pos, lower : lower + size] = self.pair_sum(
                k, 3, z_pos, lower, size
            ).astype(LOW)
        self.near(k, 0).start()
        self.near(k, 1).start()

    def two(self, k):
        lower, size = self.chunks[k]
        half = self.half(k)
        first, second = (lower, half), (lower + half, size - half)
        for rel, which, arrived, helped, plain in ((1, 2, 1, second, first), (2, 3, 0, first, second)):
            self.die(k, rel).wait_recv()
            self.near(k, arrived).wait_recv()
            for z_pos in range(self.depth):
                at = rel * self.depth + z_pos
                self.die_buf[at, plain[0] : plain[0] + plain[1]] = self.pair_sum(
                    k, rel, z_pos, *plain
                ).astype(LOW)
                self.die_buf[at, helped[0] : helped[0] + helped[1]] = (
                    self.pair_sum(k, rel, z_pos, *helped)
                    + self.d_buf[z_pos, helped[0] : helped[0] + helped[1]].astype(FULL)
                ).astype(LOW)
            self.near(k, which).start()

    def three(self, k):
        lower, size = self.chunks[k]
        self.die(k, 0).wait_recv()
        self.near(k, 2).wait_recv()
        self.near(k, 3).wait_recv()
        for z_pos in range(self.depth):
            self.die_buf[z_pos, lower : lower + size] = (
                self.pair_sum(k, 0, z_pos, lower, size)
                + self.x_buf[z_pos, lower : lower + size].astype(FULL)
                + self.y_buf[z_pos, lower : lower + size].astype(FULL)
            ).astype(LOW)
        for step in range(1, self.depth):
            self.deep(k, step).start()

    def four(self, k):
        lower, size = self.chunks[k]
        for step in range(1, self.depth):
            self.deep(k, step).wait_recv()
        value = self.die_buf[self.z_at, lower : lower + size].astype(FULL)
        for step in range(1, self.depth):
            value = value + self.z_buf[
                lax.rem(self.z_at + step, self.depth), lower : lower + size
            ].astype(FULL)
        return value

    def sent(self, k, die_too):
        if die_too:
            for rel in range(4):
                self.die(k, rel).wait_send()
        for which in range(4):
            self.near(k, which).wait_send()
        for step in range(1, self.depth):
            self.deep(k, step).wait_send()


PER_LAYER = ("normed", "mixed", "normed_two", "activated")


def backward_kernel(cuts, bounds, depth, *refs):
    (
        squares_ref,
        stats_ref,
        bases_ref,
        patches_ref,
        weights_ref,
        vectors_ref,
        final_ref,
        grad_feat_ref,
    ) = refs[:8]
    saved = dict(zip(SAVED, refs[8 : 8 + len(SAVED)]))
    (
        own_ref,
        norm_ref,
        next_stats_ref,
        basis_ref,
        grad_now,
        joint_weight,
        output_weight,
        grad_outer_all,
        grad_inner_all,
        grad_attended_all,
        grad_joint_all,
        grad_patch,
        grad_start,
        grad_rows,
        packets,
        table_packet,
        die_buf,
        d_buf,
        x_buf,
        y_buf,
        z_buf,
        stat_buf,
        square_out,
        square_all,
        segs,
        gram_buf,
        die_sent,
        die_landed,
        near_sent,
        near_landed,
        z_sent,
        z_landed,
        stat_sent,
        stat_landed,
        gram_sent,
        gram_landed,
        square_sent,
        square_landed,
    ) = refs[8 + len(SAVED) :]
    step, image = pl.program_id(0), pl.program_id(1)
    images = final_ref.shape[0]
    now = step * images + image
    layer_rows = cuts[3]
    chunks = [(layer * layer_rows, layer_rows) for layer in reversed(range(LAYERS))]
    chunks.append((LAYERS * layer_rows, table_packet.shape[1]))
    count = len(chunks)
    sources = [packets.at[k % 2] for k in range(LAYERS)] + [table_packet]
    ring = Reduce(
        depth,
        chunks,
        sources,
        (die_buf, d_buf, x_buf, y_buf, z_buf),
        (die_sent, die_landed, near_sent, near_landed, z_sent, z_landed),
    )
    me = ring.me
    total = ring.total
    core = lax.rem(me, 2)
    chip = me // 2
    matrices = stats_ref.shape[0]
    own_rows = stats_ref.shape[1]
    segment_rows = segs.shape[2]
    is_gram = (core == 0) & (chip < matrices)
    everyone = [lax.rem(me + at, total) for at in range(1, total)]

    def stat_copy(at, matrix):
        source = (stats_ref, bases_ref)[at]
        return ring.copy(
            source.at[matrix],
            stat_buf.at[at, me],
            stat_sent.at[at, matrix],
            stat_landed.at[at, me],
            gram_device(matrix),
        )

    def stat_own(at, matrix):
        source = (stats_ref, bases_ref)[at]
        return pltpu.make_async_copy(source.at[matrix], stat_buf.at[at, me], stat_landed.at[at, me])

    def gram_copy(matrix):
        return ring.copy(
            segs.at[matrix // 4, matrix % 4],
            gram_buf.at[me],
            gram_sent.at[matrix],
            gram_landed.at[me],
            gram_device(matrix),
        )

    def finish(k):
        lower, size = chunks[k]
        value = ring.four(k)
        own_ref[lower : lower + size] = value
        if k == count - 1:
            return
        layer = lower // layer_rows
        for segment, (low_row, high_row) in enumerate(bounds):
            piece = value[low_row:high_row].astype(LOW)
            if high_row - low_row < segment_rows:
                blank = jnp.zeros((segment_rows - (high_row - low_row), value.shape[1]), LOW)
                piece = jnp.concatenate([piece, blank], 0)
            matrix = 4 * layer + segment
            segs[layer, segment] = piece

            @pl.when(me != gram_device(matrix))
            def _(matrix=matrix):
                gram_copy(matrix).start()

    @pl.when(now == 0)
    def _():
        greet(everyone)
        for matrix in range(matrices):

            @pl.when(me != gram_device(matrix))
            def _(matrix=matrix):
                stat_copy(0, matrix).start()
                stat_copy(1, matrix).start()

            @pl.when(me == gram_device(matrix))
            def _(matrix=matrix):
                stat_own(0, matrix).start()
                stat_own(1, matrix).start()

        grad_rows[...] = jnp.zeros(grad_rows.shape, FULL)
        grad_patch[...] = jnp.zeros(grad_patch.shape, FULL)
        grad_start[...] = jnp.zeros(grad_start.shape, FULL)

    @pl.when(now == images)
    def _():
        ring.one(0)

    @pl.when(now == images + 1)
    def _():
        ring.two(0)

    @pl.when(now == 2 * images)
    def _():
        ring.one(1)
        ring.three(0)

    @pl.when(now == 2 * images + 1)
    def _():
        ring.two(1)
        finish(0)

    weights = weights_ref.at[0]
    vectors = vectors_ref[pl.ds(pl.multiple_of((LAYERS - 1 - step) * 8, 8), 8), :]
    tail = 8 * LAYERS

    @pl.when(image == 0)
    def _():
        unpack_blocks(weights, joint_weight, output_weight, cuts, depth)

    @pl.when(step == 0)
    def _():
        first = lax.broadcasted_iota(jnp.int32, (8, D), 0) == 0
        given = jnp.where(first, grad_feat_ref[image], 0.0)
        grad_class, grad_gain, grad_shift = norm_back(
            final_ref[image], vectors_ref[tail + 2 : tail + 3], given
        )
        grad_rows[tail + 2 : tail + 3] += grad_gain[None]
        grad_rows[tail + 3 : tail + 4] += grad_shift[None]
        grad_now[image] = jnp.zeros((TOKENS, D), FULL)
        grad_now[image, HALF_ROW : HALF_ROW + 8] = jnp.where(first, grad_class, 0.0)

    rows = pl.ds(pl.multiple_of(image * TOKENS, 16), TOKENS)
    grad_result = grad_now[image]
    grad_outer = (vectors[5:6] * grad_result).astype(LOW)
    grad_outer_all[rows, :] = grad_outer
    grad_scale_two = jnp.sum(grad_result * saved["outer"][0, 0].astype(FULL), 0, keepdims=True)
    parts = MLP // D
    grad_normed_two = jnp.zeros((TOKENS, D), FULL)
    for part in range(parts):
        columns = slice(part * D, (part + 1) * D)
        grad_activated = dot_nt(grad_outer, weight_rows(weights, cuts, 2, part, parts))
        grad_inner = (grad_activated * saved["slope"][0, 0, :, columns].astype(FULL)).astype(LOW)
        grad_inner_all[rows, columns] = grad_inner
        grad_normed_two = grad_normed_two + dot_nn(
            grad_inner, weight_rows(weights, cuts, 1, part, parts)
        )
    grad_middle_norm, grad_gain_two, grad_shift_two = norm_back(
        saved["middle"][0, 0], vectors[2:3], grad_normed_two
    )
    grad_middle = grad_result + grad_middle_norm
    grad_attended = (vectors[4:5] * grad_middle).astype(LOW)
    grad_attended_all[rows, :] = grad_attended
    grad_scale_one = jnp.sum(grad_middle * saved["attended"][0, 0].astype(FULL), 0, keepdims=True)
    grad_mixed = dot_nn(grad_attended, output_weight[...]).astype(LOW)
    lane = lax.broadcasted_iota(jnp.int32, (TOKENS, LANES), 1)
    live = lax.broadcasted_iota(jnp.int32, (TOKENS, TOKENS), 0) < SEQ
    for pair in range(D // LANES):
        lower = pair * LANES
        queries, keys_in, values_in = [
            saved["joint"][0, 0, :, third * D + lower : third * D + lower + LANES]
            for third in range(3)
        ]
        queries = (queries.astype(FULL) * HEAD_DIM ** (-0.5)).astype(LOW)
        keys_wide = keys_in.astype(FULL)
        values_wide = values_in.astype(FULL)
        keys_turned = keys_wide.T.astype(LOW)
        grad_head = grad_mixed[:, lower : lower + LANES]
        turned, grad_keys, grad_values = [], [], []
        for half in range(2):
            mine = (lane >= HEAD_DIM) == bool(half)
            share = chance(jnp.where(mine, keys_wide, 0.0).astype(LOW), queries, live)
            grad_share = dot_nt(jnp.where(mine, values_wide, 0.0).astype(LOW), grad_head)
            grad_values.append(dot_nn(share.astype(LOW), grad_head))
            grad_scores = (
                share * (grad_share - jnp.sum(share * grad_share, 0, keepdims=True))
            ).astype(LOW)
            grad_keys.append(dot_nn(grad_scores, queries))
            turned.append(dot_nn(keys_turned[half * HEAD_DIM : (half + 1) * HEAD_DIM], grad_scores))
        grad_queries = jnp.concatenate(turned, 0).T * HEAD_DIM ** (-0.5)
        low_half = lane < HEAD_DIM
        for third, value in enumerate(
            (
                grad_queries,
                jnp.where(low_half, grad_keys[0], grad_keys[1]),
                jnp.where(low_half, grad_values[0], grad_values[1]),
            )
        ):
            grad_joint_all[rows, third * D + lower : third * D + lower + LANES] = value.astype(LOW)
    grad_normed = dot_nn(grad_joint_all[rows, :], joint_weight[...])
    grad_input_norm, grad_gain_one, grad_shift_one = norm_back(
        saved["inputs"][0, 0], vectors[0:1], grad_normed
    )
    grad_input = grad_middle + grad_input_norm
    grad_now[image] = grad_input
    added = jnp.concatenate(
        [
            grad_gain_one[None],
            grad_shift_one[None],
            grad_gain_two[None],
            grad_shift_two[None],
            grad_scale_one,
            grad_scale_two,
            jnp.zeros((2, D), FULL),
        ],
        0,
    )
    grad_rows[pl.ds(pl.multiple_of((LAYERS - 1 - step) * 8, 8), 8), :] += added

    @pl.when(step == LAYERS - 1)
    def _():
        grad_patch[:, :PIX] += dot_tn(grad_input[:HALF_ROW].astype(LOW), patches_ref[image])
        grad_start[:TOKENS] += grad_input
        grad_rows[tail : tail + 1] += jnp.sum(grad_input[:HALF_ROW], 0, keepdims=True)
        grad_rows[tail + 1 : tail + 2] += grad_input[HALF_ROW : HALF_ROW + 1]

    def pack(packet):
        def flat(name):
            value = saved[name][0]
            return value.reshape(-1, value.shape[-1])

        per = cuts[0], cuts[1] - cuts[0], cuts[2] - cuts[1], cuts[3] - cuts[2]
        groups = 4
        each = total // groups
        for at in range(groups):
            first = at * each
            joint_rows = dot_tn(
                grad_joint_all[:, first * per[0] : (first + each) * per[0]], flat("normed")
            )
            output_rows = dot_tn(
                grad_attended_all[:, first * per[1] : (first + each) * per[1]], flat("mixed")
            )
            inner_rows = dot_tn(
                grad_inner_all[:, first * per[2] : (first + each) * per[2]], flat("normed_two")
            ).astype(LOW)
            outer_rows = dot_tn(
                saved["activated"][0, :, :, first * per[3] : (first + each) * per[3]].reshape(
                    -1, each * per[3]
                ),
                grad_outer_all[...],
            ).astype(LOW)
            for t in range(each):
                joined_rows = jnp.concatenate(
                    [
                        joint_rows[t * per[0] : (t + 1) * per[0]],
                        output_rows[t * per[1] : (t + 1) * per[1]],
                    ],
                    0,
                )
                packet[slot_of(first + t, depth), : cuts[1]] = joined_rows.astype(LOW)
                packet[first + t, cuts[1] : cuts[2]] = inner_rows[t * per[2] : (t + 1) * per[2]]
                packet[first + t, cuts[2] : cuts[3]] = outer_rows[t * per[3] : (t + 1) * per[3]]

    @pl.when((image == images - 1) & (step == LAYERS - 1))
    def _():
        ring.three(1)
        for rel in range(4):
            ring.die(0, rel).wait_send()

    @pl.when(image == images - 1)
    def _():
        pack(packets.at[lax.rem(step, 2)])

    for k in range(LAYERS - 1):

        @pl.when((image == images - 1) & (step == k))
        def _(k=k):
            ring.begin(k)

    @pl.when((image == images - 1) & (step == LAYERS - 1))
    def _():
        last, table = LAYERS - 1, LAYERS
        ring.begin(last)
        ring.one(last)
        blank = jnp.zeros((LANES - 32, D), FULL)
        turned_rows = jnp.concatenate([grad_rows[...], blank], 0).T
        turned = [grad_patch[:, :D], None, None]
        turned_start = grad_start[...].T
        left = VECTORS_AT - POSITION_AT
        turned[1] = jnp.concatenate([grad_patch[:, D:], turned_start[:, : 2 * D - POSITION_AT]], 1)
        turned[2] = jnp.concatenate([turned_start[:, 2 * D - POSITION_AT : left], turned_rows], 1)
        columns = D // total
        for block in range(3):
            for device in range(total):
                piece = turned[block][device * columns : (device + 1) * columns]
                piece = jnp.concatenate([piece, jnp.zeros((16 - columns, D), FULL)], 0)
                table_packet[slot_of(device, depth), 16 * block : 16 * block + 16] = piece.astype(LOW)
        ring.begin(table)
        ring.one(table)
        ring.two(last)
        finish(1)
        ring.two(table)
        ring.three(last)
        ring.three(table)
        finish(last)
        finish(table)

        own = own_ref[...]
        lane8 = lax.broadcasted_iota(jnp.int32, (8, LANES), 1)
        squares = jnp.sum(own * own) + jnp.sum(jnp.where(lane8 == 2, squares_ref[...], 0.0)) / 8.0
        square_out[...] = jnp.full((8, LANES), squares)
        square_all[me] = square_out[...]
        copies = [
            push(square_out, square_all.at[me], square_sent.at[at], square_landed.at[at], peer)
            for at, peer in enumerate(everyone)
        ]

        @pl.when(is_gram)
        def _():
            for matrix in range(matrices):

                @pl.when(matrix == chip)
                def _(matrix=matrix):
                    gram_buf[me] = segs[matrix // 4, matrix % 4]

            for source in range(total):
                for at in range(2):
                    view = stat_buf.at[at, source]
                    pltpu.make_async_copy(view, view, stat_landed.at[at, source]).wait()

                @pl.when(source != me)
                def _(source=source):
                    pltpu.make_async_copy(
                        gram_buf.at[source], gram_buf.at[source], gram_landed.at[source]
                    ).wait()

            basis_ref[...] = stat_buf[1]
            blocks = gram_buf[...].reshape(total * segment_rows, gram_buf.shape[2])
            gram = dot_tn(blocks, blocks)
            for source in range(total):
                next_stats_ref[source] = gram[source * own_rows : (source + 1) * own_rows]

        @pl.when(jnp.logical_not(is_gram))
        def _():
            next_stats_ref[...] = jnp.zeros(next_stats_ref.shape, FULL)
            basis_ref[...] = jnp.zeros(basis_ref.shape, FULL)
            stat_buf[0] = jnp.zeros(stat_buf.shape[1:], FULL)

        for copy in copies:
            copy.wait_recv()
        norm = jnp.sqrt(jnp.sum(square_all[...], 0))
        norm_ref[...] = norm
        clip = jnp.minimum(1.0, CLIP_MAX / (norm + 1e-06))[:1, :1]
        scale = (1.0 - BETA_STAT) * (clip * clip)
        for source in range(total):
            next_stats_ref[source] = BETA_STAT * stat_buf[0, source] + scale * next_stats_ref[source]

        for copy in copies:
            copy.wait_send()
        for k in range(count):
            ring.sent(k, k != 0)
        for matrix in range(matrices):

            @pl.when(me != gram_device(matrix))
            def _(matrix=matrix):
                stat_copy(0, matrix).wait_send()
                stat_copy(1, matrix).wait_send()
                gram_copy(matrix).wait_send()


def backward(
    squares, patches, vectors, blocks, final, grad_feat, saved, stats, bases, devices
):
    images = patches.shape[0]
    depth = devices // 8
    bounds = layer_bounds(devices)
    layer_rows = blocks.shape[2]
    cuts = [lower for lower, upper in bounds][1:] + [layer_rows]
    matrices, own_rows = stats.shape[:2]
    segment_rows = -(-max(high - low for low, high in bounds) // 16) * 16
    table_size = 3 * (-(-(D // devices) // 16) * 16)
    rows = LAYERS * layer_rows + table_size
    shape = jax.ShapeDtypeStruct
    dma = pltpu.SemaphoreType.DMA
    vmem = pl.BlockSpec(memory_space=pltpu.VMEM)
    anywhere = pl.BlockSpec(memory_space=pl.ANY)

    def of_layer(*dims):
        return pl.BlockSpec(
            (1,) + dims, lambda step, image: (LAYERS - 1 - step,) + (0,) * len(dims)
        )

    def of_saved(name):
        width = saved_widths()[name][0]
        if name in PER_LAYER:
            return of_layer(images, TOKENS, width)
        return pl.BlockSpec(
            (1, 1, TOKENS, width), lambda step, image: (LAYERS - 1 - step, image, 0, 0)
        )

    all_rows = images * TOKENS
    count = LAYERS + 1
    return pl.pallas_call(
        functools.partial(backward_kernel, cuts, bounds, depth),
        grid=(LAYERS, images),
        out_shape=(
            shape((rows, D), FULL),
            shape((8, LANES), FULL),
            shape((devices, own_rows, D), FULL),
            shape((devices, own_rows, D), FULL),
        ),
        in_specs=[
            vmem,
            anywhere,
            anywhere,
            vmem,
            of_layer(*blocks.shape[1:]),
            vmem,
            vmem,
            vmem,
        ]
        + [of_saved(name) for name in SAVED],
        out_specs=(vmem,) * 4,
        scratch_shapes=[
            pltpu.VMEM((images, TOKENS, D), FULL),
            pltpu.VMEM((3 * D, D), LOW),
            pltpu.VMEM((D, D), LOW),
            pltpu.VMEM((all_rows, D), LOW),
            pltpu.VMEM((all_rows, MLP), LOW),
            pltpu.VMEM((all_rows, D), LOW),
            pltpu.VMEM((all_rows, 3 * D), LOW),
            pltpu.VMEM((D, POSITION_AT), FULL),
            pltpu.VMEM((D, D), FULL),
            pltpu.VMEM((32, D), FULL),
            pltpu.VMEM((2, devices, layer_rows, D), LOW),
            pltpu.VMEM((devices, table_size, D), LOW),
            pltpu.VMEM((4 * depth, rows, D), LOW),
            pltpu.VMEM((depth, rows, D), LOW),
            pltpu.VMEM((depth, rows, D), LOW),
            pltpu.VMEM((depth, rows, D), LOW),
            pltpu.VMEM((depth, rows, D), LOW),
            pltpu.VMEM((2, devices, own_rows, D), FULL),
            pltpu.VMEM((8, LANES), FULL),
            pltpu.VMEM((devices, 8, LANES), FULL),
            pltpu.VMEM((LAYERS, 4, segment_rows, D), LOW),
            pltpu.VMEM((devices, segment_rows, D), LOW),
            dma((count, 4)),
            dma((count, 4)),
            dma((count, 4)),
            dma((count, 4)),
            dma((count, depth)),
            dma((count, depth)),
            dma((2, matrices)),
            dma((2, devices)),
            dma((matrices,)),
            dma((devices,)),
            dma((devices - 1,)),
            dma((devices - 1,)),
        ],
        compiler_params=params(3, 63 << 20),
        name="backward",
    )(squares, stats, bases, patches, blocks, vectors, final, grad_feat, *saved)


def own_table(rows, columns):
    joint = rows.reshape(3, -1, D)[:, :columns].transpose(1, 0, 2).reshape(columns, -1)
    position = joint[:, POSITION_AT : POSITION_AT + SEQ]
    layer_rows = joint[:, VECTORS_AT : VECTORS_AT + 8 * LAYERS].reshape(columns, LAYERS, 8)
    return jnp.concatenate(
        [
            joint[:, :PIX],
            position[:, SEQ - 1 :],
            position[:, : SEQ - 1],
            layer_rows[:, :, :6].reshape(columns, -1),
            joint[:, VECTORS_AT + 8 * LAYERS : VECTORS_AT + 8 * LAYERS + 4],
        ],
        1,
    ).T


def tail_fast(
    gathered,
    layer_stats,
    layer_bases,
    owners,
    embedding,
    layers,
    layers_first,
    layers_second,
    teacher_layers,
    bases_all,
    devices,
):
    own, norm, full_stats, full_bases = gathered
    own_rows = layer_stats.shape[2]
    matrices = owners.shape[0]
    count = layers.shape[0] * layers.shape[1]
    layer_outs = soap(
        norm,
        own[:count],
        bases_all,
        layers,
        layers_first,
        layers_second,
        teacher_layers,
        layer_bounds(devices),
    )
    grad_embed = own_table(own[count:], embedding.shape[1])
    renewed = renew_own(full_stats, full_bases)
    stats_own, bases_own = deal(full_stats, renewed, matrices)
    bases_own = jnp.where(
        owners[:, None, None] >= 0, bases_own, layer_bases.reshape(matrices, own_rows, D)
    )
    return (
        norm[0, 0],
        grad_embed,
        layer_outs,
        stats_own.reshape(layer_stats.shape),
        bases_own.reshape(layer_bases.shape),
    )


def split_dot(left, basis, contract):
    high = left.astype(LOW)
    rest = (left - high.astype(FULL)).astype(LOW)
    dims = (contract, ((), ()))
    return lax.dot_general(high, basis, dims, preferred_element_type=FULL) + lax.dot_general(
        rest, basis, dims, preferred_element_type=FULL
    )


def soap_kernel(
    bounds,
    depth,
    norm_ref,
    grads_ref,
    bases_ref,
    weights_ref,
    first_ref,
    second_ref,
    teacher_ref,
    first_out_ref,
    second_out_ref,
    weights_out_ref,
    teacher_out_ref,
    basis,
):
    layer = pl.program_id(0)
    devices = bases_ref.shape[0]
    own_rows = bases_ref.shape[1] // 4
    clip = jnp.minimum(1.0, CLIP_MAX / (norm_ref[0:1, 0:1] + 1e-06))
    grads = grads_ref[...] * clip
    group = 4
    firsts, seconds, updates = [], [], []
    for segment, (low_row, high_row) in enumerate(bounds):
        for at in range(0, devices, group):
            pieces = [
                bases_ref[slot_of(at + t, depth)][segment * own_rows : (segment + 1) * own_rows]
                for t in range(group)
            ]
            basis[at * own_rows : (at + group) * own_rows] = jnp.concatenate(
                [piece.astype(FULL) for piece in pieces], 0
            ).astype(LOW)
        rotated = split_dot(grads[low_row:high_row], basis[...], ((1,), (0,)))
        first_new = BETA_ONE * first_ref[0, low_row:high_row] + (1.0 - BETA_ONE) * rotated
        second_new = (
            BETA_TWO * second_ref[0, low_row:high_row] + (1.0 - BETA_TWO) * rotated * rotated
        )
        direction = (
            first_new
            / (1.0 - BETA_ONE**STEP)
            / (jnp.sqrt(second_new / (1.0 - BETA_TWO**STEP)) + ADAM_EPSILON)
        )
        firsts.append(first_new)
        seconds.append(second_new)
        updates.append(split_dot(direction, basis[...], ((1,), (1,))))
    first_out_ref[0] = jnp.concatenate(firsts, 0)
    second_out_ref[0] = jnp.concatenate(seconds, 0)
    weight = weights_ref[0]
    fresh = weight - RATE_MATRIX * (jnp.concatenate(updates, 0) + WEIGHT_DECAY * weight)
    weights_out_ref[0] = fresh
    teacher_out_ref[0] = follow(teacher_ref[0], fresh)


def soap(norm, grads, bases_all, weights, first, second, teacher, bounds):
    devices = bases_all.shape[0]
    rows = weights.shape[1]
    own_rows = bases_all.shape[1] // LAYERS
    vmem = pl.BlockSpec(memory_space=pltpu.VMEM)
    block = pl.BlockSpec((1, rows, D), lambda layer: (layer, 0, 0))
    return pl.pallas_call(
        functools.partial(soap_kernel, bounds, devices // 8),
        grid=(LAYERS,),
        out_shape=[jax.ShapeDtypeStruct(weights.shape, FULL)] * 4,
        in_specs=[
            vmem,
            pl.BlockSpec((rows, D), lambda layer: (layer, 0)),
            pl.BlockSpec((devices, own_rows, D), lambda layer: (0, layer, 0)),
            block,
            block,
            block,
            block,
        ],
        out_specs=[block] * 4,
        scratch_shapes=[pltpu.VMEM((D, D), LOW)],
        compiler_params=pltpu.CompilerParams(vmem_limit_bytes=32 << 20),
        name="soap",
    )(norm, grads, bases_all, weights, first, second, teacher)


def per_device(
    patches,
    valid_mask,
    owners,
    embedding,
    embedding_first,
    embedding_second,
    layers,
    layers_first,
    layers_second,
    layer_stats,
    layer_bases,
    head_hidden,
    hidden_first,
    hidden_second,
    head_last,
    last_first,
    last_second,
    protos,
    protos_first,
    protos_second,
    teacher_embedding,
    teacher_layers,
    teacher_hidden,
    teacher_last,
    teacher_protos,
    centre,
):
    devices = lax.axis_size("dp")
    device_index = lax.axis_index("dp")
    fast = 2 * head_hidden.shape[0] == LANES
    if not fast:
        embed_table, teacher_table = (
            lax.all_gather(embedding.astype(LOW), "dp", axis=1, tiled=True),
            lax.all_gather(teacher_embedding.astype(LOW), "dp", axis=1, tiled=True),
        )
        layer_full, teacher_full = (
            lax.all_gather(layers.astype(LOW), "dp", axis=1, tiled=True),
            lax.all_gather(teacher_layers.astype(LOW), "dp", axis=1, tiled=True),
        )
    if not fast:
        bases_full = lax.all_gather(layer_bases.astype(LOW), "dp", axis=2, tiled=True).astype(
            layer_bases.dtype
        )
        stats_full = lax.all_gather(layer_stats.astype(LOW), "dp", axis=2, tiled=True).astype(
            layer_stats.dtype
        )
    if fast:
        feature_rows, final_rows, vectors, layer_full, last_all, part, *saved = fetch_forward(
            patches,
            embedding,
            teacher_embedding,
            layers,
            teacher_layers,
            head_last,
            teacher_last,
            head_hidden,
            devices,
        )
        features = feature_rows[0, :, 0].astype(LOW)
        teacher_features = feature_rows[1, :, 0].astype(LOW)
        last_full, teacher_last_full = last_tables(
            last_all, head_last.shape[1] * devices, devices
        )
    else:
        features, layer_inputs, final_state = backbone(patches, embed_table, layer_full, devices)
        teacher_features, unused_inputs, unused_final = backbone(
            patches, teacher_table, teacher_full, devices
        )
    if fast:
        (
            loss_sum,
            loss_count,
            squares,
            grad_hidden,
            grad_last,
            grad_protos,
            grad_features,
            next_centre,
            bases_all,
        ) = head_fast(
            features,
            teacher_features,
            valid_mask,
            head_hidden,
            protos,
            teacher_hidden,
            teacher_protos,
            centre,
            part,
            last_full,
            teacher_last_full,
            layer_bases,
            devices,
            device_index,
        )
    else:
        (
            loss_sum,
            loss_count,
            grad_hidden,
            grad_last,
            grad_protos,
            grad_features,
            next_centre,
        ) = head_slow(
            features,
            teacher_features,
            valid_mask,
            head_hidden,
            head_last,
            protos,
            teacher_hidden,
            teacher_last,
            teacher_protos,
            centre,
            device_index,
        )
    if fast:
        grad_rows = jnp.pad(grad_features[:, None], ((0, 0), (0, 7), (0, 0)))
        matrices, own_rows = owners.shape[0], layer_stats.shape[2]
        gathered = backward(
            squares,
            patches,
            vectors,
            layer_full,
            final_rows[0],
            grad_rows,
            saved,
            layer_stats.reshape(matrices, own_rows, D),
            layer_bases.reshape(matrices, own_rows, D),
            devices,
        )
    else:
        grad_table, grad_layers = backbone_back(
            patches,
            embed_table,
            layer_full,
            layer_inputs,
            final_state,
            grad_features,
            devices,
            unchanged,
        )
    bounds = layer_bounds(devices)
    if fast:
        grad_norm, grad_embed, layer_outs, stats_own, bases_own = tail_fast(
            gathered,
            layer_stats,
            layer_bases,
            owners,
            embedding,
            layers,
            layers_first,
            layers_second,
            teacher_layers,
            bases_all,
            devices,
        )
    else:
        summed = (
            lax.psum_scatter(grad_table, "dp", scatter_dimension=1, tiled=True),
            lax.psum_scatter(grad_layers, "dp", scatter_dimension=1, tiled=True),
        )
        grad_embed = summed[0]
        grad_layers_own = summed[1]
        grams = jnp.stack(
            [
                matmul_high(
                    "lcd,lce->lde",
                    grad_layers_own[:, lower_row:upper_row],
                    grad_layers_own[:, lower_row:upper_row],
                )
                for lower_row, upper_row in bounds
            ],
            1,
        )
        squares = (
            jnp.sum(grad_embed * grad_embed)
            + jnp.sum(grad_layers_own * grad_layers_own)
            + jnp.sum(grad_hidden * grad_hidden)
            + jnp.sum(grad_last * grad_last)
            + jnp.sum(grad_protos * grad_protos)
        )
        totals = lax.psum((squares, grams), "dp")
        grad_norm = jnp.sqrt(totals[0])
        clip_factor = jnp.minimum(1.0, CLIP_MAX / (grad_norm + 1e-06))
        next_stats = (
            BETA_STAT * stats_full + (1.0 - BETA_STAT) * (clip_factor * clip_factor) * totals[1]
        )
    clip_factor = jnp.minimum(1.0, CLIP_MAX / (grad_norm + 1e-06))
    rows = jnp.arange(embedding.shape[0])[:, None]
    is_matrix = rows < PIX + SEQ
    embed_out = adam_step(
        embedding,
        clip_factor * grad_embed,
        embedding_first,
        embedding_second,
        jnp.where(is_matrix, RATE_MATRIX, RATE_VECTOR),
        jnp.where(is_matrix, WEIGHT_DECAY, 0.0),
    )
    hidden_out = adam_step(
        head_hidden,
        clip_factor * grad_hidden,
        hidden_first,
        hidden_second,
        RATE_MATRIX,
        WEIGHT_DECAY,
    )
    last_out = adam_step(
        head_last, clip_factor * grad_last, last_first, last_second, RATE_MATRIX, WEIGHT_DECAY
    )
    protos_out = adam_step(
        protos, clip_factor * grad_protos, protos_first, protos_second, RATE_MATRIX, WEIGHT_DECAY
    )
    if fast:
        next_layers_first, next_layers_second, next_layers, next_teacher_layers = layer_outs
    else:
        firsts, seconds, weights_new = ([], [], [])
        for segment, (lower_row, upper_row) in enumerate(bounds):
            basis = bases_full[:, segment]
            weight_block = layers[:, lower_row:upper_row]
            rotated = matmul_high(
                "lcd,ldk->lck", clip_factor * grad_layers_own[:, lower_row:upper_row], basis
            )
            first_new = BETA_ONE * layers_first[:, lower_row:upper_row] + (1.0 - BETA_ONE) * rotated
            second_new = (
                BETA_TWO * layers_second[:, lower_row:upper_row] + (1.0 - BETA_TWO) * rotated * rotated
            )
            direction = (
                first_new
                / (1.0 - BETA_ONE**STEP)
                / (jnp.sqrt(second_new / (1.0 - BETA_TWO**STEP)) + ADAM_EPSILON)
            )
            update = matmul_high("lck,ldk->lcd", direction, basis)
            firsts.append(first_new)
            seconds.append(second_new)
            weights_new.append(weight_block - RATE_MATRIX * (update + WEIGHT_DECAY * weight_block))
        next_layers = jnp.concatenate(weights_new, 1)
        next_layers_first, next_layers_second = jnp.concatenate(firsts, 1), jnp.concatenate(seconds, 1)
        next_teacher_layers = follow(teacher_layers, next_layers)
    if not fast:
        flat_stats = next_stats.reshape(-1, D, D)
        flat_bases = bases_full.reshape(-1, D, D)

        def renew_owned(operands):
            return lax.cond(operands[2] == device_index, renew, nothing, operands[0], operands[1])

        renewed = lax.psum(lax.map(renew_owned, (flat_stats, flat_bases, owners)), "dp")
        next_bases = jnp.where(owners[:, None, None] >= 0, renewed, flat_bases).reshape(
            bases_full.shape
        )
        own_rows = layer_stats.shape[2]
        stats_own = lax.dynamic_slice_in_dim(next_stats, device_index * own_rows, own_rows, 2)
        bases_own = lax.dynamic_slice_in_dim(next_bases, device_index * own_rows, own_rows, 2)
    return (
        loss_sum,
        loss_count,
        grad_norm,
        embed_out[0],
        embed_out[1],
        embed_out[2],
        next_layers_first,
        next_layers_second,
        next_layers,
        stats_own,
        bases_own,
        hidden_out[0],
        hidden_out[1],
        hidden_out[2],
        last_out[0],
        last_out[1],
        last_out[2],
        protos_out[0],
        protos_out[1],
        protos_out[2],
        follow(teacher_embedding, embed_out[2]),
        next_teacher_layers,
        follow(teacher_hidden, hidden_out[2]),
        follow(teacher_last, last_out[2]),
        follow(teacher_protos, protos_out[2]),
        next_centre,
    )


def solution(mesh):
    placed = (
        P("dp", None, None),
        P(),
        P(),
        P(None, "dp"),
        P(None, "dp"),
        P(None, "dp"),
        P(None, "dp", None),
        P(None, "dp", None),
        P(None, "dp", None),
        P(None, None, "dp", None),
        P(None, None, "dp", None),
        P("dp", None),
        P("dp", None),
        P("dp", None),
        P(None, "dp"),
        P(None, "dp"),
        P(None, "dp"),
        P(None, "dp"),
        P(None, "dp"),
        P(None, "dp"),
        P(None, "dp"),
        P(None, "dp", None),
        P("dp", None),
        P(None, "dp"),
        P(None, "dp"),
        P("dp"),
    )
    return jax.shard_map(
        per_device,
        mesh=mesh,
        in_specs=placed,
        out_specs=(
            P(),
            P(),
            P(),
            P(None, "dp"),
            P(None, "dp"),
            P(None, "dp"),
            P(None, "dp", None),
            P(None, "dp", None),
            P(None, "dp", None),
            P(None, None, "dp", None),
            P(None, None, "dp", None),
            P("dp", None),
            P("dp", None),
            P("dp", None),
            P(None, "dp"),
            P(None, "dp"),
            P(None, "dp"),
            P(None, "dp"),
            P(None, "dp"),
            P(None, "dp"),
            P(None, "dp"),
            P(None, "dp", None),
            P("dp", None),
            P(None, "dp"),
            P(None, "dp"),
            P("dp"),
        ),
        check_vma=False,
    )
```

```python
import functools

import jax
import jax.numpy as jnp
from jax import lax
from jax.experimental import pallas as pl
from jax.experimental.pallas import tpu as pltpu
from jax.sharding import PartitionSpec as P

AXIS = "dp"
D = 384
HEADS = 6
HEAD_DIM = 64
MLP = 1536
PIX = 588
LAYERS = 3
STEP = 10
SEQ = 257


NORM_EPSILON = 1e-06
UNIT_EPSILON = 1e-06
TAU_STUDENT = 0.1
TAU_TEACHER = 0.07
CLIP_MAX = 0.001
BETA_ONE = 0.9
BETA_TWO = 0.999
ADAM_EPSILON = 1e-08
WEIGHT_DECAY = 0.04
RATE_MATRIX = 0.04
RATE_VECTOR = 0.2
BETA_STAT = 0.95
TEACHER_MOMENTUM = 0.8
CENTRE_MOMENTUM = 0.9
ROOT_HALF = 0.7071067811865476
DENSITY_SCALE = 0.3989422804014327


def joined(value, axis, join):
    pieces = jax.tree.map(lambda part: lax.all_gather(part, axis), value)
    head = jax.tree.map(lambda part: part[0], pieces)
    tail = jax.tree.map(lambda part: part[1:], pieces)
    running, _ = lax.scan(lambda running, piece: (join(running, piece), None), head, tail)
    return running


def matmul_low(form, left, right):
    return jnp.einsum(form, left, right, preferred_element_type=jnp.float32)


def matmul_high(form, left, right):
    return jnp.einsum(form, left, right, precision=lax.Precision.HIGHEST)


def layer_norm(values, gain_row, shift_row):
    centred = values - jnp.mean(values, -1, keepdims=True)
    inverse_std = lax.rsqrt(jnp.mean(centred * centred, -1, keepdims=True) + NORM_EPSILON)
    return centred * inverse_std * gain_row + shift_row


def norm_back(values, gain_row, grad_out):
    centred = values - jnp.mean(values, -1, keepdims=True)
    inverse_std = lax.rsqrt(jnp.mean(centred * centred, -1, keepdims=True) + NORM_EPSILON)
    normed = centred * inverse_std
    scaled_grad = grad_out * gain_row
    grad_in = inverse_std * (
        scaled_grad
        - jnp.mean(scaled_grad, -1, keepdims=True)
        - normed * jnp.mean(scaled_grad * normed, -1, keepdims=True)
    )
    leading = tuple(range(values.ndim - 1))
    return (grad_in, jnp.sum(grad_out * normed, leading), jnp.sum(grad_out, leading))


def gelu_exact(values):
    return 0.5 * values * (1.0 + lax.erf(values * ROOT_HALF))


def gelu_slope(values):
    return (
        0.5 * (1.0 + lax.erf(values * ROOT_HALF))
        + values * jnp.exp(-0.5 * values * values) * DENSITY_SCALE
    )


def layer_bounds(devices):
    widths = [3 * D // devices, D // devices, MLP // devices, MLP // devices]
    lowers = [0, widths[0], widths[0] + widths[1], widths[0] + widths[1] + widths[2]]
    return [(lowers[segment], lowers[segment] + widths[segment]) for segment in range(4)]


def split_layer(weights, devices):
    blocks = weights.reshape(devices, -1, D)
    return [
        blocks[:, lower_row:upper_row].reshape(-1, D)
        for lower_row, upper_row in layer_bounds(devices)
    ]


def join_layer(members, devices):
    return jnp.concatenate([member.reshape(devices, -1, D) for member in members], 1).reshape(-1, D)


def layer_parts(inputs, matrices, vectors):
    joint_weight, output_weight, inner_weight, outer_weight = matrices
    images, tokens = (inputs.shape[0], inputs.shape[1])
    normed = layer_norm(inputs, vectors[0], vectors[1]).astype(jnp.bfloat16)
    joint = matmul_low("itd,ed->ite", normed, joint_weight).astype(jnp.bfloat16)
    head_split = joint.reshape(images, tokens, 3, HEADS, HEAD_DIM)
    queries, keys_in, values_in = (head_split[:, :, 0], head_split[:, :, 1], head_split[:, :, 2])
    scores = matmul_low("ithd,ishd->ihts", queries, keys_in) * HEAD_DIM ** (-0.5)
    attention = jax.nn.softmax(scores, axis=-1)
    mixed_heads = (
        matmul_low("ihts,ishd->ithd", attention.astype(jnp.bfloat16), values_in)
        .astype(jnp.bfloat16)
        .reshape(images, tokens, D)
    )
    attended = matmul_low("itd,ed->ite", mixed_heads, output_weight)
    middle = inputs + vectors[4] * attended
    normed_two = layer_norm(middle, vectors[2], vectors[3]).astype(jnp.bfloat16)
    inner_pre = matmul_low("itd,md->itm", normed_two, inner_weight)
    activated = gelu_exact(inner_pre).astype(jnp.bfloat16)
    outer_out = matmul_low("itm,md->itd", activated, outer_weight)
    result = middle + vectors[5] * outer_out
    return (
        normed,
        queries,
        keys_in,
        values_in,
        attention,
        mixed_heads,
        attended,
        middle,
        normed_two,
        inner_pre,
        activated,
        outer_out,
        result,
    )


def layer_backward(inputs, matrices, vectors, grad_result):
    joint_weight, output_weight, inner_weight, outer_weight = matrices
    (
        normed,
        queries,
        keys_in,
        values_in,
        attention,
        mixed_heads,
        attended,
        middle,
        normed_two,
        inner_pre,
        activated,
        outer_out,
        result,
    ) = layer_parts(inputs, matrices, vectors)
    images, tokens = (inputs.shape[0], inputs.shape[1])
    grad_outer = (vectors[5] * grad_result).astype(jnp.bfloat16)
    grad_scale_two = jnp.sum(grad_result * outer_out, (0, 1))
    grad_outer_weight = matmul_low("itm,itd->md", activated, grad_outer)
    grad_activated = matmul_low("itd,md->itm", grad_outer, outer_weight)
    grad_inner = (grad_activated * gelu_slope(inner_pre)).astype(jnp.bfloat16)
    grad_inner_weight = matmul_low("itm,itd->md", grad_inner, normed_two)
    grad_normed_two = matmul_low("itm,md->itd", grad_inner, inner_weight)
    grad_middle_norm, grad_gain_two, grad_shift_two = norm_back(middle, vectors[2], grad_normed_two)
    grad_middle = grad_result + grad_middle_norm
    grad_attended = (vectors[4] * grad_middle).astype(jnp.bfloat16)
    grad_scale_one = jnp.sum(grad_middle * attended, (0, 1))
    grad_output_weight = matmul_low("ite,itd->ed", grad_attended, mixed_heads)
    grad_mixed = (
        matmul_low("ite,ed->itd", grad_attended, output_weight)
        .astype(jnp.bfloat16)
        .reshape(images, tokens, HEADS, HEAD_DIM)
    )
    grad_attention = matmul_low("ithd,ishd->ihts", grad_mixed, values_in)
    grad_values = matmul_low("ihts,ithd->ishd", attention.astype(jnp.bfloat16), grad_mixed)
    grad_scores = (
        attention * (grad_attention - jnp.sum(attention * grad_attention, -1, keepdims=True))
    ).astype(jnp.bfloat16)
    grad_queries = matmul_low("ihts,ishd->ithd", grad_scores, keys_in) * HEAD_DIM ** (-0.5)
    grad_keys = matmul_low("ihts,ithd->ishd", grad_scores, queries) * HEAD_DIM ** (-0.5)
    grad_joint = (
        jnp.stack([grad_queries, grad_keys, grad_values], 2)
        .astype(jnp.bfloat16)
        .reshape(images, tokens, 3 * D)
    )
    grad_joint_weight = matmul_low("ite,itd->ed", grad_joint, normed)
    grad_normed = matmul_low("ite,ed->itd", grad_joint, joint_weight)
    grad_input_norm, grad_gain_one, grad_shift_one = norm_back(inputs, vectors[0], grad_normed)
    grad_vectors = jnp.stack(
        [
            grad_gain_one,
            grad_shift_one,
            grad_gain_two,
            grad_shift_two,
            grad_scale_one,
            grad_scale_two,
        ]
    )
    return (
        grad_middle + grad_input_norm,
        (grad_joint_weight, grad_output_weight, grad_inner_weight, grad_outer_weight),
        grad_vectors,
    )


def table_vectors(embed_table):
    return embed_table[PIX + SEQ : PIX + SEQ + 6 * LAYERS].astype(jnp.float32).reshape(LAYERS, 6, D)


def table_tail(embed_table):
    return embed_table[PIX + SEQ + 6 * LAYERS :].astype(jnp.float32)


def backbone(patches, embed_table, layer_stack, devices):
    vectors = table_vectors(embed_table)
    tail_rows = table_tail(embed_table)
    position = embed_table[PIX : PIX + SEQ].astype(jnp.float32)
    projected = matmul_low("ipc,cd->ipd", patches, embed_table[:PIX]) + tail_rows[0]
    leading = jnp.broadcast_to(tail_rows[1] + position[0], (patches.shape[0], 1, D))
    current = jnp.concatenate([leading, projected + position[1:]], 1)
    layer_inputs = []
    for layer_number in range(LAYERS):
        layer_inputs.append(current)
        current = layer_parts(
            current, split_layer(layer_stack[layer_number], devices), vectors[layer_number]
        )[-1]
    features = layer_norm(current[:, 0], tail_rows[2], tail_rows[3]).astype(jnp.bfloat16)
    return (features, layer_inputs, current)


def unchanged(values):
    return values


def backbone_back(
    patches,
    embed_table,
    layer_stack,
    layer_inputs,
    final_state,
    grad_features,
    devices,
    reduce_layer,
):
    vectors = table_vectors(embed_table)
    tail_rows = table_tail(embed_table)
    grad_cls, grad_gain, grad_shift = norm_back(final_state[:, 0], tail_rows[2], grad_features)
    grad_current = jnp.concatenate(
        [grad_cls[:, None], jnp.zeros((final_state.shape[0], SEQ - 1, D), jnp.float32)], 1
    )
    weight_grads = [None] * LAYERS
    vector_grads = [None] * LAYERS
    for layer_number in reversed(range(LAYERS)):
        grad_current, matrices, grad_vectors = layer_backward(
            layer_inputs[layer_number],
            split_layer(layer_stack[layer_number], devices),
            vectors[layer_number],
            grad_current,
        )
        weight_grads[layer_number] = reduce_layer(join_layer(matrices, devices))
        vector_grads[layer_number] = grad_vectors
    grad_patch_weight = matmul_low("ipc,ipd->cd", patches, grad_current[:, 1:].astype(jnp.bfloat16))
    grad_position = jnp.sum(grad_current, 0)
    tail_grads = jnp.stack(
        [
            jnp.sum(grad_current[:, 1:], (0, 1)),
            jnp.sum(grad_current[:, 0], 0),
            grad_gain,
            grad_shift,
        ]
    )
    grad_table = jnp.concatenate(
        [grad_patch_weight, grad_position, jnp.concatenate(vector_grads, 0), tail_grads], 0
    )
    return (grad_table, jnp.stack(weight_grads))


def unit_rows(bottle):
    inverse_norm = lax.rsqrt(jnp.sum(bottle * bottle, -1, keepdims=True) + UNIT_EPSILON)
    return (bottle * inverse_norm, inverse_norm)


def combine_parts(left_part, right_part):
    top_student = jnp.maximum(left_part[0], right_part[0])
    total_student = left_part[1] * jnp.exp(left_part[0] - top_student) + right_part[1] * jnp.exp(
        right_part[0] - top_student
    )
    top_teacher = jnp.maximum(left_part[2], right_part[2])
    left_weight = jnp.exp(left_part[2] - top_teacher)
    right_weight = jnp.exp(right_part[2] - top_teacher)
    return (
        top_student,
        total_student,
        top_teacher,
        left_part[3] * left_weight + right_part[3] * right_weight,
        left_part[4] * left_weight + right_part[4] * right_weight,
    )


def adam_step(weight, grad, first_moment, second_moment, rate, decay):
    first_new = BETA_ONE * first_moment + (1.0 - BETA_ONE) * grad
    second_new = BETA_TWO * second_moment + (1.0 - BETA_TWO) * grad * grad
    direction = (
        first_new
        / (1.0 - BETA_ONE**STEP)
        / (jnp.sqrt(second_new / (1.0 - BETA_TWO**STEP)) + ADAM_EPSILON)
    )
    return (first_new, second_new, weight - rate * (direction + decay * weight))


def renew(stat_matrix, basis):
    scaled = jnp.dot(stat_matrix, basis, precision=lax.Precision.HIGHEST) * (
        D / jnp.trace(stat_matrix)
    )
    gram = jnp.dot(scaled.T, scaled, precision=lax.Precision.HIGHEST)
    lower_factor = jnp.linalg.cholesky(gram)
    return lax.linalg.triangular_solve(lower_factor, scaled.T, left_side=True, lower=True).T


def nothing(stat_matrix, basis):
    return jnp.zeros_like(basis)


def follow(teacher_weight, student_weight):
    return TEACHER_MOMENTUM * teacher_weight + (1.0 - TEACHER_MOMENTUM) * student_weight


MESH = pl.DeviceIdType.MESH
LANES = 128
LOW = jnp.bfloat16
FULL = jnp.float32


def params(identity, vmem=None):
    return pltpu.CompilerParams(
        collective_id=identity, has_side_effects=True, vmem_limit_bytes=vmem or (48 << 20)
    )


def push(source, target, sent, landed, device):
    copy = pltpu.make_async_remote_copy(
        src_ref=source,
        dst_ref=target,
        send_sem=sent,
        recv_sem=landed,
        device_id=(device,),
        device_id_type=MESH,
    )
    copy.start()
    return copy


def greet(peers):
    barrier = pltpu.get_barrier_semaphore()
    for peer in peers:
        pl.semaphore_signal(barrier, inc=1, device_id=(peer,), device_id_type=MESH)
    pl.semaphore_wait(barrier, len(peers))


def dot_nt(left, right):
    return lax.dot_general(left, right, (((1,), (1,)), ((), ())), preferred_element_type=FULL)


def dot_nn(left, right):
    return lax.dot_general(left, right, (((1,), (0,)), ((), ())), preferred_element_type=FULL)


def dot_tn(left, right):
    return lax.dot_general(left, right, (((0,), (0,)), ((), ())), preferred_element_type=FULL)


def slot_of(device, depth):
    return (device % 8) * depth + device // 8


class Route:
    def __init__(self, depth, items, own_sem, z_sent, z_landed, near_sent, near_landed, die_sent, die_landed):
        self.depth = depth
        self.items = items
        self.sems = (own_sem, z_sent, z_landed, near_sent, near_landed, die_sent, die_landed)
        me = lax.axis_index(AXIS)
        self.me = me
        self.total = 8 * depth
        self.core = lax.rem(me, 2)
        x_at = lax.rem(me // 2, 2)
        y_at = lax.rem(me // 4, 2)
        self.z_at = me // 8
        self.partner = me + 1 - 2 * self.core
        self.to_x = me + 2 - 4 * x_at
        self.to_y = me + 4 - 8 * y_at
        places = [(y_at, x_at), (y_at, 1 - x_at), (1 - y_at, x_at), (1 - y_at, 1 - x_at)]
        self.starts = [((y * 2 + x) * 2 + self.core) * depth for y, x in places]

    def copy(self, source, target, sent, landed, device):
        return pltpu.make_async_remote_copy(
            src_ref=source,
            dst_ref=target,
            send_sem=sent,
            recv_sem=landed,
            device_id=(device,),
            device_id_type=MESH,
        )

    def half(self, at):
        size = self.items[at][3]
        return (size // 2 + 15) // 16 * 16

    def own(self, at):
        source, target, lower, size = self.items[at]
        return pltpu.make_async_copy(
            source.at[pl.ds(lower, size)],
            target.at[self.starts[0] + self.z_at, pl.ds(lower, size)],
            self.sems[0].at[at],
        )

    def deep(self, at, step):
        source, target, lower, size = self.items[at]
        return self.copy(
            source.at[pl.ds(lower, size)],
            target.at[self.starts[0] + self.z_at, pl.ds(lower, size)],
            self.sems[1].at[at, step],
            self.sems[2].at[at, step],
            lax.rem(self.me + 8 * step, self.total),
        )

    def near(self, at, which):
        source, target, lower, size = self.items[at]
        half = self.half(at)
        column, first, length, device = [
            (0, lower, size, self.to_x),
            (0, lower, size, self.to_y),
            (1, lower, half, self.to_y),
            (2, lower + half, size - half, self.to_x),
        ][which]
        view = target.at[pl.ds(self.starts[column], self.depth), pl.ds(first, length)]
        return self.copy(view, view, self.sems[3].at[at, which], self.sems[4].at[at, which], device)

    def die(self, at, column):
        source, target, lower, size = self.items[at]
        view = target.at[pl.ds(self.starts[column], self.depth), pl.ds(lower, size)]
        return self.copy(
            view, view, self.sems[5].at[at, column], self.sems[6].at[at, column], self.partner
        )

    def act(self, stage, at):
        if stage == 0:
            self.own(at).start()
            for step in range(1, self.depth):
                self.deep(at, step).start()
        elif stage == 1:
            self.own(at).wait()
            for step in range(1, self.depth):
                self.deep(at, step).wait_recv()
            self.near(at, 0).start()
            self.near(at, 1).start()
            self.die(at, 0).start()
        elif stage == 2:
            self.near(at, 0).wait_recv()
            self.near(at, 2).start()
            self.die(at, 1).start()
            self.near(at, 1).wait_recv()
            self.near(at, 3).start()
            self.die(at, 2).start()
        elif stage == 3:
            self.near(at, 2).wait_recv()
            self.near(at, 3).wait_recv()
            self.die(at, 3).start()
        elif stage == 4:
            for column in range(4):
                self.die(at, column).wait_recv()
        else:
            for step in range(1, self.depth):
                self.deep(at, step).wait_send()
            for which in range(4):
                self.near(at, which).wait_send()
                self.die(at, which).wait_send()


def route_sems(count, depth):
    dma = pltpu.SemaphoreType.DMA
    return [
        dma((count,)),
        dma((count, depth)),
        dma((count, depth)),
        dma((count, 4)),
        dma((count, 4)),
        dma((count, 4)),
        dma((count, 4)),
    ]


def head_kernel(
    devices,
    feat_ref,
    hidden_ref,
    teacher_hidden_ref,
    part_ref,
    last_ref,
    teacher_last_ref,
    protos_ref,
    teacher_protos_ref,
    centre_ref,
    mask_ref,
    mask_row_ref,
    bases_ref,
    scalars_ref,
    grad_hidden_ref,
    grad_last_ref,
    grad_protos_ref,
    grad_feat_ref,
    centre_out_ref,
    bases_all_ref,
    fb,
    hid_low,
    thid_low,
    prot_low,
    half_out,
    half_in,
    mine_buf,
    other_buf,
    act_s,
    act_t,
    act2_s,
    act2_t,
    pre1,
    pre2,
    unit_ref,
    inv_ref,
    exp_s,
    exp_t,
    stat_out,
    stat_all,
    pz_ref,
    pz_all,
    dz_own,
    dz_all,
    dp_own,
    dp_in,
    dp_cb,
    dp_half,
    dp_full,
    df_part,
    df_all,
    df_sum,
    df_other,
    die_sent,
    die_landed,
    wide_sent,
    wide_landed,
    core_sent,
    core_landed,
    *sems,
):
    me = lax.axis_index(AXIS)
    core = lax.rem(me, 2)
    chip = me // 2
    chips = devices // 2
    partner = me + 1 - 2 * core
    everyone = [lax.rem(me + step, devices) for step in range(1, devices)]
    same_core = [lax.rem(me + 2 * step, devices) for step in range(1, chips)]
    images = mask_ref.shape[0]
    units = hidden_ref.shape[0]
    groups = images // 8
    greet(everyone)
    layer_part = bases_ref.shape[0] // LAYERS
    items = [(bases_ref, bases_all_ref, at * layer_part, layer_part) for at in range(LAYERS)]
    route = Route(devices // 8, items, *sems)

    def beside(*words):
        for word in words:
            route.act(*word)

    sends = []

    def die(step, source, target):
        copy = push(source, target, die_sent.at[step], die_landed.at[step], partner)
        sends.append(copy)
        return copy

    def wide(step, source, target):
        made = [
            push(source, target, wide_sent.at[step, at], wide_landed.at[step, at], peer)
            for at, peer in enumerate(everyone)
        ]
        sends.extend(made)
        return made

    def cores(step, source_of, target):
        made = [
            push(source_of(peer), target, core_sent.at[step, at], core_landed.at[step, at], peer)
            for at, peer in enumerate(same_core)
        ]
        sends.extend(made)
        return made

    fb[me] = feat_ref[...]
    copies = wide(0, feat_ref, fb.at[me])
    hid_low[...] = hidden_ref[...].astype(LOW)
    thid_low[...] = teacher_hidden_ref[...].astype(LOW)
    prot_low[0] = protos_ref[...].astype(LOW)
    prot_low[1] = teacher_protos_ref[...].astype(LOW)
    block_rows = feat_ref.shape[0]
    row_at = lax.broadcasted_iota(jnp.int32, (images, devices * block_rows), 0)
    col_at = lax.broadcasted_iota(jnp.int32, (images, devices * block_rows), 1)
    col_dev = lax.shift_right_logical(col_at, 5)
    col_in = jnp.bitwise_and(col_at, 31)
    lead = row_at - 3 * col_dev
    for copy in copies:
        copy.wait_recv()
    beside((0, 0))
    rows_all = fb[...].reshape(devices * block_rows, LANES)

    def features_of(model):
        pieces = []
        for j in range(3):
            hit = (col_in - (16 * model + 3 * j) == lead) & (lead >= 0) & (lead < 3)
            pieces.append(dot_nn(jnp.where(hit, 1.0, 0.0).astype(LOW), rows_all).astype(LOW))
        return jnp.concatenate(pieces, 1)

    feats = features_of(0)
    tfeats = features_of(1)

    def gather_pair(step, student, teacher, out_s, out_t):
        own_model = jnp.where(core == 0, student, teacher)
        half_out[step] = jnp.where(core == 0, teacher, student)
        copy = die(2 * step, half_out.at[step], half_in.at[step])
        copy.wait_recv()
        got = half_in[step]
        block = jnp.concatenate(
            [jnp.where(core == 0, own_model, got), jnp.where(core == 0, got, own_model)], 1
        ).astype(LOW)
        mine_buf[step, chip] = block
        made = cores(step, lambda peer: mine_buf.at[step, chip], mine_buf.at[step, chip])
        for copy in made:
            copy.wait_recv()
        copy = die(2 * step + 1, mine_buf.at[step], other_buf.at[step])
        copy.wait_recv()
        for at in range(chips):
            one, two = mine_buf[step, at], other_buf[step, at]
            out_s[:, at * LANES : (at + 1) * LANES] = jnp.where(core == 0, one, two)
            out_t[:, at * LANES : (at + 1) * LANES] = jnp.where(core == 0, two, one)

    pre_one = dot_nt(feats, hid_low[:, :D])
    pre1[...] = pre_one
    tpre_one = dot_nt(tfeats, thid_low[:, :D])
    gather_pair(0, gelu_exact(pre_one).astype(LOW).astype(FULL), gelu_exact(tpre_one).astype(LOW).astype(FULL), act_s, act_t)
    beside((1, 0), (0, 1))
    pre_two = dot_nt(act_s[...], hid_low[:, D:])
    pre2[...] = pre_two
    tpre_two = dot_nt(act_t[...], thid_low[:, D:])
    gather_pair(1, gelu_exact(pre_two).astype(LOW).astype(FULL), gelu_exact(tpre_two).astype(LOW).astype(FULL), act2_s, act2_t)

    beside((2, 0), (1, 1), (0, 2))
    unit, inverse_norm = unit_rows(dot_nt(act2_s[...], last_ref[...]))
    tunit, unused = unit_rows(dot_nt(act2_t[...], teacher_last_ref[...]))
    unit_ref[...] = unit
    inv_ref[...] = jnp.broadcast_to(inverse_norm, inv_ref.shape)
    unit_low = unit.astype(LOW)
    scaled = dot_nn(unit_low, prot_low[0]) / TAU_STUDENT
    tlogits = dot_nn(tunit.astype(LOW), prot_low[1])
    top_s = jnp.max(scaled, -1, keepdims=True)
    grown_s = jnp.exp(scaled - top_s)
    exp_s[...] = grown_s
    sharp = (tlogits - centre_ref[...]) / TAU_TEACHER
    top_t = jnp.max(sharp, -1, keepdims=True)
    grown_t = jnp.exp(sharp - top_t)
    exp_t[...] = grown_t
    lane = lax.broadcasted_iota(jnp.int32, (images, LANES), 1)
    stats = jnp.where(lane == 0, top_s, 0.0)
    stats = jnp.where(lane == 1, jnp.sum(grown_s, -1, keepdims=True), stats)
    stats = jnp.where(lane == 2, top_t, stats)
    stats = jnp.where(lane == 3, jnp.sum(grown_t, -1, keepdims=True), stats)
    stats = jnp.where(lane == 4, jnp.sum(grown_t * scaled, -1, keepdims=True), stats)
    square = jnp.concatenate([stats, jnp.zeros((LANES - images, LANES), FULL)], 0)
    stat_out[...] = square.T[:8]
    stat_all[me] = stat_out[...]
    copies = wide(1, stat_out, stat_all.at[me])
    counted = mask_ref[...]
    count = jnp.sum(counted)
    centre_out_ref[...] = (
        CENTRE_MOMENTUM * centre_ref[...]
        + (1.0 - CENTRE_MOMENTUM) * jnp.sum(counted * tlogits, 0, keepdims=True) / count
    )
    for copy in copies:
        copy.wait_recv()
    beside((3, 0), (2, 1), (1, 2))
    merged = stat_all[...]
    tops, totals = merged[:, 0], merged[:, 1]
    ttops, ttotals, crosses = merged[:, 2], merged[:, 3], merged[:, 4]
    peak_s = jnp.max(tops, 0, keepdims=True)
    sum_s = jnp.sum(totals * jnp.exp(tops - peak_s), 0, keepdims=True)
    peak_t = jnp.max(ttops, 0, keepdims=True)
    shrink = jnp.exp(ttops - peak_t)
    sum_t = jnp.sum(ttotals * shrink, 0, keepdims=True)
    cross = jnp.sum(crosses * shrink, 0, keepdims=True)
    log_total = peak_s + jnp.log(sum_s)
    mask_row = mask_row_ref[...]
    losses = jnp.where(mask_row > 0.0, log_total - cross / sum_t, 0.0)
    loss = jnp.sum(losses)
    lane8 = lax.broadcasted_iota(jnp.int32, (8, LANES), 1)
    scalars_ref[...] = jnp.where(lane8 == 0, loss, jnp.where(lane8 == 1, count, 0.0))
    back = jnp.concatenate(
        [log_total, peak_t, 1.0 / sum_t, jnp.zeros((LANES - 3, LANES), FULL)], 0
    ).T
    share_s = jnp.exp(top_s - back[:images, 0:1])
    share_t = jnp.exp(top_t - back[:images, 1:2]) * back[:images, 2:3]
    grad_logits = (
        (counted / count) * (exp_s[...] * share_s - exp_t[...] * share_t) / TAU_STUDENT
    ).astype(LOW)

    pz_ref[...] = dot_nt(grad_logits, prot_low[0]).reshape(groups, 8, unit.shape[1])
    for group in range(groups):
        owner = 2 * group

        @pl.when(me != owner)
        def _(group=group, owner=owner):
            push(pz_ref.at[group], pz_all.at[me], wide_sent.at[2, group], wide_landed.at[2, me], owner)

    grad_protos_ref[...] = dot_tn(unit_low, grad_logits)

    @pl.when((core == 0) & (chip < groups))
    def _():
        pz_all[me] = pz_ref[chip]
        for source in range(devices):

            @pl.when(source != me)
            def _(source=source):
                pltpu.make_async_copy(pz_all.at[source], pz_all.at[source], wide_landed.at[2, source]).wait()

        total = jnp.sum(pz_all[...], 0)
        rows = pl.ds(pl.multiple_of(chip * 8, 8), 8)
        own_unit = unit_ref[rows, :]
        own_inv = inv_ref[rows, :][:, 0:1]
        dz_own[...] = own_inv * (total - own_unit * jnp.sum(own_unit * total, -1, keepdims=True))
        dz_all[chip] = dz_own[...]
        for step in range(1, devices):
            push(dz_own, dz_all.at[chip], wide_sent.at[3, step - 1], wide_landed.at[3, chip], lax.rem(me + step, devices))

    for group in range(groups):

        @pl.when(me != 2 * group)
        def _(group=group):
            pltpu.make_async_copy(dz_all.at[group], dz_all.at[group], wide_landed.at[3, group]).wait()

    beside((4, 0), (3, 1), (2, 2))
    grad_bottle = dz_all[...].reshape(images, unit.shape[1]).astype(LOW)
    chip_columns = pl.ds(pl.multiple_of(chip * LANES, LANES), LANES)
    pair = dot_nn(grad_bottle, last_ref[:, chip_columns])
    grad_act_two = jnp.where(core == 0, pair[:, :units], pair[:, units:])
    grad_pre_two = (grad_act_two * gelu_slope(pre2[...])).astype(LOW)

    dp_own[...] = grad_pre_two.astype(FULL)
    copy = die(4, dp_own, dp_in)
    width = last_ref.shape[0] // devices
    pick_row = lax.broadcasted_iota(jnp.int32, (width, last_ref.shape[0]), 0)
    pick_col = lax.broadcasted_iota(jnp.int32, (width, last_ref.shape[0]), 1)
    pick = jnp.where(pick_col == pick_row + me * width, 1.0, 0.0).astype(LOW)
    own_bottle = dot_nt(pick, grad_bottle).astype(LOW)
    grad_last_ref[...] = dot_nn(own_bottle, act2_s[...])
    copy.wait_recv()
    own_dp, got_dp = dp_own[...], dp_in[...]
    dp_cb[...] = jnp.concatenate(
        [jnp.where(core == 0, own_dp, got_dp), jnp.where(core == 0, got_dp, own_dp)], 1
    ).astype(LOW)
    half = images // 2
    my_rows = pl.ds(pl.multiple_of(core * half, 16), half)
    their_rows = pl.ds(pl.multiple_of((1 - core) * half, 16), half)
    dp_half[0, chip] = dp_cb[my_rows, :]
    made = cores(2, lambda peer: dp_half.at[0, chip], dp_half.at[0, chip])
    grad_hidden_ref[:, D:] = dot_tn(grad_pre_two, act_s[...])
    for copy in made:
        copy.wait_recv()
    copy = die(5, dp_half.at[0], dp_half.at[1])
    for at in range(chips):
        dp_full[my_rows, at * LANES : (at + 1) * LANES] = dp_half[0, at]
    copy.wait_recv()
    for at in range(chips):
        dp_full[their_rows, at * LANES : (at + 1) * LANES] = dp_half[1, at]
    beside((4, 1), (3, 2))
    part = jnp.concatenate([part_ref[at % 2, at // 2] for at in range(devices)], 0)
    pair = dot_nn(dp_full[...], part)
    grad_act_one = jnp.where(core == 0, pair[:, :units], pair[:, units:])
    grad_pre_one = (grad_act_one * gelu_slope(pre1[...])).astype(LOW)

    out_row = lax.broadcasted_iota(jnp.int32, (8 * chips, images), 0)
    in_row = lax.broadcasted_iota(jnp.int32, (8 * chips, images), 1)
    out_chip = lax.shift_right_logical(out_row, 3)
    out_in = jnp.bitwise_and(out_row, 7)
    hit = (in_row - 6 * out_chip == out_in) & (out_in < 6)
    moved = dot_nn(jnp.where(hit, 1.0, 0.0).astype(LOW), grad_pre_one).astype(LOW)
    df_part[...] = dot_nn(moved, hid_low[:, :D]).reshape(chips, 8, D)
    df_all[chip] = df_part[chip]
    made = cores(3, lambda peer: df_part.at[peer // 2], df_all.at[chip])
    grad_hidden_ref[:, :D] = dot_tn(grad_pre_one, feats)
    for copy in made:
        copy.wait_recv()
    df_sum[...] = jnp.sum(df_all[...], 0)
    copy = die(6, df_sum, df_other)
    copy.wait_recv()
    whole = df_sum[...] + df_other[...]
    grad_feat_ref[...] = whole
    beside((4, 2), (5, 0), (5, 1), (5, 2))
    squares = jnp.sum(grad_hidden_ref[...] * grad_hidden_ref[...])
    squares = squares + jnp.sum(grad_last_ref[...] * grad_last_ref[...])
    squares = squares + jnp.sum(grad_protos_ref[...] * grad_protos_ref[...])
    scalars_ref[...] = jnp.where(lane8 == 2, squares, scalars_ref[...])
    for copy in sends:
        copy.wait_send()
    for group in range(groups):

        @pl.when(me != 2 * group)
        def _(group=group):
            pltpu.make_async_copy(pz_ref.at[group], pz_ref.at[group], wide_sent.at[2, group]).wait()

    @pl.when((core == 0) & (chip < groups))
    def _():
        for step in range(1, devices):
            pltpu.make_async_copy(dz_own, dz_own, wide_sent.at[3, step - 1]).wait()


def head(feat, hidden, teacher_hidden, part, last, teacher_last, protos, teacher_protos, centre, mask, mask_row, bases, devices):
    images = mask.shape[0]
    units, wide = hidden.shape
    bottle, width = protos.shape
    hid = last.shape[1]
    chips = devices // 2
    groups = images // 8
    vmem = pl.BlockSpec(memory_space=pltpu.VMEM)
    shape = jax.ShapeDtypeStruct
    dma = pltpu.SemaphoreType.DMA
    return pl.pallas_call(
        functools.partial(head_kernel, devices),
        out_shape=(
            shape((8, LANES), FULL),
            shape((units, wide), FULL),
            shape((bottle // devices, hid), FULL),
            shape((bottle, width), FULL),
            shape((8, D), FULL),
            shape((1, width), FULL),
            shape((devices,) + bases.shape, LOW),
        ),
        in_specs=[vmem] * 12,
        out_specs=(vmem,) * 6 + (pl.BlockSpec(memory_space=pl.ANY),),
        scratch_shapes=[
            pltpu.VMEM((devices,) + feat.shape, LOW),
            pltpu.VMEM((units, wide), LOW),
            pltpu.VMEM((units, wide), LOW),
            pltpu.VMEM((2, bottle, width), LOW),
            pltpu.VMEM((2, images, units), FULL),
            pltpu.VMEM((2, images, units), FULL),
            pltpu.VMEM((2, chips, images, LANES), LOW),
            pltpu.VMEM((2, chips, images, LANES), LOW),
            pltpu.VMEM((images, hid), LOW),
            pltpu.VMEM((images, hid), LOW),
            pltpu.VMEM((images, hid), LOW),
            pltpu.VMEM((images, hid), LOW),
            pltpu.VMEM((images, units), FULL),
            pltpu.VMEM((images, units), FULL),
            pltpu.VMEM((images, bottle), FULL),
            pltpu.VMEM((images, LANES), FULL),
            pltpu.VMEM((images, width), FULL),
            pltpu.VMEM((images, width), FULL),
            pltpu.VMEM((8, LANES), FULL),
            pltpu.VMEM((devices, 8, LANES), FULL),
            pltpu.VMEM((groups, 8, bottle), FULL),
            pltpu.VMEM((devices, 8, bottle), FULL),
            pltpu.VMEM((8, bottle), FULL),
            pltpu.VMEM((groups, 8, bottle), FULL),
            pltpu.VMEM((images, units), FULL),
            pltpu.VMEM((images, units), FULL),
            pltpu.VMEM((images, LANES), LOW),
            pltpu.VMEM((2, chips, images // 2, LANES), LOW),
            pltpu.VMEM((images, hid), LOW),
            pltpu.VMEM((chips, 8, D), FULL),
            pltpu.VMEM((chips, 8, D), FULL),
            pltpu.VMEM((8, D), FULL),
            pltpu.VMEM((8, D), FULL),
            dma((7,)),
            dma((7,)),
            dma((4, devices)),
            dma((4, devices)),
            dma((4, chips - 1)),
            dma((4, chips - 1)),
        ]
        + route_sems(LAYERS, devices // 8),
        compiler_params=params(2),
        name="head",
    )(feat, hidden, teacher_hidden, part, last, teacher_last, protos, teacher_protos, centre, mask, mask_row, bases)


def gram_device(matrix):
    return 2 * matrix


def dot_high(left, right, contract):
    return lax.dot_general(
        left,
        right,
        (contract, ((), ())),
        precision=lax.Precision.HIGHEST,
        preferred_element_type=FULL,
    )


def inverse_factor(block):
    size = block.shape[0]
    tiles = size // 8
    wide = 8
    sub = lax.broadcasted_iota(jnp.int32, (8, size), 0)
    lane = lax.broadcasted_iota(jnp.int32, (8, size), 1)
    rest = [block[8 * t : 8 * t + 8] for t in range(tiles)]
    made = [jnp.where(lane == sub + 8 * t, 1.0, 0.0) for t in range(tiles)]

    def full(value):
        return jnp.broadcast_to(value, (8, size))

    for k in range(0, size, wide):
        tile, row = k // 8, k % 8
        factor_rows = [full(rest[tile][row + i : row + i + 1]) for i in range(wide)]
        made_rows = [full(made[tile][row + i : row + i + 1]) for i in range(wide)]
        entry = [
            [full(rest[tile][row + i : row + i + 1, k + j : k + j + 1]) for j in range(i + 1)]
            for i in range(wide)
        ]
        columns = [
            [full(rest[t][:, k + j : k + j + 1]) for j in range(wide)] for t in range(tile, tiles)
        ]
        for j in range(wide):
            scale = lax.rsqrt(entry[j][j])
            factor_rows[j] = factor_rows[j] * scale
            made_rows[j] = made_rows[j] * scale
            for i in range(j + 1, wide):
                entry[i][j] = entry[i][j] * scale
            for some in columns:
                some[j] = some[j] * scale
            for i in range(j + 1, wide):
                factor_rows[i] = factor_rows[i] - entry[i][j] * factor_rows[j]
                made_rows[i] = made_rows[i] - entry[i][j] * made_rows[j]
                for e in range(j + 1, i + 1):
                    entry[i][e] = entry[i][e] - entry[i][j] * entry[e][j]
                for some in columns:
                    some[i] = some[i] - entry[i][j] * some[j]
        for t in range(tile, tiles):
            some = columns[t - tile]
            if t == tile:
                some = [jnp.where(sub >= row + wide, column, 0.0) for column in some]
            for j in range(wide):
                rest[t] = rest[t] - some[j] * factor_rows[j]
                made[t] = made[t] - some[j] * made_rows[j]
            if t == tile:
                for j in range(wide):
                    made[t] = jnp.where(sub == row + j, made_rows[j], made[t])
    return jnp.concatenate(made, 0)


def renew_kernel(
    devices,
    stats_ref,
    basis_ref,
    own_stats_ref,
    own_bases_ref,
    stat,
    base,
    gram,
    work,
    done,
    given,
    taken,
    passed,
    sent,
    landed,
    die_sent,
    die_landed,
):
    me = lax.axis_index(AXIS)
    core = lax.rem(me, 2)
    chip = me // 2
    chips = devices // 2
    partner = me + 1 - 2 * core
    parts, rows = stats_ref.shape[:2]
    size = parts * rows
    blocks = size // LANES
    matrices = own_stats_ref.shape[0]
    is_gram = (core == 0) & (chip < matrices)
    spare = given.shape[3] - rows
    greet([lax.rem(me + 2 * at, devices) for at in range(1, chips)] + [partner])

    def out_copy(kind, at):
        peer = lax.rem(me + 2 * at, devices)
        return pltpu.make_async_remote_copy(
            src_ref=given.at[kind, peer // 2],
            dst_ref=taken.at[kind, chip],
            send_sem=sent.at[kind, at],
            recv_sem=landed.at[kind, chip],
            device_id=(peer,),
            device_id_type=MESH,
        )

    def across(kind):
        return pltpu.make_async_remote_copy(
            src_ref=taken.at[kind, :, 1],
            dst_ref=passed.at[kind],
            send_sem=die_sent.at[kind],
            recv_sem=die_landed.at[kind],
            device_id=(partner,),
            device_id_type=MESH,
        )

    def hand_out(kind, row_of):
        blank = jnp.zeros((spare, size), FULL)
        for part in range(parts):
            given[kind, part // 2, part % 2] = jnp.concatenate([row_of(part), blank], 0).astype(LOW)
        taken[kind, chip] = given[kind, chip]
        for at in range(1, chips):
            out_copy(kind, at).start()

    @pl.when(is_gram)
    def _():
        hand_out(0, lambda part: stats_ref[part])
        for part in range(parts):
            stat[part * rows : (part + 1) * rows] = stats_ref[part]
            base[part * rows : (part + 1) * rows] = basis_ref[part]
        at_row = lax.broadcasted_iota(jnp.int32, (size, size), 0)
        at_col = lax.broadcasted_iota(jnp.int32, (size, size), 1)
        trace = jnp.sum(jnp.where(at_row == at_col, stat[...], 0.0), axis=(0, 1), keepdims=True)
        scaled = dot_high(stat[...], base[...], ((1,), (0,))) * (size / trace)
        product = dot_high(scaled, scaled, ((0,), (0,)))
        for b in range(blocks):
            work[b] = scaled[:, b * LANES : (b + 1) * LANES]
            for c in range(blocks):
                gram[b, c] = product[b * LANES : (b + 1) * LANES, c * LANES : (c + 1) * LANES]

        def step(b, carried):
            inverse = inverse_factor(gram[b, b])
            made = dot_high(work[b], inverse, ((1,), (1,)))
            done[b] = made

            def trail(c, inner):
                panel = dot_high(inverse, gram[b, c], ((1,), (0,)))
                work[c] = work[c] - dot_high(made, panel, ((1,), (0,)))

                def against(e, innermost):
                    other = dot_high(inverse, gram[b, e], ((1,), (0,)))
                    gram[c, e] = gram[c, e] - dot_high(panel, other, ((0,), (0,)))
                    return innermost

                lax.fori_loop(c, blocks, against, 0)
                return inner

            lax.fori_loop(b + 1, blocks, trail, 0)
            return carried

        lax.fori_loop(0, blocks, step, 0)
        whole = jnp.concatenate([done[b] for b in range(blocks)], 1)
        hand_out(1, lambda part: whole[part * rows : (part + 1) * rows])

    @pl.when(core == 0)
    def _():
        for kind in range(2):
            for matrix in range(matrices):

                @pl.when(chip != matrix)
                def _(kind=kind, matrix=matrix):
                    view = taken.at[kind, matrix]
                    pltpu.make_async_copy(view, view, landed.at[kind, matrix]).wait()

            across(kind).start()
        own_stats_ref[...] = taken[0, :, 0, :rows].astype(FULL)
        own_bases_ref[...] = taken[1, :, 0, :rows].astype(FULL)
        for kind in range(2):
            across(kind).wait_send()

    @pl.when(core == 1)
    def _():
        for kind in range(2):
            across(kind).wait_recv()
        own_stats_ref[...] = passed[0, :, :rows].astype(FULL)
        own_bases_ref[...] = passed[1, :, :rows].astype(FULL)

    @pl.when(is_gram)
    def _():
        for kind in range(2):
            for at in range(1, chips):
                out_copy(kind, at).wait_send()


def renew_own(stats, basis, matrices):
    devices, rows, width = stats.shape
    size = devices * rows
    blocks = size // LANES
    padded = -(-rows // 16) * 16
    vmem = pl.BlockSpec(memory_space=pltpu.VMEM)
    dma = pltpu.SemaphoreType.DMA
    return pl.pallas_call(
        functools.partial(renew_kernel, devices),
        out_shape=(jax.ShapeDtypeStruct((matrices, rows, width), FULL),) * 2,
        in_specs=[vmem] * 2,
        out_specs=(vmem,) * 2,
        scratch_shapes=[
            pltpu.VMEM((size, width), FULL),
            pltpu.VMEM((size, width), FULL),
            pltpu.VMEM((blocks, blocks, LANES, LANES), FULL),
            pltpu.VMEM((blocks, size, LANES), FULL),
            pltpu.VMEM((blocks, size, LANES), FULL),
            pltpu.VMEM((2, devices // 2, 2, padded, width), LOW),
            pltpu.VMEM((2, matrices, 2, padded, width), LOW),
            pltpu.VMEM((2, matrices, padded, width), LOW),
            dma((2, devices // 2)),
            dma((2, matrices)),
            dma((2,)),
            dma((2,)),
        ],
        compiler_params=params(4, 40 << 20),
        name="renew",
    )(stats, basis)


def head_slow(
    features,
    teacher_features,
    valid_mask,
    head_hidden,
    head_last,
    protos,
    teacher_hidden,
    teacher_last,
    teacher_protos,
    centre,
    device_index,
):
    all_features, all_teacher = (
        lax.all_gather(features, AXIS, axis=0, tiled=True),
        lax.all_gather(teacher_features, AXIS, axis=0, tiled=True),
    )
    first_weight = head_hidden[:, :D].astype(jnp.bfloat16)
    second_weight = head_hidden[:, D:].astype(jnp.bfloat16)
    last_weight = head_last.astype(jnp.bfloat16)
    proto_weight = protos.astype(jnp.bfloat16)
    teacher_first = teacher_hidden[:, :D].astype(jnp.bfloat16)
    teacher_second = teacher_hidden[:, D:].astype(jnp.bfloat16)
    pre_one = matmul_low("bd,hd->bh", all_features, first_weight)
    teacher_pre_one = matmul_low("bd,hd->bh", all_teacher, teacher_first)
    act_one = (
        lax.all_gather(gelu_exact(pre_one).astype(jnp.bfloat16), AXIS, axis=1, tiled=True),
        lax.all_gather(gelu_exact(teacher_pre_one).astype(jnp.bfloat16), AXIS, axis=1, tiled=True),
    )
    pre_two = matmul_low("bh,kh->bk", act_one[0], second_weight)
    teacher_pre_two = matmul_low("bh,kh->bk", act_one[1], teacher_second)
    act_two = (
        lax.all_gather(gelu_exact(pre_two).astype(jnp.bfloat16), AXIS, axis=1, tiled=True),
        lax.all_gather(gelu_exact(teacher_pre_two).astype(jnp.bfloat16), AXIS, axis=1, tiled=True),
    )
    bottles = (
        lax.all_gather(matmul_low("bh,hc->bc", act_two[0], last_weight), AXIS, axis=1, tiled=True),
        lax.all_gather(
            matmul_low("bh,hc->bc", act_two[1], teacher_last.astype(jnp.bfloat16)),
            AXIS,
            axis=1,
            tiled=True,
        ),
    )
    unit, inverse_norm = unit_rows(bottles[0])
    teacher_unit, unused_norm = unit_rows(bottles[1])
    unit_low = unit.astype(jnp.bfloat16)
    logits = matmul_low("bc,cp->bp", unit_low, proto_weight)
    teacher_logits = matmul_low(
        "bc,cp->bp", teacher_unit.astype(jnp.bfloat16), teacher_protos.astype(jnp.bfloat16)
    )
    scaled = logits / TAU_STUDENT
    student_top = jnp.max(scaled, -1)
    student_total = jnp.sum(jnp.exp(scaled - student_top[:, None]), -1)
    sharpened = (teacher_logits - centre) / TAU_TEACHER
    teacher_top = jnp.max(sharpened, -1)
    teacher_exp = jnp.exp(sharpened - teacher_top[:, None])
    merged = joined(
        (
            student_top,
            student_total,
            teacher_top,
            jnp.sum(teacher_exp, -1),
            jnp.sum(teacher_exp * scaled, -1),
        ),
        AXIS,
        combine_parts,
    )
    log_total = merged[0] + jnp.log(merged[1])
    counted = valid_mask.astype(jnp.float32)
    loss_count = jnp.sum(counted)
    loss_sum = jnp.sum(counted * (log_total - merged[4] / merged[3]))
    student_prob = jnp.exp(scaled - log_total[:, None])
    teacher_prob = jnp.exp(sharpened - merged[2][:, None]) / merged[3][:, None]
    grad_logits = (
        (counted / loss_count)[:, None] * (student_prob - teacher_prob) / TAU_STUDENT
    ).astype(jnp.bfloat16)
    grad_protos = matmul_low("bc,bp->cp", unit_low, grad_logits)
    grad_unit = lax.psum(matmul_low("bp,cp->bc", grad_logits, proto_weight), AXIS)
    grad_bottle = inverse_norm * (grad_unit - unit * jnp.sum(unit * grad_unit, -1, keepdims=True))
    last_width = head_last.shape[1]
    grad_bottle_own = lax.dynamic_slice_in_dim(
        grad_bottle, device_index * last_width, last_width, 1
    ).astype(jnp.bfloat16)
    grad_last = matmul_low("bh,bc->hc", act_two[0], grad_bottle_own)
    grad_act_two = lax.psum_scatter(
        matmul_low("bc,hc->bh", grad_bottle_own, last_weight), AXIS, scatter_dimension=1, tiled=True
    )
    grad_pre_two = (grad_act_two * gelu_slope(pre_two)).astype(jnp.bfloat16)
    grad_second = matmul_low("bk,bh->kh", grad_pre_two, act_one[0])
    grad_act_one = lax.psum_scatter(
        matmul_low("bk,kh->bh", grad_pre_two, second_weight), AXIS, scatter_dimension=1, tiled=True
    )
    grad_pre_one = (grad_act_one * gelu_slope(pre_one)).astype(jnp.bfloat16)
    grad_first = matmul_low("bh,bd->hd", grad_pre_one, all_features)
    grad_features = lax.psum_scatter(
        matmul_low("bh,hd->bd", grad_pre_one, first_weight), AXIS, scatter_dimension=0, tiled=True
    )
    grad_hidden = jnp.concatenate([grad_first, grad_second], 1)
    next_centre = (
        CENTRE_MOMENTUM * centre
        + (1.0 - CENTRE_MOMENTUM) * jnp.sum(counted[:, None] * teacher_logits, 0) / loss_count
    )
    return (loss_sum, loss_count, grad_hidden, grad_last, grad_protos, grad_features, next_centre)


def own_feature_rows(features, teacher_features):
    def rows(value):
        count = value.shape[0]
        turned = value.reshape(count, D // LANES, LANES).transpose(1, 0, 2).reshape(-1, LANES)
        return jnp.pad(turned, ((0, 16 - turned.shape[0]), (0, 0)))

    return jnp.concatenate([rows(features), rows(teacher_features)], 0)


def head_fast(
    features,
    teacher_features,
    valid_mask,
    head_hidden,
    protos,
    teacher_hidden,
    teacher_protos,
    centre,
    part,
    last_full,
    teacher_last_full,
    layer_bases,
    devices,
    device_index,
):
    counted = valid_mask.astype(FULL)
    mask_row = jnp.pad(counted, (0, LANES - counted.size)).reshape(1, LANES)
    scalars, grad_hidden, grad_last, grad_protos, grad_feat, next_centre, bases_all = head(
        own_feature_rows(features, teacher_features),
        head_hidden,
        teacher_hidden,
        part,
        last_full,
        teacher_last_full,
        protos,
        teacher_protos,
        centre[None],
        counted[:, None],
        mask_row,
        layer_bases.reshape(-1, D).astype(LOW),
        devices,
    )
    count = features.shape[0]
    grad_features = lax.dynamic_slice_in_dim(grad_feat, (device_index % 2) * count, count, 0)
    return (
        scalars[0, 0],
        scalars[0, 1],
        scalars,
        grad_hidden,
        grad_last.T,
        grad_protos,
        grad_features,
        next_centre[0],
        bases_all,
    )


TOKENS = 272
HALF_ROW = 256
SAVED = ("inputs", "normed", "joint", "mixed", "attended", "middle", "normed_two", "activated", "slope", "outer")


def saved_widths():
    return {
        "inputs": (D, FULL),
        "normed": (D, LOW),
        "joint": (3 * D, LOW),
        "mixed": (D, LOW),
        "attended": (D, LOW),
        "middle": (D, FULL),
        "normed_two": (D, LOW),
        "activated": (MLP, LOW),
        "slope": (MLP, LOW),
        "outer": (D, LOW),
    }


def unpack_blocks(weights, joint_out, output_out, cuts, depth):
    devices = weights.shape[0]
    joint_rows, output_rows = cuts[0], cuts[1] - cuts[0]
    group = 4
    for at in range(0, devices, group):
        blocks = [
            weights[slot_of(at + t, depth), 0 : cuts[1]].astype(FULL) for t in range(group)
        ]
        joint = jnp.concatenate([block[:joint_rows] for block in blocks], 0)
        output = jnp.concatenate([block[joint_rows:] for block in blocks], 0)
        joint_out[at * joint_rows : (at + group) * joint_rows] = joint.astype(LOW)
        output_out[at * output_rows : (at + group) * output_rows] = output.astype(LOW)


def weight_rows(weights, cuts, which, part, parts):
    per = weights.shape[0] // parts
    block = weights[part * per : (part + 1) * per, cuts[which] : cuts[which + 1]]
    return block.reshape(-1, block.shape[-1])


def chance(keys_half, queries, live):
    scores = jnp.where(live, dot_nt(keys_half, queries), -jnp.inf)
    grown = jnp.exp(scores - jnp.max(scores, 0, keepdims=True))
    return grown * (1.0 / jnp.sum(grown, 0, keepdims=True))


WIDE_TABLE = 1152
POSITION_AT = 640
VECTORS_AT = 1024


def table_rows(embedding):
    turned = embedding.T
    columns = turned.shape[0]
    patch = jnp.pad(turned[:, :PIX], ((0, 0), (0, POSITION_AT - PIX)))
    position = jnp.concatenate([turned[:, PIX + 1 : PIX + SEQ], turned[:, PIX : PIX + 1]], 1)
    position = jnp.pad(position, ((0, 0), (0, VECTORS_AT - POSITION_AT - SEQ)))
    layer_rows = turned[:, PIX + SEQ : PIX + SEQ + 6 * LAYERS].reshape(columns, LAYERS, 6)
    layer_rows = jnp.pad(layer_rows, ((0, 0), (0, 0), (0, 2))).reshape(columns, -1)
    tail_rows = turned[:, PIX + SEQ + 6 * LAYERS :]
    joint = jnp.concatenate([patch, position, layer_rows, tail_rows], 1)
    rows = -(-columns // 16) * 16
    joint = jnp.pad(joint, ((0, rows - columns), (0, WIDE_TABLE - joint.shape[1]))).astype(LOW)
    return jnp.concatenate([joint[:, at : at + D] for at in range(0, WIDE_TABLE, D)], 0)


PLAN = {
    -1: ((0, 0), (0, 1), (0, 2), (1, 0), (1, 1), (0, 3), (2, 0), (1, 2), (0, 4), (2, 1), (3, 0), (4, 0), (3, 1), (1, 3), (2, 2), (4, 1)),
    0: ((1, 4), (0, 5)),
    -2: ((2, 3), (3, 2), (4, 2)),
    1: ((2, 4), (3, 3)),
    2: ((4, 3), (3, 4), (1, 5), (0, 6)),
    3: ((4, 4),),
    4: ((2, 5),),
    5: ((3, 5), (1, 6), (0, 7)),
    6: ((4, 5),),
    7: ((2, 6),),
    8: ((3, 6), (1, 7), (0, 8)),
    9: ((4, 6),),
    10: ((2, 7),),
    11: ((3, 7), (1, 8), (0, 9)),
    12: ((4, 7),),
    13: ((2, 8),),
    14: ((3, 8), (1, 9)),
    15: ((4, 8),),
    16: ((2, 9),),
    17: ((3, 9),),
    -3: ((4, 9),),
}


def fetch_kernel(
    cuts,
    depth,
    patches_ref,
    table_ref,
    teacher_table_ref,
    layers_ref,
    teacher_layers_ref,
    last_ref,
    columns_ref,
    feat_ref,
    final_ref,
    vectors_out_ref,
    weights_out_ref,
    last_out_ref,
    part_ref,
    *rest,
):
    layer, model, image = (pl.program_id(at) for at in range(3))
    images = pl.num_programs(2)
    step = (layer * 2 + model) * images + image
    outs = dict(zip(SAVED, rest[: len(SAVED)]))
    (
        current,
        joint_weight,
        output_weight,
        weights_all,
        tables,
        turned,
        vectors_all,
        out_sem,
        part_own,
        part_sent,
        part_landed,
        part_die,
        *sems,
    ) = rest[len(SAVED) :]
    sources = (layers_ref, teacher_layers_ref)
    rows = layers_ref.shape[1]
    first = cuts[1]

    def layer_item(which, at, lower, size):
        return (sources[which].at[at], weights_all.at[which, at], lower, size)

    items = [
        (table_ref, tables.at[0], 0, table_ref.shape[0]),
        layer_item(0, 0, 0, first),
        layer_item(0, 0, first, rows - first),
        (teacher_table_ref, tables.at[1], 0, table_ref.shape[0]),
        layer_item(1, 0, 0, rows),
        layer_item(0, 1, 0, rows),
        layer_item(1, 1, 0, rows),
        layer_item(0, 2, 0, rows),
        layer_item(1, 2, 0, rows),
        (last_ref, last_out_ref, 0, last_ref.shape[0]),
    ]
    route = Route(depth, items, *sems)
    total = 8 * depth
    chips = total // 2
    chip = route.me // 2
    core = route.core

    def part_copy(at):
        peer = lax.rem(route.me + 2 * at, total)
        block = columns_ref.at[:, pl.ds(pl.multiple_of((peer // 2) * LANES, LANES), LANES)]
        return route.copy(
            block, part_ref.at[core, chip], part_sent.at[at], part_landed.at[at], peer
        )

    def part_mine():
        block = columns_ref.at[:, pl.ds(pl.multiple_of(chip * LANES, LANES), LANES)]
        return pltpu.make_async_copy(block, part_ref.at[core, chip], part_own.at[0])

    def part_across():
        return route.copy(
            part_ref.at[core], part_ref.at[core], part_die.at[0], part_die.at[1], route.partner
        )

    def out_copy(at):
        return pltpu.make_async_copy(weights_all.at[0, at], weights_out_ref.at[at], out_sem.at[at])

    def run(name):
        for word in PLAN[name]:
            route.act(*word)

    @pl.when(step == 0)
    def _():
        greet([lax.rem(route.me + 2 * at, total) for at in range(1, chips)] + [route.partner])
        run(-1)

    def set_up(which):
        columns = D // total
        block_rows = table_ref.shape[0] // (WIDE_TABLE // D)
        group = 4
        for at in range(0, total, group):
            for block in range(WIDE_TABLE // D):
                lower = block * block_rows
                pieces = [
                    tables[which, slot_of(at + t, depth), lower : lower + block_rows].astype(FULL)[
                        :columns
                    ]
                    for t in range(group)
                ]
                turned[at * columns : (at + group) * columns, block * D : (block + 1) * D] = (
                    jnp.concatenate(pieces, 0).astype(LOW)
                )
        vectors = turned[:, VECTORS_AT:WIDE_TABLE].astype(FULL).T
        vectors_all[which] = vectors[:32]
        position = turned[:, POSITION_AT:VECTORS_AT].astype(FULL).T[:TOKENS]
        row = lax.broadcasted_iota(jnp.int32, (TOKENS, D), 0)
        tail = 8 * LAYERS
        extra = jnp.where(
            row < HALF_ROW,
            vectors[tail : tail + 1],
            jnp.where(row == HALF_ROW, vectors[tail + 1 : tail + 2], 0.0),
        )
        start = position + extra
        for at in range(feat_images):
            current[which, at, :HALF_ROW] = start[:HALF_ROW] + dot_nt(
                patches_ref[at], turned[:, :PIX]
            )
            current[which, at, HALF_ROW:] = start[HALF_ROW:]

    feat_images = patches_ref.shape[0]
    for at in range(18):

        @pl.when(step == at)
        def _(at=at):
            run(at)
            if at == 0:
                set_up(0)
                vectors_out_ref[...] = vectors_all[0]
            if at == 3:
                set_up(1)
            if at == 3:
                out_copy(0).start()
            if at == 6:
                out_copy(1).start()
            if at == 11:
                part_mine().start()
                for other in range(1, chips):
                    part_copy(other).start()
            if at == 12:
                out_copy(2).start()
            if at == 16:
                part_mine().wait()
                for other in range(1, chips):
                    part_copy(other).wait_recv()
                part_across().start()

    weights = weights_all.at[model, layer]

    @pl.when(image == 0)
    def _():
        unpack_blocks(weights, joint_weight, output_weight, cuts, depth)

    vectors = vectors_all[model, pl.ds(pl.multiple_of(layer * 8, 8), 8), :]
    lane = lax.broadcasted_iota(jnp.int32, (TOKENS, LANES), 1)
    live = lax.broadcasted_iota(jnp.int32, (TOKENS, TOKENS), 0) < SEQ

    def attend(save):
        def keep(name, value):
            if save:
                outs[name][0, 0] = value

        inputs = current[model, image]
        keep("inputs", inputs)
        normed = layer_norm(inputs, vectors[0:1], vectors[1:2]).astype(LOW)
        keep("normed", normed)
        mixed = []
        for pair in range(D // LANES):
            lower = pair * LANES
            parts = [
                dot_nt(normed, joint_weight[third * D + lower : third * D + lower + LANES])
                for third in range(3)
            ]
            rounded = [part.astype(LOW) for part in parts]
            if save:
                for third in range(3):
                    outs["joint"][0, 0, :, third * D + lower : third * D + lower + LANES] = rounded[
                        third
                    ]
            queries = (rounded[0].astype(FULL) * HEAD_DIM ** (-0.5)).astype(LOW)
            values = parts[2].T.astype(LOW)
            turned_heads = []
            for half in range(2):
                keys_half = jnp.where(
                    (lane >= HEAD_DIM) == bool(half), rounded[1].astype(FULL), 0.0
                ).astype(LOW)
                share = chance(keys_half, queries, live).astype(LOW)
                turned_heads.append(dot_nn(values[half * HEAD_DIM : (half + 1) * HEAD_DIM], share))
            mixed.append(jnp.concatenate(turned_heads, 0).T.astype(LOW))
        mixed = jnp.concatenate(mixed, 1)
        keep("mixed", mixed)
        attended = dot_nt(mixed, output_weight[...])
        keep("attended", attended.astype(LOW))
        middle = inputs + vectors[4:5] * attended
        keep("middle", middle)
        current[model, image] = middle

    def perceive(save):
        def keep(name, value):
            if save:
                outs[name][0, 0] = value

        middle = current[model, image]
        normed_two = layer_norm(middle, vectors[2:3], vectors[3:4]).astype(LOW)
        keep("normed_two", normed_two)
        outer = jnp.zeros((TOKENS, D), FULL)
        parts = MLP // D
        for part in range(parts):
            inner = dot_nt(normed_two, weight_rows(weights, cuts, 1, part, parts))
            spread_half = 0.5 * (1.0 + lax.erf(inner * ROOT_HALF))
            activated = (inner * spread_half).astype(LOW)
            if save:
                outs["activated"][0, 0, :, part * D : (part + 1) * D] = activated
                slope = spread_half + inner * jnp.exp(-0.5 * inner * inner) * DENSITY_SCALE
                outs["slope"][0, 0, :, part * D : (part + 1) * D] = slope.astype(LOW)
            outer = outer + dot_nn(activated, weight_rows(weights, cuts, 2, part, parts))
        keep("outer", outer.astype(LOW))
        result = middle + vectors[5:6] * outer
        current[model, image] = result
        final = result[HALF_ROW : HALF_ROW + 8]
        final_ref[model, image] = final
        tail = 8 * LAYERS
        feat_ref[model, image] = layer_norm(
            final, vectors_all[model, tail + 2 : tail + 3], vectors_all[model, tail + 3 : tail + 4]
        )

    @pl.when(model == 0)
    def _():
        attend(True)

    @pl.when(model == 1)
    def _():
        attend(False)

    @pl.when(step == 0)
    def _():
        run(-2)

    @pl.when(model == 0)
    def _():
        perceive(True)

    @pl.when(model == 1)
    def _():
        perceive(False)

    @pl.when(step == 17)
    def _():
        run(-3)
        for at in range(len(items)):
            route.act(5, at)
        for at in range(LAYERS):
            out_copy(at).wait()
        across = part_across()
        across.wait_recv()
        across.wait_send()
        for other in range(1, chips):
            part_copy(other).wait_send()


def fetch_forward(patches, embedding, teacher_embedding, layers, teacher_layers, head_last, teacher_last, head_hidden, devices):
    images = patches.shape[0]
    depth = devices // 8
    rows = layers.shape[1]
    cuts = [lower for lower, upper in layer_bounds(devices)][1:] + [rows]
    shape = jax.ShapeDtypeStruct
    vmem = pl.BlockSpec(memory_space=pltpu.VMEM)
    anywhere = pl.BlockSpec(memory_space=pl.ANY)

    def last_rows(value):
        return value.T.astype(LOW).reshape(-1, LANES)

    table = table_rows(embedding)
    last = jnp.concatenate([last_rows(head_last), last_rows(teacher_last)], 0)
    columns = head_hidden[:, D:].astype(LOW)
    outs = [shape((2, images, 8, D), FULL)] * 2
    specs = [vmem] * 2
    outs += [
        shape((32, D), FULL),
        shape((LAYERS, devices, rows, D), LOW),
        shape((devices,) + last.shape, LOW),
        shape((2, devices // 2, columns.shape[0], LANES), LOW),
    ]
    specs += [vmem, anywhere, anywhere, anywhere]
    for name in SAVED:
        width, kind = saved_widths()[name]
        outs.append(shape((LAYERS, images, TOKENS, width), kind))
        specs.append(
            pl.BlockSpec(
                (1, 1, TOKENS, width),
                lambda layer, model, image: (layer, jnp.where(model == 0, image, images - 1), 0, 0),
            )
        )
    count = 10
    dma = pltpu.SemaphoreType.DMA
    return pl.pallas_call(
        functools.partial(fetch_kernel, cuts, depth),
        grid=(LAYERS, 2, images),
        out_shape=outs,
        in_specs=[vmem] + [anywhere] * 6,
        out_specs=specs,
        scratch_shapes=[
            pltpu.VMEM((2, images, TOKENS, D), FULL),
            pltpu.VMEM((3 * D, D), LOW),
            pltpu.VMEM((D, D), LOW),
            pltpu.VMEM((2, LAYERS, devices, rows, D), LOW),
            pltpu.VMEM((2, devices) + table.shape, LOW),
            pltpu.VMEM((D, WIDE_TABLE), LOW),
            pltpu.VMEM((2, 32, D), FULL),
            dma((LAYERS,)),
            dma((1,)),
            dma((devices // 2,)),
            dma((devices // 2,)),
            dma((2,)),
        ]
        + route_sems(count, depth),
        compiler_params=params(1, 60 << 20),
        name="fetch_forward",
    )(
        patches,
        table,
        table_rows(teacher_embedding),
        layers.astype(LOW),
        teacher_layers.astype(LOW),
        last,
        columns,
    )


def last_tables(last_all, width, devices):
    ordered = last_all.reshape(8, devices // 8, 2, -1, LANES).transpose(2, 1, 0, 3, 4)
    return ordered.reshape(2, width, -1)


class Reduce:
    def __init__(self, depth, chunks, sources, buffers, sems):
        self.depth, self.chunks, self.sources = depth, chunks, sources
        self.die_buf, self.d_buf, self.x_buf, self.y_buf, self.z_buf = buffers
        self.die_sent, self.die_landed, self.near_sent, self.near_landed, self.z_sent, self.z_landed = sems
        me = lax.axis_index(AXIS)
        self.me = me
        self.total = 8 * depth
        core = lax.rem(me, 2)
        x_at = lax.rem(me // 2, 2)
        y_at = lax.rem(me // 4, 2)
        self.z_at = me // 8
        self.partner = me + 1 - 2 * core
        self.to_x = me + 2 - 4 * x_at
        self.to_y = me + 4 - 8 * y_at
        places = [(y_at, x_at), (y_at, 1 - x_at), (1 - y_at, x_at), (1 - y_at, 1 - x_at)]
        self.starts = [((y * 2 + x) * 2 + core) * depth for y, x in places]
        self.partner_starts = [((y * 2 + x) * 2 + 1 - core) * depth for y, x in places]

    def copy(self, source, target, sent, landed, device):
        return pltpu.make_async_remote_copy(
            src_ref=source,
            dst_ref=target,
            send_sem=sent,
            recv_sem=landed,
            device_id=(device,),
            device_id_type=MESH,
        )

    def half(self, k):
        return ((self.chunks[k][1] // 2 + 15) // 16) * 16

    def die(self, k, rel):
        lower, size = self.chunks[k]
        return self.copy(
            self.sources[k].at[pl.ds(self.partner_starts[rel], self.depth)],
            self.die_buf.at[pl.ds(rel * self.depth, self.depth), pl.ds(lower, size)],
            self.die_sent.at[k, rel],
            self.die_landed.at[k, rel],
            self.partner,
        )

    def near(self, k, which):
        lower, size = self.chunks[k]
        half = self.half(k)
        rel, start, length, target, device = [
            (3, lower, half, self.d_buf, self.to_x),
            (3, lower + half, size - half, self.d_buf, self.to_y),
            (1, lower, size, self.x_buf, self.to_x),
            (2, lower, size, self.y_buf, self.to_y),
        ][which]
        return self.copy(
            self.die_buf.at[pl.ds(rel * self.depth, self.depth), pl.ds(start, length)],
            target.at[:, pl.ds(start, length)],
            self.near_sent.at[k, which],
            self.near_landed.at[k, which],
            device,
        )

    def deep(self, k, step):
        lower, size = self.chunks[k]
        return self.copy(
            self.die_buf.at[lax.rem(self.z_at + step, self.depth), pl.ds(lower, size)],
            self.z_buf.at[self.z_at, pl.ds(lower, size)],
            self.z_sent.at[k, step],
            self.z_landed.at[k, step],
            lax.rem(self.me + 8 * step, self.total),
        )

    def pair_sum(self, k, rel, z_pos, first, length):
        lower, size = self.chunks[k]
        return self.sources[k][
            self.starts[rel] + z_pos, first - lower : first - lower + length
        ].astype(FULL) + self.die_buf[rel * self.depth + z_pos, first : first + length].astype(FULL)

    def begin(self, k):
        for rel in (3, 1, 2, 0):
            self.die(k, rel).start()

    def one(self, k):
        lower, size = self.chunks[k]
        self.die(k, 3).wait_recv()
        for z_pos in range(self.depth):
            self.die_buf[3 * self.depth + z_pos, lower : lower + size] = self.pair_sum(
                k, 3, z_pos, lower, size
            ).astype(LOW)
        self.near(k, 0).start()
        self.near(k, 1).start()

    def two(self, k):
        lower, size = self.chunks[k]
        half = self.half(k)
        first, second = (lower, half), (lower + half, size - half)
        for rel, which, arrived, helped, plain in ((1, 2, 1, second, first), (2, 3, 0, first, second)):
            self.die(k, rel).wait_recv()
            self.near(k, arrived).wait_recv()
            for z_pos in range(self.depth):
                at = rel * self.depth + z_pos
                self.die_buf[at, plain[0] : plain[0] + plain[1]] = self.pair_sum(
                    k, rel, z_pos, *plain
                ).astype(LOW)
                self.die_buf[at, helped[0] : helped[0] + helped[1]] = (
                    self.pair_sum(k, rel, z_pos, *helped)
                    + self.d_buf[z_pos, helped[0] : helped[0] + helped[1]].astype(FULL)
                ).astype(LOW)
            self.near(k, which).start()

    def three(self, k):
        lower, size = self.chunks[k]
        self.die(k, 0).wait_recv()
        self.near(k, 2).wait_recv()
        self.near(k, 3).wait_recv()
        for z_pos in range(self.depth):
            self.die_buf[z_pos, lower : lower + size] = (
                self.pair_sum(k, 0, z_pos, lower, size)
                + self.x_buf[z_pos, lower : lower + size].astype(FULL)
                + self.y_buf[z_pos, lower : lower + size].astype(FULL)
            ).astype(LOW)
        for step in range(1, self.depth):
            self.deep(k, step).start()

    def four(self, k):
        lower, size = self.chunks[k]
        for step in range(1, self.depth):
            self.deep(k, step).wait_recv()
        value = self.die_buf[self.z_at, lower : lower + size].astype(FULL)
        for step in range(1, self.depth):
            value = value + self.z_buf[
                lax.rem(self.z_at + step, self.depth), lower : lower + size
            ].astype(FULL)
        return value

    def sent(self, k, die_too):
        if die_too:
            for rel in range(4):
                self.die(k, rel).wait_send()
        for which in range(4):
            self.near(k, which).wait_send()
        for step in range(1, self.depth):
            self.deep(k, step).wait_send()


PER_LAYER = ("normed", "mixed", "normed_two", "activated")


def backward_kernel(cuts, bounds, depth, *refs):
    (
        squares_ref,
        stats_ref,
        bases_ref,
        patches_ref,
        weights_ref,
        vectors_ref,
        final_ref,
        grad_feat_ref,
    ) = refs[:8]
    saved = dict(zip(SAVED, refs[8 : 8 + len(SAVED)]))
    (
        own_ref,
        norm_ref,
        next_stats_ref,
        basis_ref,
        grad_now,
        joint_weight,
        output_weight,
        grad_outer_all,
        grad_inner_all,
        grad_attended_all,
        grad_joint_all,
        grad_patch,
        grad_start,
        grad_rows,
        packets,
        table_packet,
        die_buf,
        d_buf,
        x_buf,
        y_buf,
        z_buf,
        stat_buf,
        square_out,
        square_all,
        segs,
        gram_buf,
        die_sent,
        die_landed,
        near_sent,
        near_landed,
        z_sent,
        z_landed,
        stat_sent,
        stat_landed,
        gram_sent,
        gram_landed,
        square_sent,
        square_landed,
    ) = refs[8 + len(SAVED) :]
    step, image = pl.program_id(0), pl.program_id(1)
    images = final_ref.shape[0]
    now = step * images + image
    layer_rows = cuts[3]
    chunks = [(layer * layer_rows, layer_rows) for layer in reversed(range(LAYERS))]
    chunks.append((LAYERS * layer_rows, table_packet.shape[1]))
    count = len(chunks)
    sources = [packets.at[k % 2] for k in range(LAYERS)] + [table_packet]
    ring = Reduce(
        depth,
        chunks,
        sources,
        (die_buf, d_buf, x_buf, y_buf, z_buf),
        (die_sent, die_landed, near_sent, near_landed, z_sent, z_landed),
    )
    me = ring.me
    total = ring.total
    core = lax.rem(me, 2)
    chip = me // 2
    matrices = stats_ref.shape[0]
    own_rows = stats_ref.shape[1]
    segment_rows = segs.shape[2]
    is_gram = (core == 0) & (chip < matrices)
    everyone = [lax.rem(me + at, total) for at in range(1, total)]

    def stat_copy(at, matrix):
        source = (stats_ref, bases_ref)[at]
        return ring.copy(
            source.at[matrix],
            stat_buf.at[at, me],
            stat_sent.at[at, matrix],
            stat_landed.at[at, me],
            gram_device(matrix),
        )

    def stat_own(at, matrix):
        source = (stats_ref, bases_ref)[at]
        return pltpu.make_async_copy(source.at[matrix], stat_buf.at[at, me], stat_landed.at[at, me])

    def gram_copy(matrix):
        return ring.copy(
            segs.at[matrix // 4, matrix % 4],
            gram_buf.at[me],
            gram_sent.at[matrix],
            gram_landed.at[me],
            gram_device(matrix),
        )

    def finish(k):
        lower, size = chunks[k]
        value = ring.four(k)
        own_ref[lower : lower + size] = value
        if k == count - 1:
            return
        layer = lower // layer_rows
        for segment, (low_row, high_row) in enumerate(bounds):
            piece = value[low_row:high_row].astype(LOW)
            if high_row - low_row < segment_rows:
                blank = jnp.zeros((segment_rows - (high_row - low_row), value.shape[1]), LOW)
                piece = jnp.concatenate([piece, blank], 0)
            matrix = 4 * layer + segment
            segs[layer, segment] = piece

            @pl.when(me != gram_device(matrix))
            def _(matrix=matrix):
                gram_copy(matrix).start()

    @pl.when(now == 0)
    def _():
        greet(everyone)
        for matrix in range(matrices):

            @pl.when(me != gram_device(matrix))
            def _(matrix=matrix):
                stat_copy(0, matrix).start()
                stat_copy(1, matrix).start()

            @pl.when(me == gram_device(matrix))
            def _(matrix=matrix):
                stat_own(0, matrix).start()
                stat_own(1, matrix).start()

        grad_rows[...] = jnp.zeros(grad_rows.shape, FULL)
        grad_patch[...] = jnp.zeros(grad_patch.shape, FULL)
        grad_start[...] = jnp.zeros(grad_start.shape, FULL)

    @pl.when(now == images)
    def _():
        ring.one(0)

    @pl.when(now == images + 1)
    def _():
        ring.two(0)

    @pl.when(now == 2 * images)
    def _():
        ring.one(1)
        ring.three(0)

    @pl.when(now == 2 * images + 1)
    def _():
        ring.two(1)
        finish(0)

    weights = weights_ref.at[0]
    vectors = vectors_ref[pl.ds(pl.multiple_of((LAYERS - 1 - step) * 8, 8), 8), :]
    tail = 8 * LAYERS

    @pl.when(image == 0)
    def _():
        unpack_blocks(weights, joint_weight, output_weight, cuts, depth)

    @pl.when(step == 0)
    def _():
        first = lax.broadcasted_iota(jnp.int32, (8, D), 0) == 0
        given = jnp.where(first, grad_feat_ref[image], 0.0)
        grad_class, grad_gain, grad_shift = norm_back(
            final_ref[image], vectors_ref[tail + 2 : tail + 3], given
        )
        grad_rows[tail + 2 : tail + 3] += grad_gain[None]
        grad_rows[tail + 3 : tail + 4] += grad_shift[None]
        grad_now[image] = jnp.zeros((TOKENS, D), FULL)
        grad_now[image, HALF_ROW : HALF_ROW + 8] = jnp.where(first, grad_class, 0.0)

    rows = pl.ds(pl.multiple_of(image * TOKENS, 16), TOKENS)
    grad_result = grad_now[image]
    grad_outer = (vectors[5:6] * grad_result).astype(LOW)
    grad_outer_all[rows, :] = grad_outer
    grad_scale_two = jnp.sum(grad_result * saved["outer"][0, 0].astype(FULL), 0, keepdims=True)
    parts = MLP // D
    grad_normed_two = jnp.zeros((TOKENS, D), FULL)
    for part in range(parts):
        columns = slice(part * D, (part + 1) * D)
        grad_activated = dot_nt(grad_outer, weight_rows(weights, cuts, 2, part, parts))
        grad_inner = (grad_activated * saved["slope"][0, 0, :, columns].astype(FULL)).astype(LOW)
        grad_inner_all[rows, columns] = grad_inner
        grad_normed_two = grad_normed_two + dot_nn(
            grad_inner, weight_rows(weights, cuts, 1, part, parts)
        )
    grad_middle_norm, grad_gain_two, grad_shift_two = norm_back(
        saved["middle"][0, 0], vectors[2:3], grad_normed_two
    )
    grad_middle = grad_result + grad_middle_norm
    grad_attended = (vectors[4:5] * grad_middle).astype(LOW)
    grad_attended_all[rows, :] = grad_attended
    grad_scale_one = jnp.sum(grad_middle * saved["attended"][0, 0].astype(FULL), 0, keepdims=True)
    grad_mixed = dot_nn(grad_attended, output_weight[...]).astype(LOW)
    lane = lax.broadcasted_iota(jnp.int32, (TOKENS, LANES), 1)
    live = lax.broadcasted_iota(jnp.int32, (TOKENS, TOKENS), 0) < SEQ
    for pair in range(D // LANES):
        lower = pair * LANES
        queries, keys_in, values_in = [
            saved["joint"][0, 0, :, third * D + lower : third * D + lower + LANES]
            for third in range(3)
        ]
        queries = (queries.astype(FULL) * HEAD_DIM ** (-0.5)).astype(LOW)
        keys_wide = keys_in.astype(FULL)
        values_wide = values_in.astype(FULL)
        keys_turned = keys_wide.T.astype(LOW)
        grad_head = grad_mixed[:, lower : lower + LANES]
        turned, grad_keys, grad_values = [], [], []
        for half in range(2):
            mine = (lane >= HEAD_DIM) == bool(half)
            share = chance(jnp.where(mine, keys_wide, 0.0).astype(LOW), queries, live)
            grad_share = dot_nt(jnp.where(mine, values_wide, 0.0).astype(LOW), grad_head)
            grad_values.append(dot_nn(share.astype(LOW), grad_head))
            grad_scores = (
                share * (grad_share - jnp.sum(share * grad_share, 0, keepdims=True))
            ).astype(LOW)
            grad_keys.append(dot_nn(grad_scores, queries))
            turned.append(dot_nn(keys_turned[half * HEAD_DIM : (half + 1) * HEAD_DIM], grad_scores))
        grad_queries = jnp.concatenate(turned, 0).T * HEAD_DIM ** (-0.5)
        low_half = lane < HEAD_DIM
        for third, value in enumerate(
            (
                grad_queries,
                jnp.where(low_half, grad_keys[0], grad_keys[1]),
                jnp.where(low_half, grad_values[0], grad_values[1]),
            )
        ):
            grad_joint_all[rows, third * D + lower : third * D + lower + LANES] = value.astype(LOW)
    grad_normed = dot_nn(grad_joint_all[rows, :], joint_weight[...])
    grad_input_norm, grad_gain_one, grad_shift_one = norm_back(
        saved["inputs"][0, 0], vectors[0:1], grad_normed
    )
    grad_input = grad_middle + grad_input_norm
    grad_now[image] = grad_input
    added = jnp.concatenate(
        [
            grad_gain_one[None],
            grad_shift_one[None],
            grad_gain_two[None],
            grad_shift_two[None],
            grad_scale_one,
            grad_scale_two,
            jnp.zeros((2, D), FULL),
        ],
        0,
    )
    grad_rows[pl.ds(pl.multiple_of((LAYERS - 1 - step) * 8, 8), 8), :] += added

    @pl.when(step == LAYERS - 1)
    def _():
        grad_patch[:, :PIX] += dot_tn(grad_input[:HALF_ROW].astype(LOW), patches_ref[image])
        grad_start[:TOKENS] += grad_input
        grad_rows[tail : tail + 1] += jnp.sum(grad_input[:HALF_ROW], 0, keepdims=True)
        grad_rows[tail + 1 : tail + 2] += grad_input[HALF_ROW : HALF_ROW + 1]

    def pack(packet):
        def flat(name):
            value = saved[name][0]
            return value.reshape(-1, value.shape[-1])

        per = cuts[0], cuts[1] - cuts[0], cuts[2] - cuts[1], cuts[3] - cuts[2]
        groups = 4
        each = total // groups
        for at in range(groups):
            first = at * each
            joint_rows = dot_tn(
                grad_joint_all[:, first * per[0] : (first + each) * per[0]], flat("normed")
            )
            output_rows = dot_tn(
                grad_attended_all[:, first * per[1] : (first + each) * per[1]], flat("mixed")
            )
            inner_rows = dot_tn(
                grad_inner_all[:, first * per[2] : (first + each) * per[2]], flat("normed_two")
            ).astype(LOW)
            outer_rows = dot_tn(
                saved["activated"][0, :, :, first * per[3] : (first + each) * per[3]].reshape(
                    -1, each * per[3]
                ),
                grad_outer_all[...],
            ).astype(LOW)
            for t in range(each):
                joined_rows = jnp.concatenate(
                    [
                        joint_rows[t * per[0] : (t + 1) * per[0]],
                        output_rows[t * per[1] : (t + 1) * per[1]],
                    ],
                    0,
                )
                packet[slot_of(first + t, depth), : cuts[1]] = joined_rows.astype(LOW)
                packet[first + t, cuts[1] : cuts[2]] = inner_rows[t * per[2] : (t + 1) * per[2]]
                packet[first + t, cuts[2] : cuts[3]] = outer_rows[t * per[3] : (t + 1) * per[3]]

    @pl.when((image == images - 1) & (step == LAYERS - 1))
    def _():
        ring.three(1)
        for rel in range(4):
            ring.die(0, rel).wait_send()

    @pl.when(image == images - 1)
    def _():
        pack(packets.at[lax.rem(step, 2)])

    for k in range(LAYERS - 1):

        @pl.when((image == images - 1) & (step == k))
        def _(k=k):
            ring.begin(k)

    @pl.when((image == images - 1) & (step == LAYERS - 1))
    def _():
        last, table = LAYERS - 1, LAYERS
        ring.begin(last)
        ring.one(last)
        blank = jnp.zeros((LANES - 32, D), FULL)
        turned_rows = jnp.concatenate([grad_rows[...], blank], 0).T
        turned = [grad_patch[:, :D], None, None]
        turned_start = grad_start[...].T
        left = VECTORS_AT - POSITION_AT
        turned[1] = jnp.concatenate([grad_patch[:, D:], turned_start[:, : 2 * D - POSITION_AT]], 1)
        turned[2] = jnp.concatenate([turned_start[:, 2 * D - POSITION_AT : left], turned_rows], 1)
        columns = D // total
        for block in range(3):
            for device in range(total):
                piece = turned[block][device * columns : (device + 1) * columns]
                piece = jnp.concatenate([piece, jnp.zeros((16 - columns, D), FULL)], 0)
                table_packet[slot_of(device, depth), 16 * block : 16 * block + 16] = piece.astype(LOW)
        ring.begin(table)
        ring.one(table)
        ring.two(last)
        finish(1)
        ring.two(table)
        ring.three(last)
        ring.three(table)
        finish(last)
        finish(table)

        own = own_ref[...]
        lane8 = lax.broadcasted_iota(jnp.int32, (8, LANES), 1)
        squares = jnp.sum(own * own) + jnp.sum(jnp.where(lane8 == 2, squares_ref[...], 0.0)) / 8.0
        square_out[...] = jnp.full((8, LANES), squares)
        square_all[me] = square_out[...]
        copies = [
            push(square_out, square_all.at[me], square_sent.at[at], square_landed.at[at], peer)
            for at, peer in enumerate(everyone)
        ]

        @pl.when(is_gram)
        def _():
            for matrix in range(matrices):

                @pl.when(matrix == chip)
                def _(matrix=matrix):
                    gram_buf[me] = segs[matrix // 4, matrix % 4]

            for source in range(total):
                for at in range(2):
                    view = stat_buf.at[at, source]
                    pltpu.make_async_copy(view, view, stat_landed.at[at, source]).wait()

                @pl.when(source != me)
                def _(source=source):
                    pltpu.make_async_copy(
                        gram_buf.at[source], gram_buf.at[source], gram_landed.at[source]
                    ).wait()

            basis_ref[...] = stat_buf[1]
            blocks = gram_buf[...].reshape(total * segment_rows, gram_buf.shape[2])
            gram = dot_tn(blocks, blocks)
            for source in range(total):
                next_stats_ref[source] = gram[source * own_rows : (source + 1) * own_rows]

        @pl.when(jnp.logical_not(is_gram))
        def _():
            next_stats_ref[...] = jnp.zeros(next_stats_ref.shape, FULL)
            basis_ref[...] = jnp.zeros(basis_ref.shape, FULL)
            stat_buf[0] = jnp.zeros(stat_buf.shape[1:], FULL)

        for copy in copies:
            copy.wait_recv()
        norm = jnp.sqrt(jnp.sum(square_all[...], 0))
        norm_ref[...] = norm
        clip = jnp.minimum(1.0, CLIP_MAX / (norm + 1e-06))[:1, :1]
        scale = (1.0 - BETA_STAT) * (clip * clip)
        for source in range(total):
            next_stats_ref[source] = BETA_STAT * stat_buf[0, source] + scale * next_stats_ref[source]

        for copy in copies:
            copy.wait_send()
        for k in range(count):
            ring.sent(k, k != 0)
        for matrix in range(matrices):

            @pl.when(me != gram_device(matrix))
            def _(matrix=matrix):
                stat_copy(0, matrix).wait_send()
                stat_copy(1, matrix).wait_send()
                gram_copy(matrix).wait_send()


def backward(
    squares, patches, vectors, blocks, final, grad_feat, saved, stats, bases, devices
):
    images = patches.shape[0]
    depth = devices // 8
    bounds = layer_bounds(devices)
    layer_rows = blocks.shape[2]
    cuts = [lower for lower, upper in bounds][1:] + [layer_rows]
    matrices, own_rows = stats.shape[:2]
    segment_rows = -(-max(high - low for low, high in bounds) // 16) * 16
    table_size = 3 * (-(-(D // devices) // 16) * 16)
    rows = LAYERS * layer_rows + table_size
    shape = jax.ShapeDtypeStruct
    dma = pltpu.SemaphoreType.DMA
    vmem = pl.BlockSpec(memory_space=pltpu.VMEM)
    anywhere = pl.BlockSpec(memory_space=pl.ANY)

    def of_layer(*dims):
        return pl.BlockSpec(
            (1,) + dims, lambda step, image: (LAYERS - 1 - step,) + (0,) * len(dims)
        )

    def of_saved(name):
        width = saved_widths()[name][0]
        if name in PER_LAYER:
            return of_layer(images, TOKENS, width)
        return pl.BlockSpec(
            (1, 1, TOKENS, width), lambda step, image: (LAYERS - 1 - step, image, 0, 0)
        )

    all_rows = images * TOKENS
    count = LAYERS + 1
    return pl.pallas_call(
        functools.partial(backward_kernel, cuts, bounds, depth),
        grid=(LAYERS, images),
        out_shape=(
            shape((rows, D), FULL),
            shape((8, LANES), FULL),
            shape((devices, own_rows, D), FULL),
            shape((devices, own_rows, D), FULL),
        ),
        in_specs=[
            vmem,
            anywhere,
            anywhere,
            vmem,
            of_layer(*blocks.shape[1:]),
            vmem,
            vmem,
            vmem,
        ]
        + [of_saved(name) for name in SAVED],
        out_specs=(vmem,) * 4,
        scratch_shapes=[
            pltpu.VMEM((images, TOKENS, D), FULL),
            pltpu.VMEM((3 * D, D), LOW),
            pltpu.VMEM((D, D), LOW),
            pltpu.VMEM((all_rows, D), LOW),
            pltpu.VMEM((all_rows, MLP), LOW),
            pltpu.VMEM((all_rows, D), LOW),
            pltpu.VMEM((all_rows, 3 * D), LOW),
            pltpu.VMEM((D, POSITION_AT), FULL),
            pltpu.VMEM((D, D), FULL),
            pltpu.VMEM((32, D), FULL),
            pltpu.VMEM((2, devices, layer_rows, D), LOW),
            pltpu.VMEM((devices, table_size, D), LOW),
            pltpu.VMEM((4 * depth, rows, D), LOW),
            pltpu.VMEM((depth, rows, D), LOW),
            pltpu.VMEM((depth, rows, D), LOW),
            pltpu.VMEM((depth, rows, D), LOW),
            pltpu.VMEM((depth, rows, D), LOW),
            pltpu.VMEM((2, devices, own_rows, D), FULL),
            pltpu.VMEM((8, LANES), FULL),
            pltpu.VMEM((devices, 8, LANES), FULL),
            pltpu.VMEM((LAYERS, 4, segment_rows, D), LOW),
            pltpu.VMEM((devices, segment_rows, D), LOW),
            dma((count, 4)),
            dma((count, 4)),
            dma((count, 4)),
            dma((count, 4)),
            dma((count, depth)),
            dma((count, depth)),
            dma((2, matrices)),
            dma((2, devices)),
            dma((matrices,)),
            dma((devices,)),
            dma((devices - 1,)),
            dma((devices - 1,)),
        ],
        compiler_params=params(3, 63 << 20),
        name="backward",
    )(squares, stats, bases, patches, blocks, vectors, final, grad_feat, *saved)


def own_table(rows, columns):
    joint = rows.reshape(3, -1, D)[:, :columns].transpose(1, 0, 2).reshape(columns, -1)
    position = joint[:, POSITION_AT : POSITION_AT + SEQ]
    layer_rows = joint[:, VECTORS_AT : VECTORS_AT + 8 * LAYERS].reshape(columns, LAYERS, 8)
    return jnp.concatenate(
        [
            joint[:, :PIX],
            position[:, SEQ - 1 :],
            position[:, : SEQ - 1],
            layer_rows[:, :, :6].reshape(columns, -1),
            joint[:, VECTORS_AT + 8 * LAYERS : VECTORS_AT + 8 * LAYERS + 4],
        ],
        1,
    ).T


def tail_fast(
    gathered,
    layer_stats,
    layer_bases,
    owners,
    embedding,
    layers,
    layers_first,
    layers_second,
    teacher_layers,
    bases_all,
    devices,
):
    own, norm, full_stats, full_bases = gathered
    own_rows = layer_stats.shape[2]
    matrices = owners.shape[0]
    count = layers.shape[0] * layers.shape[1]
    layer_outs = soap(
        norm,
        own[:count],
        bases_all,
        layers,
        layers_first,
        layers_second,
        teacher_layers,
        layer_bounds(devices),
    )
    grad_embed = own_table(own[count:], embedding.shape[1])
    stats_own, bases_own = renew_own(full_stats, full_bases, matrices)
    bases_own = jnp.where(
        owners[:, None, None] >= 0, bases_own, layer_bases.reshape(matrices, own_rows, D)
    )
    return (
        norm[0, 0],
        grad_embed,
        layer_outs,
        stats_own.reshape(layer_stats.shape),
        bases_own.reshape(layer_bases.shape),
    )


def split_dot(left, basis, contract):
    high = left.astype(LOW)
    rest = (left - high.astype(FULL)).astype(LOW)
    dims = (contract, ((), ()))
    return lax.dot_general(high, basis, dims, preferred_element_type=FULL) + lax.dot_general(
        rest, basis, dims, preferred_element_type=FULL
    )


def soap_kernel(
    bounds,
    depth,
    norm_ref,
    grads_ref,
    bases_ref,
    weights_ref,
    first_ref,
    second_ref,
    teacher_ref,
    first_out_ref,
    second_out_ref,
    weights_out_ref,
    teacher_out_ref,
    basis,
):
    layer = pl.program_id(0)
    devices = bases_ref.shape[0]
    own_rows = bases_ref.shape[1] // 4
    clip = jnp.minimum(1.0, CLIP_MAX / (norm_ref[0:1, 0:1] + 1e-06))
    grads = grads_ref[...] * clip
    group = 4
    firsts, seconds, updates = [], [], []
    for segment, (low_row, high_row) in enumerate(bounds):
        for at in range(0, devices, group):
            pieces = [
                bases_ref[slot_of(at + t, depth)][segment * own_rows : (segment + 1) * own_rows]
                for t in range(group)
            ]
            basis[at * own_rows : (at + group) * own_rows] = jnp.concatenate(
                [piece.astype(FULL) for piece in pieces], 0
            ).astype(LOW)
        rotated = split_dot(grads[low_row:high_row], basis[...], ((1,), (0,)))
        first_new = BETA_ONE * first_ref[0, low_row:high_row] + (1.0 - BETA_ONE) * rotated
        second_new = (
            BETA_TWO * second_ref[0, low_row:high_row] + (1.0 - BETA_TWO) * rotated * rotated
        )
        direction = (
            first_new
            / (1.0 - BETA_ONE**STEP)
            / (jnp.sqrt(second_new / (1.0 - BETA_TWO**STEP)) + ADAM_EPSILON)
        )
        firsts.append(first_new)
        seconds.append(second_new)
        updates.append(split_dot(direction, basis[...], ((1,), (1,))))
    first_out_ref[0] = jnp.concatenate(firsts, 0)
    second_out_ref[0] = jnp.concatenate(seconds, 0)
    weight = weights_ref[0]
    fresh = weight - RATE_MATRIX * (jnp.concatenate(updates, 0) + WEIGHT_DECAY * weight)
    weights_out_ref[0] = fresh
    teacher_out_ref[0] = follow(teacher_ref[0], fresh)


def soap(norm, grads, bases_all, weights, first, second, teacher, bounds):
    devices = bases_all.shape[0]
    rows = weights.shape[1]
    own_rows = bases_all.shape[1] // LAYERS
    vmem = pl.BlockSpec(memory_space=pltpu.VMEM)
    block = pl.BlockSpec((1, rows, D), lambda layer: (layer, 0, 0))
    return pl.pallas_call(
        functools.partial(soap_kernel, bounds, devices // 8),
        grid=(LAYERS,),
        out_shape=[jax.ShapeDtypeStruct(weights.shape, FULL)] * 4,
        in_specs=[
            vmem,
            pl.BlockSpec((rows, D), lambda layer: (layer, 0)),
            pl.BlockSpec((devices, own_rows, D), lambda layer: (0, layer, 0)),
            block,
            block,
            block,
            block,
        ],
        out_specs=[block] * 4,
        scratch_shapes=[pltpu.VMEM((D, D), LOW)],
        compiler_params=pltpu.CompilerParams(vmem_limit_bytes=32 << 20),
        name="soap",
    )(norm, grads, bases_all, weights, first, second, teacher)


def per_device(
    patches,
    valid_mask,
    owners,
    embedding,
    embedding_first,
    embedding_second,
    layers,
    layers_first,
    layers_second,
    layer_stats,
    layer_bases,
    head_hidden,
    hidden_first,
    hidden_second,
    head_last,
    last_first,
    last_second,
    protos,
    protos_first,
    protos_second,
    teacher_embedding,
    teacher_layers,
    teacher_hidden,
    teacher_last,
    teacher_protos,
    centre,
):
    devices = lax.axis_size(AXIS)
    device_index = lax.axis_index(AXIS)
    fast = 2 * head_hidden.shape[0] == LANES
    if not fast:
        embed_table, teacher_table = (
            lax.all_gather(embedding.astype(LOW), AXIS, axis=1, tiled=True),
            lax.all_gather(teacher_embedding.astype(LOW), AXIS, axis=1, tiled=True),
        )
        layer_full, teacher_full = (
            lax.all_gather(layers.astype(LOW), AXIS, axis=1, tiled=True),
            lax.all_gather(teacher_layers.astype(LOW), AXIS, axis=1, tiled=True),
        )
    if not fast:
        bases_full = lax.all_gather(layer_bases.astype(LOW), AXIS, axis=2, tiled=True).astype(
            layer_bases.dtype
        )
        stats_full = lax.all_gather(layer_stats.astype(LOW), AXIS, axis=2, tiled=True).astype(
            layer_stats.dtype
        )
    if fast:
        feature_rows, final_rows, vectors, layer_full, last_all, part, *saved = fetch_forward(
            patches,
            embedding,
            teacher_embedding,
            layers,
            teacher_layers,
            head_last,
            teacher_last,
            head_hidden,
            devices,
        )
        features = feature_rows[0, :, 0].astype(LOW)
        teacher_features = feature_rows[1, :, 0].astype(LOW)
        last_full, teacher_last_full = last_tables(
            last_all, head_last.shape[1] * devices, devices
        )
    else:
        features, layer_inputs, final_state = backbone(patches, embed_table, layer_full, devices)
        teacher_features, unused_inputs, unused_final = backbone(
            patches, teacher_table, teacher_full, devices
        )
    if fast:
        (
            loss_sum,
            loss_count,
            squares,
            grad_hidden,
            grad_last,
            grad_protos,
            grad_features,
            next_centre,
            bases_all,
        ) = head_fast(
            features,
            teacher_features,
            valid_mask,
            head_hidden,
            protos,
            teacher_hidden,
            teacher_protos,
            centre,
            part,
            last_full,
            teacher_last_full,
            layer_bases,
            devices,
            device_index,
        )
    else:
        (
            loss_sum,
            loss_count,
            grad_hidden,
            grad_last,
            grad_protos,
            grad_features,
            next_centre,
        ) = head_slow(
            features,
            teacher_features,
            valid_mask,
            head_hidden,
            head_last,
            protos,
            teacher_hidden,
            teacher_last,
            teacher_protos,
            centre,
            device_index,
        )
    if fast:
        grad_rows = jnp.pad(grad_features[:, None], ((0, 0), (0, 7), (0, 0)))
        matrices, own_rows = owners.shape[0], layer_stats.shape[2]
        gathered = backward(
            squares,
            patches,
            vectors,
            layer_full,
            final_rows[0],
            grad_rows,
            saved,
            layer_stats.reshape(matrices, own_rows, D),
            layer_bases.reshape(matrices, own_rows, D),
            devices,
        )
    else:
        grad_table, grad_layers = backbone_back(
            patches,
            embed_table,
            layer_full,
            layer_inputs,
            final_state,
            grad_features,
            devices,
            unchanged,
        )
    bounds = layer_bounds(devices)
    if fast:
        grad_norm, grad_embed, layer_outs, stats_own, bases_own = tail_fast(
            gathered,
            layer_stats,
            layer_bases,
            owners,
            embedding,
            layers,
            layers_first,
            layers_second,
            teacher_layers,
            bases_all,
            devices,
        )
    else:
        summed = (
            lax.psum_scatter(grad_table, AXIS, scatter_dimension=1, tiled=True),
            lax.psum_scatter(grad_layers, AXIS, scatter_dimension=1, tiled=True),
        )
        grad_embed = summed[0]
        grad_layers_own = summed[1]
        grams = jnp.stack(
            [
                matmul_high(
                    "lcd,lce->lde",
                    grad_layers_own[:, lower_row:upper_row],
                    grad_layers_own[:, lower_row:upper_row],
                )
                for lower_row, upper_row in bounds
            ],
            1,
        )
        squares = (
            jnp.sum(grad_embed * grad_embed)
            + jnp.sum(grad_layers_own * grad_layers_own)
            + jnp.sum(grad_hidden * grad_hidden)
            + jnp.sum(grad_last * grad_last)
            + jnp.sum(grad_protos * grad_protos)
        )
        totals = lax.psum((squares, grams), AXIS)
        grad_norm = jnp.sqrt(totals[0])
        clip_factor = jnp.minimum(1.0, CLIP_MAX / (grad_norm + 1e-06))
        next_stats = (
            BETA_STAT * stats_full + (1.0 - BETA_STAT) * (clip_factor * clip_factor) * totals[1]
        )
    clip_factor = jnp.minimum(1.0, CLIP_MAX / (grad_norm + 1e-06))
    rows = jnp.arange(embedding.shape[0])[:, None]
    is_matrix = rows < PIX + SEQ
    embed_out = adam_step(
        embedding,
        clip_factor * grad_embed,
        embedding_first,
        embedding_second,
        jnp.where(is_matrix, RATE_MATRIX, RATE_VECTOR),
        jnp.where(is_matrix, WEIGHT_DECAY, 0.0),
    )
    hidden_out = adam_step(
        head_hidden,
        clip_factor * grad_hidden,
        hidden_first,
        hidden_second,
        RATE_MATRIX,
        WEIGHT_DECAY,
    )
    last_out = adam_step(
        head_last, clip_factor * grad_last, last_first, last_second, RATE_MATRIX, WEIGHT_DECAY
    )
    protos_out = adam_step(
        protos, clip_factor * grad_protos, protos_first, protos_second, RATE_MATRIX, WEIGHT_DECAY
    )
    if fast:
        next_layers_first, next_layers_second, next_layers, next_teacher_layers = layer_outs
    else:
        firsts, seconds, weights_new = ([], [], [])
        for segment, (lower_row, upper_row) in enumerate(bounds):
            basis = bases_full[:, segment]
            weight_block = layers[:, lower_row:upper_row]
            rotated = matmul_high(
                "lcd,ldk->lck", clip_factor * grad_layers_own[:, lower_row:upper_row], basis
            )
            first_new = BETA_ONE * layers_first[:, lower_row:upper_row] + (1.0 - BETA_ONE) * rotated
            second_new = (
                BETA_TWO * layers_second[:, lower_row:upper_row] + (1.0 - BETA_TWO) * rotated * rotated
            )
            direction = (
                first_new
                / (1.0 - BETA_ONE**STEP)
                / (jnp.sqrt(second_new / (1.0 - BETA_TWO**STEP)) + ADAM_EPSILON)
            )
            update = matmul_high("lck,ldk->lcd", direction, basis)
            firsts.append(first_new)
            seconds.append(second_new)
            weights_new.append(weight_block - RATE_MATRIX * (update + WEIGHT_DECAY * weight_block))
        next_layers = jnp.concatenate(weights_new, 1)
        next_layers_first, next_layers_second = jnp.concatenate(firsts, 1), jnp.concatenate(seconds, 1)
        next_teacher_layers = follow(teacher_layers, next_layers)
    if not fast:
        flat_stats = next_stats.reshape(-1, D, D)
        flat_bases = bases_full.reshape(-1, D, D)

        def renew_owned(operands):
            return lax.cond(operands[2] == device_index, renew, nothing, operands[0], operands[1])

        renewed = lax.psum(lax.map(renew_owned, (flat_stats, flat_bases, owners)), AXIS)
        next_bases = jnp.where(owners[:, None, None] >= 0, renewed, flat_bases).reshape(
            bases_full.shape
        )
        own_rows = layer_stats.shape[2]
        stats_own = lax.dynamic_slice_in_dim(next_stats, device_index * own_rows, own_rows, 2)
        bases_own = lax.dynamic_slice_in_dim(next_bases, device_index * own_rows, own_rows, 2)
    return (
        loss_sum,
        loss_count,
        grad_norm,
        embed_out[0],
        embed_out[1],
        embed_out[2],
        next_layers_first,
        next_layers_second,
        next_layers,
        stats_own,
        bases_own,
        hidden_out[0],
        hidden_out[1],
        hidden_out[2],
        last_out[0],
        last_out[1],
        last_out[2],
        protos_out[0],
        protos_out[1],
        protos_out[2],
        follow(teacher_embedding, embed_out[2]),
        next_teacher_layers,
        follow(teacher_hidden, hidden_out[2]),
        follow(teacher_last, last_out[2]),
        follow(teacher_protos, protos_out[2]),
        next_centre,
    )


def solution(mesh):
    placed = (
        P(AXIS, None, None),
        P(),
        P(),
        P(None, AXIS),
        P(None, AXIS),
        P(None, AXIS),
        P(None, AXIS, None),
        P(None, AXIS, None),
        P(None, AXIS, None),
        P(None, None, AXIS, None),
        P(None, None, AXIS, None),
        P(AXIS, None),
        P(AXIS, None),
        P(AXIS, None),
        P(None, AXIS),
        P(None, AXIS),
        P(None, AXIS),
        P(None, AXIS),
        P(None, AXIS),
        P(None, AXIS),
        P(None, AXIS),
        P(None, AXIS, None),
        P(AXIS, None),
        P(None, AXIS),
        P(None, AXIS),
        P(AXIS),
    )
    return jax.shard_map(
        per_device,
        mesh=mesh,
        in_specs=placed,
        out_specs=(
            P(),
            P(),
            P(),
            P(None, AXIS),
            P(None, AXIS),
            P(None, AXIS),
            P(None, AXIS, None),
            P(None, AXIS, None),
            P(None, AXIS, None),
            P(None, None, AXIS, None),
            P(None, None, AXIS, None),
            P(AXIS, None),
            P(AXIS, None),
            P(AXIS, None),
            P(None, AXIS),
            P(None, AXIS),
            P(None, AXIS),
            P(None, AXIS),
            P(None, AXIS),
            P(None, AXIS),
            P(None, AXIS),
            P(None, AXIS, None),
            P(AXIS, None),
            P(None, AXIS),
            P(None, AXIS),
            P(AXIS),
        ),
        check_vma=False,
    )
```

```python
import functools

import jax
import jax.numpy as jnp
from jax import lax
from jax.experimental import pallas as pl
from jax.experimental.pallas import tpu as pltpu
from jax.sharding import PartitionSpec as P

AXIS = "dp"
D = 384
HEADS = 6
HEAD_DIM = 64
MLP = 1536
PIX = 588
LAYERS = 3
STEP = 10
SEQ = 257


NORM_EPSILON = 1e-06
UNIT_EPSILON = 1e-06
TAU_STUDENT = 0.1
TAU_TEACHER = 0.07
CLIP_MAX = 0.001
BETA_ONE = 0.9
BETA_TWO = 0.999
ADAM_EPSILON = 1e-08
WEIGHT_DECAY = 0.04
RATE_MATRIX = 0.04
RATE_VECTOR = 0.2
BETA_STAT = 0.95
TEACHER_MOMENTUM = 0.8
CENTRE_MOMENTUM = 0.9
ROOT_HALF = 0.7071067811865476
DENSITY_SCALE = 0.3989422804014327


def joined(value, axis, join):
    pieces = jax.tree.map(lambda part: lax.all_gather(part, axis), value)
    head = jax.tree.map(lambda part: part[0], pieces)
    tail = jax.tree.map(lambda part: part[1:], pieces)
    running, _ = lax.scan(lambda running, piece: (join(running, piece), None), head, tail)
    return running


def matmul_low(form, left, right):
    return jnp.einsum(form, left, right, preferred_element_type=jnp.float32)


def matmul_high(form, left, right):
    return jnp.einsum(form, left, right, precision=lax.Precision.HIGHEST)


def layer_norm(values, gain_row, shift_row):
    centred = values - jnp.mean(values, -1, keepdims=True)
    inverse_std = lax.rsqrt(jnp.mean(centred * centred, -1, keepdims=True) + NORM_EPSILON)
    return centred * inverse_std * gain_row + shift_row


def norm_back(values, gain_row, grad_out):
    centred = values - jnp.mean(values, -1, keepdims=True)
    inverse_std = lax.rsqrt(jnp.mean(centred * centred, -1, keepdims=True) + NORM_EPSILON)
    normed = centred * inverse_std
    scaled_grad = grad_out * gain_row
    grad_in = inverse_std * (
        scaled_grad
        - jnp.mean(scaled_grad, -1, keepdims=True)
        - normed * jnp.mean(scaled_grad * normed, -1, keepdims=True)
    )
    leading = tuple(range(values.ndim - 1))
    return (grad_in, jnp.sum(grad_out * normed, leading), jnp.sum(grad_out, leading))


def gelu_exact(values):
    return 0.5 * values * (1.0 + lax.erf(values * ROOT_HALF))


def gelu_slope(values):
    return (
        0.5 * (1.0 + lax.erf(values * ROOT_HALF))
        + values * jnp.exp(-0.5 * values * values) * DENSITY_SCALE
    )


def layer_bounds(devices):
    widths = [3 * D // devices, D // devices, MLP // devices, MLP // devices]
    lowers = [0, widths[0], widths[0] + widths[1], widths[0] + widths[1] + widths[2]]
    return [(lowers[segment], lowers[segment] + widths[segment]) for segment in range(4)]


def split_layer(weights, devices):
    blocks = weights.reshape(devices, -1, D)
    return [
        blocks[:, lower_row:upper_row].reshape(-1, D)
        for lower_row, upper_row in layer_bounds(devices)
    ]


def join_layer(members, devices):
    return jnp.concatenate([member.reshape(devices, -1, D) for member in members], 1).reshape(-1, D)


def layer_parts(inputs, matrices, vectors):
    joint_weight, output_weight, inner_weight, outer_weight = matrices
    images, tokens = (inputs.shape[0], inputs.shape[1])
    normed = layer_norm(inputs, vectors[0], vectors[1]).astype(jnp.bfloat16)
    joint = matmul_low("itd,ed->ite", normed, joint_weight).astype(jnp.bfloat16)
    head_split = joint.reshape(images, tokens, 3, HEADS, HEAD_DIM)
    queries, keys_in, values_in = (head_split[:, :, 0], head_split[:, :, 1], head_split[:, :, 2])
    scores = matmul_low("ithd,ishd->ihts", queries, keys_in) * HEAD_DIM ** (-0.5)
    attention = jax.nn.softmax(scores, axis=-1)
    mixed_heads = (
        matmul_low("ihts,ishd->ithd", attention.astype(jnp.bfloat16), values_in)
        .astype(jnp.bfloat16)
        .reshape(images, tokens, D)
    )
    attended = matmul_low("itd,ed->ite", mixed_heads, output_weight)
    middle = inputs + vectors[4] * attended
    normed_two = layer_norm(middle, vectors[2], vectors[3]).astype(jnp.bfloat16)
    inner_pre = matmul_low("itd,md->itm", normed_two, inner_weight)
    activated = gelu_exact(inner_pre).astype(jnp.bfloat16)
    outer_out = matmul_low("itm,md->itd", activated, outer_weight)
    result = middle + vectors[5] * outer_out
    return (
        normed,
        queries,
        keys_in,
        values_in,
        attention,
        mixed_heads,
        attended,
        middle,
        normed_two,
        inner_pre,
        activated,
        outer_out,
        result,
    )


def layer_backward(inputs, matrices, vectors, grad_result):
    joint_weight, output_weight, inner_weight, outer_weight = matrices
    (
        normed,
        queries,
        keys_in,
        values_in,
        attention,
        mixed_heads,
        attended,
        middle,
        normed_two,
        inner_pre,
        activated,
        outer_out,
        result,
    ) = layer_parts(inputs, matrices, vectors)
    images, tokens = (inputs.shape[0], inputs.shape[1])
    grad_outer = (vectors[5] * grad_result).astype(jnp.bfloat16)
    grad_scale_two = jnp.sum(grad_result * outer_out, (0, 1))
    grad_outer_weight = matmul_low("itm,itd->md", activated, grad_outer)
    grad_activated = matmul_low("itd,md->itm", grad_outer, outer_weight)
    grad_inner = (grad_activated * gelu_slope(inner_pre)).astype(jnp.bfloat16)
    grad_inner_weight = matmul_low("itm,itd->md", grad_inner, normed_two)
    grad_normed_two = matmul_low("itm,md->itd", grad_inner, inner_weight)
    grad_middle_norm, grad_gain_two, grad_shift_two = norm_back(middle, vectors[2], grad_normed_two)
    grad_middle = grad_result + grad_middle_norm
    grad_attended = (vectors[4] * grad_middle).astype(jnp.bfloat16)
    grad_scale_one = jnp.sum(grad_middle * attended, (0, 1))
    grad_output_weight = matmul_low("ite,itd->ed", grad_attended, mixed_heads)
    grad_mixed = (
        matmul_low("ite,ed->itd", grad_attended, output_weight)
        .astype(jnp.bfloat16)
        .reshape(images, tokens, HEADS, HEAD_DIM)
    )
    grad_attention = matmul_low("ithd,ishd->ihts", grad_mixed, values_in)
    grad_values = matmul_low("ihts,ithd->ishd", attention.astype(jnp.bfloat16), grad_mixed)
    grad_scores = (
        attention * (grad_attention - jnp.sum(attention * grad_attention, -1, keepdims=True))
    ).astype(jnp.bfloat16)
    grad_queries = matmul_low("ihts,ishd->ithd", grad_scores, keys_in) * HEAD_DIM ** (-0.5)
    grad_keys = matmul_low("ihts,ithd->ishd", grad_scores, queries) * HEAD_DIM ** (-0.5)
    grad_joint = (
        jnp.stack([grad_queries, grad_keys, grad_values], 2)
        .astype(jnp.bfloat16)
        .reshape(images, tokens, 3 * D)
    )
    grad_joint_weight = matmul_low("ite,itd->ed", grad_joint, normed)
    grad_normed = matmul_low("ite,ed->itd", grad_joint, joint_weight)
    grad_input_norm, grad_gain_one, grad_shift_one = norm_back(inputs, vectors[0], grad_normed)
    grad_vectors = jnp.stack(
        [
            grad_gain_one,
            grad_shift_one,
            grad_gain_two,
            grad_shift_two,
            grad_scale_one,
            grad_scale_two,
        ]
    )
    return (
        grad_middle + grad_input_norm,
        (grad_joint_weight, grad_output_weight, grad_inner_weight, grad_outer_weight),
        grad_vectors,
    )


def table_vectors(embed_table):
    return embed_table[PIX + SEQ : PIX + SEQ + 6 * LAYERS].astype(jnp.float32).reshape(LAYERS, 6, D)


def table_tail(embed_table):
    return embed_table[PIX + SEQ + 6 * LAYERS :].astype(jnp.float32)


def backbone(patches, embed_table, layer_stack, devices):
    vectors = table_vectors(embed_table)
    tail_rows = table_tail(embed_table)
    position = embed_table[PIX : PIX + SEQ].astype(jnp.float32)
    projected = matmul_low("ipc,cd->ipd", patches, embed_table[:PIX]) + tail_rows[0]
    leading = jnp.broadcast_to(tail_rows[1] + position[0], (patches.shape[0], 1, D))
    current = jnp.concatenate([leading, projected + position[1:]], 1)
    layer_inputs = []
    for layer_number in range(LAYERS):
        layer_inputs.append(current)
        current = layer_parts(
            current, split_layer(layer_stack[layer_number], devices), vectors[layer_number]
        )[-1]
    features = layer_norm(current[:, 0], tail_rows[2], tail_rows[3]).astype(jnp.bfloat16)
    return (features, layer_inputs, current)


def unchanged(values):
    return values


def backbone_back(
    patches,
    embed_table,
    layer_stack,
    layer_inputs,
    final_state,
    grad_features,
    devices,
    reduce_layer,
):
    vectors = table_vectors(embed_table)
    tail_rows = table_tail(embed_table)
    grad_cls, grad_gain, grad_shift = norm_back(final_state[:, 0], tail_rows[2], grad_features)
    grad_current = jnp.concatenate(
        [grad_cls[:, None], jnp.zeros((final_state.shape[0], SEQ - 1, D), jnp.float32)], 1
    )
    weight_grads = [None] * LAYERS
    vector_grads = [None] * LAYERS
    for layer_number in reversed(range(LAYERS)):
        grad_current, matrices, grad_vectors = layer_backward(
            layer_inputs[layer_number],
            split_layer(layer_stack[layer_number], devices),
            vectors[layer_number],
            grad_current,
        )
        weight_grads[layer_number] = reduce_layer(join_layer(matrices, devices))
        vector_grads[layer_number] = grad_vectors
    grad_patch_weight = matmul_low("ipc,ipd->cd", patches, grad_current[:, 1:].astype(jnp.bfloat16))
    grad_position = jnp.sum(grad_current, 0)
    tail_grads = jnp.stack(
        [
            jnp.sum(grad_current[:, 1:], (0, 1)),
            jnp.sum(grad_current[:, 0], 0),
            grad_gain,
            grad_shift,
        ]
    )
    grad_table = jnp.concatenate(
        [grad_patch_weight, grad_position, jnp.concatenate(vector_grads, 0), tail_grads], 0
    )
    return (grad_table, jnp.stack(weight_grads))


def unit_rows(bottle):
    inverse_norm = lax.rsqrt(jnp.sum(bottle * bottle, -1, keepdims=True) + UNIT_EPSILON)
    return (bottle * inverse_norm, inverse_norm)


def combine_parts(left_part, right_part):
    top_student = jnp.maximum(left_part[0], right_part[0])
    total_student = left_part[1] * jnp.exp(left_part[0] - top_student) + right_part[1] * jnp.exp(
        right_part[0] - top_student
    )
    top_teacher = jnp.maximum(left_part[2], right_part[2])
    left_weight = jnp.exp(left_part[2] - top_teacher)
    right_weight = jnp.exp(right_part[2] - top_teacher)
    return (
        top_student,
        total_student,
        top_teacher,
        left_part[3] * left_weight + right_part[3] * right_weight,
        left_part[4] * left_weight + right_part[4] * right_weight,
    )


def adam_step(weight, grad, first_moment, second_moment, rate, decay):
    first_new = BETA_ONE * first_moment + (1.0 - BETA_ONE) * grad
    second_new = BETA_TWO * second_moment + (1.0 - BETA_TWO) * grad * grad
    direction = (
        first_new
        / (1.0 - BETA_ONE**STEP)
        / (jnp.sqrt(second_new / (1.0 - BETA_TWO**STEP)) + ADAM_EPSILON)
    )
    return (first_new, second_new, weight - rate * (direction + decay * weight))


def renew(stat_matrix, basis):
    scaled = jnp.dot(stat_matrix, basis, precision=lax.Precision.HIGHEST) * (
        D / jnp.trace(stat_matrix)
    )
    gram = jnp.dot(scaled.T, scaled, precision=lax.Precision.HIGHEST)
    lower_factor = jnp.linalg.cholesky(gram)
    return lax.linalg.triangular_solve(lower_factor, scaled.T, left_side=True, lower=True).T


def nothing(stat_matrix, basis):
    return jnp.zeros_like(basis)


def follow(teacher_weight, student_weight):
    return TEACHER_MOMENTUM * teacher_weight + (1.0 - TEACHER_MOMENTUM) * student_weight


MESH = pl.DeviceIdType.MESH
LANES = 128
LOW = jnp.bfloat16
FULL = jnp.float32


def params(identity, vmem=None):
    return pltpu.CompilerParams(
        collective_id=identity, has_side_effects=True, vmem_limit_bytes=vmem or (48 << 20)
    )


def push(source, target, sent, landed, device):
    copy = pltpu.make_async_remote_copy(
        src_ref=source,
        dst_ref=target,
        send_sem=sent,
        recv_sem=landed,
        device_id=(device,),
        device_id_type=MESH,
    )
    copy.start()
    return copy


def greet(peers):
    barrier = pltpu.get_barrier_semaphore()
    for peer in peers:
        pl.semaphore_signal(barrier, inc=1, device_id=(peer,), device_id_type=MESH)
    pl.semaphore_wait(barrier, len(peers))


def dot_nt(left, right):
    return lax.dot_general(left, right, (((1,), (1,)), ((), ())), preferred_element_type=FULL)


def dot_nn(left, right):
    return lax.dot_general(left, right, (((1,), (0,)), ((), ())), preferred_element_type=FULL)


def dot_tn(left, right):
    return lax.dot_general(left, right, (((0,), (0,)), ((), ())), preferred_element_type=FULL)


def slot_of(device, depth):
    return (device % 8) * depth + device // 8


class Route:
    def __init__(self, depth, items, own_sem, z_sent, z_landed, near_sent, near_landed, die_sent, die_landed):
        self.depth = depth
        self.items = items
        self.sems = (own_sem, z_sent, z_landed, near_sent, near_landed, die_sent, die_landed)
        me = lax.axis_index(AXIS)
        self.me = me
        self.total = 8 * depth
        self.core = lax.rem(me, 2)
        x_at = lax.rem(me // 2, 2)
        y_at = lax.rem(me // 4, 2)
        self.z_at = me // 8
        self.partner = me + 1 - 2 * self.core
        self.to_x = me + 2 - 4 * x_at
        self.to_y = me + 4 - 8 * y_at
        places = [(y_at, x_at), (y_at, 1 - x_at), (1 - y_at, x_at), (1 - y_at, 1 - x_at)]
        self.starts = [((y * 2 + x) * 2 + self.core) * depth for y, x in places]

    def copy(self, source, target, sent, landed, device):
        return pltpu.make_async_remote_copy(
            src_ref=source,
            dst_ref=target,
            send_sem=sent,
            recv_sem=landed,
            device_id=(device,),
            device_id_type=MESH,
        )

    def half(self, at):
        size = self.items[at][3]
        return (size // 2 + 15) // 16 * 16

    def own(self, at):
        source, target, lower, size = self.items[at]
        return pltpu.make_async_copy(
            source.at[pl.ds(lower, size)],
            target.at[self.starts[0] + self.z_at, pl.ds(lower, size)],
            self.sems[0].at[at],
        )

    def deep(self, at, step):
        source, target, lower, size = self.items[at]
        return self.copy(
            source.at[pl.ds(lower, size)],
            target.at[self.starts[0] + self.z_at, pl.ds(lower, size)],
            self.sems[1].at[at, step],
            self.sems[2].at[at, step],
            lax.rem(self.me + 8 * step, self.total),
        )

    def near(self, at, which):
        source, target, lower, size = self.items[at]
        half = self.half(at)
        column, first, length, device = [
            (0, lower, size, self.to_x),
            (0, lower, size, self.to_y),
            (1, lower, half, self.to_y),
            (2, lower + half, size - half, self.to_x),
        ][which]
        view = target.at[pl.ds(self.starts[column], self.depth), pl.ds(first, length)]
        return self.copy(view, view, self.sems[3].at[at, which], self.sems[4].at[at, which], device)

    def die(self, at, column):
        source, target, lower, size = self.items[at]
        view = target.at[pl.ds(self.starts[column], self.depth), pl.ds(lower, size)]
        return self.copy(
            view, view, self.sems[5].at[at, column], self.sems[6].at[at, column], self.partner
        )

    def act(self, stage, at):
        if stage == 0:
            self.own(at).start()
            for step in range(1, self.depth):
                self.deep(at, step).start()
        elif stage == 1:
            self.own(at).wait()
            for step in range(1, self.depth):
                self.deep(at, step).wait_recv()
            self.near(at, 0).start()
            self.near(at, 1).start()
            self.die(at, 0).start()
        elif stage == 2:
            self.near(at, 0).wait_recv()
            self.near(at, 2).start()
            self.die(at, 1).start()
            self.near(at, 1).wait_recv()
            self.near(at, 3).start()
            self.die(at, 2).start()
        elif stage == 3:
            self.near(at, 2).wait_recv()
            self.near(at, 3).wait_recv()
            self.die(at, 3).start()
        elif stage == 4:
            for column in range(4):
                self.die(at, column).wait_recv()
        else:
            for step in range(1, self.depth):
                self.deep(at, step).wait_send()
            for which in range(4):
                self.near(at, which).wait_send()
                self.die(at, which).wait_send()


def route_sems(count, depth):
    dma = pltpu.SemaphoreType.DMA
    return [
        dma((count,)),
        dma((count, depth)),
        dma((count, depth)),
        dma((count, 4)),
        dma((count, 4)),
        dma((count, 4)),
        dma((count, 4)),
    ]


def head_kernel(
    devices,
    rows_ref,
    hidden_ref,
    teacher_hidden_ref,
    part_ref,
    last_all_ref,
    protos_ref,
    teacher_protos_ref,
    centre_ref,
    mask_ref,
    mask_row_ref,
    scalars_ref,
    grad_hidden_ref,
    grad_last_ref,
    grad_protos_ref,
    grad_feat_ref,
    centre_out_ref,
    feat_ref,
    last_ref,
    teacher_last_ref,
    fb,
    hid_low,
    thid_low,
    prot_low,
    half_out,
    half_in,
    mine_buf,
    other_buf,
    act_s,
    act_t,
    act2_s,
    act2_t,
    pre1,
    pre2,
    unit_ref,
    inv_ref,
    exp_s,
    exp_t,
    stat_out,
    stat_all,
    pz_ref,
    pz_all,
    dz_own,
    dz_all,
    dp_own,
    dp_in,
    dp_cb,
    dp_half,
    dp_full,
    df_part,
    df_all,
    df_sum,
    df_other,
    die_sent,
    die_landed,
    wide_sent,
    wide_landed,
    core_sent,
    core_landed,
):
    me = lax.axis_index(AXIS)
    core = lax.rem(me, 2)
    chip = me // 2
    chips = devices // 2
    partner = me + 1 - 2 * core
    everyone = [lax.rem(me + step, devices) for step in range(1, devices)]
    same_core = [lax.rem(me + 2 * step, devices) for step in range(1, chips)]
    images = mask_ref.shape[0]
    units = hidden_ref.shape[0]
    groups = images // 8
    greet(everyone)
    sends = []

    def die(step, source, target):
        copy = push(source, target, die_sent.at[step], die_landed.at[step], partner)
        sends.append(copy)
        return copy

    def wide(step, source, target):
        made = [
            push(source, target, wide_sent.at[step, at], wide_landed.at[step, at], peer)
            for at, peer in enumerate(everyone)
        ]
        sends.extend(made)
        return made

    def cores(step, source_of, target):
        made = [
            push(source_of(peer), target, core_sent.at[step, at], core_landed.at[step, at], peer)
            for at, peer in enumerate(same_core)
        ]
        sends.extend(made)
        return made

    pieces = [
        rows_ref[model, image, 0:1, j * LANES : (j + 1) * LANES]
        for model in range(2)
        for j in range(D // LANES)
        for image in range(rows_ref.shape[1])
    ]
    blank = jnp.zeros((16 - len(pieces) // 2, LANES), FULL)
    half_count = len(pieces) // 2
    feat_ref[...] = jnp.concatenate(
        pieces[:half_count] + [blank] + pieces[half_count:] + [blank], 0
    ).astype(LOW)
    fb[me] = feat_ref[...]
    copies = wide(0, feat_ref, fb.at[me])
    hid_low[...] = hidden_ref[...].astype(LOW)
    thid_low[...] = teacher_hidden_ref[...].astype(LOW)
    prot_low[0] = protos_ref[...].astype(LOW)
    prot_low[1] = teacher_protos_ref[...].astype(LOW)
    last_width = last_ref.shape[0] // devices
    across = last_all_ref.shape[2]
    for model, table in enumerate((last_ref, teacher_last_ref)):
        for half in range(2):
            first = (2 * half + model) * last_width
            for at in range(0, devices, 2):
                pair_rows = [
                    last_all_ref[slot_of(at + t, devices // 8), first : first + last_width].astype(FULL)
                    for t in range(2)
                ]
                table[
                    at * last_width : (at + 2) * last_width, half * across : (half + 1) * across
                ] = jnp.concatenate(pair_rows, 0).astype(LOW)
    block_rows = feat_ref.shape[0]
    row_at = lax.broadcasted_iota(jnp.int32, (images, devices * block_rows), 0)
    col_at = lax.broadcasted_iota(jnp.int32, (images, devices * block_rows), 1)
    col_dev = lax.shift_right_logical(col_at, 5)
    col_in = jnp.bitwise_and(col_at, 31)
    lead = row_at - 3 * col_dev
    for copy in copies:
        copy.wait_recv()
    rows_all = fb[...].reshape(devices * block_rows, LANES)

    def features_of(model):
        pieces = []
        for j in range(3):
            hit = (col_in - (16 * model + 3 * j) == lead) & (lead >= 0) & (lead < 3)
            pieces.append(dot_nn(jnp.where(hit, 1.0, 0.0).astype(LOW), rows_all).astype(LOW))
        return jnp.concatenate(pieces, 1)

    feats = features_of(0)
    tfeats = features_of(1)

    def gather_pair(step, student, teacher, out_s, out_t):
        own_model = jnp.where(core == 0, student, teacher)
        half_out[step] = jnp.where(core == 0, teacher, student)
        copy = die(2 * step, half_out.at[step], half_in.at[step])
        copy.wait_recv()
        got = half_in[step]
        block = jnp.concatenate(
            [jnp.where(core == 0, own_model, got), jnp.where(core == 0, got, own_model)], 1
        ).astype(LOW)
        mine_buf[step, chip] = block
        made = cores(step, lambda peer: mine_buf.at[step, chip], mine_buf.at[step, chip])
        for copy in made:
            copy.wait_recv()
        copy = die(2 * step + 1, mine_buf.at[step], other_buf.at[step])
        copy.wait_recv()
        for at in range(chips):
            one, two = mine_buf[step, at], other_buf[step, at]
            out_s[:, at * LANES : (at + 1) * LANES] = jnp.where(core == 0, one, two)
            out_t[:, at * LANES : (at + 1) * LANES] = jnp.where(core == 0, two, one)

    pre_one = dot_nt(feats, hid_low[:, :D])
    pre1[...] = pre_one
    tpre_one = dot_nt(tfeats, thid_low[:, :D])
    gather_pair(0, gelu_exact(pre_one).astype(LOW).astype(FULL), gelu_exact(tpre_one).astype(LOW).astype(FULL), act_s, act_t)
    pre_two = dot_nt(act_s[...], hid_low[:, D:])
    pre2[...] = pre_two
    tpre_two = dot_nt(act_t[...], thid_low[:, D:])
    gather_pair(1, gelu_exact(pre_two).astype(LOW).astype(FULL), gelu_exact(tpre_two).astype(LOW).astype(FULL), act2_s, act2_t)

    unit, inverse_norm = unit_rows(dot_nt(act2_s[...], last_ref[...]))
    tunit, unused = unit_rows(dot_nt(act2_t[...], teacher_last_ref[...]))
    unit_ref[...] = unit
    inv_ref[...] = jnp.broadcast_to(inverse_norm, inv_ref.shape)
    unit_low = unit.astype(LOW)
    scaled = dot_nn(unit_low, prot_low[0]) / TAU_STUDENT
    tlogits = dot_nn(tunit.astype(LOW), prot_low[1])
    top_s = jnp.max(scaled, -1, keepdims=True)
    grown_s = jnp.exp(scaled - top_s)
    exp_s[...] = grown_s
    sharp = (tlogits - centre_ref[...]) / TAU_TEACHER
    top_t = jnp.max(sharp, -1, keepdims=True)
    grown_t = jnp.exp(sharp - top_t)
    exp_t[...] = grown_t
    lane = lax.broadcasted_iota(jnp.int32, (images, LANES), 1)
    stats = jnp.where(lane == 0, top_s, 0.0)
    stats = jnp.where(lane == 1, jnp.sum(grown_s, -1, keepdims=True), stats)
    stats = jnp.where(lane == 2, top_t, stats)
    stats = jnp.where(lane == 3, jnp.sum(grown_t, -1, keepdims=True), stats)
    stats = jnp.where(lane == 4, jnp.sum(grown_t * scaled, -1, keepdims=True), stats)
    square = jnp.concatenate([stats, jnp.zeros((LANES - images, LANES), FULL)], 0)
    stat_out[...] = square.T[:8]
    stat_all[me] = stat_out[...]
    copies = wide(1, stat_out, stat_all.at[me])
    counted = mask_ref[...]
    count = jnp.sum(counted)
    centre_out_ref[...] = (
        CENTRE_MOMENTUM * centre_ref[...]
        + (1.0 - CENTRE_MOMENTUM) * jnp.sum(counted * tlogits, 0, keepdims=True) / count
    )
    for copy in copies:
        copy.wait_recv()
    merged = stat_all[...]
    tops, totals = merged[:, 0], merged[:, 1]
    ttops, ttotals, crosses = merged[:, 2], merged[:, 3], merged[:, 4]
    peak_s = jnp.max(tops, 0, keepdims=True)
    sum_s = jnp.sum(totals * jnp.exp(tops - peak_s), 0, keepdims=True)
    peak_t = jnp.max(ttops, 0, keepdims=True)
    shrink = jnp.exp(ttops - peak_t)
    sum_t = jnp.sum(ttotals * shrink, 0, keepdims=True)
    cross = jnp.sum(crosses * shrink, 0, keepdims=True)
    log_total = peak_s + jnp.log(sum_s)
    mask_row = mask_row_ref[...]
    losses = jnp.where(mask_row > 0.0, log_total - cross / sum_t, 0.0)
    loss = jnp.sum(losses)
    lane8 = lax.broadcasted_iota(jnp.int32, (8, LANES), 1)
    scalars_ref[...] = jnp.where(lane8 == 0, loss, jnp.where(lane8 == 1, count, 0.0))
    back = jnp.concatenate(
        [log_total, peak_t, 1.0 / sum_t, jnp.zeros((LANES - 3, LANES), FULL)], 0
    ).T
    share_s = jnp.exp(top_s - back[:images, 0:1])
    share_t = jnp.exp(top_t - back[:images, 1:2]) * back[:images, 2:3]
    grad_logits = (
        (counted / count) * (exp_s[...] * share_s - exp_t[...] * share_t) / TAU_STUDENT
    ).astype(LOW)

    pz_ref[...] = dot_nt(grad_logits, prot_low[0]).reshape(groups, 8, unit.shape[1])
    for group in range(groups):
        owner = 2 * group

        @pl.when(me != owner)
        def _(group=group, owner=owner):
            push(pz_ref.at[group], pz_all.at[me], wide_sent.at[2, group], wide_landed.at[2, me], owner)

    grad_protos_ref[...] = dot_tn(unit_low, grad_logits)

    @pl.when((core == 0) & (chip < groups))
    def _():
        pz_all[me] = pz_ref[chip]
        for source in range(devices):

            @pl.when(source != me)
            def _(source=source):
                pltpu.make_async_copy(pz_all.at[source], pz_all.at[source], wide_landed.at[2, source]).wait()

        total = jnp.sum(pz_all[...], 0)
        rows = pl.ds(pl.multiple_of(chip * 8, 8), 8)
        own_unit = unit_ref[rows, :]
        own_inv = inv_ref[rows, :][:, 0:1]
        dz_own[...] = own_inv * (total - own_unit * jnp.sum(own_unit * total, -1, keepdims=True))
        dz_all[chip] = dz_own[...]
        for step in range(1, devices):
            push(dz_own, dz_all.at[chip], wide_sent.at[3, step - 1], wide_landed.at[3, chip], lax.rem(me + step, devices))

    for group in range(groups):

        @pl.when(me != 2 * group)
        def _(group=group):
            pltpu.make_async_copy(dz_all.at[group], dz_all.at[group], wide_landed.at[3, group]).wait()

    grad_bottle = dz_all[...].reshape(images, unit.shape[1]).astype(LOW)
    chip_columns = pl.ds(pl.multiple_of(chip * LANES, LANES), LANES)
    pair = dot_nn(grad_bottle, last_ref[:, chip_columns])
    grad_act_two = jnp.where(core == 0, pair[:, :units], pair[:, units:])
    grad_pre_two = (grad_act_two * gelu_slope(pre2[...])).astype(LOW)

    dp_own[...] = grad_pre_two.astype(FULL)
    copy = die(4, dp_own, dp_in)
    width = last_ref.shape[0] // devices
    pick_row = lax.broadcasted_iota(jnp.int32, (width, last_ref.shape[0]), 0)
    pick_col = lax.broadcasted_iota(jnp.int32, (width, last_ref.shape[0]), 1)
    pick = jnp.where(pick_col == pick_row + me * width, 1.0, 0.0).astype(LOW)
    own_bottle = dot_nt(pick, grad_bottle).astype(LOW)
    grad_last_ref[...] = dot_nn(own_bottle, act2_s[...])
    copy.wait_recv()
    own_dp, got_dp = dp_own[...], dp_in[...]
    dp_cb[...] = jnp.concatenate(
        [jnp.where(core == 0, own_dp, got_dp), jnp.where(core == 0, got_dp, own_dp)], 1
    ).astype(LOW)
    half = images // 2
    my_rows = pl.ds(pl.multiple_of(core * half, 16), half)
    their_rows = pl.ds(pl.multiple_of((1 - core) * half, 16), half)
    dp_half[0, chip] = dp_cb[my_rows, :]
    made = cores(2, lambda peer: dp_half.at[0, chip], dp_half.at[0, chip])
    grad_hidden_ref[:, D:] = dot_tn(grad_pre_two, act_s[...])
    for copy in made:
        copy.wait_recv()
    copy = die(5, dp_half.at[0], dp_half.at[1])
    for at in range(chips):
        dp_full[my_rows, at * LANES : (at + 1) * LANES] = dp_half[0, at]
    copy.wait_recv()
    for at in range(chips):
        dp_full[their_rows, at * LANES : (at + 1) * LANES] = dp_half[1, at]
    part = jnp.concatenate([part_ref[at % 2, at // 2] for at in range(devices)], 0)
    pair = dot_nn(dp_full[...], part)
    grad_act_one = jnp.where(core == 0, pair[:, :units], pair[:, units:])
    grad_pre_one = (grad_act_one * gelu_slope(pre1[...])).astype(LOW)

    out_row = lax.broadcasted_iota(jnp.int32, (8 * chips, images), 0)
    in_row = lax.broadcasted_iota(jnp.int32, (8 * chips, images), 1)
    out_chip = lax.shift_right_logical(out_row, 3)
    out_in = jnp.bitwise_and(out_row, 7)
    hit = (in_row - 6 * out_chip == out_in) & (out_in < 6)
    moved = dot_nn(jnp.where(hit, 1.0, 0.0).astype(LOW), grad_pre_one).astype(LOW)
    df_part[...] = dot_nn(moved, hid_low[:, :D]).reshape(chips, 8, D)
    df_all[chip] = df_part[chip]
    made = cores(3, lambda peer: df_part.at[peer // 2], df_all.at[chip])
    grad_hidden_ref[:, :D] = dot_tn(grad_pre_one, feats)
    for copy in made:
        copy.wait_recv()
    df_sum[...] = jnp.sum(df_all[...], 0)
    copy = die(6, df_sum, df_other)
    copy.wait_recv()
    whole = df_sum[...] + df_other[...]
    grad_feat_ref[...] = whole
    squares = jnp.sum(grad_hidden_ref[...] * grad_hidden_ref[...])
    squares = squares + jnp.sum(grad_last_ref[...] * grad_last_ref[...])
    squares = squares + jnp.sum(grad_protos_ref[...] * grad_protos_ref[...])
    scalars_ref[...] = jnp.where(lane8 == 2, squares, scalars_ref[...])
    for copy in sends:
        copy.wait_send()
    for group in range(groups):

        @pl.when(me != 2 * group)
        def _(group=group):
            pltpu.make_async_copy(pz_ref.at[group], pz_ref.at[group], wide_sent.at[2, group]).wait()

    @pl.when((core == 0) & (chip < groups))
    def _():
        for step in range(1, devices):
            pltpu.make_async_copy(dz_own, dz_own, wide_sent.at[3, step - 1]).wait()


def head(rows, hidden, teacher_hidden, part, last_all, protos, teacher_protos, centre, mask, mask_row, devices):
    images = mask.shape[0]
    units, wide = hidden.shape
    bottle, width = protos.shape
    hid = 2 * last_all.shape[2]
    chips = devices // 2
    groups = images // 8
    vmem = pl.BlockSpec(memory_space=pltpu.VMEM)
    shape = jax.ShapeDtypeStruct
    dma = pltpu.SemaphoreType.DMA
    return pl.pallas_call(
        functools.partial(head_kernel, devices),
        out_shape=(
            shape((8, LANES), FULL),
            shape((units, wide), FULL),
            shape((bottle // devices, hid), FULL),
            shape((bottle, width), FULL),
            shape((8, D), FULL),
            shape((1, width), FULL),
        ),
        in_specs=[vmem] * 10,
        out_specs=(vmem,) * 6,
        scratch_shapes=[
            pltpu.VMEM((32, LANES), LOW),
            pltpu.VMEM((bottle, hid), LOW),
            pltpu.VMEM((bottle, hid), LOW),
            pltpu.VMEM((devices, 32, LANES), LOW),
            pltpu.VMEM((units, wide), LOW),
            pltpu.VMEM((units, wide), LOW),
            pltpu.VMEM((2, bottle, width), LOW),
            pltpu.VMEM((2, images, units), FULL),
            pltpu.VMEM((2, images, units), FULL),
            pltpu.VMEM((2, chips, images, LANES), LOW),
            pltpu.VMEM((2, chips, images, LANES), LOW),
            pltpu.VMEM((images, hid), LOW),
            pltpu.VMEM((images, hid), LOW),
            pltpu.VMEM((images, hid), LOW),
            pltpu.VMEM((images, hid), LOW),
            pltpu.VMEM((images, units), FULL),
            pltpu.VMEM((images, units), FULL),
            pltpu.VMEM((images, bottle), FULL),
            pltpu.VMEM((images, LANES), FULL),
            pltpu.VMEM((images, width), FULL),
            pltpu.VMEM((images, width), FULL),
            pltpu.VMEM((8, LANES), FULL),
            pltpu.VMEM((devices, 8, LANES), FULL),
            pltpu.VMEM((groups, 8, bottle), FULL),
            pltpu.VMEM((devices, 8, bottle), FULL),
            pltpu.VMEM((8, bottle), FULL),
            pltpu.VMEM((groups, 8, bottle), FULL),
            pltpu.VMEM((images, units), FULL),
            pltpu.VMEM((images, units), FULL),
            pltpu.VMEM((images, LANES), LOW),
            pltpu.VMEM((2, chips, images // 2, LANES), LOW),
            pltpu.VMEM((images, hid), LOW),
            pltpu.VMEM((chips, 8, D), FULL),
            pltpu.VMEM((chips, 8, D), FULL),
            pltpu.VMEM((8, D), FULL),
            pltpu.VMEM((8, D), FULL),
            dma((7,)),
            dma((7,)),
            dma((4, devices)),
            dma((4, devices)),
            dma((4, chips - 1)),
            dma((4, chips - 1)),
        ],
        compiler_params=params(2),
        name="head",
    )(rows, hidden, teacher_hidden, part, last_all, protos, teacher_protos, centre, mask, mask_row)


def gram_device(matrix):
    return 2 * matrix


def dot_high(left, right, contract):
    return lax.dot_general(
        left,
        right,
        (contract, ((), ())),
        precision=lax.Precision.HIGHEST,
        preferred_element_type=FULL,
    )


def inverse_factor(block):
    size = block.shape[0]
    tiles = size // 8
    wide = 8
    sub = lax.broadcasted_iota(jnp.int32, (8, size), 0)
    lane = lax.broadcasted_iota(jnp.int32, (8, size), 1)
    rest = [block[8 * t : 8 * t + 8] for t in range(tiles)]
    made = [jnp.where(lane == sub + 8 * t, 1.0, 0.0) for t in range(tiles)]

    def full(value):
        return jnp.broadcast_to(value, (8, size))

    for k in range(0, size, wide):
        tile, row = k // 8, k % 8
        factor_rows = [full(rest[tile][row + i : row + i + 1]) for i in range(wide)]
        made_rows = [full(made[tile][row + i : row + i + 1]) for i in range(wide)]
        entry = [
            [full(rest[tile][row + i : row + i + 1, k + j : k + j + 1]) for j in range(i + 1)]
            for i in range(wide)
        ]
        columns = [
            [full(rest[t][:, k + j : k + j + 1]) for j in range(wide)] for t in range(tile, tiles)
        ]
        for j in range(wide):
            scale = lax.rsqrt(entry[j][j])
            factor_rows[j] = factor_rows[j] * scale
            made_rows[j] = made_rows[j] * scale
            for i in range(j + 1, wide):
                entry[i][j] = entry[i][j] * scale
            for some in columns:
                some[j] = some[j] * scale
            for i in range(j + 1, wide):
                factor_rows[i] = factor_rows[i] - entry[i][j] * factor_rows[j]
                made_rows[i] = made_rows[i] - entry[i][j] * made_rows[j]
                for e in range(j + 1, i + 1):
                    entry[i][e] = entry[i][e] - entry[i][j] * entry[e][j]
                for some in columns:
                    some[i] = some[i] - entry[i][j] * some[j]
        for t in range(tile, tiles):
            some = columns[t - tile]
            if t == tile:
                some = [jnp.where(sub >= row + wide, column, 0.0) for column in some]
            for j in range(wide):
                rest[t] = rest[t] - some[j] * factor_rows[j]
                made[t] = made[t] - some[j] * made_rows[j]
            if t == tile:
                for j in range(wide):
                    made[t] = jnp.where(sub == row + j, made_rows[j], made[t])
    return jnp.concatenate(made, 0)


def renew_kernel(
    devices,
    stats_ref,
    basis_ref,
    own_stats_ref,
    own_bases_ref,
    stat,
    base,
    gram,
    work,
    done,
    given,
    taken,
    passed,
    sent,
    landed,
    die_sent,
    die_landed,
):
    me = lax.axis_index(AXIS)
    core = lax.rem(me, 2)
    chip = me // 2
    chips = devices // 2
    partner = me + 1 - 2 * core
    parts, rows = stats_ref.shape[:2]
    size = parts * rows
    blocks = size // LANES
    matrices = own_stats_ref.shape[0]
    is_gram = (core == 0) & (chip < matrices)
    spare = given.shape[3] - rows
    greet([lax.rem(me + 2 * at, devices) for at in range(1, chips)] + [partner])

    def out_copy(kind, at):
        peer = lax.rem(me + 2 * at, devices)
        return pltpu.make_async_remote_copy(
            src_ref=given.at[kind, peer // 2],
            dst_ref=taken.at[kind, chip],
            send_sem=sent.at[kind, at],
            recv_sem=landed.at[kind, chip],
            device_id=(peer,),
            device_id_type=MESH,
        )

    def across(kind):
        return pltpu.make_async_remote_copy(
            src_ref=taken.at[kind, :, 1],
            dst_ref=passed.at[kind],
            send_sem=die_sent.at[kind],
            recv_sem=die_landed.at[kind],
            device_id=(partner,),
            device_id_type=MESH,
        )

    def hand_out(kind, row_of):
        blank = jnp.zeros((spare, size), FULL)
        for part in range(parts):
            given[kind, part // 2, part % 2] = jnp.concatenate([row_of(part), blank], 0).astype(LOW)
        taken[kind, chip] = given[kind, chip]
        for at in range(1, chips):
            out_copy(kind, at).start()

    @pl.when(is_gram)
    def _():
        hand_out(0, lambda part: stats_ref[part])
        for part in range(parts):
            stat[part * rows : (part + 1) * rows] = stats_ref[part]
            base[part * rows : (part + 1) * rows] = basis_ref[part]
        at_row = lax.broadcasted_iota(jnp.int32, (size, size), 0)
        at_col = lax.broadcasted_iota(jnp.int32, (size, size), 1)
        trace = jnp.sum(jnp.where(at_row == at_col, stat[...], 0.0), axis=(0, 1), keepdims=True)
        scaled = dot_high(stat[...], base[...], ((1,), (0,))) * (size / trace)
        product = dot_high(scaled, scaled, ((0,), (0,)))
        for b in range(blocks):
            work[b] = scaled[:, b * LANES : (b + 1) * LANES]
            for c in range(blocks):
                gram[b, c] = product[b * LANES : (b + 1) * LANES, c * LANES : (c + 1) * LANES]

        def step(b, carried):
            inverse = inverse_factor(gram[b, b])
            made = dot_high(work[b], inverse, ((1,), (1,)))
            done[b] = made

            def trail(c, inner):
                panel = dot_high(inverse, gram[b, c], ((1,), (0,)))
                work[c] = work[c] - dot_high(made, panel, ((1,), (0,)))

                def against(e, innermost):
                    other = dot_high(inverse, gram[b, e], ((1,), (0,)))
                    gram[c, e] = gram[c, e] - dot_high(panel, other, ((0,), (0,)))
                    return innermost

                lax.fori_loop(c, blocks, against, 0)
                return inner

            lax.fori_loop(b + 1, blocks, trail, 0)
            return carried

        lax.fori_loop(0, blocks, step, 0)
        whole = jnp.concatenate([done[b] for b in range(blocks)], 1)
        hand_out(1, lambda part: whole[part * rows : (part + 1) * rows])

    @pl.when(core == 0)
    def _():
        for kind in range(2):
            for matrix in range(matrices):

                @pl.when(chip != matrix)
                def _(kind=kind, matrix=matrix):
                    view = taken.at[kind, matrix]
                    pltpu.make_async_copy(view, view, landed.at[kind, matrix]).wait()

            across(kind).start()
        own_stats_ref[...] = taken[0, :, 0, :rows].astype(FULL)
        own_bases_ref[...] = taken[1, :, 0, :rows].astype(FULL)
        for kind in range(2):
            across(kind).wait_send()

    @pl.when(core == 1)
    def _():
        for kind in range(2):
            across(kind).wait_recv()
        own_stats_ref[...] = passed[0, :, :rows].astype(FULL)
        own_bases_ref[...] = passed[1, :, :rows].astype(FULL)

    @pl.when(is_gram)
    def _():
        for kind in range(2):
            for at in range(1, chips):
                out_copy(kind, at).wait_send()


def renew_own(stats, basis, matrices):
    devices, rows, width = stats.shape
    size = devices * rows
    blocks = size // LANES
    padded = -(-rows // 16) * 16
    vmem = pl.BlockSpec(memory_space=pltpu.VMEM)
    dma = pltpu.SemaphoreType.DMA
    return pl.pallas_call(
        functools.partial(renew_kernel, devices),
        out_shape=(jax.ShapeDtypeStruct((matrices, rows, width), FULL),) * 2,
        in_specs=[vmem] * 2,
        out_specs=(vmem,) * 2,
        scratch_shapes=[
            pltpu.VMEM((size, width), FULL),
            pltpu.VMEM((size, width), FULL),
            pltpu.VMEM((blocks, blocks, LANES, LANES), FULL),
            pltpu.VMEM((blocks, size, LANES), FULL),
            pltpu.VMEM((blocks, size, LANES), FULL),
            pltpu.VMEM((2, devices // 2, 2, padded, width), LOW),
            pltpu.VMEM((2, matrices, 2, padded, width), LOW),
            pltpu.VMEM((2, matrices, padded, width), LOW),
            dma((2, devices // 2)),
            dma((2, matrices)),
            dma((2,)),
            dma((2,)),
        ],
        compiler_params=params(4, 40 << 20),
        name="renew",
    )(stats, basis)


def head_slow(
    features,
    teacher_features,
    valid_mask,
    head_hidden,
    head_last,
    protos,
    teacher_hidden,
    teacher_last,
    teacher_protos,
    centre,
    device_index,
):
    all_features, all_teacher = (
        lax.all_gather(features, AXIS, axis=0, tiled=True),
        lax.all_gather(teacher_features, AXIS, axis=0, tiled=True),
    )
    first_weight = head_hidden[:, :D].astype(jnp.bfloat16)
    second_weight = head_hidden[:, D:].astype(jnp.bfloat16)
    last_weight = head_last.astype(jnp.bfloat16)
    proto_weight = protos.astype(jnp.bfloat16)
    teacher_first = teacher_hidden[:, :D].astype(jnp.bfloat16)
    teacher_second = teacher_hidden[:, D:].astype(jnp.bfloat16)
    pre_one = matmul_low("bd,hd->bh", all_features, first_weight)
    teacher_pre_one = matmul_low("bd,hd->bh", all_teacher, teacher_first)
    act_one = (
        lax.all_gather(gelu_exact(pre_one).astype(jnp.bfloat16), AXIS, axis=1, tiled=True),
        lax.all_gather(gelu_exact(teacher_pre_one).astype(jnp.bfloat16), AXIS, axis=1, tiled=True),
    )
    pre_two = matmul_low("bh,kh->bk", act_one[0], second_weight)
    teacher_pre_two = matmul_low("bh,kh->bk", act_one[1], teacher_second)
    act_two = (
        lax.all_gather(gelu_exact(pre_two).astype(jnp.bfloat16), AXIS, axis=1, tiled=True),
        lax.all_gather(gelu_exact(teacher_pre_two).astype(jnp.bfloat16), AXIS, axis=1, tiled=True),
    )
    bottles = (
        lax.all_gather(matmul_low("bh,hc->bc", act_two[0], last_weight), AXIS, axis=1, tiled=True),
        lax.all_gather(
            matmul_low("bh,hc->bc", act_two[1], teacher_last.astype(jnp.bfloat16)),
            AXIS,
            axis=1,
            tiled=True,
        ),
    )
    unit, inverse_norm = unit_rows(bottles[0])
    teacher_unit, unused_norm = unit_rows(bottles[1])
    unit_low = unit.astype(jnp.bfloat16)
    logits = matmul_low("bc,cp->bp", unit_low, proto_weight)
    teacher_logits = matmul_low(
        "bc,cp->bp", teacher_unit.astype(jnp.bfloat16), teacher_protos.astype(jnp.bfloat16)
    )
    scaled = logits / TAU_STUDENT
    student_top = jnp.max(scaled, -1)
    student_total = jnp.sum(jnp.exp(scaled - student_top[:, None]), -1)
    sharpened = (teacher_logits - centre) / TAU_TEACHER
    teacher_top = jnp.max(sharpened, -1)
    teacher_exp = jnp.exp(sharpened - teacher_top[:, None])
    merged = joined(
        (
            student_top,
            student_total,
            teacher_top,
            jnp.sum(teacher_exp, -1),
            jnp.sum(teacher_exp * scaled, -1),
        ),
        AXIS,
        combine_parts,
    )
    log_total = merged[0] + jnp.log(merged[1])
    counted = valid_mask.astype(jnp.float32)
    loss_count = jnp.sum(counted)
    loss_sum = jnp.sum(counted * (log_total - merged[4] / merged[3]))
    student_prob = jnp.exp(scaled - log_total[:, None])
    teacher_prob = jnp.exp(sharpened - merged[2][:, None]) / merged[3][:, None]
    grad_logits = (
        (counted / loss_count)[:, None] * (student_prob - teacher_prob) / TAU_STUDENT
    ).astype(jnp.bfloat16)
    grad_protos = matmul_low("bc,bp->cp", unit_low, grad_logits)
    grad_unit = lax.psum(matmul_low("bp,cp->bc", grad_logits, proto_weight), AXIS)
    grad_bottle = inverse_norm * (grad_unit - unit * jnp.sum(unit * grad_unit, -1, keepdims=True))
    last_width = head_last.shape[1]
    grad_bottle_own = lax.dynamic_slice_in_dim(
        grad_bottle, device_index * last_width, last_width, 1
    ).astype(jnp.bfloat16)
    grad_last = matmul_low("bh,bc->hc", act_two[0], grad_bottle_own)
    grad_act_two = lax.psum_scatter(
        matmul_low("bc,hc->bh", grad_bottle_own, last_weight), AXIS, scatter_dimension=1, tiled=True
    )
    grad_pre_two = (grad_act_two * gelu_slope(pre_two)).astype(jnp.bfloat16)
    grad_second = matmul_low("bk,bh->kh", grad_pre_two, act_one[0])
    grad_act_one = lax.psum_scatter(
        matmul_low("bk,kh->bh", grad_pre_two, second_weight), AXIS, scatter_dimension=1, tiled=True
    )
    grad_pre_one = (grad_act_one * gelu_slope(pre_one)).astype(jnp.bfloat16)
    grad_first = matmul_low("bh,bd->hd", grad_pre_one, all_features)
    grad_features = lax.psum_scatter(
        matmul_low("bh,hd->bd", grad_pre_one, first_weight), AXIS, scatter_dimension=0, tiled=True
    )
    grad_hidden = jnp.concatenate([grad_first, grad_second], 1)
    next_centre = (
        CENTRE_MOMENTUM * centre
        + (1.0 - CENTRE_MOMENTUM) * jnp.sum(counted[:, None] * teacher_logits, 0) / loss_count
    )
    return (loss_sum, loss_count, grad_hidden, grad_last, grad_protos, grad_features, next_centre)


def head_fast(
    feature_rows,
    valid_mask,
    head_hidden,
    protos,
    teacher_hidden,
    teacher_protos,
    centre,
    part,
    last_all,
    devices,
):
    counted = valid_mask.astype(FULL)
    mask_row = jnp.pad(counted, (0, LANES - counted.size)).reshape(1, LANES)
    scalars, grad_hidden, grad_last, grad_protos, grad_feat, next_centre = head(
        feature_rows,
        head_hidden,
        teacher_hidden,
        part,
        last_all,
        protos,
        teacher_protos,
        centre[None],
        counted[:, None],
        mask_row,
        devices,
    )
    return (
        scalars[0, 0],
        scalars[0, 1],
        scalars,
        grad_hidden,
        grad_last.T,
        grad_protos,
        grad_feat,
        next_centre[0],
    )


TOKENS = 272
HALF_ROW = 256
SAVED = ("inputs", "normed", "joint", "mixed", "attended", "middle", "normed_two", "activated", "slope", "outer")


def saved_widths():
    return {
        "inputs": (D, FULL),
        "normed": (D, LOW),
        "joint": (3 * D, LOW),
        "mixed": (D, LOW),
        "attended": (D, LOW),
        "middle": (D, FULL),
        "normed_two": (D, LOW),
        "activated": (MLP, LOW),
        "slope": (MLP, LOW),
        "outer": (D, LOW),
    }


def unpack_blocks(weights, joint_out, output_out, cuts, depth):
    devices = weights.shape[0]
    joint_rows, output_rows = cuts[0], cuts[1] - cuts[0]
    group = 4
    for at in range(0, devices, group):
        blocks = [
            weights[slot_of(at + t, depth), 0 : cuts[1]].astype(FULL) for t in range(group)
        ]
        joint = jnp.concatenate([block[:joint_rows] for block in blocks], 0)
        output = jnp.concatenate([block[joint_rows:] for block in blocks], 0)
        joint_out[at * joint_rows : (at + group) * joint_rows] = joint.astype(LOW)
        output_out[at * output_rows : (at + group) * output_rows] = output.astype(LOW)


def weight_rows(weights, cuts, which, part, parts):
    per = weights.shape[0] // parts
    block = weights[part * per : (part + 1) * per, cuts[which] : cuts[which + 1]]
    return block.reshape(-1, block.shape[-1])


def chance(keys_half, queries, live):
    scores = jnp.where(live, dot_nt(keys_half, queries), -jnp.inf)
    grown = jnp.exp(scores - jnp.max(scores, 0, keepdims=True))
    return grown * (1.0 / jnp.sum(grown, 0, keepdims=True))


WIDE_TABLE = 1152
POSITION_AT = 640
VECTORS_AT = 1024


CLASS_ROWS = 16


def by_head(row):
    head = lax.broadcasted_iota(jnp.int32, (CLASS_ROWS, D), 0)
    lane = lax.broadcasted_iota(jnp.int32, (CLASS_ROWS, D), 1)
    return jnp.where(lax.shift_right_logical(lane, 6) == head, row, 0.0)


def tail_rows_of(row):
    at = lax.broadcasted_iota(jnp.int32, (TOKENS - HALF_ROW, D), 0)
    return jnp.where(at == 0, row, 0.0)


def head_halves(wide):
    lane = lax.broadcasted_iota(jnp.int32, wide.shape, 1)
    low_half = jnp.where(lane < HEAD_DIM, wide, 0.0)
    return low_half.astype(LOW), (wide - low_half).astype(LOW)


def live_keys(columns):
    return lax.broadcasted_iota(jnp.int32, (TOKENS, columns), 0) < SEQ


def table_rows(embedding):
    turned = embedding.T
    columns = turned.shape[0]
    patch = jnp.pad(turned[:, :PIX], ((0, 0), (0, POSITION_AT - PIX)))
    position = jnp.concatenate([turned[:, PIX + 1 : PIX + SEQ], turned[:, PIX : PIX + 1]], 1)
    position = jnp.pad(position, ((0, 0), (0, VECTORS_AT - POSITION_AT - SEQ)))
    layer_rows = turned[:, PIX + SEQ : PIX + SEQ + 6 * LAYERS].reshape(columns, LAYERS, 6)
    layer_rows = jnp.pad(layer_rows, ((0, 0), (0, 0), (0, 2))).reshape(columns, -1)
    tail_rows = turned[:, PIX + SEQ + 6 * LAYERS :]
    joint = jnp.concatenate([patch, position, layer_rows, tail_rows], 1)
    rows = -(-columns // 16) * 16
    joint = jnp.pad(joint, ((0, rows - columns), (0, WIDE_TABLE - joint.shape[1]))).astype(LOW)
    return jnp.concatenate([joint[:, at : at + D] for at in range(0, WIDE_TABLE, D)], 0)


PLAN = {
    -1: ((0, 0), (0, 1), (0, 2), (1, 0), (1, 1), (0, 3), (2, 0), (1, 2), (0, 4), (2, 1), (3, 0), (4, 0), (3, 1), (1, 3), (2, 2), (4, 1)),
    0: ((1, 4), (0, 5)),
    -2: ((2, 3), (3, 2), (4, 2)),
    1: ((2, 4), (3, 3)),
    2: ((4, 3), (3, 4), (1, 5), (0, 6)),
    3: ((4, 4),),
    4: ((2, 5),),
    5: ((3, 5), (1, 6), (0, 7)),
    6: ((4, 5),),
    7: ((2, 6),),
    8: ((3, 6), (1, 7), (0, 8)),
    9: ((4, 6),),
    10: ((2, 7),),
    11: ((3, 7), (1, 8), (0, 9)),
    12: ((4, 7),),
    13: ((2, 8),),
    14: ((3, 8), (1, 9)),
    15: ((4, 8),),
    16: ((2, 9),),
    17: ((3, 9),),
    -3: ((4, 9),),
}


def fetch_kernel(
    cuts,
    depth,
    patches_ref,
    table_ref,
    teacher_table_ref,
    layers_ref,
    teacher_layers_ref,
    last_ref,
    columns_ref,
    feat_ref,
    final_ref,
    vectors_out_ref,
    weights_out_ref,
    last_out_ref,
    part_ref,
    *rest,
):
    layer, model, image = (pl.program_id(at) for at in range(3))
    images = pl.num_programs(2)
    step = (layer * 2 + model) * images + image
    outs = dict(zip(SAVED, rest[: len(SAVED)]))
    (
        current,
        joint_weight,
        output_weight,
        weights_all,
        tables,
        turned,
        vectors_all,
        out_sem,
        part_own,
        part_sent,
        part_landed,
        part_die,
        *sems,
    ) = rest[len(SAVED) :]
    sources = (layers_ref, teacher_layers_ref)
    rows = layers_ref.shape[1]
    first = cuts[1]

    def layer_item(which, at, lower, size):
        return (sources[which].at[at], weights_all.at[which, at], lower, size)

    items = [
        (table_ref, tables.at[0], 0, table_ref.shape[0]),
        layer_item(0, 0, 0, first),
        layer_item(0, 0, first, rows - first),
        (teacher_table_ref, tables.at[1], 0, table_ref.shape[0]),
        layer_item(1, 0, 0, rows),
        layer_item(0, 1, 0, rows),
        layer_item(1, 1, 0, rows),
        layer_item(0, 2, 0, rows),
        layer_item(1, 2, 0, rows),
        (last_ref, last_out_ref, 0, last_ref.shape[0]),
    ]
    route = Route(depth, items, *sems)
    total = 8 * depth
    chips = total // 2
    chip = route.me // 2
    core = route.core

    def part_copy(at):
        peer = lax.rem(route.me + 2 * at, total)
        block = columns_ref.at[:, pl.ds(pl.multiple_of((peer // 2) * LANES, LANES), LANES)]
        return route.copy(
            block, part_ref.at[core, chip], part_sent.at[at], part_landed.at[at], peer
        )

    def part_mine():
        block = columns_ref.at[:, pl.ds(pl.multiple_of(chip * LANES, LANES), LANES)]
        return pltpu.make_async_copy(block, part_ref.at[core, chip], part_own.at[0])

    def part_across():
        return route.copy(
            part_ref.at[core], part_ref.at[core], part_die.at[0], part_die.at[1], route.partner
        )

    def out_copy(at):
        return pltpu.make_async_copy(weights_all.at[0, at], weights_out_ref.at[at], out_sem.at[at])

    def run(name):
        for word in PLAN[name]:
            route.act(*word)

    @pl.when(step == 0)
    def _():
        greet([lax.rem(route.me + 2 * at, total) for at in range(1, chips)] + [route.partner])
        run(-1)

    def set_up(which):
        columns = D // total
        block_rows = table_ref.shape[0] // (WIDE_TABLE // D)
        group = 4
        for at in range(0, total, group):
            for block in range(WIDE_TABLE // D):
                lower = block * block_rows
                pieces = [
                    tables[which, slot_of(at + t, depth), lower : lower + block_rows].astype(FULL)[
                        :columns
                    ]
                    for t in range(group)
                ]
                turned[at * columns : (at + group) * columns, block * D : (block + 1) * D] = (
                    jnp.concatenate(pieces, 0).astype(LOW)
                )
        vectors = turned[:, VECTORS_AT:WIDE_TABLE].astype(FULL).T
        vectors_all[which] = vectors[:32]
        position = turned[:, POSITION_AT:VECTORS_AT].astype(FULL).T[:TOKENS]
        row = lax.broadcasted_iota(jnp.int32, (TOKENS, D), 0)
        tail = 8 * LAYERS
        extra = jnp.where(
            row < HALF_ROW,
            vectors[tail : tail + 1],
            jnp.where(row == HALF_ROW, vectors[tail + 1 : tail + 2], 0.0),
        )
        start = position + extra
        for at in range(feat_images):
            current[which, at, :HALF_ROW] = start[:HALF_ROW] + dot_nt(
                patches_ref[at], turned[:, :PIX]
            )
            current[which, at, HALF_ROW:] = start[HALF_ROW:]

    feat_images = patches_ref.shape[0]
    for at in range(18):

        @pl.when(step == at)
        def _(at=at):
            run(at)
            if at == 0:
                set_up(0)
                vectors_out_ref[...] = vectors_all[0]
            if at == 3:
                set_up(1)
            if at == 3:
                out_copy(0).start()
            if at == 6:
                out_copy(1).start()
            if at == 11:
                part_mine().start()
                for other in range(1, chips):
                    part_copy(other).start()
            if at == 12:
                out_copy(2).start()
            if at == 16:
                part_mine().wait()
                for other in range(1, chips):
                    part_copy(other).wait_recv()
                part_across().start()

    weights = weights_all.at[model, layer]

    @pl.when(image == 0)
    def _():
        unpack_blocks(weights, joint_weight, output_weight, cuts, depth)

    vectors = vectors_all[model, pl.ds(pl.multiple_of(layer * 8, 8), 8), :]
    live = live_keys(HALF_ROW)

    def attend(save):
        def keep(name, value):
            if save:
                outs[name][0, 0] = value

        inputs = current[model, image]
        keep("inputs", inputs)
        normed = layer_norm(inputs, vectors[0:1], vectors[1:2]).astype(LOW)
        keep("normed", normed)
        joint = dot_nt(normed, joint_weight[...])
        rounded = joint.astype(LOW)
        keep("joint", rounded)
        queries = (rounded[:, :D].astype(FULL) * HEAD_DIM ** (-0.5)).astype(LOW)
        keys_in, values_in = rounded[:, D : 2 * D], rounded[:, 2 * D :]
        values = joint[:, 2 * D :].T.astype(LOW)
        turned_heads = []
        for pair in range(D // LANES):
            columns = slice(pair * LANES, (pair + 1) * LANES)
            for half, keys_half in enumerate(head_halves(keys_in[:, columns].astype(FULL))):
                lower = pair * LANES + half * HEAD_DIM
                share = chance(keys_half, queries[:HALF_ROW, columns], live).astype(LOW)
                turned_heads.append(dot_nn(values[lower : lower + HEAD_DIM], share))
        class_query = by_head(queries[HALF_ROW:].astype(FULL)[:1]).astype(LOW)
        class_share = chance(keys_in, class_query, live_keys(CLASS_ROWS)).astype(LOW)
        class_mixed = jnp.sum(by_head(dot_tn(class_share, values_in)), 0, keepdims=True)
        mixed = jnp.concatenate(
            [
                jnp.concatenate(turned_heads, 0).T.astype(LOW),
                tail_rows_of(class_mixed).astype(LOW),
            ],
            0,
        )
        keep("mixed", mixed)
        attended = dot_nt(mixed, output_weight[...])
        keep("attended", attended.astype(LOW))
        middle = inputs + vectors[4:5] * attended
        keep("middle", middle)
        current[model, image] = middle

    def perceive(save):
        def keep(name, value):
            if save:
                outs[name][0, 0] = value

        middle = current[model, image]
        normed_two = layer_norm(middle, vectors[2:3], vectors[3:4]).astype(LOW)
        keep("normed_two", normed_two)
        outer = jnp.zeros((TOKENS, D), FULL)
        parts = MLP // D
        for part in range(parts):
            inner = dot_nt(normed_two, weight_rows(weights, cuts, 1, part, parts))
            spread_half = 0.5 * (1.0 + lax.erf(inner * ROOT_HALF))
            activated = (inner * spread_half).astype(LOW)
            if save:
                outs["activated"][0, 0, :, part * D : (part + 1) * D] = activated
                slope = spread_half + inner * jnp.exp(-0.5 * inner * inner) * DENSITY_SCALE
                outs["slope"][0, 0, :, part * D : (part + 1) * D] = slope.astype(LOW)
            outer = outer + dot_nn(activated, weight_rows(weights, cuts, 2, part, parts))
        keep("outer", outer.astype(LOW))
        result = middle + vectors[5:6] * outer
        current[model, image] = result
        final = result[HALF_ROW : HALF_ROW + 8]
        final_ref[model, image] = final
        tail = 8 * LAYERS
        feat_ref[model, image] = layer_norm(
            final, vectors_all[model, tail + 2 : tail + 3], vectors_all[model, tail + 3 : tail + 4]
        )

    @pl.when(model == 0)
    def _():
        attend(True)

    @pl.when(model == 1)
    def _():
        attend(False)

    @pl.when(step == 0)
    def _():
        run(-2)

    @pl.when(model == 0)
    def _():
        perceive(True)

    @pl.when(model == 1)
    def _():
        perceive(False)

    @pl.when(step == 17)
    def _():
        run(-3)
        for at in range(len(items)):
            route.act(5, at)
        for at in range(LAYERS):
            out_copy(at).wait()
        across = part_across()
        across.wait_recv()
        across.wait_send()
        for other in range(1, chips):
            part_copy(other).wait_send()


def fetch_forward(patches, embedding, teacher_embedding, layers, teacher_layers, head_last, teacher_last, head_hidden, devices):
    images = patches.shape[0]
    depth = devices // 8
    rows = layers.shape[1]
    cuts = [lower for lower, upper in layer_bounds(devices)][1:] + [rows]
    shape = jax.ShapeDtypeStruct
    vmem = pl.BlockSpec(memory_space=pltpu.VMEM)
    anywhere = pl.BlockSpec(memory_space=pl.ANY)

    table = table_rows(embedding)
    last = jnp.concatenate([head_last, teacher_last], 1).T.astype(LOW)
    across = last.shape[1] // 2
    last = jnp.concatenate([last[:, :across], last[:, across:]], 0)
    columns = head_hidden[:, D:].astype(LOW)
    outs = [shape((2, images, 8, D), FULL)] * 2
    specs = [vmem] * 2
    outs += [
        shape((32, D), FULL),
        shape((LAYERS, devices, rows, D), LOW),
        shape((devices,) + last.shape, LOW),
        shape((2, devices // 2, columns.shape[0], LANES), LOW),
    ]
    specs += [vmem, anywhere, anywhere, anywhere]
    for name in SAVED:
        width, kind = saved_widths()[name]
        outs.append(shape((LAYERS, images, TOKENS, width), kind))
        specs.append(
            pl.BlockSpec(
                (1, 1, TOKENS, width),
                lambda layer, model, image: (layer, jnp.where(model == 0, image, images - 1), 0, 0),
            )
        )
    count = 10
    dma = pltpu.SemaphoreType.DMA
    return pl.pallas_call(
        functools.partial(fetch_kernel, cuts, depth),
        grid=(LAYERS, 2, images),
        out_shape=outs,
        in_specs=[vmem] + [anywhere] * 6,
        out_specs=specs,
        scratch_shapes=[
            pltpu.VMEM((2, images, TOKENS, D), FULL),
            pltpu.VMEM((3 * D, D), LOW),
            pltpu.VMEM((D, D), LOW),
            pltpu.VMEM((2, LAYERS, devices, rows, D), LOW),
            pltpu.VMEM((2, devices) + table.shape, LOW),
            pltpu.VMEM((D, WIDE_TABLE), LOW),
            pltpu.VMEM((2, 32, D), FULL),
            dma((LAYERS,)),
            dma((1,)),
            dma((devices // 2,)),
            dma((devices // 2,)),
            dma((2,)),
        ]
        + route_sems(count, depth),
        compiler_params=params(1, 60 << 20),
        name="fetch_forward",
    )(
        patches,
        table,
        table_rows(teacher_embedding),
        layers.astype(LOW),
        teacher_layers.astype(LOW),
        last,
        columns,
    )


class Reduce:
    def __init__(self, depth, chunks, sources, buffers, sems):
        self.depth, self.chunks, self.sources = depth, chunks, sources
        self.die_buf, self.d_buf, self.x_buf, self.y_buf, self.z_buf = buffers
        self.die_sent, self.die_landed, self.near_sent, self.near_landed, self.z_sent, self.z_landed = sems
        me = lax.axis_index(AXIS)
        self.me = me
        self.total = 8 * depth
        core = lax.rem(me, 2)
        x_at = lax.rem(me // 2, 2)
        y_at = lax.rem(me // 4, 2)
        self.z_at = me // 8
        self.partner = me + 1 - 2 * core
        self.to_x = me + 2 - 4 * x_at
        self.to_y = me + 4 - 8 * y_at
        places = [(y_at, x_at), (y_at, 1 - x_at), (1 - y_at, x_at), (1 - y_at, 1 - x_at)]
        self.starts = [((y * 2 + x) * 2 + core) * depth for y, x in places]
        self.partner_starts = [((y * 2 + x) * 2 + 1 - core) * depth for y, x in places]

    def copy(self, source, target, sent, landed, device):
        return pltpu.make_async_remote_copy(
            src_ref=source,
            dst_ref=target,
            send_sem=sent,
            recv_sem=landed,
            device_id=(device,),
            device_id_type=MESH,
        )

    def half(self, k):
        return ((self.chunks[k][1] // 2 + 15) // 16) * 16

    def die(self, k, rel):
        lower, size = self.chunks[k]
        return self.copy(
            self.sources[k].at[pl.ds(self.partner_starts[rel], self.depth)],
            self.die_buf.at[pl.ds(rel * self.depth, self.depth), pl.ds(lower, size)],
            self.die_sent.at[k, rel],
            self.die_landed.at[k, rel],
            self.partner,
        )

    def near(self, k, which):
        lower, size = self.chunks[k]
        half = self.half(k)
        rel, start, length, target, device = [
            (3, lower, half, self.d_buf, self.to_x),
            (3, lower + half, size - half, self.d_buf, self.to_y),
            (1, lower, size, self.x_buf, self.to_x),
            (2, lower, size, self.y_buf, self.to_y),
        ][which]
        return self.copy(
            self.die_buf.at[pl.ds(rel * self.depth, self.depth), pl.ds(start, length)],
            target.at[:, pl.ds(start, length)],
            self.near_sent.at[k, which],
            self.near_landed.at[k, which],
            device,
        )

    def deep(self, k, step):
        lower, size = self.chunks[k]
        return self.copy(
            self.die_buf.at[lax.rem(self.z_at + step, self.depth), pl.ds(lower, size)],
            self.z_buf.at[self.z_at, pl.ds(lower, size)],
            self.z_sent.at[k, step],
            self.z_landed.at[k, step],
            lax.rem(self.me + 8 * step, self.total),
        )

    def pair_sum(self, k, rel, z_pos, first, length):
        lower, size = self.chunks[k]
        return self.sources[k][
            self.starts[rel] + z_pos, first - lower : first - lower + length
        ].astype(FULL) + self.die_buf[rel * self.depth + z_pos, first : first + length].astype(FULL)

    def begin(self, k):
        for rel in (3, 1, 2, 0):
            self.die(k, rel).start()

    def one(self, k):
        lower, size = self.chunks[k]
        self.die(k, 3).wait_recv()
        for z_pos in range(self.depth):
            self.die_buf[3 * self.depth + z_pos, lower : lower + size] = self.pair_sum(
                k, 3, z_pos, lower, size
            ).astype(LOW)
        self.near(k, 0).start()
        self.near(k, 1).start()

    def two(self, k):
        lower, size = self.chunks[k]
        half = self.half(k)
        first, second = (lower, half), (lower + half, size - half)
        for rel, which, arrived, helped, plain in ((1, 2, 1, second, first), (2, 3, 0, first, second)):
            self.die(k, rel).wait_recv()
            self.near(k, arrived).wait_recv()
            for z_pos in range(self.depth):
                at = rel * self.depth + z_pos
                self.die_buf[at, plain[0] : plain[0] + plain[1]] = self.pair_sum(
                    k, rel, z_pos, *plain
                ).astype(LOW)
                self.die_buf[at, helped[0] : helped[0] + helped[1]] = (
                    self.pair_sum(k, rel, z_pos, *helped)
                    + self.d_buf[z_pos, helped[0] : helped[0] + helped[1]].astype(FULL)
                ).astype(LOW)
            self.near(k, which).start()

    def three(self, k):
        lower, size = self.chunks[k]
        self.die(k, 0).wait_recv()
        self.near(k, 2).wait_recv()
        self.near(k, 3).wait_recv()
        for z_pos in range(self.depth):
            self.die_buf[z_pos, lower : lower + size] = (
                self.pair_sum(k, 0, z_pos, lower, size)
                + self.x_buf[z_pos, lower : lower + size].astype(FULL)
                + self.y_buf[z_pos, lower : lower + size].astype(FULL)
            ).astype(LOW)
        for step in range(1, self.depth):
            self.deep(k, step).start()

    def four(self, k):
        lower, size = self.chunks[k]
        for step in range(1, self.depth):
            self.deep(k, step).wait_recv()
        value = self.die_buf[self.z_at, lower : lower + size].astype(FULL)
        for step in range(1, self.depth):
            value = value + self.z_buf[
                lax.rem(self.z_at + step, self.depth), lower : lower + size
            ].astype(FULL)
        return value

    def sent(self, k, die_too):
        if die_too:
            for rel in range(4):
                self.die(k, rel).wait_send()
        for which in range(4):
            self.near(k, which).wait_send()
        for step in range(1, self.depth):
            self.deep(k, step).wait_send()


PER_LAYER = ("normed", "mixed", "normed_two", "activated")


def backward_kernel(cuts, bounds, depth, *refs):
    (
        squares_ref,
        stats_ref,
        bases_ref,
        bases_low_ref,
        patches_ref,
        weights_ref,
        vectors_ref,
        final_ref,
        grad_feat_ref,
    ) = refs[:9]
    saved = dict(zip(SAVED, refs[9 : 9 + len(SAVED)]))
    (
        own_ref,
        norm_ref,
        next_stats_ref,
        basis_ref,
        bases_all_ref,
        grad_now,
        joint_weight,
        output_weight,
        grad_outer_all,
        grad_inner_all,
        grad_attended_all,
        grad_joint_all,
        grad_patch,
        grad_start,
        grad_rows,
        packets,
        table_packet,
        die_buf,
        d_buf,
        x_buf,
        y_buf,
        z_buf,
        stat_buf,
        square_out,
        square_all,
        segs,
        gram_buf,
        die_sent,
        die_landed,
        near_sent,
        near_landed,
        z_sent,
        z_landed,
        stat_sent,
        stat_landed,
        gram_sent,
        gram_landed,
        square_sent,
        square_landed,
        *sems,
    ) = refs[9 + len(SAVED) :]
    step, image = pl.program_id(0), pl.program_id(1)
    images = final_ref.shape[1]
    route = Route(depth, [(bases_low_ref, bases_all_ref, 0, bases_low_ref.shape[0])], *sems)
    now = step * images + image
    layer_rows = cuts[3]
    chunks = [(layer * layer_rows, layer_rows) for layer in reversed(range(LAYERS))]
    chunks.append((LAYERS * layer_rows, table_packet.shape[1]))
    count = len(chunks)
    sources = [packets.at[k % 2] for k in range(LAYERS)] + [table_packet]
    ring = Reduce(
        depth,
        chunks,
        sources,
        (die_buf, d_buf, x_buf, y_buf, z_buf),
        (die_sent, die_landed, near_sent, near_landed, z_sent, z_landed),
    )
    me = ring.me
    total = ring.total
    core = lax.rem(me, 2)
    chip = me // 2
    matrices = stats_ref.shape[0]
    own_rows = stats_ref.shape[1]
    segment_rows = segs.shape[2]
    is_gram = (core == 0) & (chip < matrices)
    everyone = [lax.rem(me + at, total) for at in range(1, total)]

    def stat_copy(at, matrix):
        source = (stats_ref, bases_ref)[at]
        return ring.copy(
            source.at[matrix],
            stat_buf.at[at, me],
            stat_sent.at[at, matrix],
            stat_landed.at[at, me],
            gram_device(matrix),
        )

    def stat_own(at, matrix):
        source = (stats_ref, bases_ref)[at]
        return pltpu.make_async_copy(source.at[matrix], stat_buf.at[at, me], stat_landed.at[at, me])

    def gram_copy(matrix):
        return ring.copy(
            segs.at[matrix // 4, matrix % 4],
            gram_buf.at[me],
            gram_sent.at[matrix],
            gram_landed.at[me],
            gram_device(matrix),
        )

    def finish(k):
        lower, size = chunks[k]
        value = ring.four(k)
        own_ref[lower : lower + size] = value
        if k == count - 1:
            return
        layer = lower // layer_rows
        for segment, (low_row, high_row) in enumerate(bounds):
            piece = value[low_row:high_row].astype(LOW)
            if high_row - low_row < segment_rows:
                blank = jnp.zeros((segment_rows - (high_row - low_row), value.shape[1]), LOW)
                piece = jnp.concatenate([piece, blank], 0)
            matrix = 4 * layer + segment
            segs[layer, segment] = piece

            @pl.when(me != gram_device(matrix))
            def _(matrix=matrix):
                gram_copy(matrix).start()

    @pl.when(now == 0)
    def _():
        greet(everyone)
        route.act(0, 0)
        for matrix in range(matrices):

            @pl.when(me != gram_device(matrix))
            def _(matrix=matrix):
                stat_copy(0, matrix).start()
                stat_copy(1, matrix).start()

            @pl.when(me == gram_device(matrix))
            def _(matrix=matrix):
                stat_own(0, matrix).start()
                stat_own(1, matrix).start()

        grad_rows[...] = jnp.zeros(grad_rows.shape, FULL)
        grad_patch[...] = jnp.zeros(grad_patch.shape, FULL)
        grad_start[...] = jnp.zeros(grad_start.shape, FULL)

    @pl.when(now == 1)
    def _():
        route.act(1, 0)

    @pl.when(now == images)
    def _():
        ring.one(0)

    @pl.when(now == images + 1)
    def _():
        route.act(3, 0)
        ring.two(0)

    @pl.when(now == 2 * images)
    def _():
        ring.one(1)
        route.act(4, 0)
        ring.three(0)

    @pl.when(now == 2 * images + 1)
    def _():
        ring.two(1)
        finish(0)

    weights = weights_ref.at[0]
    vectors = vectors_ref[pl.ds(pl.multiple_of((LAYERS - 1 - step) * 8, 8), 8), :]
    tail = 8 * LAYERS

    @pl.when(image == 0)
    def _():
        unpack_blocks(weights, joint_weight, output_weight, cuts, depth)

    @pl.when(step == 0)
    def _():
        first = lax.broadcasted_iota(jnp.int32, (8, D), 0) == 0
        given = jnp.where(first, grad_feat_ref[pl.ds(core * images + image, 1), :], 0.0)
        grad_class, grad_gain, grad_shift = norm_back(
            final_ref[0, image], vectors_ref[tail + 2 : tail + 3], given
        )
        grad_rows[tail + 2 : tail + 3] += grad_gain[None]
        grad_rows[tail + 3 : tail + 4] += grad_shift[None]
        grad_now[image] = jnp.zeros((TOKENS, D), FULL)
        grad_now[image, HALF_ROW : HALF_ROW + 8] = jnp.where(first, grad_class, 0.0)

    rows = pl.ds(pl.multiple_of(image * TOKENS, 16), TOKENS)
    grad_result = grad_now[image]
    grad_outer = (vectors[5:6] * grad_result).astype(LOW)
    grad_outer_all[rows, :] = grad_outer
    grad_scale_two = jnp.sum(grad_result * saved["outer"][0, 0].astype(FULL), 0, keepdims=True)
    parts = MLP // D
    grad_normed_two = jnp.zeros((TOKENS, D), FULL)
    for part in range(parts):
        columns = slice(part * D, (part + 1) * D)
        grad_activated = dot_nt(grad_outer, weight_rows(weights, cuts, 2, part, parts))
        grad_inner = (grad_activated * saved["slope"][0, 0, :, columns].astype(FULL)).astype(LOW)
        grad_inner_all[rows, columns] = grad_inner
        grad_normed_two = grad_normed_two + dot_nn(
            grad_inner, weight_rows(weights, cuts, 1, part, parts)
        )
    grad_middle_norm, grad_gain_two, grad_shift_two = norm_back(
        saved["middle"][0, 0], vectors[2:3], grad_normed_two
    )
    grad_middle = grad_result + grad_middle_norm
    grad_attended = (vectors[4:5] * grad_middle).astype(LOW)
    grad_attended_all[rows, :] = grad_attended
    grad_scale_one = jnp.sum(grad_middle * saved["attended"][0, 0].astype(FULL), 0, keepdims=True)
    grad_mixed = dot_nn(grad_attended, output_weight[...]).astype(LOW)
    live = live_keys(HALF_ROW)
    rounded = saved["joint"][0, 0]
    queries = (rounded[:, :D].astype(FULL) * HEAD_DIM ** (-0.5)).astype(LOW)
    keys_in, values_in = rounded[:, D : 2 * D], rounded[:, 2 * D :]
    keys_turned = keys_in.astype(FULL).T.astype(LOW)
    turned, grad_keys, grad_values = [], [], []
    low_half = lax.broadcasted_iota(jnp.int32, (TOKENS, LANES), 1) < HEAD_DIM
    for pair in range(D // LANES):
        columns = slice(pair * LANES, (pair + 1) * LANES)
        pair_queries, grad_head = queries[:HALF_ROW, columns], grad_mixed[:HALF_ROW, columns]
        keys_halves = head_halves(keys_in[:, columns].astype(FULL))
        values_halves = head_halves(values_in[:, columns].astype(FULL))
        both_keys, both_values = [], []
        for half in range(2):
            lower = pair * LANES + half * HEAD_DIM
            share = chance(keys_halves[half], pair_queries, live)
            grad_share = dot_nt(values_halves[half], grad_head)
            both_values.append(dot_nn(share.astype(LOW), grad_head))
            grad_scores = (
                share * (grad_share - jnp.sum(share * grad_share, 0, keepdims=True))
            ).astype(LOW)
            both_keys.append(dot_nn(grad_scores, pair_queries))
            turned.append(dot_nn(keys_turned[lower : lower + HEAD_DIM], grad_scores))
        grad_keys.append(jnp.where(low_half, both_keys[0], both_keys[1]))
        grad_values.append(jnp.where(low_half, both_values[0], both_values[1]))
    class_query = by_head(queries[HALF_ROW:].astype(FULL)[:1]).astype(LOW)
    class_grad = by_head(grad_mixed[HALF_ROW:].astype(FULL)[:1]).astype(LOW)
    share = chance(keys_in, class_query, live_keys(CLASS_ROWS))
    grad_share = dot_nt(values_in, class_grad)
    grad_scores = (share * (grad_share - jnp.sum(share * grad_share, 0, keepdims=True))).astype(LOW)
    class_row = jnp.sum(by_head(dot_tn(grad_scores, keys_in)), 0, keepdims=True)
    grad_queries = jnp.concatenate(
        [jnp.concatenate(turned, 0).T, tail_rows_of(class_row)], 0
    ) * HEAD_DIM ** (-0.5)
    grad_joint_all[rows, :D] = grad_queries.astype(LOW)
    grad_joint_all[rows, D : 2 * D] = (
        jnp.concatenate(grad_keys, 1) + dot_nn(grad_scores, class_query)
    ).astype(LOW)
    grad_joint_all[rows, 2 * D :] = (
        jnp.concatenate(grad_values, 1) + dot_nn(share.astype(LOW), class_grad)
    ).astype(LOW)
    grad_normed = dot_nn(grad_joint_all[rows, :], joint_weight[...])
    grad_input_norm, grad_gain_one, grad_shift_one = norm_back(
        saved["inputs"][0, 0], vectors[0:1], grad_normed
    )
    grad_input = grad_middle + grad_input_norm
    grad_now[image] = grad_input
    added = jnp.concatenate(
        [
            grad_gain_one[None],
            grad_shift_one[None],
            grad_gain_two[None],
            grad_shift_two[None],
            grad_scale_one,
            grad_scale_two,
            jnp.zeros((2, D), FULL),
        ],
        0,
    )
    grad_rows[pl.ds(pl.multiple_of((LAYERS - 1 - step) * 8, 8), 8), :] += added

    @pl.when(step == LAYERS - 1)
    def _():
        grad_patch[:, :PIX] += dot_tn(grad_input[:HALF_ROW].astype(LOW), patches_ref[image])
        grad_start[:TOKENS] += grad_input
        grad_rows[tail : tail + 1] += jnp.sum(grad_input[:HALF_ROW], 0, keepdims=True)
        grad_rows[tail + 1 : tail + 2] += grad_input[HALF_ROW : HALF_ROW + 1]

    def pack(packet):
        def flat(name):
            value = saved[name][0]
            return value.reshape(-1, value.shape[-1])

        per = cuts[0], cuts[1] - cuts[0], cuts[2] - cuts[1], cuts[3] - cuts[2]
        groups = 4
        each = total // groups
        for at in range(groups):
            first = at * each
            joint_rows = dot_tn(
                grad_joint_all[:, first * per[0] : (first + each) * per[0]], flat("normed")
            )
            output_rows = dot_tn(
                grad_attended_all[:, first * per[1] : (first + each) * per[1]], flat("mixed")
            )
            inner_rows = dot_tn(
                grad_inner_all[:, first * per[2] : (first + each) * per[2]], flat("normed_two")
            ).astype(LOW)
            outer_rows = dot_tn(
                saved["activated"][0, :, :, first * per[3] : (first + each) * per[3]].reshape(
                    -1, each * per[3]
                ),
                grad_outer_all[...],
            ).astype(LOW)
            for t in range(each):
                joined_rows = jnp.concatenate(
                    [
                        joint_rows[t * per[0] : (t + 1) * per[0]],
                        output_rows[t * per[1] : (t + 1) * per[1]],
                    ],
                    0,
                )
                packet[slot_of(first + t, depth), : cuts[1]] = joined_rows.astype(LOW)
                packet[first + t, cuts[1] : cuts[2]] = inner_rows[t * per[2] : (t + 1) * per[2]]
                packet[first + t, cuts[2] : cuts[3]] = outer_rows[t * per[3] : (t + 1) * per[3]]

    @pl.when(now == images - 1)
    def _():
        route.act(2, 0)

    @pl.when((image == images - 1) & (step == LAYERS - 1))
    def _():
        ring.three(1)
        for rel in range(4):
            ring.die(0, rel).wait_send()

    @pl.when(image == images - 1)
    def _():
        pack(packets.at[lax.rem(step, 2)])

    for k in range(LAYERS - 1):

        @pl.when((image == images - 1) & (step == k))
        def _(k=k):
            ring.begin(k)

    @pl.when((image == images - 1) & (step == LAYERS - 1))
    def _():
        last, table = LAYERS - 1, LAYERS
        ring.begin(last)
        ring.one(last)
        blank = jnp.zeros((LANES - 32, D), FULL)
        turned_rows = jnp.concatenate([grad_rows[...], blank], 0).T
        turned = [grad_patch[:, :D], None, None]
        turned_start = grad_start[...].T
        left = VECTORS_AT - POSITION_AT
        turned[1] = jnp.concatenate([grad_patch[:, D:], turned_start[:, : 2 * D - POSITION_AT]], 1)
        turned[2] = jnp.concatenate([turned_start[:, 2 * D - POSITION_AT : left], turned_rows], 1)
        columns = D // total
        for block in range(3):
            for device in range(total):
                piece = turned[block][device * columns : (device + 1) * columns]
                piece = jnp.concatenate([piece, jnp.zeros((16 - columns, D), FULL)], 0)
                table_packet[slot_of(device, depth), 16 * block : 16 * block + 16] = piece.astype(LOW)
        ring.begin(table)
        ring.one(table)
        ring.two(last)
        finish(1)
        ring.two(table)
        ring.three(last)
        ring.three(table)
        finish(last)
        finish(table)

        own = own_ref[...]
        lane8 = lax.broadcasted_iota(jnp.int32, (8, LANES), 1)
        squares = jnp.sum(own * own) + jnp.sum(jnp.where(lane8 == 2, squares_ref[...], 0.0)) / 8.0
        square_out[...] = jnp.full((8, LANES), squares)
        square_all[me] = square_out[...]
        copies = [
            push(square_out, square_all.at[me], square_sent.at[at], square_landed.at[at], peer)
            for at, peer in enumerate(everyone)
        ]

        @pl.when(is_gram)
        def _():
            for matrix in range(matrices):

                @pl.when(matrix == chip)
                def _(matrix=matrix):
                    gram_buf[me] = segs[matrix // 4, matrix % 4]

            for source in range(total):
                for at in range(2):
                    view = stat_buf.at[at, source]
                    pltpu.make_async_copy(view, view, stat_landed.at[at, source]).wait()

                @pl.when(source != me)
                def _(source=source):
                    pltpu.make_async_copy(
                        gram_buf.at[source], gram_buf.at[source], gram_landed.at[source]
                    ).wait()

            basis_ref[...] = stat_buf[1]
            blocks = gram_buf[...].reshape(total * segment_rows, gram_buf.shape[2])
            gram = dot_tn(blocks, blocks)
            for source in range(total):
                next_stats_ref[source] = gram[source * own_rows : (source + 1) * own_rows]

        @pl.when(jnp.logical_not(is_gram))
        def _():
            next_stats_ref[...] = jnp.zeros(next_stats_ref.shape, FULL)
            basis_ref[...] = jnp.zeros(basis_ref.shape, FULL)
            stat_buf[0] = jnp.zeros(stat_buf.shape[1:], FULL)

        for copy in copies:
            copy.wait_recv()
        norm = jnp.sqrt(jnp.sum(square_all[...], 0))
        norm_ref[...] = norm
        clip = jnp.minimum(1.0, CLIP_MAX / (norm + 1e-06))[:1, :1]
        scale = (1.0 - BETA_STAT) * (clip * clip)
        for source in range(total):
            next_stats_ref[source] = BETA_STAT * stat_buf[0, source] + scale * next_stats_ref[source]

        route.act(5, 0)
        for copy in copies:
            copy.wait_send()
        for k in range(count):
            ring.sent(k, k != 0)
        for matrix in range(matrices):

            @pl.when(me != gram_device(matrix))
            def _(matrix=matrix):
                stat_copy(0, matrix).wait_send()
                stat_copy(1, matrix).wait_send()
                gram_copy(matrix).wait_send()


def backward(
    squares, patches, vectors, blocks, final, grad_feat, saved, stats, bases, bases_low, devices
):
    images = patches.shape[0]
    depth = devices // 8
    bounds = layer_bounds(devices)
    layer_rows = blocks.shape[2]
    cuts = [lower for lower, upper in bounds][1:] + [layer_rows]
    matrices, own_rows = stats.shape[:2]
    segment_rows = -(-max(high - low for low, high in bounds) // 16) * 16
    table_size = 3 * (-(-(D // devices) // 16) * 16)
    rows = LAYERS * layer_rows + table_size
    shape = jax.ShapeDtypeStruct
    dma = pltpu.SemaphoreType.DMA
    vmem = pl.BlockSpec(memory_space=pltpu.VMEM)
    anywhere = pl.BlockSpec(memory_space=pl.ANY)

    def of_layer(*dims):
        return pl.BlockSpec(
            (1,) + dims, lambda step, image: (LAYERS - 1 - step,) + (0,) * len(dims)
        )

    def of_saved(name):
        width = saved_widths()[name][0]
        if name in PER_LAYER:
            return of_layer(images, TOKENS, width)
        return pl.BlockSpec(
            (1, 1, TOKENS, width), lambda step, image: (LAYERS - 1 - step, image, 0, 0)
        )

    all_rows = images * TOKENS
    count = LAYERS + 1
    return pl.pallas_call(
        functools.partial(backward_kernel, cuts, bounds, depth),
        grid=(LAYERS, images),
        out_shape=(
            shape((rows, D), FULL),
            shape((8, LANES), FULL),
            shape((devices, own_rows, D), FULL),
            shape((devices, own_rows, D), FULL),
            shape((devices,) + bases_low.shape, LOW),
        ),
        in_specs=[
            vmem,
            anywhere,
            anywhere,
            anywhere,
            vmem,
            of_layer(*blocks.shape[1:]),
            vmem,
            vmem,
            vmem,
        ]
        + [of_saved(name) for name in SAVED],
        out_specs=(vmem,) * 4 + (anywhere,),
        scratch_shapes=[
            pltpu.VMEM((images, TOKENS, D), FULL),
            pltpu.VMEM((3 * D, D), LOW),
            pltpu.VMEM((D, D), LOW),
            pltpu.VMEM((all_rows, D), LOW),
            pltpu.VMEM((all_rows, MLP), LOW),
            pltpu.VMEM((all_rows, D), LOW),
            pltpu.VMEM((all_rows, 3 * D), LOW),
            pltpu.VMEM((D, POSITION_AT), FULL),
            pltpu.VMEM((D, D), FULL),
            pltpu.VMEM((32, D), FULL),
            pltpu.VMEM((2, devices, layer_rows, D), LOW),
            pltpu.VMEM((devices, table_size, D), LOW),
            pltpu.VMEM((4 * depth, rows, D), LOW),
            pltpu.VMEM((depth, rows, D), LOW),
            pltpu.VMEM((depth, rows, D), LOW),
            pltpu.VMEM((depth, rows, D), LOW),
            pltpu.VMEM((depth, rows, D), LOW),
            pltpu.VMEM((2, devices, own_rows, D), FULL),
            pltpu.VMEM((8, LANES), FULL),
            pltpu.VMEM((devices, 8, LANES), FULL),
            pltpu.VMEM((LAYERS, 4, segment_rows, D), LOW),
            pltpu.VMEM((devices, segment_rows, D), LOW),
            dma((count, 4)),
            dma((count, 4)),
            dma((count, 4)),
            dma((count, 4)),
            dma((count, depth)),
            dma((count, depth)),
            dma((2, matrices)),
            dma((2, devices)),
            dma((matrices,)),
            dma((devices,)),
            dma((devices - 1,)),
            dma((devices - 1,)),
        ]
        + route_sems(1, depth),
        compiler_params=params(3, 63 << 20),
        name="backward",
    )(squares, stats, bases, bases_low, patches, blocks, vectors, final, grad_feat, *saved)


def own_table(rows, columns):
    joint = rows.reshape(3, -1, D)[:, :columns].transpose(1, 0, 2).reshape(columns, -1)
    position = joint[:, POSITION_AT : POSITION_AT + SEQ]
    layer_rows = joint[:, VECTORS_AT : VECTORS_AT + 8 * LAYERS].reshape(columns, LAYERS, 8)
    return jnp.concatenate(
        [
            joint[:, :PIX],
            position[:, SEQ - 1 :],
            position[:, : SEQ - 1],
            layer_rows[:, :, :6].reshape(columns, -1),
            joint[:, VECTORS_AT + 8 * LAYERS : VECTORS_AT + 8 * LAYERS + 4],
        ],
        1,
    ).T


def tail_fast(
    gathered,
    layer_stats,
    layer_bases,
    owners,
    embedding,
    layers,
    layers_first,
    layers_second,
    teacher_layers,
    devices,
):
    own, norm, full_stats, full_bases, bases_all = gathered
    own_rows = layer_stats.shape[2]
    matrices = owners.shape[0]
    count = layers.shape[0] * layers.shape[1]
    layer_outs = soap(
        norm,
        own[:count],
        bases_all,
        layers,
        layers_first,
        layers_second,
        teacher_layers,
        layer_bounds(devices),
    )
    grad_embed = own_table(own[count:], embedding.shape[1])
    stats_own, bases_own = renew_own(full_stats, full_bases, matrices)
    bases_own = jnp.where(
        owners[:, None, None] >= 0, bases_own, layer_bases.reshape(matrices, own_rows, D)
    )
    return (
        norm[0, 0],
        grad_embed,
        layer_outs,
        stats_own.reshape(layer_stats.shape),
        bases_own.reshape(layer_bases.shape),
    )


def split_dot(left, basis, contract):
    high = left.astype(LOW)
    rest = (left - high.astype(FULL)).astype(LOW)
    dims = (contract, ((), ()))
    return lax.dot_general(high, basis, dims, preferred_element_type=FULL) + lax.dot_general(
        rest, basis, dims, preferred_element_type=FULL
    )


def soap_kernel(
    bounds,
    depth,
    norm_ref,
    grads_ref,
    bases_ref,
    weights_ref,
    first_ref,
    second_ref,
    teacher_ref,
    first_out_ref,
    second_out_ref,
    weights_out_ref,
    teacher_out_ref,
    basis,
):
    layer = pl.program_id(0)
    devices = bases_ref.shape[0]
    own_rows = bases_ref.shape[1] // 4
    clip = jnp.minimum(1.0, CLIP_MAX / (norm_ref[0:1, 0:1] + 1e-06))
    grads = grads_ref[...] * clip
    group = 4
    firsts, seconds, updates = [], [], []
    for segment, (low_row, high_row) in enumerate(bounds):
        for at in range(0, devices, group):
            pieces = [
                bases_ref[slot_of(at + t, depth)][segment * own_rows : (segment + 1) * own_rows]
                for t in range(group)
            ]
            basis[at * own_rows : (at + group) * own_rows] = jnp.concatenate(
                [piece.astype(FULL) for piece in pieces], 0
            ).astype(LOW)
        rotated = split_dot(grads[low_row:high_row], basis[...], ((1,), (0,)))
        first_new = BETA_ONE * first_ref[0, low_row:high_row] + (1.0 - BETA_ONE) * rotated
        second_new = (
            BETA_TWO * second_ref[0, low_row:high_row] + (1.0 - BETA_TWO) * rotated * rotated
        )
        direction = (
            first_new
            / (1.0 - BETA_ONE**STEP)
            / (jnp.sqrt(second_new / (1.0 - BETA_TWO**STEP)) + ADAM_EPSILON)
        )
        firsts.append(first_new)
        seconds.append(second_new)
        updates.append(split_dot(direction, basis[...], ((1,), (1,))))
    first_out_ref[0] = jnp.concatenate(firsts, 0)
    second_out_ref[0] = jnp.concatenate(seconds, 0)
    weight = weights_ref[0]
    fresh = weight - RATE_MATRIX * (jnp.concatenate(updates, 0) + WEIGHT_DECAY * weight)
    weights_out_ref[0] = fresh
    teacher_out_ref[0] = follow(teacher_ref[0], fresh)


def soap(norm, grads, bases_all, weights, first, second, teacher, bounds):
    devices = bases_all.shape[0]
    rows = weights.shape[1]
    own_rows = bases_all.shape[1] // LAYERS
    vmem = pl.BlockSpec(memory_space=pltpu.VMEM)
    block = pl.BlockSpec((1, rows, D), lambda layer: (layer, 0, 0))
    return pl.pallas_call(
        functools.partial(soap_kernel, bounds, devices // 8),
        grid=(LAYERS,),
        out_shape=[jax.ShapeDtypeStruct(weights.shape, FULL)] * 4,
        in_specs=[
            vmem,
            pl.BlockSpec((rows, D), lambda layer: (layer, 0)),
            pl.BlockSpec((devices, own_rows, D), lambda layer: (0, layer, 0)),
            block,
            block,
            block,
            block,
        ],
        out_specs=[block] * 4,
        scratch_shapes=[pltpu.VMEM((D, D), LOW)],
        compiler_params=pltpu.CompilerParams(vmem_limit_bytes=32 << 20),
        name="soap",
    )(norm, grads, bases_all, weights, first, second, teacher)


def per_device(
    patches,
    valid_mask,
    owners,
    embedding,
    embedding_first,
    embedding_second,
    layers,
    layers_first,
    layers_second,
    layer_stats,
    layer_bases,
    head_hidden,
    hidden_first,
    hidden_second,
    head_last,
    last_first,
    last_second,
    protos,
    protos_first,
    protos_second,
    teacher_embedding,
    teacher_layers,
    teacher_hidden,
    teacher_last,
    teacher_protos,
    centre,
):
    devices = lax.axis_size(AXIS)
    device_index = lax.axis_index(AXIS)
    fast = 2 * head_hidden.shape[0] == LANES
    if not fast:
        embed_table, teacher_table = (
            lax.all_gather(embedding.astype(LOW), AXIS, axis=1, tiled=True),
            lax.all_gather(teacher_embedding.astype(LOW), AXIS, axis=1, tiled=True),
        )
        layer_full, teacher_full = (
            lax.all_gather(layers.astype(LOW), AXIS, axis=1, tiled=True),
            lax.all_gather(teacher_layers.astype(LOW), AXIS, axis=1, tiled=True),
        )
    if not fast:
        bases_full = lax.all_gather(layer_bases.astype(LOW), AXIS, axis=2, tiled=True).astype(
            layer_bases.dtype
        )
        stats_full = lax.all_gather(layer_stats.astype(LOW), AXIS, axis=2, tiled=True).astype(
            layer_stats.dtype
        )
    if fast:
        feature_rows, final_rows, vectors, layer_full, last_all, part, *saved = fetch_forward(
            patches,
            embedding,
            teacher_embedding,
            layers,
            teacher_layers,
            head_last,
            teacher_last,
            head_hidden,
            devices,
        )
    else:
        features, layer_inputs, final_state = backbone(patches, embed_table, layer_full, devices)
        teacher_features, unused_inputs, unused_final = backbone(
            patches, teacher_table, teacher_full, devices
        )
    if fast:
        (
            loss_sum,
            loss_count,
            squares,
            grad_hidden,
            grad_last,
            grad_protos,
            grad_features,
            next_centre,
        ) = head_fast(
            feature_rows,
            valid_mask,
            head_hidden,
            protos,
            teacher_hidden,
            teacher_protos,
            centre,
            part,
            last_all,
            devices,
        )
    else:
        (
            loss_sum,
            loss_count,
            grad_hidden,
            grad_last,
            grad_protos,
            grad_features,
            next_centre,
        ) = head_slow(
            features,
            teacher_features,
            valid_mask,
            head_hidden,
            head_last,
            protos,
            teacher_hidden,
            teacher_last,
            teacher_protos,
            centre,
            device_index,
        )
    if fast:
        matrices, own_rows = owners.shape[0], layer_stats.shape[2]
        gathered = backward(
            squares,
            patches,
            vectors,
            layer_full,
            final_rows,
            grad_features,
            saved,
            layer_stats.reshape(matrices, own_rows, D),
            layer_bases.reshape(matrices, own_rows, D),
            layer_bases.reshape(matrices * own_rows, D).astype(LOW),
            devices,
        )
    else:
        grad_table, grad_layers = backbone_back(
            patches,
            embed_table,
            layer_full,
            layer_inputs,
            final_state,
            grad_features,
            devices,
            unchanged,
        )
    bounds = layer_bounds(devices)
    if fast:
        grad_norm, grad_embed, layer_outs, stats_own, bases_own = tail_fast(
            gathered,
            layer_stats,
            layer_bases,
            owners,
            embedding,
            layers,
            layers_first,
            layers_second,
            teacher_layers,
            devices,
        )
    else:
        summed = (
            lax.psum_scatter(grad_table, AXIS, scatter_dimension=1, tiled=True),
            lax.psum_scatter(grad_layers, AXIS, scatter_dimension=1, tiled=True),
        )
        grad_embed = summed[0]
        grad_layers_own = summed[1]
        grams = jnp.stack(
            [
                matmul_high(
                    "lcd,lce->lde",
                    grad_layers_own[:, lower_row:upper_row],
                    grad_layers_own[:, lower_row:upper_row],
                )
                for lower_row, upper_row in bounds
            ],
            1,
        )
        squares = (
            jnp.sum(grad_embed * grad_embed)
            + jnp.sum(grad_layers_own * grad_layers_own)
            + jnp.sum(grad_hidden * grad_hidden)
            + jnp.sum(grad_last * grad_last)
            + jnp.sum(grad_protos * grad_protos)
        )
        totals = lax.psum((squares, grams), AXIS)
        grad_norm = jnp.sqrt(totals[0])
        clip_factor = jnp.minimum(1.0, CLIP_MAX / (grad_norm + 1e-06))
        next_stats = (
            BETA_STAT * stats_full + (1.0 - BETA_STAT) * (clip_factor * clip_factor) * totals[1]
        )
    clip_factor = jnp.minimum(1.0, CLIP_MAX / (grad_norm + 1e-06))
    rows = jnp.arange(embedding.shape[0])[:, None]
    is_matrix = rows < PIX + SEQ
    embed_out = adam_step(
        embedding,
        clip_factor * grad_embed,
        embedding_first,
        embedding_second,
        jnp.where(is_matrix, RATE_MATRIX, RATE_VECTOR),
        jnp.where(is_matrix, WEIGHT_DECAY, 0.0),
    )
    hidden_out = adam_step(
        head_hidden,
        clip_factor * grad_hidden,
        hidden_first,
        hidden_second,
        RATE_MATRIX,
        WEIGHT_DECAY,
    )
    last_out = adam_step(
        head_last, clip_factor * grad_last, last_first, last_second, RATE_MATRIX, WEIGHT_DECAY
    )
    protos_out = adam_step(
        protos, clip_factor * grad_protos, protos_first, protos_second, RATE_MATRIX, WEIGHT_DECAY
    )
    if fast:
        next_layers_first, next_layers_second, next_layers, next_teacher_layers = layer_outs
    else:
        firsts, seconds, weights_new = ([], [], [])
        for segment, (lower_row, upper_row) in enumerate(bounds):
            basis = bases_full[:, segment]
            weight_block = layers[:, lower_row:upper_row]
            rotated = matmul_high(
                "lcd,ldk->lck", clip_factor * grad_layers_own[:, lower_row:upper_row], basis
            )
            first_new = BETA_ONE * layers_first[:, lower_row:upper_row] + (1.0 - BETA_ONE) * rotated
            second_new = (
                BETA_TWO * layers_second[:, lower_row:upper_row] + (1.0 - BETA_TWO) * rotated * rotated
            )
            direction = (
                first_new
                / (1.0 - BETA_ONE**STEP)
                / (jnp.sqrt(second_new / (1.0 - BETA_TWO**STEP)) + ADAM_EPSILON)
            )
            update = matmul_high("lck,ldk->lcd", direction, basis)
            firsts.append(first_new)
            seconds.append(second_new)
            weights_new.append(weight_block - RATE_MATRIX * (update + WEIGHT_DECAY * weight_block))
        next_layers = jnp.concatenate(weights_new, 1)
        next_layers_first, next_layers_second = jnp.concatenate(firsts, 1), jnp.concatenate(seconds, 1)
        next_teacher_layers = follow(teacher_layers, next_layers)
    if not fast:
        flat_stats = next_stats.reshape(-1, D, D)
        flat_bases = bases_full.reshape(-1, D, D)

        def renew_owned(operands):
            return lax.cond(operands[2] == device_index, renew, nothing, operands[0], operands[1])

        renewed = lax.psum(lax.map(renew_owned, (flat_stats, flat_bases, owners)), AXIS)
        next_bases = jnp.where(owners[:, None, None] >= 0, renewed, flat_bases).reshape(
            bases_full.shape
        )
        own_rows = layer_stats.shape[2]
        stats_own = lax.dynamic_slice_in_dim(next_stats, device_index * own_rows, own_rows, 2)
        bases_own = lax.dynamic_slice_in_dim(next_bases, device_index * own_rows, own_rows, 2)
    return (
        loss_sum,
        loss_count,
        grad_norm,
        embed_out[0],
        embed_out[1],
        embed_out[2],
        next_layers_first,
        next_layers_second,
        next_layers,
        stats_own,
        bases_own,
        hidden_out[0],
        hidden_out[1],
        hidden_out[2],
        last_out[0],
        last_out[1],
        last_out[2],
        protos_out[0],
        protos_out[1],
        protos_out[2],
        follow(teacher_embedding, embed_out[2]),
        next_teacher_layers,
        follow(teacher_hidden, hidden_out[2]),
        follow(teacher_last, last_out[2]),
        follow(teacher_protos, protos_out[2]),
        next_centre,
    )


def solution(mesh):
    placed = (
        P(AXIS, None, None),
        P(),
        P(),
        P(None, AXIS),
        P(None, AXIS),
        P(None, AXIS),
        P(None, AXIS, None),
        P(None, AXIS, None),
        P(None, AXIS, None),
        P(None, None, AXIS, None),
        P(None, None, AXIS, None),
        P(AXIS, None),
        P(AXIS, None),
        P(AXIS, None),
        P(None, AXIS),
        P(None, AXIS),
        P(None, AXIS),
        P(None, AXIS),
        P(None, AXIS),
        P(None, AXIS),
        P(None, AXIS),
        P(None, AXIS, None),
        P(AXIS, None),
        P(None, AXIS),
        P(None, AXIS),
        P(AXIS),
    )
    return jax.shard_map(
        per_device,
        mesh=mesh,
        in_specs=placed,
        out_specs=(
            P(),
            P(),
            P(),
            P(None, AXIS),
            P(None, AXIS),
            P(None, AXIS),
            P(None, AXIS, None),
            P(None, AXIS, None),
            P(None, AXIS, None),
            P(None, None, AXIS, None),
            P(None, None, AXIS, None),
            P(AXIS, None),
            P(AXIS, None),
            P(AXIS, None),
            P(None, AXIS),
            P(None, AXIS),
            P(None, AXIS),
            P(None, AXIS),
            P(None, AXIS),
            P(None, AXIS),
            P(None, AXIS),
            P(None, AXIS, None),
            P(AXIS, None),
            P(None, AXIS),
            P(None, AXIS),
            P(AXIS),
        ),
        check_vma=False,
    )
```

```python
import functools

import jax
import jax.numpy as jnp
from jax import lax
from jax.experimental import pallas as pl
from jax.experimental.pallas import tpu as pltpu
from jax.sharding import PartitionSpec as P

AXIS = "dp"
D = 384
HEADS = 6
HEAD_DIM = 64
MLP = 1536
PIX = 588
LAYERS = 3
STEP = 10
SEQ = 257


NORM_EPSILON = 1e-06
UNIT_EPSILON = 1e-06
TAU_STUDENT = 0.1
TAU_TEACHER = 0.07
CLIP_MAX = 0.001
BETA_ONE = 0.9
BETA_TWO = 0.999
ADAM_EPSILON = 1e-08
WEIGHT_DECAY = 0.04
RATE_MATRIX = 0.04
RATE_VECTOR = 0.2
BETA_STAT = 0.95
TEACHER_MOMENTUM = 0.8
CENTRE_MOMENTUM = 0.9
ROOT_HALF = 0.7071067811865476
DENSITY_SCALE = 0.3989422804014327


def joined(value, axis, join):
    pieces = jax.tree.map(lambda part: lax.all_gather(part, axis), value)
    head = jax.tree.map(lambda part: part[0], pieces)
    tail = jax.tree.map(lambda part: part[1:], pieces)
    running, _ = lax.scan(lambda running, piece: (join(running, piece), None), head, tail)
    return running


def matmul_low(form, left, right):
    return jnp.einsum(form, left, right, preferred_element_type=jnp.float32)


def matmul_high(form, left, right):
    return jnp.einsum(form, left, right, precision=lax.Precision.HIGHEST)


def layer_norm(values, gain_row, shift_row):
    centred = values - jnp.mean(values, -1, keepdims=True)
    inverse_std = lax.rsqrt(jnp.mean(centred * centred, -1, keepdims=True) + NORM_EPSILON)
    return centred * inverse_std * gain_row + shift_row


def norm_back(values, gain_row, grad_out):
    centred = values - jnp.mean(values, -1, keepdims=True)
    inverse_std = lax.rsqrt(jnp.mean(centred * centred, -1, keepdims=True) + NORM_EPSILON)
    normed = centred * inverse_std
    scaled_grad = grad_out * gain_row
    grad_in = inverse_std * (
        scaled_grad
        - jnp.mean(scaled_grad, -1, keepdims=True)
        - normed * jnp.mean(scaled_grad * normed, -1, keepdims=True)
    )
    leading = tuple(range(values.ndim - 1))
    return (grad_in, jnp.sum(grad_out * normed, leading), jnp.sum(grad_out, leading))


def gelu_exact(values):
    return 0.5 * values * (1.0 + lax.erf(values * ROOT_HALF))


def gelu_slope(values):
    return (
        0.5 * (1.0 + lax.erf(values * ROOT_HALF))
        + values * jnp.exp(-0.5 * values * values) * DENSITY_SCALE
    )


def layer_bounds(devices):
    widths = [3 * D // devices, D // devices, MLP // devices, MLP // devices]
    lowers = [0, widths[0], widths[0] + widths[1], widths[0] + widths[1] + widths[2]]
    return [(lowers[segment], lowers[segment] + widths[segment]) for segment in range(4)]


def split_layer(weights, devices):
    blocks = weights.reshape(devices, -1, D)
    return [
        blocks[:, lower_row:upper_row].reshape(-1, D)
        for lower_row, upper_row in layer_bounds(devices)
    ]


def join_layer(members, devices):
    return jnp.concatenate([member.reshape(devices, -1, D) for member in members], 1).reshape(-1, D)


def layer_parts(inputs, matrices, vectors):
    joint_weight, output_weight, inner_weight, outer_weight = matrices
    images, tokens = (inputs.shape[0], inputs.shape[1])
    normed = layer_norm(inputs, vectors[0], vectors[1]).astype(jnp.bfloat16)
    joint = matmul_low("itd,ed->ite", normed, joint_weight).astype(jnp.bfloat16)
    head_split = joint.reshape(images, tokens, 3, HEADS, HEAD_DIM)
    queries, keys_in, values_in = (head_split[:, :, 0], head_split[:, :, 1], head_split[:, :, 2])
    scores = matmul_low("ithd,ishd->ihts", queries, keys_in) * HEAD_DIM ** (-0.5)
    attention = jax.nn.softmax(scores, axis=-1)
    mixed_heads = (
        matmul_low("ihts,ishd->ithd", attention.astype(jnp.bfloat16), values_in)
        .astype(jnp.bfloat16)
        .reshape(images, tokens, D)
    )
    attended = matmul_low("itd,ed->ite", mixed_heads, output_weight)
    middle = inputs + vectors[4] * attended
    normed_two = layer_norm(middle, vectors[2], vectors[3]).astype(jnp.bfloat16)
    inner_pre = matmul_low("itd,md->itm", normed_two, inner_weight)
    activated = gelu_exact(inner_pre).astype(jnp.bfloat16)
    outer_out = matmul_low("itm,md->itd", activated, outer_weight)
    result = middle + vectors[5] * outer_out
    return (
        normed,
        queries,
        keys_in,
        values_in,
        attention,
        mixed_heads,
        attended,
        middle,
        normed_two,
        inner_pre,
        activated,
        outer_out,
        result,
    )


def layer_backward(inputs, matrices, vectors, grad_result):
    joint_weight, output_weight, inner_weight, outer_weight = matrices
    (
        normed,
        queries,
        keys_in,
        values_in,
        attention,
        mixed_heads,
        attended,
        middle,
        normed_two,
        inner_pre,
        activated,
        outer_out,
        result,
    ) = layer_parts(inputs, matrices, vectors)
    images, tokens = (inputs.shape[0], inputs.shape[1])
    grad_outer = (vectors[5] * grad_result).astype(jnp.bfloat16)
    grad_scale_two = jnp.sum(grad_result * outer_out, (0, 1))
    grad_outer_weight = matmul_low("itm,itd->md", activated, grad_outer)
    grad_activated = matmul_low("itd,md->itm", grad_outer, outer_weight)
    grad_inner = (grad_activated * gelu_slope(inner_pre)).astype(jnp.bfloat16)
    grad_inner_weight = matmul_low("itm,itd->md", grad_inner, normed_two)
    grad_normed_two = matmul_low("itm,md->itd", grad_inner, inner_weight)
    grad_middle_norm, grad_gain_two, grad_shift_two = norm_back(middle, vectors[2], grad_normed_two)
    grad_middle = grad_result + grad_middle_norm
    grad_attended = (vectors[4] * grad_middle).astype(jnp.bfloat16)
    grad_scale_one = jnp.sum(grad_middle * attended, (0, 1))
    grad_output_weight = matmul_low("ite,itd->ed", grad_attended, mixed_heads)
    grad_mixed = (
        matmul_low("ite,ed->itd", grad_attended, output_weight)
        .astype(jnp.bfloat16)
        .reshape(images, tokens, HEADS, HEAD_DIM)
    )
    grad_attention = matmul_low("ithd,ishd->ihts", grad_mixed, values_in)
    grad_values = matmul_low("ihts,ithd->ishd", attention.astype(jnp.bfloat16), grad_mixed)
    grad_scores = (
        attention * (grad_attention - jnp.sum(attention * grad_attention, -1, keepdims=True))
    ).astype(jnp.bfloat16)
    grad_queries = matmul_low("ihts,ishd->ithd", grad_scores, keys_in) * HEAD_DIM ** (-0.5)
    grad_keys = matmul_low("ihts,ithd->ishd", grad_scores, queries) * HEAD_DIM ** (-0.5)
    grad_joint = (
        jnp.stack([grad_queries, grad_keys, grad_values], 2)
        .astype(jnp.bfloat16)
        .reshape(images, tokens, 3 * D)
    )
    grad_joint_weight = matmul_low("ite,itd->ed", grad_joint, normed)
    grad_normed = matmul_low("ite,ed->itd", grad_joint, joint_weight)
    grad_input_norm, grad_gain_one, grad_shift_one = norm_back(inputs, vectors[0], grad_normed)
    grad_vectors = jnp.stack(
        [
            grad_gain_one,
            grad_shift_one,
            grad_gain_two,
            grad_shift_two,
            grad_scale_one,
            grad_scale_two,
        ]
    )
    return (
        grad_middle + grad_input_norm,
        (grad_joint_weight, grad_output_weight, grad_inner_weight, grad_outer_weight),
        grad_vectors,
    )


def table_vectors(embed_table):
    return embed_table[PIX + SEQ : PIX + SEQ + 6 * LAYERS].astype(jnp.float32).reshape(LAYERS, 6, D)


def table_tail(embed_table):
    return embed_table[PIX + SEQ + 6 * LAYERS :].astype(jnp.float32)


def backbone(patches, embed_table, layer_stack, devices):
    vectors = table_vectors(embed_table)
    tail_rows = table_tail(embed_table)
    position = embed_table[PIX : PIX + SEQ].astype(jnp.float32)
    projected = matmul_low("ipc,cd->ipd", patches, embed_table[:PIX]) + tail_rows[0]
    leading = jnp.broadcast_to(tail_rows[1] + position[0], (patches.shape[0], 1, D))
    current = jnp.concatenate([leading, projected + position[1:]], 1)
    layer_inputs = []
    for layer_number in range(LAYERS):
        layer_inputs.append(current)
        current = layer_parts(
            current, split_layer(layer_stack[layer_number], devices), vectors[layer_number]
        )[-1]
    features = layer_norm(current[:, 0], tail_rows[2], tail_rows[3]).astype(jnp.bfloat16)
    return (features, layer_inputs, current)


def unchanged(values):
    return values


def backbone_back(
    patches,
    embed_table,
    layer_stack,
    layer_inputs,
    final_state,
    grad_features,
    devices,
    reduce_layer,
):
    vectors = table_vectors(embed_table)
    tail_rows = table_tail(embed_table)
    grad_cls, grad_gain, grad_shift = norm_back(final_state[:, 0], tail_rows[2], grad_features)
    grad_current = jnp.concatenate(
        [grad_cls[:, None], jnp.zeros((final_state.shape[0], SEQ - 1, D), jnp.float32)], 1
    )
    weight_grads = [None] * LAYERS
    vector_grads = [None] * LAYERS
    for layer_number in reversed(range(LAYERS)):
        grad_current, matrices, grad_vectors = layer_backward(
            layer_inputs[layer_number],
            split_layer(layer_stack[layer_number], devices),
            vectors[layer_number],
            grad_current,
        )
        weight_grads[layer_number] = reduce_layer(join_layer(matrices, devices))
        vector_grads[layer_number] = grad_vectors
    grad_patch_weight = matmul_low("ipc,ipd->cd", patches, grad_current[:, 1:].astype(jnp.bfloat16))
    grad_position = jnp.sum(grad_current, 0)
    tail_grads = jnp.stack(
        [
            jnp.sum(grad_current[:, 1:], (0, 1)),
            jnp.sum(grad_current[:, 0], 0),
            grad_gain,
            grad_shift,
        ]
    )
    grad_table = jnp.concatenate(
        [grad_patch_weight, grad_position, jnp.concatenate(vector_grads, 0), tail_grads], 0
    )
    return (grad_table, jnp.stack(weight_grads))


def unit_rows(bottle):
    inverse_norm = lax.rsqrt(jnp.sum(bottle * bottle, -1, keepdims=True) + UNIT_EPSILON)
    return (bottle * inverse_norm, inverse_norm)


def combine_parts(left_part, right_part):
    top_student = jnp.maximum(left_part[0], right_part[0])
    total_student = left_part[1] * jnp.exp(left_part[0] - top_student) + right_part[1] * jnp.exp(
        right_part[0] - top_student
    )
    top_teacher = jnp.maximum(left_part[2], right_part[2])
    left_weight = jnp.exp(left_part[2] - top_teacher)
    right_weight = jnp.exp(right_part[2] - top_teacher)
    return (
        top_student,
        total_student,
        top_teacher,
        left_part[3] * left_weight + right_part[3] * right_weight,
        left_part[4] * left_weight + right_part[4] * right_weight,
    )


def adam_step(weight, grad, first_moment, second_moment, rate, decay):
    first_new = BETA_ONE * first_moment + (1.0 - BETA_ONE) * grad
    second_new = BETA_TWO * second_moment + (1.0 - BETA_TWO) * grad * grad
    direction = (
        first_new
        / (1.0 - BETA_ONE**STEP)
        / (jnp.sqrt(second_new / (1.0 - BETA_TWO**STEP)) + ADAM_EPSILON)
    )
    return (first_new, second_new, weight - rate * (direction + decay * weight))


def renew(stat_matrix, basis):
    scaled = jnp.dot(stat_matrix, basis, precision=lax.Precision.HIGHEST) * (
        D / jnp.trace(stat_matrix)
    )
    gram = jnp.dot(scaled.T, scaled, precision=lax.Precision.HIGHEST)
    lower_factor = jnp.linalg.cholesky(gram)
    return lax.linalg.triangular_solve(lower_factor, scaled.T, left_side=True, lower=True).T


def nothing(stat_matrix, basis):
    return jnp.zeros_like(basis)


def follow(teacher_weight, student_weight):
    return TEACHER_MOMENTUM * teacher_weight + (1.0 - TEACHER_MOMENTUM) * student_weight


MESH = pl.DeviceIdType.MESH
LANES = 128
LOW = jnp.bfloat16
FULL = jnp.float32


def params(identity, vmem=None):
    return pltpu.CompilerParams(
        collective_id=identity, has_side_effects=True, vmem_limit_bytes=vmem or (48 << 20)
    )


def push(source, target, sent, landed, device):
    copy = pltpu.make_async_remote_copy(
        src_ref=source,
        dst_ref=target,
        send_sem=sent,
        recv_sem=landed,
        device_id=(device,),
        device_id_type=MESH,
    )
    copy.start()
    return copy


def greet(peers):
    barrier = pltpu.get_barrier_semaphore()
    for peer in peers:
        pl.semaphore_signal(barrier, inc=1, device_id=(peer,), device_id_type=MESH)
    pl.semaphore_wait(barrier, len(peers))


def dot_nt(left, right):
    return lax.dot_general(left, right, (((1,), (1,)), ((), ())), preferred_element_type=FULL)


def dot_nn(left, right):
    return lax.dot_general(left, right, (((1,), (0,)), ((), ())), preferred_element_type=FULL)


def dot_tn(left, right):
    return lax.dot_general(left, right, (((0,), (0,)), ((), ())), preferred_element_type=FULL)


def slot_of(device, depth):
    return (device % 8) * depth + device // 8


class Route:
    def __init__(self, depth, items, own_sem, z_sent, z_landed, near_sent, near_landed, die_sent, die_landed):
        self.depth = depth
        self.items = items
        self.sems = (own_sem, z_sent, z_landed, near_sent, near_landed, die_sent, die_landed)
        me = lax.axis_index(AXIS)
        self.me = me
        self.total = 8 * depth
        self.core = lax.rem(me, 2)
        x_at = lax.rem(me // 2, 2)
        y_at = lax.rem(me // 4, 2)
        self.z_at = me // 8
        self.partner = me + 1 - 2 * self.core
        self.to_x = me + 2 - 4 * x_at
        self.to_y = me + 4 - 8 * y_at
        places = [(y_at, x_at), (y_at, 1 - x_at), (1 - y_at, x_at), (1 - y_at, 1 - x_at)]
        self.starts = [((y * 2 + x) * 2 + self.core) * depth for y, x in places]

    def copy(self, source, target, sent, landed, device):
        return pltpu.make_async_remote_copy(
            src_ref=source,
            dst_ref=target,
            send_sem=sent,
            recv_sem=landed,
            device_id=(device,),
            device_id_type=MESH,
        )

    def half(self, at):
        size = self.items[at][3]
        return (size // 2 + 15) // 16 * 16

    def own(self, at):
        source, target, lower, size = self.items[at]
        return pltpu.make_async_copy(
            source.at[pl.ds(lower, size)],
            target.at[self.starts[0] + self.z_at, pl.ds(lower, size)],
            self.sems[0].at[at],
        )

    def deep(self, at, step):
        source, target, lower, size = self.items[at]
        return self.copy(
            source.at[pl.ds(lower, size)],
            target.at[self.starts[0] + self.z_at, pl.ds(lower, size)],
            self.sems[1].at[at, step],
            self.sems[2].at[at, step],
            lax.rem(self.me + 8 * step, self.total),
        )

    def near(self, at, which):
        source, target, lower, size = self.items[at]
        half = self.half(at)
        column, first, length, device = [
            (0, lower, size, self.to_x),
            (0, lower, size, self.to_y),
            (1, lower, half, self.to_y),
            (2, lower + half, size - half, self.to_x),
        ][which]
        view = target.at[pl.ds(self.starts[column], self.depth), pl.ds(first, length)]
        return self.copy(view, view, self.sems[3].at[at, which], self.sems[4].at[at, which], device)

    def die(self, at, column):
        source, target, lower, size = self.items[at]
        view = target.at[pl.ds(self.starts[column], self.depth), pl.ds(lower, size)]
        return self.copy(
            view, view, self.sems[5].at[at, column], self.sems[6].at[at, column], self.partner
        )

    def act(self, stage, at):
        if stage == 0:
            self.own(at).start()
            for step in range(1, self.depth):
                self.deep(at, step).start()
        elif stage == 1:
            self.own(at).wait()
            for step in range(1, self.depth):
                self.deep(at, step).wait_recv()
            self.near(at, 0).start()
            self.near(at, 1).start()
            self.die(at, 0).start()
        elif stage == 2:
            self.near(at, 0).wait_recv()
            self.near(at, 2).start()
            self.die(at, 1).start()
            self.near(at, 1).wait_recv()
            self.near(at, 3).start()
            self.die(at, 2).start()
        elif stage == 3:
            self.near(at, 2).wait_recv()
            self.near(at, 3).wait_recv()
            self.die(at, 3).start()
        elif stage == 4:
            for column in range(4):
                self.die(at, column).wait_recv()
        else:
            for step in range(1, self.depth):
                self.deep(at, step).wait_send()
            for which in range(4):
                self.near(at, which).wait_send()
                self.die(at, which).wait_send()


def route_sems(count, depth):
    dma = pltpu.SemaphoreType.DMA
    return [
        dma((count,)),
        dma((count, depth)),
        dma((count, depth)),
        dma((count, 4)),
        dma((count, 4)),
        dma((count, 4)),
        dma((count, 4)),
    ]


def head_kernel(
    devices,
    rows_ref,
    hidden_ref,
    teacher_hidden_ref,
    part_ref,
    last_all_ref,
    protos_ref,
    teacher_protos_ref,
    centre_ref,
    mask_ref,
    mask_row_ref,
    scalars_ref,
    grad_hidden_ref,
    grad_last_ref,
    grad_protos_ref,
    grad_feat_ref,
    centre_out_ref,
    feat_ref,
    last_ref,
    teacher_last_ref,
    fb,
    hid_low,
    thid_low,
    prot_low,
    half_out,
    half_in,
    mine_buf,
    other_buf,
    act_s,
    act_t,
    act2_s,
    act2_t,
    pre1,
    pre2,
    unit_ref,
    inv_ref,
    exp_s,
    exp_t,
    stat_out,
    stat_all,
    pz_ref,
    pz_all,
    dz_own,
    dz_all,
    dp_own,
    dp_in,
    dp_cb,
    dp_half,
    dp_full,
    df_part,
    df_all,
    df_sum,
    df_other,
    die_sent,
    die_landed,
    wide_sent,
    wide_landed,
    core_sent,
    core_landed,
):
    me = lax.axis_index(AXIS)
    core = lax.rem(me, 2)
    chip = me // 2
    chips = devices // 2
    partner = me + 1 - 2 * core
    everyone = [lax.rem(me + step, devices) for step in range(1, devices)]
    same_core = [lax.rem(me + 2 * step, devices) for step in range(1, chips)]
    images = mask_ref.shape[0]
    units = hidden_ref.shape[0]
    groups = images // 8
    greet(everyone)
    sends = []

    def die(step, source, target):
        copy = push(source, target, die_sent.at[step], die_landed.at[step], partner)
        sends.append(copy)
        return copy

    def wide(step, source, target):
        made = [
            push(source, target, wide_sent.at[step, at], wide_landed.at[step, at], peer)
            for at, peer in enumerate(everyone)
        ]
        sends.extend(made)
        return made

    def cores(step, source_of, target):
        made = [
            push(source_of(peer), target, core_sent.at[step, at], core_landed.at[step, at], peer)
            for at, peer in enumerate(same_core)
        ]
        sends.extend(made)
        return made

    pieces = [
        rows_ref[model, image, 0:1, j * LANES : (j + 1) * LANES]
        for model in range(2)
        for j in range(D // LANES)
        for image in range(rows_ref.shape[1])
    ]
    blank = jnp.zeros((16 - len(pieces) // 2, LANES), FULL)
    half_count = len(pieces) // 2
    feat_ref[...] = jnp.concatenate(
        pieces[:half_count] + [blank] + pieces[half_count:] + [blank], 0
    ).astype(LOW)
    fb[me] = feat_ref[...]
    copies = wide(0, feat_ref, fb.at[me])
    hid_low[...] = hidden_ref[...].astype(LOW)
    thid_low[...] = teacher_hidden_ref[...].astype(LOW)
    prot_low[0] = protos_ref[...].astype(LOW)
    prot_low[1] = teacher_protos_ref[...].astype(LOW)
    last_width = last_ref.shape[0] // devices
    across = last_all_ref.shape[2]
    for model, table in enumerate((last_ref, teacher_last_ref)):
        for half in range(2):
            first = (2 * half + model) * last_width
            for at in range(0, devices, 2):
                pair_rows = [
                    last_all_ref[slot_of(at + t, devices // 8), first : first + last_width].astype(FULL)
                    for t in range(2)
                ]
                table[
                    at * last_width : (at + 2) * last_width, half * across : (half + 1) * across
                ] = jnp.concatenate(pair_rows, 0).astype(LOW)
    block_rows = feat_ref.shape[0]
    row_at = lax.broadcasted_iota(jnp.int32, (images, devices * block_rows), 0)
    col_at = lax.broadcasted_iota(jnp.int32, (images, devices * block_rows), 1)
    col_dev = lax.shift_right_logical(col_at, 5)
    col_in = jnp.bitwise_and(col_at, 31)
    lead = row_at - 3 * col_dev
    for copy in copies:
        copy.wait_recv()
    rows_all = fb[...].reshape(devices * block_rows, LANES)

    def features_of(model):
        pieces = []
        for j in range(3):
            hit = (col_in - (16 * model + 3 * j) == lead) & (lead >= 0) & (lead < 3)
            pieces.append(dot_nn(jnp.where(hit, 1.0, 0.0).astype(LOW), rows_all).astype(LOW))
        return jnp.concatenate(pieces, 1)

    feats = features_of(0)
    tfeats = features_of(1)

    def gather_pair(step, student, teacher, out_s, out_t):
        own_model = jnp.where(core == 0, student, teacher)
        half_out[step] = jnp.where(core == 0, teacher, student)
        copy = die(2 * step, half_out.at[step], half_in.at[step])
        copy.wait_recv()
        got = half_in[step]
        block = jnp.concatenate(
            [jnp.where(core == 0, own_model, got), jnp.where(core == 0, got, own_model)], 1
        ).astype(LOW)
        mine_buf[step, chip] = block
        made = cores(step, lambda peer: mine_buf.at[step, chip], mine_buf.at[step, chip])
        for copy in made:
            copy.wait_recv()
        copy = die(2 * step + 1, mine_buf.at[step], other_buf.at[step])
        copy.wait_recv()
        for at in range(chips):
            one, two = mine_buf[step, at], other_buf[step, at]
            out_s[:, at * LANES : (at + 1) * LANES] = jnp.where(core == 0, one, two)
            out_t[:, at * LANES : (at + 1) * LANES] = jnp.where(core == 0, two, one)

    pre_one = dot_nt(feats, hid_low[:, :D])
    pre1[...] = pre_one
    tpre_one = dot_nt(tfeats, thid_low[:, :D])
    gather_pair(0, gelu_exact(pre_one).astype(LOW).astype(FULL), gelu_exact(tpre_one).astype(LOW).astype(FULL), act_s, act_t)
    pre_two = dot_nt(act_s[...], hid_low[:, D:])
    pre2[...] = pre_two
    tpre_two = dot_nt(act_t[...], thid_low[:, D:])
    gather_pair(1, gelu_exact(pre_two).astype(LOW).astype(FULL), gelu_exact(tpre_two).astype(LOW).astype(FULL), act2_s, act2_t)

    unit, inverse_norm = unit_rows(dot_nt(act2_s[...], last_ref[...]))
    tunit, unused = unit_rows(dot_nt(act2_t[...], teacher_last_ref[...]))
    unit_ref[...] = unit
    inv_ref[...] = jnp.broadcast_to(inverse_norm, inv_ref.shape)
    unit_low = unit.astype(LOW)
    scaled = dot_nn(unit_low, prot_low[0]) / TAU_STUDENT
    tlogits = dot_nn(tunit.astype(LOW), prot_low[1])
    top_s = jnp.max(scaled, -1, keepdims=True)
    grown_s = jnp.exp(scaled - top_s)
    exp_s[...] = grown_s
    sharp = (tlogits - centre_ref[...]) / TAU_TEACHER
    top_t = jnp.max(sharp, -1, keepdims=True)
    grown_t = jnp.exp(sharp - top_t)
    exp_t[...] = grown_t
    lane = lax.broadcasted_iota(jnp.int32, (images, LANES), 1)
    stats = jnp.where(lane == 0, top_s, 0.0)
    stats = jnp.where(lane == 1, jnp.sum(grown_s, -1, keepdims=True), stats)
    stats = jnp.where(lane == 2, top_t, stats)
    stats = jnp.where(lane == 3, jnp.sum(grown_t, -1, keepdims=True), stats)
    stats = jnp.where(lane == 4, jnp.sum(grown_t * scaled, -1, keepdims=True), stats)
    square = jnp.concatenate([stats, jnp.zeros((LANES - images, LANES), FULL)], 0)
    stat_out[...] = square.T[:8]
    stat_all[me] = stat_out[...]
    copies = wide(1, stat_out, stat_all.at[me])
    counted = mask_ref[...]
    count = jnp.sum(counted)
    centre_out_ref[...] = (
        CENTRE_MOMENTUM * centre_ref[...]
        + (1.0 - CENTRE_MOMENTUM) * jnp.sum(counted * tlogits, 0, keepdims=True) / count
    )
    for copy in copies:
        copy.wait_recv()
    merged = stat_all[...]
    tops, totals = merged[:, 0], merged[:, 1]
    ttops, ttotals, crosses = merged[:, 2], merged[:, 3], merged[:, 4]
    peak_s = jnp.max(tops, 0, keepdims=True)
    sum_s = jnp.sum(totals * jnp.exp(tops - peak_s), 0, keepdims=True)
    peak_t = jnp.max(ttops, 0, keepdims=True)
    shrink = jnp.exp(ttops - peak_t)
    sum_t = jnp.sum(ttotals * shrink, 0, keepdims=True)
    cross = jnp.sum(crosses * shrink, 0, keepdims=True)
    log_total = peak_s + jnp.log(sum_s)
    mask_row = mask_row_ref[...]
    losses = jnp.where(mask_row > 0.0, log_total - cross / sum_t, 0.0)
    loss = jnp.sum(losses)
    lane8 = lax.broadcasted_iota(jnp.int32, (8, LANES), 1)
    scalars_ref[...] = jnp.where(lane8 == 0, loss, jnp.where(lane8 == 1, count, 0.0))
    back = jnp.concatenate(
        [log_total, peak_t, 1.0 / sum_t, jnp.zeros((LANES - 3, LANES), FULL)], 0
    ).T
    share_s = jnp.exp(top_s - back[:images, 0:1])
    share_t = jnp.exp(top_t - back[:images, 1:2]) * back[:images, 2:3]
    grad_logits = (
        (counted / count) * (exp_s[...] * share_s - exp_t[...] * share_t) / TAU_STUDENT
    ).astype(LOW)

    pz_ref[...] = dot_nt(grad_logits, prot_low[0]).reshape(groups, 8, unit.shape[1])
    for group in range(groups):
        owner = 2 * group

        @pl.when(me != owner)
        def _(group=group, owner=owner):
            push(pz_ref.at[group], pz_all.at[me], wide_sent.at[2, group], wide_landed.at[2, me], owner)

    grad_protos_ref[...] = dot_tn(unit_low, grad_logits)

    @pl.when((core == 0) & (chip < groups))
    def _():
        pz_all[me] = pz_ref[chip]
        for source in range(devices):

            @pl.when(source != me)
            def _(source=source):
                pltpu.make_async_copy(pz_all.at[source], pz_all.at[source], wide_landed.at[2, source]).wait()

        total = jnp.sum(pz_all[...], 0)
        rows = pl.ds(pl.multiple_of(chip * 8, 8), 8)
        own_unit = unit_ref[rows, :]
        own_inv = inv_ref[rows, :][:, 0:1]
        dz_own[...] = own_inv * (total - own_unit * jnp.sum(own_unit * total, -1, keepdims=True))
        dz_all[chip] = dz_own[...]
        for step in range(1, devices):
            push(dz_own, dz_all.at[chip], wide_sent.at[3, step - 1], wide_landed.at[3, chip], lax.rem(me + step, devices))

    for group in range(groups):

        @pl.when(me != 2 * group)
        def _(group=group):
            pltpu.make_async_copy(dz_all.at[group], dz_all.at[group], wide_landed.at[3, group]).wait()

    grad_bottle = dz_all[...].reshape(images, unit.shape[1]).astype(LOW)
    chip_columns = pl.ds(pl.multiple_of(chip * LANES, LANES), LANES)
    pair = dot_nn(grad_bottle, last_ref[:, chip_columns])
    grad_act_two = jnp.where(core == 0, pair[:, :units], pair[:, units:])
    grad_pre_two = (grad_act_two * gelu_slope(pre2[...])).astype(LOW)

    dp_own[...] = grad_pre_two.astype(FULL)
    copy = die(4, dp_own, dp_in)
    width = last_ref.shape[0] // devices
    pick_row = lax.broadcasted_iota(jnp.int32, (width, last_ref.shape[0]), 0)
    pick_col = lax.broadcasted_iota(jnp.int32, (width, last_ref.shape[0]), 1)
    pick = jnp.where(pick_col == pick_row + me * width, 1.0, 0.0).astype(LOW)
    own_bottle = dot_nt(pick, grad_bottle).astype(LOW)
    grad_last_ref[...] = dot_nn(own_bottle, act2_s[...])
    copy.wait_recv()
    own_dp, got_dp = dp_own[...], dp_in[...]
    dp_cb[...] = jnp.concatenate(
        [jnp.where(core == 0, own_dp, got_dp), jnp.where(core == 0, got_dp, own_dp)], 1
    ).astype(LOW)
    half = images // 2
    my_rows = pl.ds(pl.multiple_of(core * half, 16), half)
    their_rows = pl.ds(pl.multiple_of((1 - core) * half, 16), half)
    dp_half[0, chip] = dp_cb[my_rows, :]
    made = cores(2, lambda peer: dp_half.at[0, chip], dp_half.at[0, chip])
    grad_hidden_ref[:, D:] = dot_tn(grad_pre_two, act_s[...])
    for copy in made:
        copy.wait_recv()
    copy = die(5, dp_half.at[0], dp_half.at[1])
    for at in range(chips):
        dp_full[my_rows, at * LANES : (at + 1) * LANES] = dp_half[0, at]
    copy.wait_recv()
    for at in range(chips):
        dp_full[their_rows, at * LANES : (at + 1) * LANES] = dp_half[1, at]
    part = jnp.concatenate([part_ref[at % 2, at // 2] for at in range(devices)], 0)
    pair = dot_nn(dp_full[...], part)
    grad_act_one = jnp.where(core == 0, pair[:, :units], pair[:, units:])
    grad_pre_one = (grad_act_one * gelu_slope(pre1[...])).astype(LOW)

    out_row = lax.broadcasted_iota(jnp.int32, (8 * chips, images), 0)
    in_row = lax.broadcasted_iota(jnp.int32, (8 * chips, images), 1)
    out_chip = lax.shift_right_logical(out_row, 3)
    out_in = jnp.bitwise_and(out_row, 7)
    hit = (in_row - 6 * out_chip == out_in) & (out_in < 6)
    moved = dot_nn(jnp.where(hit, 1.0, 0.0).astype(LOW), grad_pre_one).astype(LOW)
    df_part[...] = dot_nn(moved, hid_low[:, :D]).reshape(chips, 8, D)
    df_all[chip] = df_part[chip]
    made = cores(3, lambda peer: df_part.at[peer // 2], df_all.at[chip])
    grad_hidden_ref[:, :D] = dot_tn(grad_pre_one, feats)
    for copy in made:
        copy.wait_recv()
    df_sum[...] = jnp.sum(df_all[...], 0)
    copy = die(6, df_sum, df_other)
    copy.wait_recv()
    whole = df_sum[...] + df_other[...]
    grad_feat_ref[...] = whole
    squares = jnp.sum(grad_hidden_ref[...] * grad_hidden_ref[...])
    squares = squares + jnp.sum(grad_last_ref[...] * grad_last_ref[...])
    squares = squares + jnp.sum(grad_protos_ref[...] * grad_protos_ref[...])
    scalars_ref[...] = jnp.where(lane8 == 2, squares, scalars_ref[...])
    for copy in sends:
        copy.wait_send()
    for group in range(groups):

        @pl.when(me != 2 * group)
        def _(group=group):
            pltpu.make_async_copy(pz_ref.at[group], pz_ref.at[group], wide_sent.at[2, group]).wait()

    @pl.when((core == 0) & (chip < groups))
    def _():
        for step in range(1, devices):
            pltpu.make_async_copy(dz_own, dz_own, wide_sent.at[3, step - 1]).wait()


def head(rows, hidden, teacher_hidden, part, last_all, protos, teacher_protos, centre, mask, mask_row, devices):
    images = mask.shape[0]
    units, wide = hidden.shape
    bottle, width = protos.shape
    hid = 2 * last_all.shape[2]
    chips = devices // 2
    groups = images // 8
    vmem = pl.BlockSpec(memory_space=pltpu.VMEM)
    shape = jax.ShapeDtypeStruct
    dma = pltpu.SemaphoreType.DMA
    return pl.pallas_call(
        functools.partial(head_kernel, devices),
        out_shape=(
            shape((8, LANES), FULL),
            shape((units, wide), FULL),
            shape((bottle // devices, hid), FULL),
            shape((bottle, width), FULL),
            shape((8, D), FULL),
            shape((1, width), FULL),
        ),
        in_specs=[vmem] * 10,
        out_specs=(vmem,) * 6,
        scratch_shapes=[
            pltpu.VMEM((32, LANES), LOW),
            pltpu.VMEM((bottle, hid), LOW),
            pltpu.VMEM((bottle, hid), LOW),
            pltpu.VMEM((devices, 32, LANES), LOW),
            pltpu.VMEM((units, wide), LOW),
            pltpu.VMEM((units, wide), LOW),
            pltpu.VMEM((2, bottle, width), LOW),
            pltpu.VMEM((2, images, units), FULL),
            pltpu.VMEM((2, images, units), FULL),
            pltpu.VMEM((2, chips, images, LANES), LOW),
            pltpu.VMEM((2, chips, images, LANES), LOW),
            pltpu.VMEM((images, hid), LOW),
            pltpu.VMEM((images, hid), LOW),
            pltpu.VMEM((images, hid), LOW),
            pltpu.VMEM((images, hid), LOW),
            pltpu.VMEM((images, units), FULL),
            pltpu.VMEM((images, units), FULL),
            pltpu.VMEM((images, bottle), FULL),
            pltpu.VMEM((images, LANES), FULL),
            pltpu.VMEM((images, width), FULL),
            pltpu.VMEM((images, width), FULL),
            pltpu.VMEM((8, LANES), FULL),
            pltpu.VMEM((devices, 8, LANES), FULL),
            pltpu.VMEM((groups, 8, bottle), FULL),
            pltpu.VMEM((devices, 8, bottle), FULL),
            pltpu.VMEM((8, bottle), FULL),
            pltpu.VMEM((groups, 8, bottle), FULL),
            pltpu.VMEM((images, units), FULL),
            pltpu.VMEM((images, units), FULL),
            pltpu.VMEM((images, LANES), LOW),
            pltpu.VMEM((2, chips, images // 2, LANES), LOW),
            pltpu.VMEM((images, hid), LOW),
            pltpu.VMEM((chips, 8, D), FULL),
            pltpu.VMEM((chips, 8, D), FULL),
            pltpu.VMEM((8, D), FULL),
            pltpu.VMEM((8, D), FULL),
            dma((7,)),
            dma((7,)),
            dma((4, devices)),
            dma((4, devices)),
            dma((4, chips - 1)),
            dma((4, chips - 1)),
        ],
        compiler_params=params(2),
        name="head",
    )(rows, hidden, teacher_hidden, part, last_all, protos, teacher_protos, centre, mask, mask_row)


def gram_device(matrix):
    return 2 * matrix


def dot_high(left, right, contract):
    return lax.dot_general(
        left,
        right,
        (contract, ((), ())),
        precision=lax.Precision.HIGHEST,
        preferred_element_type=FULL,
    )


def inverse_factor(block):
    size = block.shape[0]
    tiles = size // 8
    wide = 8
    sub = lax.broadcasted_iota(jnp.int32, (8, size), 0)
    lane = lax.broadcasted_iota(jnp.int32, (8, size), 1)
    rest = [block[8 * t : 8 * t + 8] for t in range(tiles)]
    made = [jnp.where(lane == sub + 8 * t, 1.0, 0.0) for t in range(tiles)]

    def full(value):
        return jnp.broadcast_to(value, (8, size))

    for k in range(0, size, wide):
        tile, row = k // 8, k % 8
        factor_rows = [full(rest[tile][row + i : row + i + 1]) for i in range(wide)]
        made_rows = [full(made[tile][row + i : row + i + 1]) for i in range(wide)]
        entry = [
            [full(rest[tile][row + i : row + i + 1, k + j : k + j + 1]) for j in range(i + 1)]
            for i in range(wide)
        ]
        columns = [
            [full(rest[t][:, k + j : k + j + 1]) for j in range(wide)] for t in range(tile, tiles)
        ]
        for j in range(wide):
            scale = lax.rsqrt(entry[j][j])
            factor_rows[j] = factor_rows[j] * scale
            made_rows[j] = made_rows[j] * scale
            for i in range(j + 1, wide):
                entry[i][j] = entry[i][j] * scale
            for some in columns:
                some[j] = some[j] * scale
            for i in range(j + 1, wide):
                factor_rows[i] = factor_rows[i] - entry[i][j] * factor_rows[j]
                made_rows[i] = made_rows[i] - entry[i][j] * made_rows[j]
                for e in range(j + 1, i + 1):
                    entry[i][e] = entry[i][e] - entry[i][j] * entry[e][j]
                for some in columns:
                    some[i] = some[i] - entry[i][j] * some[j]
        for t in range(tile, tiles):
            some = columns[t - tile]
            if t == tile:
                some = [jnp.where(sub >= row + wide, column, 0.0) for column in some]
            for j in range(wide):
                rest[t] = rest[t] - some[j] * factor_rows[j]
                made[t] = made[t] - some[j] * made_rows[j]
            if t == tile:
                for j in range(wide):
                    made[t] = jnp.where(sub == row + j, made_rows[j], made[t])
    return jnp.concatenate(made, 0)


def renew_kernel(
    devices,
    stats_ref,
    basis_ref,
    own_stats_ref,
    own_bases_ref,
    stat,
    base,
    gram,
    work,
    done,
    given,
    taken,
    passed,
    sent,
    landed,
    die_sent,
    die_landed,
):
    me = lax.axis_index(AXIS)
    core = lax.rem(me, 2)
    chip = me // 2
    chips = devices // 2
    partner = me + 1 - 2 * core
    parts, rows = stats_ref.shape[:2]
    size = parts * rows
    blocks = size // LANES
    matrices = own_stats_ref.shape[0]
    is_gram = (core == 0) & (chip < matrices)
    spare = given.shape[3] - rows
    greet([lax.rem(me + 2 * at, devices) for at in range(1, chips)] + [partner])

    def out_copy(kind, at):
        peer = lax.rem(me + 2 * at, devices)
        return pltpu.make_async_remote_copy(
            src_ref=given.at[kind, peer // 2],
            dst_ref=taken.at[kind, chip],
            send_sem=sent.at[kind, at],
            recv_sem=landed.at[kind, chip],
            device_id=(peer,),
            device_id_type=MESH,
        )

    def across(kind):
        return pltpu.make_async_remote_copy(
            src_ref=taken.at[kind, :, 1],
            dst_ref=passed.at[kind],
            send_sem=die_sent.at[kind],
            recv_sem=die_landed.at[kind],
            device_id=(partner,),
            device_id_type=MESH,
        )

    def hand_out(kind, row_of):
        blank = jnp.zeros((spare, size), FULL)
        for part in range(parts):
            given[kind, part // 2, part % 2] = jnp.concatenate([row_of(part), blank], 0).astype(LOW)
        taken[kind, chip] = given[kind, chip]
        for at in range(1, chips):
            out_copy(kind, at).start()

    @pl.when(is_gram)
    def _():
        hand_out(0, lambda part: stats_ref[part])
        for part in range(parts):
            stat[part * rows : (part + 1) * rows] = stats_ref[part]
            base[part * rows : (part + 1) * rows] = basis_ref[part]
        at_row = lax.broadcasted_iota(jnp.int32, (size, size), 0)
        at_col = lax.broadcasted_iota(jnp.int32, (size, size), 1)
        trace = jnp.sum(jnp.where(at_row == at_col, stat[...], 0.0), axis=(0, 1), keepdims=True)
        scaled = dot_high(stat[...], base[...], ((1,), (0,))) * (size / trace)
        product = dot_high(scaled, scaled, ((0,), (0,)))
        for b in range(blocks):
            work[b] = scaled[:, b * LANES : (b + 1) * LANES]
            for c in range(blocks):
                gram[b, c] = product[b * LANES : (b + 1) * LANES, c * LANES : (c + 1) * LANES]

        def step(b, carried):
            inverse = inverse_factor(gram[b, b])
            made = dot_high(work[b], inverse, ((1,), (1,)))
            done[b] = made

            def trail(c, inner):
                panel = dot_high(inverse, gram[b, c], ((1,), (0,)))
                work[c] = work[c] - dot_high(made, panel, ((1,), (0,)))

                def against(e, innermost):
                    other = dot_high(inverse, gram[b, e], ((1,), (0,)))
                    gram[c, e] = gram[c, e] - dot_high(panel, other, ((0,), (0,)))
                    return innermost

                lax.fori_loop(c, blocks, against, 0)
                return inner

            lax.fori_loop(b + 1, blocks, trail, 0)
            return carried

        lax.fori_loop(0, blocks, step, 0)
        whole = jnp.concatenate([done[b] for b in range(blocks)], 1)
        hand_out(1, lambda part: whole[part * rows : (part + 1) * rows])

    @pl.when(core == 0)
    def _():
        for kind in range(2):
            for matrix in range(matrices):

                @pl.when(chip != matrix)
                def _(kind=kind, matrix=matrix):
                    view = taken.at[kind, matrix]
                    pltpu.make_async_copy(view, view, landed.at[kind, matrix]).wait()

            across(kind).start()
        own_stats_ref[...] = taken[0, :, 0, :rows].astype(FULL)
        own_bases_ref[...] = taken[1, :, 0, :rows].astype(FULL)
        for kind in range(2):
            across(kind).wait_send()

    @pl.when(core == 1)
    def _():
        for kind in range(2):
            across(kind).wait_recv()
        own_stats_ref[...] = passed[0, :, :rows].astype(FULL)
        own_bases_ref[...] = passed[1, :, :rows].astype(FULL)

    @pl.when(is_gram)
    def _():
        for kind in range(2):
            for at in range(1, chips):
                out_copy(kind, at).wait_send()


def renew_own(stats, basis, matrices):
    devices, rows, width = stats.shape
    size = devices * rows
    blocks = size // LANES
    padded = -(-rows // 16) * 16
    vmem = pl.BlockSpec(memory_space=pltpu.VMEM)
    dma = pltpu.SemaphoreType.DMA
    return pl.pallas_call(
        functools.partial(renew_kernel, devices),
        out_shape=(jax.ShapeDtypeStruct((matrices, rows, width), FULL),) * 2,
        in_specs=[vmem] * 2,
        out_specs=(vmem,) * 2,
        scratch_shapes=[
            pltpu.VMEM((size, width), FULL),
            pltpu.VMEM((size, width), FULL),
            pltpu.VMEM((blocks, blocks, LANES, LANES), FULL),
            pltpu.VMEM((blocks, size, LANES), FULL),
            pltpu.VMEM((blocks, size, LANES), FULL),
            pltpu.VMEM((2, devices // 2, 2, padded, width), LOW),
            pltpu.VMEM((2, matrices, 2, padded, width), LOW),
            pltpu.VMEM((2, matrices, padded, width), LOW),
            dma((2, devices // 2)),
            dma((2, matrices)),
            dma((2,)),
            dma((2,)),
        ],
        compiler_params=params(4, 40 << 20),
        name="renew",
    )(stats, basis)


def head_slow(
    features,
    teacher_features,
    valid_mask,
    head_hidden,
    head_last,
    protos,
    teacher_hidden,
    teacher_last,
    teacher_protos,
    centre,
    device_index,
):
    all_features, all_teacher = (
        lax.all_gather(features, AXIS, axis=0, tiled=True),
        lax.all_gather(teacher_features, AXIS, axis=0, tiled=True),
    )
    first_weight = head_hidden[:, :D].astype(jnp.bfloat16)
    second_weight = head_hidden[:, D:].astype(jnp.bfloat16)
    last_weight = head_last.astype(jnp.bfloat16)
    proto_weight = protos.astype(jnp.bfloat16)
    teacher_first = teacher_hidden[:, :D].astype(jnp.bfloat16)
    teacher_second = teacher_hidden[:, D:].astype(jnp.bfloat16)
    pre_one = matmul_low("bd,hd->bh", all_features, first_weight)
    teacher_pre_one = matmul_low("bd,hd->bh", all_teacher, teacher_first)
    act_one = (
        lax.all_gather(gelu_exact(pre_one).astype(jnp.bfloat16), AXIS, axis=1, tiled=True),
        lax.all_gather(gelu_exact(teacher_pre_one).astype(jnp.bfloat16), AXIS, axis=1, tiled=True),
    )
    pre_two = matmul_low("bh,kh->bk", act_one[0], second_weight)
    teacher_pre_two = matmul_low("bh,kh->bk", act_one[1], teacher_second)
    act_two = (
        lax.all_gather(gelu_exact(pre_two).astype(jnp.bfloat16), AXIS, axis=1, tiled=True),
        lax.all_gather(gelu_exact(teacher_pre_two).astype(jnp.bfloat16), AXIS, axis=1, tiled=True),
    )
    bottles = (
        lax.all_gather(matmul_low("bh,hc->bc", act_two[0], last_weight), AXIS, axis=1, tiled=True),
        lax.all_gather(
            matmul_low("bh,hc->bc", act_two[1], teacher_last.astype(jnp.bfloat16)),
            AXIS,
            axis=1,
            tiled=True,
        ),
    )
    unit, inverse_norm = unit_rows(bottles[0])
    teacher_unit, unused_norm = unit_rows(bottles[1])
    unit_low = unit.astype(jnp.bfloat16)
    logits = matmul_low("bc,cp->bp", unit_low, proto_weight)
    teacher_logits = matmul_low(
        "bc,cp->bp", teacher_unit.astype(jnp.bfloat16), teacher_protos.astype(jnp.bfloat16)
    )
    scaled = logits / TAU_STUDENT
    student_top = jnp.max(scaled, -1)
    student_total = jnp.sum(jnp.exp(scaled - student_top[:, None]), -1)
    sharpened = (teacher_logits - centre) / TAU_TEACHER
    teacher_top = jnp.max(sharpened, -1)
    teacher_exp = jnp.exp(sharpened - teacher_top[:, None])
    merged = joined(
        (
            student_top,
            student_total,
            teacher_top,
            jnp.sum(teacher_exp, -1),
            jnp.sum(teacher_exp * scaled, -1),
        ),
        AXIS,
        combine_parts,
    )
    log_total = merged[0] + jnp.log(merged[1])
    counted = valid_mask.astype(jnp.float32)
    loss_count = jnp.sum(counted)
    loss_sum = jnp.sum(counted * (log_total - merged[4] / merged[3]))
    student_prob = jnp.exp(scaled - log_total[:, None])
    teacher_prob = jnp.exp(sharpened - merged[2][:, None]) / merged[3][:, None]
    grad_logits = (
        (counted / loss_count)[:, None] * (student_prob - teacher_prob) / TAU_STUDENT
    ).astype(jnp.bfloat16)
    grad_protos = matmul_low("bc,bp->cp", unit_low, grad_logits)
    grad_unit = lax.psum(matmul_low("bp,cp->bc", grad_logits, proto_weight), AXIS)
    grad_bottle = inverse_norm * (grad_unit - unit * jnp.sum(unit * grad_unit, -1, keepdims=True))
    last_width = head_last.shape[1]
    grad_bottle_own = lax.dynamic_slice_in_dim(
        grad_bottle, device_index * last_width, last_width, 1
    ).astype(jnp.bfloat16)
    grad_last = matmul_low("bh,bc->hc", act_two[0], grad_bottle_own)
    grad_act_two = lax.psum_scatter(
        matmul_low("bc,hc->bh", grad_bottle_own, last_weight), AXIS, scatter_dimension=1, tiled=True
    )
    grad_pre_two = (grad_act_two * gelu_slope(pre_two)).astype(jnp.bfloat16)
    grad_second = matmul_low("bk,bh->kh", grad_pre_two, act_one[0])
    grad_act_one = lax.psum_scatter(
        matmul_low("bk,kh->bh", grad_pre_two, second_weight), AXIS, scatter_dimension=1, tiled=True
    )
    grad_pre_one = (grad_act_one * gelu_slope(pre_one)).astype(jnp.bfloat16)
    grad_first = matmul_low("bh,bd->hd", grad_pre_one, all_features)
    grad_features = lax.psum_scatter(
        matmul_low("bh,hd->bd", grad_pre_one, first_weight), AXIS, scatter_dimension=0, tiled=True
    )
    grad_hidden = jnp.concatenate([grad_first, grad_second], 1)
    next_centre = (
        CENTRE_MOMENTUM * centre
        + (1.0 - CENTRE_MOMENTUM) * jnp.sum(counted[:, None] * teacher_logits, 0) / loss_count
    )
    return (loss_sum, loss_count, grad_hidden, grad_last, grad_protos, grad_features, next_centre)


def head_fast(
    feature_rows,
    valid_mask,
    head_hidden,
    protos,
    teacher_hidden,
    teacher_protos,
    centre,
    part,
    last_all,
    devices,
):
    counted = valid_mask.astype(FULL)
    mask_row = jnp.pad(counted, (0, LANES - counted.size)).reshape(1, LANES)
    scalars, grad_hidden, grad_last, grad_protos, grad_feat, next_centre = head(
        feature_rows,
        head_hidden,
        teacher_hidden,
        part,
        last_all,
        protos,
        teacher_protos,
        centre[None],
        counted[:, None],
        mask_row,
        devices,
    )
    return (
        scalars[0, 0],
        scalars[0, 1],
        scalars,
        grad_hidden,
        grad_last.T,
        grad_protos,
        grad_feat,
        next_centre[0],
    )


TOKENS = 272
HALF_ROW = 256
SAVED = ("inputs", "normed", "joint", "mixed", "attended", "middle", "normed_two", "activated", "slope", "outer")


def saved_widths():
    return {
        "inputs": (D, FULL),
        "normed": (D, LOW),
        "joint": (3 * D, LOW),
        "mixed": (D, LOW),
        "attended": (D, LOW),
        "middle": (D, FULL),
        "normed_two": (D, LOW),
        "activated": (MLP, LOW),
        "slope": (MLP, LOW),
        "outer": (D, LOW),
    }


def unpack_blocks(weights, joint_out, output_out, cuts, depth):
    devices = weights.shape[0]
    joint_rows, output_rows = cuts[0], cuts[1] - cuts[0]
    group = 4
    for at in range(0, devices, group):
        blocks = [
            weights[slot_of(at + t, depth), 0 : cuts[1]].astype(FULL) for t in range(group)
        ]
        joint = jnp.concatenate([block[:joint_rows] for block in blocks], 0)
        output = jnp.concatenate([block[joint_rows:] for block in blocks], 0)
        joint_out[at * joint_rows : (at + group) * joint_rows] = joint.astype(LOW)
        output_out[at * output_rows : (at + group) * output_rows] = output.astype(LOW)


def weight_rows(weights, cuts, which, part, parts):
    per = weights.shape[0] // parts
    block = weights[part * per : (part + 1) * per, cuts[which] : cuts[which + 1]]
    return block.reshape(-1, block.shape[-1])


def chance(keys_half, queries, live):
    scores = jnp.where(live, dot_nt(keys_half, queries), -jnp.inf)
    grown = jnp.exp(scores - jnp.max(scores, 0, keepdims=True))
    return grown * (1.0 / jnp.sum(grown, 0, keepdims=True))


WIDE_TABLE = 1152
POSITION_AT = 640
VECTORS_AT = 1024


CLASS_ROWS = 16


def by_head(row):
    head = lax.broadcasted_iota(jnp.int32, (CLASS_ROWS, D), 0)
    lane = lax.broadcasted_iota(jnp.int32, (CLASS_ROWS, D), 1)
    return jnp.where(lax.shift_right_logical(lane, 6) == head, row, 0.0)


def tail_rows_of(row):
    at = lax.broadcasted_iota(jnp.int32, (TOKENS - HALF_ROW, D), 0)
    return jnp.where(at == 0, row, 0.0)


def head_halves(wide):
    lane = lax.broadcasted_iota(jnp.int32, wide.shape, 1)
    low_half = jnp.where(lane < HEAD_DIM, wide, 0.0)
    return low_half.astype(LOW), (wide - low_half).astype(LOW)


def live_keys(columns):
    return lax.broadcasted_iota(jnp.int32, (TOKENS, columns), 0) < SEQ


def table_rows(embedding):
    turned = embedding.T
    columns = turned.shape[0]
    patch = jnp.pad(turned[:, :PIX], ((0, 0), (0, POSITION_AT - PIX)))
    position = jnp.concatenate([turned[:, PIX + 1 : PIX + SEQ], turned[:, PIX : PIX + 1]], 1)
    position = jnp.pad(position, ((0, 0), (0, VECTORS_AT - POSITION_AT - SEQ)))
    layer_rows = turned[:, PIX + SEQ : PIX + SEQ + 6 * LAYERS].reshape(columns, LAYERS, 6)
    layer_rows = jnp.pad(layer_rows, ((0, 0), (0, 0), (0, 2))).reshape(columns, -1)
    tail_rows = turned[:, PIX + SEQ + 6 * LAYERS :]
    joint = jnp.concatenate([patch, position, layer_rows, tail_rows], 1)
    rows = -(-columns // 16) * 16
    joint = jnp.pad(joint, ((0, rows - columns), (0, WIDE_TABLE - joint.shape[1]))).astype(LOW)
    return jnp.concatenate([joint[:, at : at + D] for at in range(0, WIDE_TABLE, D)], 0)


PLAN = {
    -1: ((0, 0), (0, 1), (0, 2), (1, 0), (1, 1), (0, 3), (2, 0), (1, 2), (0, 4), (2, 1), (3, 0), (4, 0), (3, 1), (1, 3), (2, 2), (4, 1)),
    0: ((1, 4), (0, 5)),
    -2: ((2, 3), (3, 2), (4, 2)),
    1: ((2, 4), (3, 3)),
    2: ((4, 3), (3, 4), (1, 5), (0, 6)),
    3: ((4, 4),),
    4: ((2, 5),),
    5: ((3, 5), (1, 6), (0, 7)),
    6: ((4, 5),),
    7: ((2, 6),),
    8: ((3, 6), (1, 7), (0, 8)),
    9: ((4, 6),),
    10: ((2, 7),),
    11: ((3, 7), (1, 8), (0, 9)),
    12: ((4, 7),),
    13: ((2, 8),),
    14: ((3, 8), (1, 9)),
    15: ((4, 8),),
    16: ((2, 9),),
    17: ((3, 9),),
    -3: ((4, 9),),
}


def fetch_kernel(
    cuts,
    depth,
    patches_ref,
    table_ref,
    teacher_table_ref,
    layers_ref,
    teacher_layers_ref,
    last_ref,
    columns_ref,
    feat_ref,
    final_ref,
    vectors_out_ref,
    weights_out_ref,
    last_out_ref,
    part_ref,
    *rest,
):
    layer, model, image = (pl.program_id(at) for at in range(3))
    images = pl.num_programs(2)
    step = (layer * 2 + model) * images + image
    outs = dict(zip(SAVED, rest[: len(SAVED)]))
    (
        current,
        joint_weight,
        output_weight,
        weights_all,
        tables,
        turned,
        vectors_all,
        out_sem,
        part_own,
        part_sent,
        part_landed,
        part_die,
        *sems,
    ) = rest[len(SAVED) :]
    sources = (layers_ref, teacher_layers_ref)
    rows = layers_ref.shape[1]
    first = cuts[1]

    def layer_item(which, at, lower, size):
        return (sources[which].at[at], weights_all.at[which, at], lower, size)

    items = [
        (table_ref, tables.at[0], 0, table_ref.shape[0]),
        layer_item(0, 0, 0, first),
        layer_item(0, 0, first, rows - first),
        (teacher_table_ref, tables.at[1], 0, table_ref.shape[0]),
        layer_item(1, 0, 0, rows),
        layer_item(0, 1, 0, rows),
        layer_item(1, 1, 0, rows),
        layer_item(0, 2, 0, rows),
        layer_item(1, 2, 0, rows),
        (last_ref, last_out_ref, 0, last_ref.shape[0]),
    ]
    route = Route(depth, items, *sems)
    total = 8 * depth
    chips = total // 2
    chip = route.me // 2
    core = route.core

    def part_copy(at):
        peer = lax.rem(route.me + 2 * at, total)
        block = columns_ref.at[:, pl.ds(pl.multiple_of((peer // 2) * LANES, LANES), LANES)]
        return route.copy(
            block, part_ref.at[core, chip], part_sent.at[at], part_landed.at[at], peer
        )

    def part_mine():
        block = columns_ref.at[:, pl.ds(pl.multiple_of(chip * LANES, LANES), LANES)]
        return pltpu.make_async_copy(block, part_ref.at[core, chip], part_own.at[0])

    def part_across():
        return route.copy(
            part_ref.at[core], part_ref.at[core], part_die.at[0], part_die.at[1], route.partner
        )

    def out_copy(at):
        return pltpu.make_async_copy(weights_all.at[0, at], weights_out_ref.at[at], out_sem.at[at])

    def run(name):
        for word in PLAN[name]:
            route.act(*word)

    @pl.when(step == 0)
    def _():
        greet([lax.rem(route.me + 2 * at, total) for at in range(1, chips)] + [route.partner])
        run(-1)

    def set_up(which):
        columns = D // total
        block_rows = table_ref.shape[0] // (WIDE_TABLE // D)
        group = 4
        for at in range(0, total, group):
            for block in range(WIDE_TABLE // D):
                lower = block * block_rows
                pieces = [
                    tables[which, slot_of(at + t, depth), lower : lower + block_rows].astype(FULL)[
                        :columns
                    ]
                    for t in range(group)
                ]
                turned[at * columns : (at + group) * columns, block * D : (block + 1) * D] = (
                    jnp.concatenate(pieces, 0).astype(LOW)
                )
        vectors = turned[:, VECTORS_AT:WIDE_TABLE].astype(FULL).T
        vectors_all[which] = vectors[:32]
        position = turned[:, POSITION_AT:VECTORS_AT].astype(FULL).T[:TOKENS]
        row = lax.broadcasted_iota(jnp.int32, (TOKENS, D), 0)
        tail = 8 * LAYERS
        extra = jnp.where(
            row < HALF_ROW,
            vectors[tail : tail + 1],
            jnp.where(row == HALF_ROW, vectors[tail + 1 : tail + 2], 0.0),
        )
        start = position + extra
        for at in range(feat_images):
            current[which, at, :HALF_ROW] = start[:HALF_ROW] + dot_nt(
                patches_ref[at], turned[:, :PIX]
            )
            current[which, at, HALF_ROW:] = start[HALF_ROW:]

    feat_images = patches_ref.shape[0]
    for at in range(18):

        @pl.when(step == at)
        def _(at=at):
            run(at)
            if at == 0:
                set_up(0)
                vectors_out_ref[...] = vectors_all[0]
            if at == 3:
                set_up(1)
            if at == 3:
                out_copy(0).start()
            if at == 6:
                out_copy(1).start()
            if at == 11:
                part_mine().start()
                for other in range(1, chips):
                    part_copy(other).start()
            if at == 12:
                out_copy(2).start()
            if at == 16:
                part_mine().wait()
                for other in range(1, chips):
                    part_copy(other).wait_recv()
                part_across().start()

    weights = weights_all.at[model, layer]

    @pl.when(image == 0)
    def _():
        unpack_blocks(weights, joint_weight, output_weight, cuts, depth)

    vectors = vectors_all[model, pl.ds(pl.multiple_of(layer * 8, 8), 8), :]
    live = live_keys(HALF_ROW)

    def attend(save):
        def keep(name, value):
            if save:
                outs[name][0, 0] = value

        inputs = current[model, image]
        keep("inputs", inputs)
        normed = layer_norm(inputs, vectors[0:1], vectors[1:2]).astype(LOW)
        keep("normed", normed)
        joint = dot_nt(normed, joint_weight[...])
        rounded = joint.astype(LOW)
        keep("joint", rounded)
        queries = (rounded[:, :D].astype(FULL) * HEAD_DIM ** (-0.5)).astype(LOW)
        keys_in, values_in = rounded[:, D : 2 * D], rounded[:, 2 * D :]
        values = joint[:, 2 * D :].T.astype(LOW)
        turned_heads = []
        for pair in range(D // LANES):
            columns = slice(pair * LANES, (pair + 1) * LANES)
            for half, keys_half in enumerate(head_halves(keys_in[:, columns].astype(FULL))):
                lower = pair * LANES + half * HEAD_DIM
                scores = jnp.where(live, dot_nt(keys_half, queries[:HALF_ROW, columns]), -jnp.inf)
                grown = jnp.exp(scores - jnp.max(scores, 0, keepdims=True))
                scale = 1.0 / jnp.sum(grown, 0, keepdims=True)
                value = dot_nn(values[lower : lower + HEAD_DIM], grown.astype(LOW))
                turned_heads.append(value * scale)
        class_query = by_head(queries[HALF_ROW:].astype(FULL)[:1]).astype(LOW)
        class_share = chance(keys_in, class_query, live_keys(CLASS_ROWS)).astype(LOW)
        class_mixed = jnp.sum(by_head(dot_tn(class_share, values_in)), 0, keepdims=True)
        mixed = jnp.concatenate(
            [
                jnp.concatenate(turned_heads, 0).T.astype(LOW),
                tail_rows_of(class_mixed).astype(LOW),
            ],
            0,
        )
        keep("mixed", mixed)
        attended = dot_nt(mixed, output_weight[...])
        keep("attended", attended.astype(LOW))
        middle = inputs + vectors[4:5] * attended
        keep("middle", middle)
        current[model, image] = middle

    def perceive(save):
        def keep(name, value):
            if save:
                outs[name][0, 0] = value

        middle = current[model, image]
        normed_two = layer_norm(middle, vectors[2:3], vectors[3:4]).astype(LOW)
        keep("normed_two", normed_two)
        outer = jnp.zeros((TOKENS, D), FULL)
        parts = MLP // D
        for part in range(parts):
            inner = dot_nt(normed_two, weight_rows(weights, cuts, 1, part, parts))
            spread_half = 0.5 * (1.0 + lax.erf(inner * ROOT_HALF))
            activated = (inner * spread_half).astype(LOW)
            if save:
                outs["activated"][0, 0, :, part * D : (part + 1) * D] = activated
                slope = spread_half + inner * jnp.exp(-0.5 * inner * inner) * DENSITY_SCALE
                outs["slope"][0, 0, :, part * D : (part + 1) * D] = slope.astype(LOW)
            outer = outer + dot_nn(activated, weight_rows(weights, cuts, 2, part, parts))
        keep("outer", outer.astype(LOW))
        result = middle + vectors[5:6] * outer
        current[model, image] = result
        final = result[HALF_ROW : HALF_ROW + 8]
        final_ref[model, image] = final
        tail = 8 * LAYERS
        feat_ref[model, image] = layer_norm(
            final, vectors_all[model, tail + 2 : tail + 3], vectors_all[model, tail + 3 : tail + 4]
        )

    @pl.when(model == 0)
    def _():
        attend(True)

    @pl.when(model == 1)
    def _():
        attend(False)

    @pl.when(step == 0)
    def _():
        run(-2)

    @pl.when(model == 0)
    def _():
        perceive(True)

    @pl.when(model == 1)
    def _():
        perceive(False)

    @pl.when(step == 17)
    def _():
        run(-3)
        for at in range(len(items)):
            route.act(5, at)
        for at in range(LAYERS):
            out_copy(at).wait()
        across = part_across()
        across.wait_recv()
        across.wait_send()
        for other in range(1, chips):
            part_copy(other).wait_send()


def fetch_forward(patches, embedding, teacher_embedding, layers, teacher_layers, head_last, teacher_last, head_hidden, devices):
    images = patches.shape[0]
    depth = devices // 8
    rows = layers.shape[1]
    cuts = [lower for lower, upper in layer_bounds(devices)][1:] + [rows]
    shape = jax.ShapeDtypeStruct
    vmem = pl.BlockSpec(memory_space=pltpu.VMEM)
    anywhere = pl.BlockSpec(memory_space=pl.ANY)

    table = table_rows(embedding)
    last = jnp.concatenate([head_last, teacher_last], 1).T.astype(LOW)
    across = last.shape[1] // 2
    last = jnp.concatenate([last[:, :across], last[:, across:]], 0)
    columns = head_hidden[:, D:].astype(LOW)
    outs = [shape((2, images, 8, D), FULL)] * 2
    specs = [vmem] * 2
    outs += [
        shape((32, D), FULL),
        shape((LAYERS, devices, rows, D), LOW),
        shape((devices,) + last.shape, LOW),
        shape((2, devices // 2, columns.shape[0], LANES), LOW),
    ]
    specs += [vmem, anywhere, anywhere, anywhere]
    for name in SAVED:
        width, kind = saved_widths()[name]
        outs.append(shape((LAYERS, images, TOKENS, width), kind))
        specs.append(
            pl.BlockSpec(
                (1, 1, TOKENS, width),
                lambda layer, model, image: (layer, jnp.where(model == 0, image, images - 1), 0, 0),
            )
        )
    count = 10
    dma = pltpu.SemaphoreType.DMA
    return pl.pallas_call(
        functools.partial(fetch_kernel, cuts, depth),
        grid=(LAYERS, 2, images),
        out_shape=outs,
        in_specs=[vmem] + [anywhere] * 6,
        out_specs=specs,
        scratch_shapes=[
            pltpu.VMEM((2, images, TOKENS, D), FULL),
            pltpu.VMEM((3 * D, D), LOW),
            pltpu.VMEM((D, D), LOW),
            pltpu.VMEM((2, LAYERS, devices, rows, D), LOW),
            pltpu.VMEM((2, devices) + table.shape, LOW),
            pltpu.VMEM((D, WIDE_TABLE), LOW),
            pltpu.VMEM((2, 32, D), FULL),
            dma((LAYERS,)),
            dma((1,)),
            dma((devices // 2,)),
            dma((devices // 2,)),
            dma((2,)),
        ]
        + route_sems(count, depth),
        compiler_params=params(1, 60 << 20),
        name="fetch_forward",
    )(
        patches,
        table,
        table_rows(teacher_embedding),
        layers.astype(LOW),
        teacher_layers.astype(LOW),
        last,
        columns,
    )


class Reduce:
    def __init__(self, depth, chunks, sources, buffers, sems):
        self.depth, self.chunks, self.sources = depth, chunks, sources
        self.die_buf, self.d_buf, self.x_buf, self.y_buf, self.z_buf = buffers
        self.die_sent, self.die_landed, self.near_sent, self.near_landed, self.z_sent, self.z_landed = sems
        me = lax.axis_index(AXIS)
        self.me = me
        self.total = 8 * depth
        core = lax.rem(me, 2)
        x_at = lax.rem(me // 2, 2)
        y_at = lax.rem(me // 4, 2)
        self.z_at = me // 8
        self.partner = me + 1 - 2 * core
        self.to_x = me + 2 - 4 * x_at
        self.to_y = me + 4 - 8 * y_at
        places = [(y_at, x_at), (y_at, 1 - x_at), (1 - y_at, x_at), (1 - y_at, 1 - x_at)]
        self.starts = [((y * 2 + x) * 2 + core) * depth for y, x in places]
        self.partner_starts = [((y * 2 + x) * 2 + 1 - core) * depth for y, x in places]

    def copy(self, source, target, sent, landed, device):
        return pltpu.make_async_remote_copy(
            src_ref=source,
            dst_ref=target,
            send_sem=sent,
            recv_sem=landed,
            device_id=(device,),
            device_id_type=MESH,
        )

    def half(self, k):
        return ((self.chunks[k][1] // 2 + 15) // 16) * 16

    def die(self, k, rel):
        lower, size = self.chunks[k]
        return self.copy(
            self.sources[k].at[pl.ds(self.partner_starts[rel], self.depth)],
            self.die_buf.at[pl.ds(rel * self.depth, self.depth), pl.ds(lower, size)],
            self.die_sent.at[k, rel],
            self.die_landed.at[k, rel],
            self.partner,
        )

    def near(self, k, which):
        lower, size = self.chunks[k]
        half = self.half(k)
        rel, start, length, target, device = [
            (3, lower, half, self.d_buf, self.to_x),
            (3, lower + half, size - half, self.d_buf, self.to_y),
            (1, lower, size, self.x_buf, self.to_x),
            (2, lower, size, self.y_buf, self.to_y),
        ][which]
        return self.copy(
            self.die_buf.at[pl.ds(rel * self.depth, self.depth), pl.ds(start, length)],
            target.at[:, pl.ds(start, length)],
            self.near_sent.at[k, which],
            self.near_landed.at[k, which],
            device,
        )

    def deep(self, k, step):
        lower, size = self.chunks[k]
        return self.copy(
            self.die_buf.at[lax.rem(self.z_at + step, self.depth), pl.ds(lower, size)],
            self.z_buf.at[self.z_at, pl.ds(lower, size)],
            self.z_sent.at[k, step],
            self.z_landed.at[k, step],
            lax.rem(self.me + 8 * step, self.total),
        )

    def pair_sum(self, k, rel, z_pos, first, length):
        lower, size = self.chunks[k]
        return self.sources[k][
            self.starts[rel] + z_pos, first - lower : first - lower + length
        ].astype(FULL) + self.die_buf[rel * self.depth + z_pos, first : first + length].astype(FULL)

    def begin(self, k):
        for rel in (3, 1, 2, 0):
            self.die(k, rel).start()

    def one(self, k):
        lower, size = self.chunks[k]
        self.die(k, 3).wait_recv()
        for z_pos in range(self.depth):
            self.die_buf[3 * self.depth + z_pos, lower : lower + size] = self.pair_sum(
                k, 3, z_pos, lower, size
            ).astype(LOW)
        self.near(k, 0).start()
        self.near(k, 1).start()

    def two(self, k):
        lower, size = self.chunks[k]
        half = self.half(k)
        first, second = (lower, half), (lower + half, size - half)
        for rel, which, arrived, helped, plain in ((1, 2, 1, second, first), (2, 3, 0, first, second)):
            self.die(k, rel).wait_recv()
            self.near(k, arrived).wait_recv()
            for z_pos in range(self.depth):
                at = rel * self.depth + z_pos
                self.die_buf[at, plain[0] : plain[0] + plain[1]] = self.pair_sum(
                    k, rel, z_pos, *plain
                ).astype(LOW)
                self.die_buf[at, helped[0] : helped[0] + helped[1]] = (
                    self.pair_sum(k, rel, z_pos, *helped)
                    + self.d_buf[z_pos, helped[0] : helped[0] + helped[1]].astype(FULL)
                ).astype(LOW)
            self.near(k, which).start()

    def three(self, k):
        lower, size = self.chunks[k]
        self.die(k, 0).wait_recv()
        self.near(k, 2).wait_recv()
        self.near(k, 3).wait_recv()
        for z_pos in range(self.depth):
            self.die_buf[z_pos, lower : lower + size] = (
                self.pair_sum(k, 0, z_pos, lower, size)
                + self.x_buf[z_pos, lower : lower + size].astype(FULL)
                + self.y_buf[z_pos, lower : lower + size].astype(FULL)
            ).astype(LOW)
        for step in range(1, self.depth):
            self.deep(k, step).start()

    def four(self, k):
        lower, size = self.chunks[k]
        for step in range(1, self.depth):
            self.deep(k, step).wait_recv()
        value = self.die_buf[self.z_at, lower : lower + size].astype(FULL)
        for step in range(1, self.depth):
            value = value + self.z_buf[
                lax.rem(self.z_at + step, self.depth), lower : lower + size
            ].astype(FULL)
        return value

    def sent(self, k, die_too):
        if die_too:
            for rel in range(4):
                self.die(k, rel).wait_send()
        for which in range(4):
            self.near(k, which).wait_send()
        for step in range(1, self.depth):
            self.deep(k, step).wait_send()


PER_LAYER = ("normed", "mixed", "normed_two", "activated")


def backward_kernel(cuts, bounds, depth, *refs):
    (
        squares_ref,
        stats_ref,
        bases_ref,
        bases_low_ref,
        patches_ref,
        weights_ref,
        vectors_ref,
        final_ref,
        grad_feat_ref,
    ) = refs[:9]
    saved = dict(zip(SAVED, refs[9 : 9 + len(SAVED)]))
    (
        own_ref,
        norm_ref,
        next_stats_ref,
        basis_ref,
        bases_all_ref,
        grad_now,
        joint_weight,
        output_weight,
        grad_outer_all,
        grad_inner_all,
        grad_attended_all,
        grad_joint_all,
        grad_patch,
        grad_start,
        grad_rows,
        packets,
        table_packet,
        die_buf,
        d_buf,
        x_buf,
        y_buf,
        z_buf,
        stat_buf,
        square_out,
        square_all,
        segs,
        gram_buf,
        die_sent,
        die_landed,
        near_sent,
        near_landed,
        z_sent,
        z_landed,
        stat_sent,
        stat_landed,
        gram_sent,
        gram_landed,
        square_sent,
        square_landed,
        *sems,
    ) = refs[9 + len(SAVED) :]
    step, image = pl.program_id(0), pl.program_id(1)
    images = final_ref.shape[1]
    route = Route(depth, [(bases_low_ref, bases_all_ref, 0, bases_low_ref.shape[0])], *sems)
    now = step * images + image
    layer_rows = cuts[3]
    chunks = [(layer * layer_rows, layer_rows) for layer in reversed(range(LAYERS))]
    chunks.append((LAYERS * layer_rows, table_packet.shape[1]))
    count = len(chunks)
    sources = [packets.at[k % 2] for k in range(LAYERS)] + [table_packet]
    ring = Reduce(
        depth,
        chunks,
        sources,
        (die_buf, d_buf, x_buf, y_buf, z_buf),
        (die_sent, die_landed, near_sent, near_landed, z_sent, z_landed),
    )
    me = ring.me
    total = ring.total
    core = lax.rem(me, 2)
    chip = me // 2
    matrices = stats_ref.shape[0]
    own_rows = stats_ref.shape[1]
    segment_rows = segs.shape[2]
    is_gram = (core == 0) & (chip < matrices)
    everyone = [lax.rem(me + at, total) for at in range(1, total)]

    def stat_copy(at, matrix):
        source = (stats_ref, bases_ref)[at]
        return ring.copy(
            source.at[matrix],
            stat_buf.at[at, me],
            stat_sent.at[at, matrix],
            stat_landed.at[at, me],
            gram_device(matrix),
        )

    def stat_own(at, matrix):
        source = (stats_ref, bases_ref)[at]
        return pltpu.make_async_copy(source.at[matrix], stat_buf.at[at, me], stat_landed.at[at, me])

    def gram_copy(matrix):
        return ring.copy(
            segs.at[matrix // 4, matrix % 4],
            gram_buf.at[me],
            gram_sent.at[matrix],
            gram_landed.at[me],
            gram_device(matrix),
        )

    def finish(k):
        lower, size = chunks[k]
        value = ring.four(k)
        own_ref[lower : lower + size] = value
        if k == count - 1:
            return
        layer = lower // layer_rows
        for segment, (low_row, high_row) in enumerate(bounds):
            piece = value[low_row:high_row].astype(LOW)
            if high_row - low_row < segment_rows:
                blank = jnp.zeros((segment_rows - (high_row - low_row), value.shape[1]), LOW)
                piece = jnp.concatenate([piece, blank], 0)
            matrix = 4 * layer + segment
            segs[layer, segment] = piece

            @pl.when(me != gram_device(matrix))
            def _(matrix=matrix):
                gram_copy(matrix).start()

    @pl.when(now == 0)
    def _():
        greet(everyone)
        route.act(0, 0)
        for matrix in range(matrices):

            @pl.when(me != gram_device(matrix))
            def _(matrix=matrix):
                stat_copy(0, matrix).start()
                stat_copy(1, matrix).start()

            @pl.when(me == gram_device(matrix))
            def _(matrix=matrix):
                stat_own(0, matrix).start()
                stat_own(1, matrix).start()

        grad_rows[...] = jnp.zeros(grad_rows.shape, FULL)
        grad_patch[...] = jnp.zeros(grad_patch.shape, FULL)
        grad_start[...] = jnp.zeros(grad_start.shape, FULL)

    @pl.when(now == 1)
    def _():
        route.act(1, 0)

    @pl.when(now == images)
    def _():
        ring.one(0)

    @pl.when(now == images + 1)
    def _():
        route.act(3, 0)
        ring.two(0)

    @pl.when(now == 2 * images)
    def _():
        ring.one(1)
        route.act(4, 0)
        ring.three(0)

    @pl.when(now == 2 * images + 1)
    def _():
        ring.two(1)
        finish(0)

    weights = weights_ref.at[0]
    vectors = vectors_ref[pl.ds(pl.multiple_of((LAYERS - 1 - step) * 8, 8), 8), :]
    tail = 8 * LAYERS

    @pl.when(image == 0)
    def _():
        unpack_blocks(weights, joint_weight, output_weight, cuts, depth)

    @pl.when(step == 0)
    def _():
        first = lax.broadcasted_iota(jnp.int32, (8, D), 0) == 0
        given = jnp.where(first, grad_feat_ref[pl.ds(core * images + image, 1), :], 0.0)
        grad_class, grad_gain, grad_shift = norm_back(
            final_ref[0, image], vectors_ref[tail + 2 : tail + 3], given
        )
        grad_rows[tail + 2 : tail + 3] += grad_gain[None]
        grad_rows[tail + 3 : tail + 4] += grad_shift[None]
        grad_now[image] = jnp.zeros((TOKENS, D), FULL)
        grad_now[image, HALF_ROW : HALF_ROW + 8] = jnp.where(first, grad_class, 0.0)

    rows = pl.ds(pl.multiple_of(image * TOKENS, 16), TOKENS)
    grad_result = grad_now[image]
    grad_outer = (vectors[5:6] * grad_result).astype(LOW)
    grad_outer_all[rows, :] = grad_outer
    grad_scale_two = jnp.sum(grad_result * saved["outer"][0, 0].astype(FULL), 0, keepdims=True)
    parts = MLP // D
    grad_normed_two = jnp.zeros((TOKENS, D), FULL)
    for part in range(parts):
        columns = slice(part * D, (part + 1) * D)
        grad_activated = dot_nt(grad_outer, weight_rows(weights, cuts, 2, part, parts))
        grad_inner = (grad_activated * saved["slope"][0, 0, :, columns].astype(FULL)).astype(LOW)
        grad_inner_all[rows, columns] = grad_inner
        grad_normed_two = grad_normed_two + dot_nn(
            grad_inner, weight_rows(weights, cuts, 1, part, parts)
        )
    grad_middle_norm, grad_gain_two, grad_shift_two = norm_back(
        saved["middle"][0, 0], vectors[2:3], grad_normed_two
    )
    grad_middle = grad_result + grad_middle_norm
    grad_attended = (vectors[4:5] * grad_middle).astype(LOW)
    grad_attended_all[rows, :] = grad_attended
    grad_scale_one = jnp.sum(grad_middle * saved["attended"][0, 0].astype(FULL), 0, keepdims=True)
    grad_mixed = dot_nn(grad_attended, output_weight[...]).astype(LOW)
    live = live_keys(HALF_ROW)
    rounded = saved["joint"][0, 0]
    queries = (rounded[:, :D].astype(FULL) * HEAD_DIM ** (-0.5)).astype(LOW)
    keys_in, values_in = rounded[:, D : 2 * D], rounded[:, 2 * D :]
    keys_turned = keys_in.astype(FULL).T.astype(LOW)
    turned, grad_keys, grad_values = [], [], []
    low_half = lax.broadcasted_iota(jnp.int32, (TOKENS, LANES), 1) < HEAD_DIM
    for pair in range(D // LANES):
        columns = slice(pair * LANES, (pair + 1) * LANES)
        pair_queries, grad_head = queries[:HALF_ROW, columns], grad_mixed[:HALF_ROW, columns]
        keys_halves = head_halves(keys_in[:, columns].astype(FULL))
        values_halves = head_halves(values_in[:, columns].astype(FULL))
        both_keys, both_values = [], []
        for half in range(2):
            lower = pair * LANES + half * HEAD_DIM
            share = chance(keys_halves[half], pair_queries, live)
            grad_share = dot_nt(values_halves[half], grad_head)
            both_values.append(dot_nn(share.astype(LOW), grad_head))
            grad_scores = (
                share * (grad_share - jnp.sum(share * grad_share, 0, keepdims=True))
            ).astype(LOW)
            both_keys.append(dot_nn(grad_scores, pair_queries))
            turned.append(dot_nn(keys_turned[lower : lower + HEAD_DIM], grad_scores))
        grad_keys.append(jnp.where(low_half, both_keys[0], both_keys[1]))
        grad_values.append(jnp.where(low_half, both_values[0], both_values[1]))
    class_query = by_head(queries[HALF_ROW:].astype(FULL)[:1]).astype(LOW)
    class_grad = by_head(grad_mixed[HALF_ROW:].astype(FULL)[:1]).astype(LOW)
    share = chance(keys_in, class_query, live_keys(CLASS_ROWS))
    grad_share = dot_nt(values_in, class_grad)
    grad_scores = (share * (grad_share - jnp.sum(share * grad_share, 0, keepdims=True))).astype(LOW)
    class_row = jnp.sum(by_head(dot_tn(grad_scores, keys_in)), 0, keepdims=True)
    grad_queries = jnp.concatenate(
        [jnp.concatenate(turned, 0).T, tail_rows_of(class_row)], 0
    ) * HEAD_DIM ** (-0.5)
    grad_joint_all[rows, :D] = grad_queries.astype(LOW)
    grad_joint_all[rows, D : 2 * D] = (
        jnp.concatenate(grad_keys, 1) + dot_nn(grad_scores, class_query)
    ).astype(LOW)
    grad_joint_all[rows, 2 * D :] = (
        jnp.concatenate(grad_values, 1) + dot_nn(share.astype(LOW), class_grad)
    ).astype(LOW)
    grad_normed = dot_nn(grad_joint_all[rows, :], joint_weight[...])
    grad_input_norm, grad_gain_one, grad_shift_one = norm_back(
        saved["inputs"][0, 0], vectors[0:1], grad_normed
    )
    grad_input = grad_middle + grad_input_norm
    grad_now[image] = grad_input
    added = jnp.concatenate(
        [
            grad_gain_one[None],
            grad_shift_one[None],
            grad_gain_two[None],
            grad_shift_two[None],
            grad_scale_one,
            grad_scale_two,
            jnp.zeros((2, D), FULL),
        ],
        0,
    )
    grad_rows[pl.ds(pl.multiple_of((LAYERS - 1 - step) * 8, 8), 8), :] += added

    @pl.when(step == LAYERS - 1)
    def _():
        grad_patch[:, :PIX] += dot_tn(grad_input[:HALF_ROW].astype(LOW), patches_ref[image])
        grad_start[:TOKENS] += grad_input
        grad_rows[tail : tail + 1] += jnp.sum(grad_input[:HALF_ROW], 0, keepdims=True)
        grad_rows[tail + 1 : tail + 2] += grad_input[HALF_ROW : HALF_ROW + 1]

    def pack(packet):
        def flat(name):
            value = saved[name][0]
            return value.reshape(-1, value.shape[-1])

        per = cuts[0], cuts[1] - cuts[0], cuts[2] - cuts[1], cuts[3] - cuts[2]
        groups = 4
        each = total // groups
        for at in range(groups):
            first = at * each
            joint_rows = dot_tn(
                grad_joint_all[:, first * per[0] : (first + each) * per[0]], flat("normed")
            )
            output_rows = dot_tn(
                grad_attended_all[:, first * per[1] : (first + each) * per[1]], flat("mixed")
            )
            inner_rows = dot_tn(
                grad_inner_all[:, first * per[2] : (first + each) * per[2]], flat("normed_two")
            ).astype(LOW)
            outer_rows = dot_tn(
                saved["activated"][0, :, :, first * per[3] : (first + each) * per[3]].reshape(
                    -1, each * per[3]
                ),
                grad_outer_all[...],
            ).astype(LOW)
            for t in range(each):
                joined_rows = jnp.concatenate(
                    [
                        joint_rows[t * per[0] : (t + 1) * per[0]],
                        output_rows[t * per[1] : (t + 1) * per[1]],
                    ],
                    0,
                )
                packet[slot_of(first + t, depth), : cuts[1]] = joined_rows.astype(LOW)
                packet[first + t, cuts[1] : cuts[2]] = inner_rows[t * per[2] : (t + 1) * per[2]]
                packet[first + t, cuts[2] : cuts[3]] = outer_rows[t * per[3] : (t + 1) * per[3]]

    @pl.when(now == images - 1)
    def _():
        route.act(2, 0)

    @pl.when((image == images - 1) & (step == LAYERS - 1))
    def _():
        ring.three(1)
        for rel in range(4):
            ring.die(0, rel).wait_send()

    @pl.when(image == images - 1)
    def _():
        pack(packets.at[lax.rem(step, 2)])

    for k in range(LAYERS - 1):

        @pl.when((image == images - 1) & (step == k))
        def _(k=k):
            ring.begin(k)

    @pl.when((image == images - 1) & (step == LAYERS - 1))
    def _():
        last, table = LAYERS - 1, LAYERS
        ring.begin(last)
        ring.one(last)
        blank = jnp.zeros((LANES - 32, D), FULL)
        turned_rows = jnp.concatenate([grad_rows[...], blank], 0).T
        turned = [grad_patch[:, :D], None, None]
        turned_start = grad_start[...].T
        left = VECTORS_AT - POSITION_AT
        turned[1] = jnp.concatenate([grad_patch[:, D:], turned_start[:, : 2 * D - POSITION_AT]], 1)
        turned[2] = jnp.concatenate([turned_start[:, 2 * D - POSITION_AT : left], turned_rows], 1)
        columns = D // total
        for block in range(3):
            for device in range(total):
                piece = turned[block][device * columns : (device + 1) * columns]
                piece = jnp.concatenate([piece, jnp.zeros((16 - columns, D), FULL)], 0)
                table_packet[slot_of(device, depth), 16 * block : 16 * block + 16] = piece.astype(LOW)
        ring.begin(table)
        ring.one(table)
        ring.two(last)
        finish(1)
        ring.two(table)
        ring.three(last)
        ring.three(table)
        finish(last)
        finish(table)

        own = own_ref[...]
        lane8 = lax.broadcasted_iota(jnp.int32, (8, LANES), 1)
        squares = jnp.sum(own * own) + jnp.sum(jnp.where(lane8 == 2, squares_ref[...], 0.0)) / 8.0
        square_out[...] = jnp.full((8, LANES), squares)
        square_all[me] = square_out[...]
        copies = [
            push(square_out, square_all.at[me], square_sent.at[at], square_landed.at[at], peer)
            for at, peer in enumerate(everyone)
        ]

        @pl.when(is_gram)
        def _():
            for matrix in range(matrices):

                @pl.when(matrix == chip)
                def _(matrix=matrix):
                    gram_buf[me] = segs[matrix // 4, matrix % 4]

            for source in range(total):
                for at in range(2):
                    view = stat_buf.at[at, source]
                    pltpu.make_async_copy(view, view, stat_landed.at[at, source]).wait()

                @pl.when(source != me)
                def _(source=source):
                    pltpu.make_async_copy(
                        gram_buf.at[source], gram_buf.at[source], gram_landed.at[source]
                    ).wait()

            basis_ref[...] = stat_buf[1]
            blocks = gram_buf[...].reshape(total * segment_rows, gram_buf.shape[2])
            gram = dot_tn(blocks, blocks)
            for source in range(total):
                next_stats_ref[source] = gram[source * own_rows : (source + 1) * own_rows]

        @pl.when(jnp.logical_not(is_gram))
        def _():
            next_stats_ref[...] = jnp.zeros(next_stats_ref.shape, FULL)
            basis_ref[...] = jnp.zeros(basis_ref.shape, FULL)
            stat_buf[0] = jnp.zeros(stat_buf.shape[1:], FULL)

        for copy in copies:
            copy.wait_recv()
        norm = jnp.sqrt(jnp.sum(square_all[...], 0))
        norm_ref[...] = norm
        clip = jnp.minimum(1.0, CLIP_MAX / (norm + 1e-06))[:1, :1]
        scale = (1.0 - BETA_STAT) * (clip * clip)
        for source in range(total):
            next_stats_ref[source] = BETA_STAT * stat_buf[0, source] + scale * next_stats_ref[source]

        route.act(5, 0)
        for copy in copies:
            copy.wait_send()
        for k in range(count):
            ring.sent(k, k != 0)
        for matrix in range(matrices):

            @pl.when(me != gram_device(matrix))
            def _(matrix=matrix):
                stat_copy(0, matrix).wait_send()
                stat_copy(1, matrix).wait_send()
                gram_copy(matrix).wait_send()


def backward(
    squares, patches, vectors, blocks, final, grad_feat, saved, stats, bases, bases_low, devices
):
    images = patches.shape[0]
    depth = devices // 8
    bounds = layer_bounds(devices)
    layer_rows = blocks.shape[2]
    cuts = [lower for lower, upper in bounds][1:] + [layer_rows]
    matrices, own_rows = stats.shape[:2]
    segment_rows = -(-max(high - low for low, high in bounds) // 16) * 16
    table_size = 3 * (-(-(D // devices) // 16) * 16)
    rows = LAYERS * layer_rows + table_size
    shape = jax.ShapeDtypeStruct
    dma = pltpu.SemaphoreType.DMA
    vmem = pl.BlockSpec(memory_space=pltpu.VMEM)
    anywhere = pl.BlockSpec(memory_space=pl.ANY)

    def of_layer(*dims):
        return pl.BlockSpec(
            (1,) + dims, lambda step, image: (LAYERS - 1 - step,) + (0,) * len(dims)
        )

    def of_saved(name):
        width = saved_widths()[name][0]
        if name in PER_LAYER:
            return of_layer(images, TOKENS, width)
        return pl.BlockSpec(
            (1, 1, TOKENS, width), lambda step, image: (LAYERS - 1 - step, image, 0, 0)
        )

    all_rows = images * TOKENS
    count = LAYERS + 1
    return pl.pallas_call(
        functools.partial(backward_kernel, cuts, bounds, depth),
        grid=(LAYERS, images),
        out_shape=(
            shape((rows, D), FULL),
            shape((8, LANES), FULL),
            shape((devices, own_rows, D), FULL),
            shape((devices, own_rows, D), FULL),
            shape((devices,) + bases_low.shape, LOW),
        ),
        in_specs=[
            vmem,
            anywhere,
            anywhere,
            anywhere,
            vmem,
            of_layer(*blocks.shape[1:]),
            vmem,
            vmem,
            vmem,
        ]
        + [of_saved(name) for name in SAVED],
        out_specs=(vmem,) * 4 + (anywhere,),
        scratch_shapes=[
            pltpu.VMEM((images, TOKENS, D), FULL),
            pltpu.VMEM((3 * D, D), LOW),
            pltpu.VMEM((D, D), LOW),
            pltpu.VMEM((all_rows, D), LOW),
            pltpu.VMEM((all_rows, MLP), LOW),
            pltpu.VMEM((all_rows, D), LOW),
            pltpu.VMEM((all_rows, 3 * D), LOW),
            pltpu.VMEM((D, POSITION_AT), FULL),
            pltpu.VMEM((D, D), FULL),
            pltpu.VMEM((32, D), FULL),
            pltpu.VMEM((2, devices, layer_rows, D), LOW),
            pltpu.VMEM((devices, table_size, D), LOW),
            pltpu.VMEM((4 * depth, rows, D), LOW),
            pltpu.VMEM((depth, rows, D), LOW),
            pltpu.VMEM((depth, rows, D), LOW),
            pltpu.VMEM((depth, rows, D), LOW),
            pltpu.VMEM((depth, rows, D), LOW),
            pltpu.VMEM((2, devices, own_rows, D), FULL),
            pltpu.VMEM((8, LANES), FULL),
            pltpu.VMEM((devices, 8, LANES), FULL),
            pltpu.VMEM((LAYERS, 4, segment_rows, D), LOW),
            pltpu.VMEM((devices, segment_rows, D), LOW),
            dma((count, 4)),
            dma((count, 4)),
            dma((count, 4)),
            dma((count, 4)),
            dma((count, depth)),
            dma((count, depth)),
            dma((2, matrices)),
            dma((2, devices)),
            dma((matrices,)),
            dma((devices,)),
            dma((devices - 1,)),
            dma((devices - 1,)),
        ]
        + route_sems(1, depth),
        compiler_params=params(3, 63 << 20),
        name="backward",
    )(squares, stats, bases, bases_low, patches, blocks, vectors, final, grad_feat, *saved)


def own_table(rows, columns):
    joint = rows.reshape(3, -1, D)[:, :columns].transpose(1, 0, 2).reshape(columns, -1)
    position = joint[:, POSITION_AT : POSITION_AT + SEQ]
    layer_rows = joint[:, VECTORS_AT : VECTORS_AT + 8 * LAYERS].reshape(columns, LAYERS, 8)
    return jnp.concatenate(
        [
            joint[:, :PIX],
            position[:, SEQ - 1 :],
            position[:, : SEQ - 1],
            layer_rows[:, :, :6].reshape(columns, -1),
            joint[:, VECTORS_AT + 8 * LAYERS : VECTORS_AT + 8 * LAYERS + 4],
        ],
        1,
    ).T


def tail_fast(
    gathered,
    layer_stats,
    layer_bases,
    owners,
    embedding,
    layers,
    layers_first,
    layers_second,
    teacher_layers,
    devices,
):
    own, norm, full_stats, full_bases, bases_all = gathered
    own_rows = layer_stats.shape[2]
    matrices = owners.shape[0]
    count = layers.shape[0] * layers.shape[1]
    layer_outs = soap(
        norm,
        own[:count],
        bases_all,
        layers,
        layers_first,
        layers_second,
        teacher_layers,
        layer_bounds(devices),
    )
    grad_embed = own_table(own[count:], embedding.shape[1])
    stats_own, bases_own = renew_own(full_stats, full_bases, matrices)
    bases_own = jnp.where(
        owners[:, None, None] >= 0, bases_own, layer_bases.reshape(matrices, own_rows, D)
    )
    return (
        norm[0, 0],
        grad_embed,
        layer_outs,
        stats_own.reshape(layer_stats.shape),
        bases_own.reshape(layer_bases.shape),
    )


def split_dot(left, basis, contract):
    high = left.astype(LOW)
    rest = (left - high.astype(FULL)).astype(LOW)
    dims = (contract, ((), ()))
    return lax.dot_general(high, basis, dims, preferred_element_type=FULL) + lax.dot_general(
        rest, basis, dims, preferred_element_type=FULL
    )


def soap_kernel(
    bounds,
    depth,
    norm_ref,
    grads_ref,
    bases_ref,
    weights_ref,
    first_ref,
    second_ref,
    teacher_ref,
    first_out_ref,
    second_out_ref,
    weights_out_ref,
    teacher_out_ref,
    basis,
):
    layer = pl.program_id(0)
    devices = bases_ref.shape[0]
    own_rows = bases_ref.shape[1] // 4
    clip = jnp.minimum(1.0, CLIP_MAX / (norm_ref[0:1, 0:1] + 1e-06))
    grads = grads_ref[...] * clip
    group = 4
    firsts, seconds, updates = [], [], []
    for segment, (low_row, high_row) in enumerate(bounds):
        for at in range(0, devices, group):
            pieces = [
                bases_ref[slot_of(at + t, depth)][segment * own_rows : (segment + 1) * own_rows]
                for t in range(group)
            ]
            basis[at * own_rows : (at + group) * own_rows] = jnp.concatenate(
                [piece.astype(FULL) for piece in pieces], 0
            ).astype(LOW)
        rotated = split_dot(grads[low_row:high_row], basis[...], ((1,), (0,)))
        first_new = BETA_ONE * first_ref[0, low_row:high_row] + (1.0 - BETA_ONE) * rotated
        second_new = (
            BETA_TWO * second_ref[0, low_row:high_row] + (1.0 - BETA_TWO) * rotated * rotated
        )
        direction = (
            first_new
            / (1.0 - BETA_ONE**STEP)
            / (jnp.sqrt(second_new / (1.0 - BETA_TWO**STEP)) + ADAM_EPSILON)
        )
        firsts.append(first_new)
        seconds.append(second_new)
        updates.append(split_dot(direction, basis[...], ((1,), (1,))))
    first_out_ref[0] = jnp.concatenate(firsts, 0)
    second_out_ref[0] = jnp.concatenate(seconds, 0)
    weight = weights_ref[0]
    fresh = weight - RATE_MATRIX * (jnp.concatenate(updates, 0) + WEIGHT_DECAY * weight)
    weights_out_ref[0] = fresh
    teacher_out_ref[0] = follow(teacher_ref[0], fresh)


def soap(norm, grads, bases_all, weights, first, second, teacher, bounds):
    devices = bases_all.shape[0]
    rows = weights.shape[1]
    own_rows = bases_all.shape[1] // LAYERS
    vmem = pl.BlockSpec(memory_space=pltpu.VMEM)
    block = pl.BlockSpec((1, rows, D), lambda layer: (layer, 0, 0))
    return pl.pallas_call(
        functools.partial(soap_kernel, bounds, devices // 8),
        grid=(LAYERS,),
        out_shape=[jax.ShapeDtypeStruct(weights.shape, FULL)] * 4,
        in_specs=[
            vmem,
            pl.BlockSpec((rows, D), lambda layer: (layer, 0)),
            pl.BlockSpec((devices, own_rows, D), lambda layer: (0, layer, 0)),
            block,
            block,
            block,
            block,
        ],
        out_specs=[block] * 4,
        scratch_shapes=[pltpu.VMEM((D, D), LOW)],
        compiler_params=pltpu.CompilerParams(vmem_limit_bytes=32 << 20),
        name="soap",
    )(norm, grads, bases_all, weights, first, second, teacher)


def per_device(
    patches,
    valid_mask,
    owners,
    embedding,
    embedding_first,
    embedding_second,
    layers,
    layers_first,
    layers_second,
    layer_stats,
    layer_bases,
    head_hidden,
    hidden_first,
    hidden_second,
    head_last,
    last_first,
    last_second,
    protos,
    protos_first,
    protos_second,
    teacher_embedding,
    teacher_layers,
    teacher_hidden,
    teacher_last,
    teacher_protos,
    centre,
):
    devices = lax.axis_size(AXIS)
    device_index = lax.axis_index(AXIS)
    fast = 2 * head_hidden.shape[0] == LANES
    if not fast:
        embed_table, teacher_table = (
            lax.all_gather(embedding.astype(LOW), AXIS, axis=1, tiled=True),
            lax.all_gather(teacher_embedding.astype(LOW), AXIS, axis=1, tiled=True),
        )
        layer_full, teacher_full = (
            lax.all_gather(layers.astype(LOW), AXIS, axis=1, tiled=True),
            lax.all_gather(teacher_layers.astype(LOW), AXIS, axis=1, tiled=True),
        )
    if not fast:
        bases_full = lax.all_gather(layer_bases.astype(LOW), AXIS, axis=2, tiled=True).astype(
            layer_bases.dtype
        )
        stats_full = lax.all_gather(layer_stats.astype(LOW), AXIS, axis=2, tiled=True).astype(
            layer_stats.dtype
        )
    if fast:
        feature_rows, final_rows, vectors, layer_full, last_all, part, *saved = fetch_forward(
            patches,
            embedding,
            teacher_embedding,
            layers,
            teacher_layers,
            head_last,
            teacher_last,
            head_hidden,
            devices,
        )
    else:
        features, layer_inputs, final_state = backbone(patches, embed_table, layer_full, devices)
        teacher_features, unused_inputs, unused_final = backbone(
            patches, teacher_table, teacher_full, devices
        )
    if fast:
        (
            loss_sum,
            loss_count,
            squares,
            grad_hidden,
            grad_last,
            grad_protos,
            grad_features,
            next_centre,
        ) = head_fast(
            feature_rows,
            valid_mask,
            head_hidden,
            protos,
            teacher_hidden,
            teacher_protos,
            centre,
            part,
            last_all,
            devices,
        )
    else:
        (
            loss_sum,
            loss_count,
            grad_hidden,
            grad_last,
            grad_protos,
            grad_features,
            next_centre,
        ) = head_slow(
            features,
            teacher_features,
            valid_mask,
            head_hidden,
            head_last,
            protos,
            teacher_hidden,
            teacher_last,
            teacher_protos,
            centre,
            device_index,
        )
    if fast:
        matrices, own_rows = owners.shape[0], layer_stats.shape[2]
        gathered = backward(
            squares,
            patches,
            vectors,
            layer_full,
            final_rows,
            grad_features,
            saved,
            layer_stats.reshape(matrices, own_rows, D),
            layer_bases.reshape(matrices, own_rows, D),
            layer_bases.reshape(matrices * own_rows, D).astype(LOW),
            devices,
        )
    else:
        grad_table, grad_layers = backbone_back(
            patches,
            embed_table,
            layer_full,
            layer_inputs,
            final_state,
            grad_features,
            devices,
            unchanged,
        )
    bounds = layer_bounds(devices)
    if fast:
        grad_norm, grad_embed, layer_outs, stats_own, bases_own = tail_fast(
            gathered,
            layer_stats,
            layer_bases,
            owners,
            embedding,
            layers,
            layers_first,
            layers_second,
            teacher_layers,
            devices,
        )
    else:
        summed = (
            lax.psum_scatter(grad_table, AXIS, scatter_dimension=1, tiled=True),
            lax.psum_scatter(grad_layers, AXIS, scatter_dimension=1, tiled=True),
        )
        grad_embed = summed[0]
        grad_layers_own = summed[1]
        grams = jnp.stack(
            [
                matmul_high(
                    "lcd,lce->lde",
                    grad_layers_own[:, lower_row:upper_row],
                    grad_layers_own[:, lower_row:upper_row],
                )
                for lower_row, upper_row in bounds
            ],
            1,
        )
        squares = (
            jnp.sum(grad_embed * grad_embed)
            + jnp.sum(grad_layers_own * grad_layers_own)
            + jnp.sum(grad_hidden * grad_hidden)
            + jnp.sum(grad_last * grad_last)
            + jnp.sum(grad_protos * grad_protos)
        )
        totals = lax.psum((squares, grams), AXIS)
        grad_norm = jnp.sqrt(totals[0])
        clip_factor = jnp.minimum(1.0, CLIP_MAX / (grad_norm + 1e-06))
        next_stats = (
            BETA_STAT * stats_full + (1.0 - BETA_STAT) * (clip_factor * clip_factor) * totals[1]
        )
    clip_factor = jnp.minimum(1.0, CLIP_MAX / (grad_norm + 1e-06))
    rows = jnp.arange(embedding.shape[0])[:, None]
    is_matrix = rows < PIX + SEQ
    embed_out = adam_step(
        embedding,
        clip_factor * grad_embed,
        embedding_first,
        embedding_second,
        jnp.where(is_matrix, RATE_MATRIX, RATE_VECTOR),
        jnp.where(is_matrix, WEIGHT_DECAY, 0.0),
    )
    hidden_out = adam_step(
        head_hidden,
        clip_factor * grad_hidden,
        hidden_first,
        hidden_second,
        RATE_MATRIX,
        WEIGHT_DECAY,
    )
    last_out = adam_step(
        head_last, clip_factor * grad_last, last_first, last_second, RATE_MATRIX, WEIGHT_DECAY
    )
    protos_out = adam_step(
        protos, clip_factor * grad_protos, protos_first, protos_second, RATE_MATRIX, WEIGHT_DECAY
    )
    if fast:
        next_layers_first, next_layers_second, next_layers, next_teacher_layers = layer_outs
    else:
        firsts, seconds, weights_new = ([], [], [])
        for segment, (lower_row, upper_row) in enumerate(bounds):
            basis = bases_full[:, segment]
            weight_block = layers[:, lower_row:upper_row]
            rotated = matmul_high(
                "lcd,ldk->lck", clip_factor * grad_layers_own[:, lower_row:upper_row], basis
            )
            first_new = BETA_ONE * layers_first[:, lower_row:upper_row] + (1.0 - BETA_ONE) * rotated
            second_new = (
                BETA_TWO * layers_second[:, lower_row:upper_row] + (1.0 - BETA_TWO) * rotated * rotated
            )
            direction = (
                first_new
                / (1.0 - BETA_ONE**STEP)
                / (jnp.sqrt(second_new / (1.0 - BETA_TWO**STEP)) + ADAM_EPSILON)
            )
            update = matmul_high("lck,ldk->lcd", direction, basis)
            firsts.append(first_new)
            seconds.append(second_new)
            weights_new.append(weight_block - RATE_MATRIX * (update + WEIGHT_DECAY * weight_block))
        next_layers = jnp.concatenate(weights_new, 1)
        next_layers_first, next_layers_second = jnp.concatenate(firsts, 1), jnp.concatenate(seconds, 1)
        next_teacher_layers = follow(teacher_layers, next_layers)
    if not fast:
        flat_stats = next_stats.reshape(-1, D, D)
        flat_bases = bases_full.reshape(-1, D, D)

        def renew_owned(operands):
            return lax.cond(operands[2] == device_index, renew, nothing, operands[0], operands[1])

        renewed = lax.psum(lax.map(renew_owned, (flat_stats, flat_bases, owners)), AXIS)
        next_bases = jnp.where(owners[:, None, None] >= 0, renewed, flat_bases).reshape(
            bases_full.shape
        )
        own_rows = layer_stats.shape[2]
        stats_own = lax.dynamic_slice_in_dim(next_stats, device_index * own_rows, own_rows, 2)
        bases_own = lax.dynamic_slice_in_dim(next_bases, device_index * own_rows, own_rows, 2)
    return (
        loss_sum,
        loss_count,
        grad_norm,
        embed_out[0],
        embed_out[1],
        embed_out[2],
        next_layers_first,
        next_layers_second,
        next_layers,
        stats_own,
        bases_own,
        hidden_out[0],
        hidden_out[1],
        hidden_out[2],
        last_out[0],
        last_out[1],
        last_out[2],
        protos_out[0],
        protos_out[1],
        protos_out[2],
        follow(teacher_embedding, embed_out[2]),
        next_teacher_layers,
        follow(teacher_hidden, hidden_out[2]),
        follow(teacher_last, last_out[2]),
        follow(teacher_protos, protos_out[2]),
        next_centre,
    )


def solution(mesh):
    placed = (
        P(AXIS, None, None),
        P(),
        P(),
        P(None, AXIS),
        P(None, AXIS),
        P(None, AXIS),
        P(None, AXIS, None),
        P(None, AXIS, None),
        P(None, AXIS, None),
        P(None, None, AXIS, None),
        P(None, None, AXIS, None),
        P(AXIS, None),
        P(AXIS, None),
        P(AXIS, None),
        P(None, AXIS),
        P(None, AXIS),
        P(None, AXIS),
        P(None, AXIS),
        P(None, AXIS),
        P(None, AXIS),
        P(None, AXIS),
        P(None, AXIS, None),
        P(AXIS, None),
        P(None, AXIS),
        P(None, AXIS),
        P(AXIS),
    )
    return jax.shard_map(
        per_device,
        mesh=mesh,
        in_specs=placed,
        out_specs=(
            P(),
            P(),
            P(),
            P(None, AXIS),
            P(None, AXIS),
            P(None, AXIS),
            P(None, AXIS, None),
            P(None, AXIS, None),
            P(None, AXIS, None),
            P(None, None, AXIS, None),
            P(None, None, AXIS, None),
            P(AXIS, None),
            P(AXIS, None),
            P(AXIS, None),
            P(None, AXIS),
            P(None, AXIS),
            P(None, AXIS),
            P(None, AXIS),
            P(None, AXIS),
            P(None, AXIS),
            P(None, AXIS),
            P(None, AXIS, None),
            P(AXIS, None),
            P(None, AXIS),
            P(None, AXIS),
            P(AXIS),
        ),
        check_vma=False,
    )
```
